32 devices in a mesh: img: 8 (over z, core), row: 4 (over y, x).
Axes of the slice: x: 2, y: 2, z: 4, core: 2. Of those that a mesh axis runs over, the one named last changes fastest.
Arguments:
- patches: bfloat16 [16, 32, 32, 192], P('img', 'row'), may hold values from -6 to 6
- valid_mask: int32 [16, 32, 32], P('img'), may hold values from 0 to 1, as said below
- norm_gains: float32 [2, 192], replicated, may hold values from 0.5 to 1.5
- w_u: bfloat16 [192, 192], P('row', 'img'), may hold values from -0.4375 to 0.4375
- decay_rate: bfloat16 [192, 64], P('row', 'img'), may hold values from 0.019897461 to 1
- out_coef: bfloat16 [192, 64], P('row', 'img'), may hold values from -0.8984375 to 0.8984375
- w_qkv: bfloat16 [192, 576], P('row', 'img'), may hold values from -0.4375 to 0.4375
- w_o: bfloat16 [192, 192], P('row', 'img'), may hold values from -1.75 to 1.75
- w_fc1: bfloat16 [192, 768], P('row', 'img'), may hold values from -0.4375 to 0.4375
- w_fc2: bfloat16 [768, 192], P('row', 'img'), may hold values from -0.21875 to 0.21875
- cotangent: bfloat16 [16, 32, 32, 192], P('img', 'row'), may hold values from -6 to 6
Outputs:
- block_out: bfloat16 [16, 32, 32, 192], P('img', 'row')
- grad_patches: bfloat16 [16, 32, 32, 192], P('img', 'row')
- grad_gain_one: float32 [192], replicated
- grad_gain_two: float32 [192], replicated
- grad_w_u: float32 [192, 192], P('row', 'img')
- grad_decay: float32 [192, 64], P('row', 'img')
- grad_coef: float32 [192, 64], P('row', 'img')
- grad_w_qkv: float32 [192, 576], P('row', 'img')
- grad_w_o: float32 [192, 192], P('row', 'img')
- grad_w_fc1: float32 [192, 768], P('row', 'img')
- grad_w_fc2: float32 [768, 192], P('row', 'img')
The draws below stay inside these ranges and needn't reach their ends.
Inputs may be any that keep to these rules, and one draw needn't show every extreme that they name: `valid_mask`: the valid slots of an image are those in its first h rows or in its first w columns (or both), with 16 <= h, w <= 31 drawn for each image.
All inputs are finite; a program needn't handle non-finite values.
Results may differ from the reference program's by a relative error of at most 0.025.
The reference program's roundings to bfloat16 on the way count: a program that leaves them out, or rounds other values in their place, can miss the bound.
Values may be sent and summed in bfloat16 or wider, within the bound.
No kernel may reach another device: no remote copies, remote signals or barrier semaphores. Data moves between devices by JAX's collectives and lax.ppermute only.
A program may use at most 128 MiB of HBM per device.

```python
import math
from functools import partial
import jax
import jax.numpy as jnp
import numpy as np
from jax import lax

D = 192
HEADS = 3
HEAD_DIM = 64
FF = 768
STATE = 16
GRID = 32
IMAGES = 16


def draw_valid_mask(key, part):
    key = jax.random.fold_in(key, 11)
    key_height, key_width = jax.random.split(key, 2)
    heights = jax.random.randint(key_height, (IMAGES,), GRID // 2, GRID)
    widths = jax.random.randint(key_width, (IMAGES,), GRID // 2, GRID)
    positions = jnp.arange(GRID)
    in_rows = positions[None, :, None] < heights[:, None, None]
    in_cols = positions[None, None, :] < widths[:, None, None]
    inside = in_rows | in_cols
    return inside.astype(jnp.int32)


def levels(rng, extent, cuts, low, top_value):
    def one(position, shards_of):
        steps = jax.random.uniform(jax.random.fold_in(jax.random.fold_in(rng, 6), position), (shards_of,), jnp.float32, low / len(cuts), top_value / len(cuts))
        return jnp.repeat(jnp.exp(steps), extent[position] // shards_of).reshape((-1,) + (1,) * (len(extent) - position - 1))

    loudness = one(*cuts[0])
    for cut in cuts[1:]:
        loudness = loudness * one(*cut)
    return loudness


def scatter_about(key, shape, scale, most, cuts=(), kind=jnp.bfloat16):
    level = levels(key, shape, cuts, -0.22, 0.18) if cuts else 1.0
    values = jax.random.normal(key, shape, jnp.float32) * scale * level
    return jnp.minimum(jnp.maximum(values, -most), most).astype(kind)


def setup_inputs(seed: int = 0) -> dict:
    streams_of = jax.random.split(jax.random.key(seed), 12)
    return {
        "patches": scatter_about(streams_of[0], (IMAGES, GRID, GRID, D), 1.0, 6.0, ((0, 8), (1, 4))),
        "valid_mask": draw_valid_mask(jax.random.fold_in(streams_of[11], 71), 0),
        "norm_gains": jnp.clip(1.0 + 0.1 * jax.random.normal(streams_of[2], (2, D), jnp.float32), 0.5, 1.5),
        "w_u": scatter_about(streams_of[3], (D, D), D ** -0.5, 0.4375, ((0, 4), (1, 8))),
        "decay_rate": jnp.clip(jnp.exp(math.log(1.0) - 3.9171631 * jax.random.uniform(streams_of[4], (D, 4 * STATE), jnp.float32) ** levels(streams_of[4], (D, 4 * STATE), ((0, 4), (1, 8)), -0.2, 0.2)), 0.019897461, 1.0).astype(jnp.bfloat16),
        "out_coef": scatter_about(streams_of[5], (D, 4 * STATE), 0.15, 0.8984375, ((0, 4), (1, 8))),
        "w_qkv": scatter_about(streams_of[6], (D, 3 * D), D ** -0.5, 0.4375, ((0, 4), (1, 8))),
        "w_o": scatter_about(streams_of[7], (D, D), (D // 16) ** -0.5, 1.75, ((0, 4), (1, 8))),
        "w_fc1": scatter_about(streams_of[8], (D, FF), D ** -0.5, 0.4375, ((0, 4), (1, 8))),
        "w_fc2": scatter_about(streams_of[9], (FF, D), FF ** -0.5, 0.21875, ((0, 4), (1, 8))),
        "cotangent": scatter_about(streams_of[10], (IMAGES, GRID, GRID, D), 1.0, 6.0, ((0, 8), (1, 4))),
    }


@jax.custom_vjp
def low(v):
    return lax.optimization_barrier(v.astype(jnp.bfloat16)).astype(jnp.float32)

@jax.custom_vjp
def low_back(v):
    return v

def low_keep(v):
    return (low(v), None)

def low_pass(kept, grad):
    return (grad,)

def back_keep(v):
    return (v, None)

def back_low(kept, grad):
    return (low(grad),)
low.defvjp(low_keep, low_pass)
low_back.defvjp(back_keep, back_low)
HIGHEST = lax.Precision.HIGHEST

def layer_norm(values, gain):
    center = values - lax.optimization_barrier(jnp.mean(values, -1, keepdims=True))
    spread = lax.optimization_barrier(jnp.mean(center * center, -1, keepdims=True))
    return center * lax.rsqrt(spread + 1e-05) * gain

def kernels(rate_values, coef_values):
    lag_steps = jnp.arange(GRID, dtype=jnp.float32)
    powers = jnp.exp(-rate_values[None, :, :] * lag_steps[:, None, None])
    kernel_table = lax.optimization_barrier(jnp.sum((coef_values[None, :, :] * powers).reshape(GRID, rate_values.shape[0], 4, STATE), -1))
    offset = np.abs(np.arange(GRID)[:, None] - np.arange(GRID)[None, :])
    lower_part = (np.arange(GRID)[:, None] >= np.arange(GRID)[None, :])[:, :, None]
    upper_part = (np.arange(GRID)[:, None] <= np.arange(GRID)[None, :])[:, :, None]
    picked = kernel_table[offset]
    across = jnp.where(lower_part, picked[:, :, :, 0], 0.0) + jnp.where(upper_part, picked[:, :, :, 1], 0.0)
    downward = jnp.where(lower_part, picked[:, :, :, 2], 0.0) + jnp.where(upper_part, picked[:, :, :, 3], 0.0)
    return (across, downward)

def attend(block):
    queries, key_rows, value_rows, usable = block
    scores = low_back(jnp.einsum('qhe,khe->hqk', queries, key_rows, precision=HIGHEST))
    scores = jnp.where(usable[None, None, :] > 0, scores, -1e+30)
    weights = low(jax.nn.softmax(scores, axis=-1))
    return jnp.einsum('hqk,khe->qhe', weights, value_rows, precision=HIGHEST)

def forward(source, norm_gains, w_u, rate_values, coef_values, w_qkv, w_o, w_fc1, w_fc2, valid):
    image_count = source.shape[0]
    slot_masks = valid[..., None]
    first_low = low(layer_norm(source, norm_gains[0]))
    mixed_low = low(low_back(jnp.einsum('bijd,de->bije', first_low, w_u, precision=HIGHEST) * slot_masks))
    across, downward = kernels(rate_values, coef_values)
    across = low(across)
    downward = low(downward)
    along_rows = jnp.einsum('tsc,bisc->bitc', across, mixed_low, precision=HIGHEST)
    along_cols = low(jnp.einsum('tsc,bsjc->btjc', downward, low_back(mixed_low), precision=HIGHEST))
    scanned = low(low_back((along_rows + along_cols) * slot_masks))
    triple = jnp.einsum('bijd,de->bije', scanned, w_qkv, precision=HIGHEST)
    head_shape = (image_count, GRID * GRID, HEADS, HEAD_DIM)
    queries = low(low_back(triple[..., :D] * HEAD_DIM ** (-0.5))).reshape(head_shape)
    key_rows = low(low_back(triple[..., D:2 * D])).reshape(head_shape)
    value_rows = low(low_back(triple[..., 2 * D:])).reshape(head_shape)
    attended = lax.map(jax.checkpoint(attend), (queries, key_rows, value_rows, valid.reshape(image_count, GRID * GRID)))
    attended = low(low_back(attended.reshape(source.shape)))
    branch = low_back(jnp.einsum('bijd,de->bije', attended, w_o, precision=HIGHEST))
    middle = source + branch * slot_masks
    second_low = low(layer_norm(middle, norm_gains[1]))
    pre_act = low_back(jnp.einsum('bijd,df->bijf', second_low, w_fc1, precision=HIGHEST))
    hidden = low(jax.nn.gelu(pre_act, approximate=False))
    return middle + low_back(jnp.einsum('bijf,fd->bijd', hidden, w_fc2, precision=HIGHEST))

def reference(patches, valid_mask, norm_gains, w_u, decay_rate, out_coef, w_qkv, w_o, w_fc1, w_fc2, cotangent):
    valid = valid_mask.astype(jnp.float32)
    inputs = (patches.astype(jnp.float32), norm_gains, w_u.astype(jnp.float32), decay_rate.astype(jnp.float32), out_coef.astype(jnp.float32), w_qkv.astype(jnp.float32), w_o.astype(jnp.float32), w_fc1.astype(jnp.float32), w_fc2.astype(jnp.float32))
    result, pull_back = jax.vjp(partial(forward, valid=valid), *inputs)
    gradients = pull_back(cotangent.astype(jnp.float32))
    return (result.astype(jnp.bfloat16), gradients[0].astype(jnp.bfloat16), gradients[1][0], gradients[1][1], gradients[2], gradients[3], gradients[4], gradients[5], gradients[6], gradients[7], gradients[8])
```

```python
import jax
import jax.numpy as jnp
import numpy as np
from jax import lax
from jax.experimental import pallas as pl
from jax.experimental.pallas import tpu as pltpu
from jax.sharding import Mesh
from jax.sharding import PartitionSpec as P

HEADS = 3
HEAD_DIM = 64
STATE = 16
GRID = 32
SLOTS = GRID * GRID
OWN = SLOTS // 2
D = HEADS * HEAD_DIM
FF = 4 * D
LANES = 128
TILE = HEADS * LANES
LAGS = 2 * GRID
CENTER = GRID - 1
EPS = 1e-05
BF16 = jnp.bfloat16
F32 = jnp.float32


def late_layout(parts):
    a_u, a_r, a_q = D // parts, 4 * STATE // parts, 3 * D // parts
    return a_u, a_r, a_q, (0, a_u, a_u + a_r, a_u + 2 * a_r)


def late_selections(parts):
    a_u, a_r, a_q, (o_u, o_r, o_c, o_q) = late_layout(parts)
    sel_u = np.zeros((parts, LANES, D), np.float32)
    sel_rc = np.zeros((parts, LANES, LANES), np.float32)
    full = np.zeros((parts, LANES, 3, TILE), np.float32)
    for m in range(parts):
        for col in range(a_u):
            sel_u[m, o_u + col, m * a_u + col] = 1
        for col in range(a_r):
            sel_rc[m, o_r + col, m * a_r + col] = 1
            sel_rc[m, o_c + col, 4 * STATE + m * a_r + col] = 1
        for col in range(a_q):
            whole = m * a_q + col
            third, rest = divmod(whole, D)
            head, lane = divmod(rest, HEAD_DIM)
            full[m, o_q + col, third, head * LANES + lane] = 1
    spans = []
    for third in range(3):
        used = [m for m in range(parts) if full[m, :, third].any()]
        spans.append((min(used), max(used) + 1))
    width = max(stop - start for start, stop in spans)
    starts = [min(start, parts - width) for start, _ in spans]
    sel_q = np.stack(
        [full[s : s + width, :, third].reshape(width * LANES, TILE) for third, s in enumerate(starts)]
    )
    return (
        sel_u.reshape(parts * LANES, D).astype(BF16),
        sel_rc.reshape(parts * LANES, LANES).astype(BF16),
        sel_q.astype(BF16),
        starts,
        width,
    )


def early_selections(parts):
    a_1, a_o = FF // parts, D // parts
    half = parts // 2
    sel_1 = np.zeros((half, LANES, FF // 2), np.float32)
    sel_o = np.zeros((parts, LANES, D), np.float32)
    sel_2 = np.zeros((4, parts, LANES, D), np.float32)
    for m in range(half):
        for col in range(a_1):
            sel_1[m, col, m * a_1 + col] = 1
    for m in range(parts):
        for col in range(a_o):
            sel_o[m, a_1 + col, m * a_o + col] = 1
            for g in range(4):
                sel_2[g, m, g * a_o + col, m * a_o + col] = 1
    return (
        sel_1.reshape(half * LANES, FF // 2).astype(BF16),
        sel_o.reshape(parts * LANES, D).astype(BF16),
        sel_2.reshape(4, parts * LANES, D).astype(BF16),
    )


def dot(a, b):
    return lax.dot_general(a, b, (((1,), (0,)), ((), ())), preferred_element_type=F32)


def dot_nt(a, b):
    return lax.dot_general(a, b, (((1,), (1,)), ((), ())), preferred_element_type=F32)


def dot_tn(a, b):
    return lax.dot_general(a, b, (((0,), (0,)), ((), ())), preferred_element_type=F32)


def normalise(values):
    center = values - jnp.mean(values, -1, keepdims=True)
    spread = jnp.mean(center * center, -1, keepdims=True)
    inverse = lax.rsqrt(spread + EPS)
    return center * inverse, inverse


def norm_back(grad, gain, unit, inverse):
    scaled = grad * gain
    first = jnp.mean(scaled, -1, keepdims=True)
    second = jnp.mean(scaled * unit, -1, keepdims=True)
    return inverse * (scaled - first - unit * second)


def widen(mask):
    return jnp.concatenate([mask, mask[:, : D - LANES]], axis=1)


def put_lanes(ref, rows, values):
    ref[0, rows, :] = values[:, :LANES]
    ref[1, rows, : D - LANES] = values[:, LANES:]


def block_sum(src, table, way, lane, first, count, step, offset, sublane, sign):
    total = [None] * count
    for base in range(0, GRID, 8):
        low, high = -(base + 7), count - 1 - base
        coef = {
            lag: table[way, lane, first * sign + (lag * sign + CENTER)]
            for lag in range(low, high + 1)
        }
        for s in range(base, base + 8):
            x = src[lane, pl.ds(pl.multiple_of(s * step + sublane, 8), 8), :]
            for t in range(count):
                term = coef[t - s] * x
                total[t] = term if total[t] is None else total[t] + term
    return total


def compiler(limit=60 << 20):
    return pltpu.CompilerParams(vmem_limit_bytes=limit)


VMEM = pl.BlockSpec(memory_space=pltpu.VMEM)
SMEM = pl.BlockSpec(memory_space=pltpu.SMEM)


def scan_kernel(
    starts,
    width,
    core_ref,
    own_ref,
    other_ref,
    mask_ref,
    gains_ref,
    late_ref,
    sel_u_ref,
    sel_rc_ref,
    sel_q_ref,
    q_ref,
    k_ref,
    v_ref,
    scanned_ref,
    mixed_ref,
    table_ref,
    rates_ref,
    wu_ref,
    wqkv_ref,
    first_ref,
    xs,
    xt,
    cols,
    rows,
    scanned_own,
):
    core = core_ref[0]
    blocks, _, rows_slots, _ = own_ref.shape
    half_rows = rows_slots // GRID
    parts = late_ref.shape[0]
    gain = gains_ref[0:1, :]

    late = jnp.concatenate([late_ref[m] for m in range(parts)], axis=1)
    wu = dot(late, sel_u_ref[...]).astype(BF16)
    wu_ref[...] = wu
    rates = dot(late, sel_rc_ref[...])
    rates = jnp.concatenate([rates.T, jnp.zeros((LANES, 2 * LANES - D), F32)], axis=1)
    rates_ref[...] = rates
    for third in range(3):
        window = late[:, starts[third] * LANES : (starts[third] + width) * LANES]
        wqkv_ref[third] = dot(window, sel_q_ref[third]).astype(BF16)

    decay, coef = rates[: 4 * STATE], rates[4 * STATE :]

    def lag_row(k):
        powers = jnp.exp(-decay * k) * coef
        return [jnp.sum(powers[d * STATE : (d + 1) * STATE], 0, keepdims=True) for d in range(4)]

    def store_lag(way, lag, row):
        row = row.astype(BF16).astype(F32)
        for lane in range(2):
            table_ref[way, lane, lag + CENTER] = jnp.broadcast_to(
                row[:, lane * LANES : (lane + 1) * LANES], (8, LANES)
            )

    def lag_step(k, _):
        found = lag_row(k.astype(F32))
        for way in range(2):
            store_lag(way, k, found[2 * way])
            store_lag(way, -k, found[2 * way + 1])
        return 0

    lax.fori_loop(1, GRID, lag_step, 0)
    found = lag_row(0.0)
    for way in range(2):
        store_lag(way, 0, found[2 * way] + found[2 * way + 1])

    xs[1, :, D - LANES :] = jnp.zeros((SLOTS, 2 * LANES - D), F32)

    def norm_step(block, _):
        for which in range(2):
            ref = own_ref.at[block, 0] if which == 0 else other_ref.at[block]
            place = core if which == 0 else 1 - core
            unit, _ = normalise(ref[...].astype(F32))
            start = pl.multiple_of((block * 2 + place) * rows_slots, rows_slots)
            first_ref[pl.ds(start, rows_slots), :] = (unit * gain).astype(BF16)
        return 0

    lax.fori_loop(0, blocks, norm_step, 0)
    mixed = dot(first_ref[...], wu) * widen(mask_ref[...])
    mixed = mixed.astype(BF16)
    mixed_ref[...] = mixed
    mixed = mixed.astype(F32)
    put_lanes(xs, slice(None), mixed)
    for lane in range(2):
        for j in range(GRID):
            xt[lane, j * GRID : (j + 1) * GRID, :] = xs[lane, pl.ds(j, GRID, stride=GRID), :]

    def scan_step(index, _):
        sublane = pl.multiple_of((index % 4) * 8, 8)
        first = (index // 4) * 8
        for way, src, dst in ((0, xt, rows), (1, xs, cols)):
            for lane in range(2):
                total = block_sum(src, table_ref, way, lane, first, 8, GRID, 0, sublane, 1)
                for t in range(8):
                    place = pl.multiple_of((first + t) * GRID + sublane, 8)
                    dst[lane, pl.ds(place, 8), :] = total[t]
        return 0

    lax.fori_loop(0, 16, scan_step, 0)

    def join_step(i, _):
        place = pl.ds(pl.multiple_of(i * GRID, GRID), GRID)
        mask = mask_ref[place, :]
        both = []
        for lane in range(2):
            down = cols[lane, place, :].astype(BF16).astype(F32)
            both.append((rows[lane, pl.ds(i, GRID, stride=GRID), :] + down) * mask)
        both = jnp.concatenate([both[0], both[1][:, : D - LANES]], axis=1)
        scanned_ref[place, :] = both.astype(BF16)
        return 0

    lax.fori_loop(0, GRID, join_step, 0)

    for block in range(blocks):
        start = pl.multiple_of((block * 2 + core) * rows_slots, rows_slots)
        scanned_own[block * rows_slots : (block + 1) * rows_slots, :] = scanned_ref[
            pl.ds(start, rows_slots), :
        ]

    lane_own = lax.broadcasted_iota(jnp.int32, (OWN, LANES), 1)
    lane_all = lax.broadcasted_iota(jnp.int32, (SLOTS, LANES), 1)
    bias = jnp.where(lane_all == HEAD_DIM, (mask_ref[...] - 1.0) * 1e30, 0.0)
    ones = jnp.where((lane_all == HEAD_DIM) | (lane_all == HEAD_DIM + 1), 1.0, 0.0)
    one_own = jnp.where(lane_own == HEAD_DIM, 1.0, 0.0)
    for h in range(HEADS):
        tile = slice(h * LANES, (h + 1) * LANES)
        q_ref[h] = (
            dot(scanned_own[...], wqkv_ref[0, :, tile]) * HEAD_DIM ** (-0.5) + one_own
        ).astype(BF16)
        k_ref[h] = (dot(scanned_ref[...], wqkv_ref[1, :, tile]) + bias).astype(BF16)
        v_ref[h] = (dot(scanned_ref[...], wqkv_ref[2, :, tile]) + ones).astype(BF16)


def middle_kernel(
    core_ref,
    own_ref,
    mask_ref,
    gains_ref,
    early_ref,
    sel_1_ref,
    sel_o_ref,
    sel_2_ref,
    q_ref,
    k_ref,
    v_ref,
    soft_ref,
    lifted_ref,
    out_ref,
    grad_middle_ref,
    gain_ref,
    keep_ref,
    send_ref,
    scores,
    wo,
    w1,
    w2,
    att,
    outs,
    sums,
    middle,
    second,
    pre,
    hidden,
    grad_pre,
    wire,
):
    core = core_ref[0]
    blocks, _, rows_slots, _ = own_ref.shape
    parts = early_ref.shape[0]
    per_block = D // blocks
    gain = gains_ref[1:2, :]

    left = jnp.concatenate([early_ref[m, :, :LANES] for m in range(parts)], axis=1)
    right = jnp.concatenate([early_ref[m, :, LANES:] for m in range(parts)], axis=1)
    span = parts // 2 * LANES
    for half in range(2):
        w1[:, half * FF // 2 : (half + 1) * FF // 2] = dot(
            left[:, half * span : (half + 1) * span], sel_1_ref[...]
        ).astype(BF16)
    out_weight = dot(left, sel_o_ref[...]).astype(BF16)
    for h in range(HEADS):
        wo[h, :HEAD_DIM] = out_weight[h * HEAD_DIM : (h + 1) * HEAD_DIM]
        wo[h, HEAD_DIM:] = jnp.zeros((LANES - HEAD_DIM, D), BF16)
    for g in range(4):
        part = dot(right, sel_2_ref[g])
        for r in range(blocks):
            start = r * 4 * per_block + g * per_block
            w2[start : start + per_block] = part[r * per_block : (r + 1) * per_block].astype(BF16)

    for h in range(HEADS):
        scores[...] = dot_nt(q_ref[h], k_ref[h])

        def soft_step(i, _, h=h):
            place = pl.ds(pl.multiple_of(i * 32, 32), 32)
            values = scores[place, :]
            top = jnp.max(values, -1, keepdims=True)
            soft_ref[h, place, :] = jnp.exp(values - top).astype(BF16)
            return 0

        lax.fori_loop(0, OWN // 32, soft_step, 0)
        raw = dot(soft_ref[h], v_ref[h])
        total = raw[:, HEAD_DIM : HEAD_DIM + 1]
        sums[h] = jnp.broadcast_to(1.0 / total, (OWN, LANES))
        result = raw * sums[h]
        outs[h] = result
        att[h] = result.astype(BF16)

    branch = dot(att[0], wo[0]) + dot(att[1], wo[1]) + dot(att[2], wo[2])
    middle[...] = branch

    def own_mask(block):
        start = pl.multiple_of((block * 2 + core) * rows_slots, rows_slots)
        return widen(mask_ref[pl.ds(start, rows_slots), :])

    def norm_step(block, _):
        place = pl.ds(pl.multiple_of(block * rows_slots, rows_slots), rows_slots)
        mid = own_ref[block, 0].astype(F32) + middle[place, :] * own_mask(block)
        middle[place, :] = mid
        unit, _ = normalise(mid)
        second[place, :] = (unit * gain).astype(BF16)
        return 0

    lax.fori_loop(0, blocks, norm_step, 0)

    pre[...] = dot(second[...], w1[...])
    cot = jnp.concatenate([own_ref[b, 1] for b in range(blocks)], axis=0)
    grad_hidden = scores.at[:, :FF]
    grad_hidden[...] = dot_nt(cot, w2[...])

    def gelu_step(i, _):
        place = pl.ds(pl.multiple_of(i * 16, 16), 16)
        x = pre[place, :]
        phi = 0.5 * (1.0 + lax.erf(x * np.float32(0.5**0.5)))
        hidden[place, :] = (x * phi).astype(BF16)
        slope = phi + x * jnp.exp(x * x * -0.5) * np.float32((2 * np.pi) ** -0.5)
        grad_pre[place, :] = (scores[place, :FF] * slope).astype(BF16)
        return 0

    lax.fori_loop(0, OWN // 16, gelu_step, 0)

    out_ref[...] = (middle[...] + dot(hidden[...], w2[...])).astype(BF16)
    grad_2 = dot_tn(hidden[...], cot).astype(BF16)
    grad_1 = dot_tn(second[...], grad_pre[...]).astype(BF16)
    grad_middle_ref[...] = dot_nt(grad_pre[...], w1[...])

    def back_step(block, total):
        place = pl.ds(pl.multiple_of(block * rows_slots, rows_slots), rows_slots)
        unit, inverse = normalise(middle[place, :])
        grad = grad_middle_ref[place, :]
        total = total + jnp.sum(grad * unit, 0, keepdims=True)
        grad = own_ref[block, 1].astype(F32) + norm_back(grad, gain, unit, inverse)
        grad_middle_ref[place, :] = grad
        second[place, :] = (grad * own_mask(block)).astype(BF16)
        return total

    gain_ref[...] = lax.fori_loop(0, blocks, back_step, jnp.zeros((1, D), F32))

    grad_o = []
    lane_own = lax.broadcasted_iota(jnp.int32, (OWN, LANES), 1)
    for h in range(HEADS):
        grad_o.append(dot_tn(att[h], second[...])[:HEAD_DIM])
        grad_att = dot_nt(second[...], wo[h]).astype(BF16).astype(F32)
        scaled = (grad_att * sums[h]).astype(BF16).astype(F32)
        shift = -jnp.sum(scaled * outs[h], -1, keepdims=True)
        high = shift.astype(BF16).astype(F32)
        lifted = jnp.where(
            lane_own == HEAD_DIM, high, jnp.where(lane_own == HEAD_DIM + 1, shift - high, scaled)
        )
        lifted_ref[h] = lifted.astype(BF16)

    for half in range(2):
        wire[:, half * span : (half + 1) * span] = dot_nt(
            grad_1[:, half * FF // 2 : (half + 1) * FF // 2], sel_1_ref[...]
        )
    grad_o = jnp.concatenate(grad_o, axis=0).astype(BF16)
    wire[...] += dot_nt(grad_o, sel_o_ref[...])

    def deliver(lanes):
        for m in range(parts):
            value = wire[:, m * LANES : (m + 1) * LANES].astype(BF16)

            @pl.when(core == m % 2)
            def _(value=value, m=m):
                keep_ref[m // 2, :, lanes] = value

            @pl.when(core != m % 2)
            def _(value=value, m=m):
                send_ref[m // 2, :, lanes] = value

    deliver(slice(0, LANES))
    total = None
    for g in range(4):
        rows = [
            grad_2[r * 4 * per_block + g * per_block : r * 4 * per_block + (g + 1) * per_block]
            for r in range(blocks)
        ]
        part = dot_nt(jnp.concatenate(rows, axis=0), sel_2_ref[g])
        total = part if total is None else total + part
    wire[...] = total
    deliver(slice(LANES, 2 * LANES))


def attention_back_kernel(
    core_ref,
    soft_ref,
    lifted_ref,
    q_ref,
    k_ref,
    v_ref,
    scanned_ref,
    wqkv_ref,
    part_ref,
    grad_w_ref,
    scores,
    grad_scores,
    triple,
    grad_q,
    scanned_own,
    part,
    *,
    blocks,
):
    core = core_ref[0]
    rows_slots = OWN // blocks
    for h in range(HEADS):
        tile = slice(h * LANES, (h + 1) * LANES)
        scores[...] = dot_nt(lifted_ref[h], v_ref[h])

        def back_step(i, _, h=h):
            place = pl.ds(pl.multiple_of(i * 32, 32), 32)
            grad_scores[place, :] = (soft_ref[h, place, :].astype(F32) * scores[place, :]).astype(
                BF16
            )
            return 0

        lax.fori_loop(0, OWN // 32, back_step, 0)
        grad_q[:, tile] = (dot(grad_scores[...], k_ref[h]).astype(BF16) * HEAD_DIM ** (-0.5)).astype(
            BF16
        )
        triple[0, :, tile] = dot_tn(grad_scores[...], q_ref[h]).astype(BF16)
        triple[1, :, tile] = dot_tn(soft_ref[h], lifted_ref[h]).astype(BF16)

    part[...] = dot_nt(triple[0], wqkv_ref[1]) + dot_nt(triple[1], wqkv_ref[2])
    from_q = dot_nt(grad_q[...], wqkv_ref[0])
    for block in range(blocks):
        here = slice(block * rows_slots, (block + 1) * rows_slots)
        place = pl.ds(pl.multiple_of((block * 2 + core) * rows_slots, rows_slots), rows_slots)
        part[place, :] += from_q[here]
        scanned_own[here, :] = scanned_ref[place, :]
    part_ref[...] = part[...].astype(BF16)
    grad_w_ref[0] = dot_tn(scanned_own[...], grad_q[...]).astype(BF16)
    grad_w_ref[1] = dot_tn(scanned_ref[...], triple[0]).astype(BF16)
    grad_w_ref[2] = dot_tn(scanned_ref[...], triple[1]).astype(BF16)


def scan_back_kernel(
    starts,
    width,
    core_ref,
    own_ref,
    mask_ref,
    gains_ref,
    part_ref,
    got_ref,
    mixed_ref,
    first_ref,
    table_ref,
    rates_ref,
    wu_ref,
    grad_middle_ref,
    grad_w_ref,
    gain_two_ref,
    sel_u_ref,
    sel_rc_ref,
    sel_q_ref,
    grad_ref,
    keep_ref,
    send_ref,
    gains_out_ref,
    gs,
    gt,
    xs,
    xt,
    own,
    rows,
    cols,
    lag_sums,
    lag_rows,
    mixed_back,
    first_own,
    wire,
):
    core = core_ref[0]
    blocks, _, rows_slots, _ = own_ref.shape
    half_rows = rows_slots // GRID
    own_rows = GRID // 2
    parts = sel_rc_ref.shape[0] // LANES
    gain = gains_ref[0:1, :]
    pad = jnp.zeros((SLOTS, 2 * LANES - D), F32)

    xs[1, :, D - LANES :] = pad
    gs[1, :, D - LANES :] = pad
    put_lanes(xs, slice(None), mixed_ref[...].astype(F32))
    grads = (part_ref[...].astype(F32) + got_ref[...].astype(F32)) * widen(mask_ref[...])
    put_lanes(gs, slice(None), grads.astype(BF16).astype(F32))

    def place_of(block):
        return pl.ds(pl.multiple_of((block * 2 + core) * rows_slots, rows_slots), rows_slots)

    for block in range(blocks):
        here = slice(block * rows_slots, (block + 1) * rows_slots)
        first_own[here, :] = first_ref[place_of(block), :]
    for src, dst in ((gs, gt), (xs, xt)):
        for lane in range(2):
            for block in range(blocks):
                here = slice(block * rows_slots, (block + 1) * rows_slots)
                own[lane, here, :] = src[lane, place_of(block), :]
            for j in range(GRID):
                dst[lane, j * own_rows : (j + 1) * own_rows, :] = own[
                    lane, pl.ds(j, own_rows, stride=GRID), :
                ]

    def row_step(index, _):
        sublane = pl.multiple_of((index % 2) * 8, 8)
        first = (index // 2) * 8
        for lane in range(2):
            total = block_sum(gt, table_ref, 0, lane, first, 8, own_rows, 0, sublane, -1)
            for t in range(8):
                rows[lane, pl.ds(pl.multiple_of((first + t) * own_rows + sublane, 8), 8), :] = total[
                    t
                ]
        return 0

    lax.fori_loop(0, 8, row_step, 0)

    def col_step(index, _):
        sublane = pl.multiple_of((index % 4) * 8, 8)
        block = index // 4
        first = (block * 2 + core) * half_rows
        for lane in range(2):
            total = block_sum(gs, table_ref, 1, lane, first, half_rows, GRID, 0, sublane, -1)
            for t in range(half_rows):
                at = pl.multiple_of((block * half_rows + t) * GRID + sublane, 8)
                cols[lane, pl.ds(at, 8), :] = total[t]
        return 0

    lax.fori_loop(0, blocks * 4, col_step, 0)

    lag_sums[...] = jnp.zeros_like(lag_sums)

    def add_lags(way, lane, first, count, base, gref, xref, step, groups):
        total = {}
        for u in range(groups):
            g = [
                gref[lane, pl.ds(pl.multiple_of((first + t) * step + u * 8, 8), 8), :]
                for t in range(count)
            ]
            for s in range(8):
                x = xref[lane, pl.ds(pl.multiple_of((base + s) * step + u * 8, 8), 8), :]
                for t in range(count):
                    term = g[t] * x
                    total[t - s] = term if t - s not in total else total[t - s] + term
        for lag, value in total.items():
            at = first - base + (lag + CENTER)
            lag_sums[way, lane, at] += value

    def lag_row_step(index, _):
        first, base = (index // 4) * 8, (index % 4) * 8
        for lane in range(2):
            add_lags(0, lane, first, 8, base, gt, xt, own_rows, own_rows // 8)
        return 0

    lax.fori_loop(0, 16, lag_row_step, 0)

    def lag_col_step(index, _):
        first, base = ((index // 4) * 2 + core) * half_rows, (index % 4) * 8
        for lane in range(2):
            add_lags(1, lane, first, half_rows, base, gs, xs, GRID, GRID // 8)
        return 0

    lax.fori_loop(0, blocks * 4, lag_col_step, 0)

    for way in range(2):
        for lane in range(2):
            lag_rows[way, :, lane * LANES : (lane + 1) * LANES] = jnp.sum(lag_sums[way, lane], 1)

    decay, coef = rates_ref[: 4 * STATE], rates_ref[4 * STATE :]

    def table_step(k, carry):
        to_rate, to_coef = carry
        lag = k.astype(F32)
        powers = jnp.exp(-decay * lag)
        grads = []
        for way in range(2):
            for at in (CENTER + k, CENTER - k):
                grads.append(
                    jnp.broadcast_to(lag_rows[way, pl.ds(at, 1), :], (STATE, 2 * LANES))
                )
        scaled = jnp.concatenate(grads, axis=0) * powers
        return to_rate - lag * scaled, to_coef + scaled

    zero = jnp.zeros((4 * STATE, 2 * LANES), F32)
    to_rate, to_coef = lax.fori_loop(0, GRID, table_step, (zero, zero))
    grad_rc = jnp.concatenate([to_rate * coef, to_coef], axis=0).T[:D].astype(BF16)

    def join_step(i, _):
        place = pl.ds(pl.multiple_of(i * GRID, GRID), GRID)
        block = i // half_rows
        at = ((block * 2 + core) * half_rows + i % half_rows) * GRID
        mask = mask_ref[pl.ds(pl.multiple_of(at, GRID), GRID), :]
        both = []
        for lane in range(2):
            down = cols[lane, place, :].astype(BF16).astype(F32)
            both.append((rows[lane, pl.ds(i, GRID, stride=own_rows), :] + down) * mask)
        both = jnp.concatenate([both[0], both[1][:, : D - LANES]], axis=1)
        mixed_back[place, :] = both.astype(BF16)
        return 0

    lax.fori_loop(0, own_rows, join_step, 0)
    grad_u = dot_tn(first_own[...], mixed_back[...]).astype(BF16)
    grad_first = dot_nt(mixed_back[...], wu_ref[...])
    gain_one = jnp.zeros((1, D), F32)
    for block in range(blocks):
        here = slice(block * rows_slots, (block + 1) * rows_slots)
        unit, inverse = normalise(own_ref[block, 0].astype(F32))
        grad = grad_first[here]
        gain_one = gain_one + jnp.sum(grad * unit, 0, keepdims=True)
        grad = grad_middle_ref[here, :] + norm_back(grad, gain, unit, inverse)
        grad_ref[here, :] = grad.astype(BF16)

    wire[...] = dot_nt(grad_u, sel_u_ref[...]) + dot_nt(grad_rc, sel_rc_ref[...])
    for third in range(3):
        span = slice(starts[third] * LANES, (starts[third] + width) * LANES)
        wire[:, span] += dot_nt(grad_w_ref[third], sel_q_ref[third])
    for m in range(parts):
        value = wire[:, m * LANES : (m + 1) * LANES].astype(BF16)

        @pl.when(core == m % 2)
        def _(value=value, m=m):
            keep_ref[m // 2] = value

        @pl.when(core != m % 2)
        def _(value=value, m=m):
            send_ref[m // 2] = value

    lines = []
    for value in (gain_one, gain_two_ref[...]):
        high = value.astype(BF16).astype(F32)
        for piece in (high, value - high):
            lines.append(piece[:, :LANES])
            lines.append(
                jnp.concatenate([piece[:, LANES:], jnp.zeros((1, 2 * LANES - D), F32)], axis=1)
            )
    lines.append(jnp.zeros((8, LANES), F32))
    gains_out_ref[...] = jnp.concatenate(lines, axis=0).astype(BF16)


def pair_sum_kernel(keep_ref, got_ref, gains_ref, gains_got_ref, out_ref):
    depth, blocks, rows, _ = out_ref.shape
    rows -= 16
    gains = gains_ref[...].astype(F32) + gains_got_ref[...].astype(F32)
    lines = []
    for g in range(2):
        for lane in range(2):
            at = 4 * g + lane
            lines.append(gains[at : at + 1] + gains[at + 2 : at + 3])
    value = jnp.concatenate(lines, axis=0)
    high = value.astype(BF16).astype(F32)
    gains = jnp.concatenate([high, value - high, jnp.zeros((8, LANES), F32)], axis=0).astype(BF16)
    for z in range(depth):
        total = keep_ref[z].astype(F32) + got_ref[z].astype(F32)
        for r in range(blocks):
            out_ref[z, r, :rows] = total[r * rows : (r + 1) * rows].astype(BF16)
            out_ref[z, r, rows:] = gains


def final_kernel(
    parts,
    late_ref,
    early_ref,
    g1_ref,
    g2_ref,
    wu_ref,
    rate_ref,
    coef_ref,
    qkv_ref,
    wo_ref,
    fc1_ref,
    fc2_ref,
):
    a_u, a_r, a_q, (o_u, o_r, o_c, o_q) = late_layout(parts)
    count = late_ref.shape[0]
    total = late_ref[0].astype(F32)
    early = early_ref[0].astype(F32)
    for i in range(1, count):
        total = total + late_ref[i].astype(F32)
        early = early + early_ref[i].astype(F32)
    rows = wu_ref.shape[0]
    weights, gains = total[:rows], total[rows:]
    wu_ref[...] = weights[:, o_u : o_u + a_u]
    rate_ref[...] = weights[:, o_r : o_r + a_r]
    coef_ref[...] = weights[:, o_c : o_c + a_r]
    qkv_ref[...] = weights[:, o_q : o_q + a_q]
    gains = gains[0:4] + gains[4:8]
    for g, ref in ((0, g1_ref), (1, g2_ref)):
        ref[...] = jnp.concatenate(
            [gains[2 * g : 2 * g + 1], gains[2 * g + 1 : 2 * g + 2, : D - LANES]], axis=1
        )
    a_1, a_o = FF // parts, D // parts
    fc1_ref[...] = early[:, :a_1]
    wo_ref[...] = early[:, a_1 : a_1 + a_o]
    for g in range(4):
        fc2_ref[g * rows : (g + 1) * rows] = early[
            :, LANES + g * a_o : LANES + (g + 1) * a_o
        ]


def per_device(
    patches, valid_mask, norm_gains, w_u, decay_rate, out_coef, w_qkv, w_o, w_fc1, w_fc2, cotangent
):
    images, rows_here, _, _ = patches.shape
    depth, blocks = lax.axis_size("z"), lax.axis_size("row")
    parts = 2 * depth
    half_rows = rows_here // 2
    rows_slots = half_rows * GRID
    core = lax.axis_index("core")
    row = lax.axis_index("row")
    first_core = core == 0
    swap = [(0, 1), (1, 0)]
    core_index = core.astype(jnp.int32).reshape(1)
    shape = jax.ShapeDtypeStruct

    sel_u, sel_rc, sel_q, starts, width = late_selections(parts)
    sel_1, sel_o, sel_2 = early_selections(parts)

    late = jnp.concatenate([w_u, decay_rate, out_coef, w_qkv], axis=1)
    late = jnp.pad(late, ((0, 0), (0, LANES - late.shape[1])))
    late_all = lax.all_to_all(
        jnp.broadcast_to(late[None], (parts * blocks,) + late.shape),
        ("z", "core", "row"),
        0,
        0,
        tiled=True,
    ).reshape(parts, D, LANES)
    rows_weight = w_u.shape[0]
    left = jnp.concatenate([w_fc1, w_o], axis=1)
    right = jnp.concatenate(
        [w_fc2[g * rows_weight : (g + 1) * rows_weight] for g in range(4)], axis=1
    )
    early = jnp.concatenate(
        [
            jnp.pad(left, ((0, 0), (0, LANES - left.shape[1]))),
            jnp.pad(right, ((0, 0), (0, LANES - right.shape[1]))),
        ],
        axis=1,
    )
    early_all = lax.all_gather(lax.all_gather(early, "row"), ("z", "core")).reshape(
        parts, D, 2 * LANES
    )

    both = jnp.stack([patches, cotangent], axis=1)
    both = both.reshape(images, 2, 2, rows_slots, D)
    mine = lax.dynamic_index_in_dim(both, core, 2, keepdims=False)
    theirs = lax.dynamic_index_in_dim(both, 1 - core, 2, keepdims=False)
    got = lax.ppermute(theirs, "core", swap)
    plane = jnp.where(
        first_core, jnp.concatenate([mine, got], axis=0), jnp.concatenate([got, mine], axis=0)
    )
    own = lax.all_to_all(plane, "row", 0, 0, tiled=True)
    other = lax.ppermute(own[:, 0], "core", swap)

    mask_got = lax.ppermute(valid_mask, "core", swap)
    mask_plane = jnp.where(
        first_core,
        jnp.concatenate([valid_mask, mask_got], axis=0),
        jnp.concatenate([mask_got, valid_mask], axis=0),
    )
    mask = lax.dynamic_index_in_dim(mask_plane, row, 0, keepdims=False)
    mask = jnp.broadcast_to(mask.reshape(SLOTS, 1).astype(F32), (SLOTS, LANES))

    head_own = shape((HEADS, OWN, LANES), BF16)
    head_all = shape((HEADS, SLOTS, LANES), BF16)
    q, k, v, scanned, mixed, table, rates, wu, wqkv, first = pl.pallas_call(
        lambda *refs: scan_kernel(starts, width, *refs),
        name="scan_forward",
        out_shape=(
            head_own,
            head_all,
            head_all,
            shape((SLOTS, D), BF16),
            shape((SLOTS, D), BF16),
            shape((2, 2, LAGS, 8, LANES), F32),
            shape((LANES, 2 * LANES), F32),
            shape((D, D), BF16),
            shape((3, D, TILE), BF16),
            shape((SLOTS, D), BF16),
        ),
        in_specs=[SMEM] + [VMEM] * 8,
        out_specs=[VMEM] * 10,
        scratch_shapes=[pltpu.VMEM((2, SLOTS, LANES), F32)] * 4 + [pltpu.VMEM((OWN, D), BF16)],
        compiler_params=compiler(),
    )(core_index, own, other, mask, norm_gains, late_all, sel_u, sel_rc, sel_q)

    wire_early = shape((depth, D, 2 * LANES), BF16)
    soft, lifted, out_own, grad_middle, gain_two, early_keep, early_send = pl.pallas_call(
        middle_kernel,
        name="attention_and_feed_forward",
        out_shape=(
            shape((HEADS, OWN, SLOTS), BF16),
            head_own,
            shape((OWN, D), BF16),
            shape((OWN, D), F32),
            shape((1, D), F32),
            wire_early,
            wire_early,
        ),
        in_specs=[SMEM] + [VMEM] * 10,
        out_specs=[VMEM] * 7,
        scratch_shapes=[
            pltpu.VMEM((OWN, SLOTS), F32),
            pltpu.VMEM((HEADS, LANES, D), BF16),
            pltpu.VMEM((D, FF), BF16),
            pltpu.VMEM((FF, D), BF16),
            pltpu.VMEM((HEADS, OWN, LANES), BF16),
            pltpu.VMEM((HEADS, OWN, LANES), F32),
            pltpu.VMEM((HEADS, OWN, LANES), F32),
            pltpu.VMEM((OWN, D), F32),
            pltpu.VMEM((OWN, D), BF16),
            pltpu.VMEM((OWN, FF), F32),
            pltpu.VMEM((OWN, FF), BF16),
            pltpu.VMEM((OWN, FF), BF16),
            pltpu.VMEM((D, parts * LANES), F32),
        ],
        compiler_params=compiler(),
    )(core_index, own, mask, norm_gains, early_all, sel_1, sel_o, sel_2, q, k, v)

    early_sum = (
        early_keep.astype(F32) + lax.ppermute(early_send, "core", swap).astype(F32)
    ).astype(BF16)
    early_sum = early_sum.reshape(depth * blocks, D // blocks, 2 * LANES)
    early_got = lax.all_to_all(early_sum, ("z", "row"), 0, 0, tiled=True)

    part, grad_w = pl.pallas_call(
        lambda *refs: attention_back_kernel(*refs, blocks=blocks),
        name="attention_backward",
        out_shape=(shape((SLOTS, D), BF16), shape((3, D, TILE), BF16)),
        in_specs=[SMEM] + [VMEM] * 7,
        out_specs=[VMEM] * 2,
        scratch_shapes=[
            pltpu.VMEM((OWN, SLOTS), F32),
            pltpu.VMEM((OWN, SLOTS), BF16),
            pltpu.VMEM((2, SLOTS, TILE), BF16),
            pltpu.VMEM((OWN, TILE), BF16),
            pltpu.VMEM((OWN, D), BF16),
            pltpu.VMEM((SLOTS, D), F32),
        ],
        compiler_params=compiler(),
    )(core_index, soft, lifted, q, k, v, scanned, wqkv)

    part_got = lax.ppermute(part, "core", swap)
    wire_late = shape((depth, D, LANES), BF16)
    grad_own, late_keep, late_send, gains_keep = pl.pallas_call(
        lambda *refs: scan_back_kernel(starts, width, *refs),
        name="scan_backward",
        out_shape=(shape((OWN, D), BF16), wire_late, wire_late, shape((16, LANES), BF16)),
        in_specs=[SMEM] + [VMEM] * 16,
        out_specs=[VMEM] * 4,
        scratch_shapes=[
            pltpu.VMEM((2, SLOTS, LANES), F32),
            pltpu.VMEM((2, OWN, LANES), F32),
            pltpu.VMEM((2, SLOTS, LANES), F32),
            pltpu.VMEM((2, OWN, LANES), F32),
            pltpu.VMEM((2, OWN, LANES), F32),
            pltpu.VMEM((2, OWN, LANES), F32),
            pltpu.VMEM((2, OWN, LANES), F32),
            pltpu.VMEM((2, 2, LAGS, 8, LANES), F32),
            pltpu.VMEM((2, LAGS, 2 * LANES), F32),
            pltpu.VMEM((OWN, D), BF16),
            pltpu.VMEM((OWN, D), BF16),
            pltpu.VMEM((D, parts * LANES), F32),
        ],
        compiler_params=compiler(),
    )(
        core_index,
        own,
        mask,
        norm_gains,
        part,
        part_got,
        mixed,
        first,
        table,
        rates,
        wu,
        grad_middle,
        grad_w,
        gain_two,
        sel_u,
        sel_rc,
        sel_q,
    )

    late_recv = lax.ppermute(late_send, "core", swap)
    gains_recv = lax.ppermute(gains_keep, "core", swap)
    rows_weight = D // blocks
    late_sum = pl.pallas_call(
        pair_sum_kernel,
        name="pair_sum",
        out_shape=shape((depth, blocks, rows_weight + 16, LANES), BF16),
        in_specs=[VMEM] * 4,
        out_specs=VMEM,
        compiler_params=compiler(),
    )(late_keep, late_recv, gains_keep, gains_recv)
    late_got = lax.all_to_all(
        late_sum.reshape(depth * blocks, rows_weight + 16, LANES), ("z", "row"), 0, 0, tiled=True
    )

    results = jnp.stack(
        [out_own.reshape(blocks, rows_slots, D), grad_own.reshape(blocks, rows_slots, D)], axis=1
    )
    results = lax.all_to_all(results, "row", 0, 0, tiled=True)
    mine = jnp.where(first_core, results[:images], results[images:])
    theirs = jnp.where(first_core, results[images:], results[:images])
    got = lax.ppermute(theirs, "core", swap)
    whole = jnp.where(
        first_core, jnp.stack([mine, got], axis=2), jnp.stack([got, mine], axis=2)
    )
    block_out = whole[:, 0].reshape(patches.shape)
    grad_patches = whole[:, 1].reshape(patches.shape)

    weight = (rows_weight,)
    g1, g2, f_u, f_rate, f_coef, f_qkv, f_o, f_1, f_2 = pl.pallas_call(
        lambda *refs: final_kernel(parts, *refs),
        name="final_sum",
        out_shape=(
            shape((1, D), F32),
            shape((1, D), F32),
            shape(weight + (D // parts,), F32),
            shape(weight + (4 * STATE // parts,), F32),
            shape(weight + (4 * STATE // parts,), F32),
            shape(weight + (3 * D // parts,), F32),
            shape(weight + (D // parts,), F32),
            shape(weight + (FF // parts,), F32),
            shape((4 * rows_weight, D // parts), F32),
        ),
        in_specs=[VMEM] * 2,
        out_specs=[VMEM] * 9,
        compiler_params=compiler(),
    )(late_got, early_got)
    return (
        block_out,
        grad_patches,
        g1.reshape(D),
        g2.reshape(D),
        f_u,
        f_rate,
        f_coef,
        f_qkv,
        f_o,
        f_1,
        f_2,
    )


def solution(mesh):
    images, rows = mesh.devices.shape
    fine = Mesh(mesh.devices.reshape(images // 2, 2, rows), ("z", "core", "row"))
    img = ("z", "core")
    grid = P(img, "row", None, None)
    weight = P("row", img)
    in_specs = (grid, P(img, None, None), P()) + (weight,) * 7 + (grid,)
    out_specs = (grid, grid, P(), P()) + (weight,) * 7
    return jax.shard_map(
        per_device, mesh=fine, in_specs=in_specs, out_specs=out_specs, check_vma=False
    )
```

```python
import jax
import jax.numpy as jnp
import numpy as np
from jax import lax
from jax.experimental import pallas as pl
from jax.experimental.pallas import tpu as pltpu
from jax.sharding import Mesh
from jax.sharding import PartitionSpec as P

HEADS = 3
HEAD_DIM = 64
STATE = 16
GRID = 32
SLOTS = GRID * GRID
OWN = SLOTS // 2
D = HEADS * HEAD_DIM
FF = 4 * D
LANES = 128
TILE = HEADS * LANES
LAGS = 2 * GRID
CENTER = GRID - 1
EPS = 1e-05
BF16 = jnp.bfloat16
F32 = jnp.float32


def late_layout(parts):
    a_u, a_r, a_q = D // parts, 4 * STATE // parts, 3 * D // parts
    return a_u, a_r, a_q, (0, a_u, a_u + a_r, a_u + 2 * a_r)


def late_selections(parts):
    a_u, a_r, a_q, (o_u, o_r, o_c, o_q) = late_layout(parts)
    sel_u = np.zeros((parts, LANES, D), np.float32)
    sel_rc = np.zeros((parts, LANES, LANES), np.float32)
    full = np.zeros((parts, LANES, 3, TILE), np.float32)
    for m in range(parts):
        for col in range(a_u):
            sel_u[m, o_u + col, m * a_u + col] = 1
        for col in range(a_r):
            sel_rc[m, o_r + col, m * a_r + col] = 1
            sel_rc[m, o_c + col, 4 * STATE + m * a_r + col] = 1
        for col in range(a_q):
            whole = m * a_q + col
            third, rest = divmod(whole, D)
            head, lane = divmod(rest, HEAD_DIM)
            full[m, o_q + col, third, head * LANES + lane] = 1
    spans = []
    for third in range(3):
        used = [m for m in range(parts) if full[m, :, third].any()]
        spans.append((min(used), max(used) + 1))
    width = max(stop - start for start, stop in spans)
    starts = [min(start, parts - width) for start, _ in spans]
    sel_q = np.stack(
        [full[s : s + width, :, third].reshape(width * LANES, TILE) for third, s in enumerate(starts)]
    )
    return (
        sel_u.reshape(parts * LANES, D).astype(BF16),
        sel_rc.reshape(parts * LANES, LANES).astype(BF16),
        sel_q.astype(BF16),
        starts,
        width,
    )


def early_selections(parts):
    a_1, a_o = FF // parts, D // parts
    half = parts // 2
    sel_1 = np.zeros((half, LANES, FF // 2), np.float32)
    sel_o = np.zeros((parts, LANES, D), np.float32)
    sel_2 = np.zeros((4, parts, LANES, D), np.float32)
    for m in range(half):
        for col in range(a_1):
            sel_1[m, col, m * a_1 + col] = 1
    for m in range(parts):
        for col in range(a_o):
            sel_o[m, a_1 + col, m * a_o + col] = 1
            for g in range(4):
                sel_2[g, m, g * a_o + col, m * a_o + col] = 1
    return (
        sel_1.reshape(half * LANES, FF // 2).astype(BF16),
        sel_o.reshape(parts * LANES, D).astype(BF16),
        sel_2.reshape(4, parts * LANES, D).astype(BF16),
    )


def dot(a, b):
    return lax.dot_general(a, b, (((1,), (0,)), ((), ())), preferred_element_type=F32)


def dot_nt(a, b):
    return lax.dot_general(a, b, (((1,), (1,)), ((), ())), preferred_element_type=F32)


def dot_tn(a, b):
    return lax.dot_general(a, b, (((0,), (0,)), ((), ())), preferred_element_type=F32)


def normalise(values):
    center = values - jnp.mean(values, -1, keepdims=True)
    spread = jnp.mean(center * center, -1, keepdims=True)
    inverse = lax.rsqrt(spread + EPS)
    return center * inverse, inverse


def norm_back(grad, gain, unit, inverse):
    scaled = grad * gain
    first = jnp.mean(scaled, -1, keepdims=True)
    second = jnp.mean(scaled * unit, -1, keepdims=True)
    return inverse * (scaled - first - unit * second)


def widen(mask):
    return jnp.concatenate([mask, mask[:, : D - LANES]], axis=1)


def put_blocks(ref, z, lanes, value):
    rows = ref.shape[2]
    for r in range(ref.shape[0]):
        ref[r, z, :, lanes] = value[r * rows : (r + 1) * rows]


def put_lanes(ref, rows, values):
    ref[0, rows, :] = values[:, :LANES]
    ref[1, rows, : D - LANES] = values[:, LANES:]


def block_sum(src, table, way, lane, first, count, step, offset, sublane, sign):
    total = [None] * count
    for base in range(0, GRID, 8):
        low, high = -(base + 7), count - 1 - base
        coef = {
            lag: table[way, lane, first * sign + (lag * sign + CENTER)]
            for lag in range(low, high + 1)
        }
        for s in range(base, base + 8):
            x = src[lane, pl.ds(pl.multiple_of(s * step + sublane, 8), 8), :]
            for t in range(count):
                term = coef[t - s] * x
                total[t] = term if total[t] is None else total[t] + term
    return total


def gather_parts(place_ref, mine_refs, got_refs, block, out_ref):
    core, row, depth = place_ref[0], place_ref[1], place_ref[2]
    lanes = slice(block * LANES, (block + 1) * LANES)
    count = out_ref.shape[0] // 2
    rows = out_ref.shape[2]
    for refs, which in ((mine_refs, core), (got_refs, 1 - core)):
        for k, ref in enumerate(refs):
            for j in range(count):
                value = ref[j * rows : (j + 1) * rows, lanes]
                out_ref[2 * (depth ^ j) + which, row ^ k] = value
    wide = []
    for m in range(2 * count):
        wide.append(jnp.concatenate([out_ref[m, r] for r in range(out_ref.shape[1])], axis=0))
    return jnp.concatenate(wide, axis=1)


LARGE = 60 << 20


def compiler(limit=24 << 20):
    return pltpu.CompilerParams(vmem_limit_bytes=limit)


VMEM = pl.BlockSpec(memory_space=pltpu.VMEM)
SMEM = pl.BlockSpec(memory_space=pltpu.SMEM)


def pack(values):
    half = values.shape[0] // 2
    tail = jnp.concatenate([values[:half, LANES:], values[half:, LANES:]], axis=1)
    return jnp.concatenate([values[:, :LANES], tail], axis=0)


def unpack(packed):
    count = packed.shape[0] * 2 // 3
    tail = packed[count:]
    tail = jnp.concatenate([tail[:, : D - LANES], tail[:, D - LANES :]], axis=0)
    return jnp.concatenate([packed[:count], tail], axis=1)


def pack_weights_kernel(turned_refs, qkv_ref, fc1_ref, out_ref):
    wu, rate, coef, wo, fc2 = [ref[...].astype(F32) for ref in turned_refs]
    rows = qkv_ref.shape[0]
    a_o, a_r = wo.shape[0], rate.shape[0]
    pieces = [wu, rate, coef, wo] + [fc2[:, g * rows : (g + 1) * rows] for g in range(4)]
    joined = jnp.concatenate(pieces, axis=0)
    joined = jnp.concatenate([joined, jnp.zeros((joined.shape[0], LANES - rows), F32)], axis=1)
    joined = joined.T[:rows]
    first, second = a_o + 2 * a_r, 2 * a_o + 2 * a_r

    def fill(parts):
        used = sum(part.shape[1] for part in parts)
        return parts + [jnp.zeros((rows, LANES - used), F32)]

    packed = jnp.concatenate(
        fill([joined[:, :first], qkv_ref[...].astype(F32)])
        + fill([fc1_ref[...].astype(F32), joined[:, first:second]])
        + fill([joined[:, second:]]),
        axis=1,
    ).astype(BF16)
    out_ref[...] = packed


def route_kernel(place_ref, patch_ref, cot_ref, valid_ref, *out_refs):
    row = place_ref[1]
    images, slots, _ = patch_ref.shape
    half = slots // 2
    packed = half * 3 // 2
    for j, out_ref in enumerate(out_refs):
        target = row ^ j
        core, image = target // images, target % images
        out_ref[:packed] = pack(patch_ref[image, :half])
        out_ref[packed : 2 * packed] = pack(patch_ref[image, half:])
        start = pl.multiple_of(core * half, half)
        out_ref[2 * packed : 3 * packed] = pack(cot_ref[image, pl.ds(start, half), :])
        valid = valid_ref[image].astype(F32).astype(BF16)
        out_ref[3 * packed :] = jnp.concatenate(
            [valid, jnp.zeros((GRID, LANES - GRID), BF16)], axis=1
        )


def depart_kernel(place_ref, *refs):
    turned, (qkv_ref, fc1_ref, patch_ref, cot_ref, valid_ref, out_ref) = refs[:5], refs[5:11]
    pack_weights_kernel(turned, qkv_ref, fc1_ref, out_ref)
    route_kernel(place_ref, patch_ref, cot_ref, valid_ref, *refs[11:])


def norm_kernel(place_ref, gains_ref, *refs):
    core, row = place_ref[0], place_ref[1]
    got_refs, (own_ref, first_ref, mask_ref) = refs[:-3], refs[-3:]
    images = len(got_refs) // 2
    gain = gains_ref[0:1, :]
    slots = own_ref.shape[2]
    packed = slots * 3 // 2
    valid = got_refs[0][3 * packed :].astype(F32).T
    for i in range(GRID):
        mask_ref[i * GRID : (i + 1) * GRID, :] = jnp.broadcast_to(
            valid[:GRID, i : i + 1], (GRID, LANES)
        )
    for j, got in enumerate(got_refs):
        block = (core * images + row % images) ^ j
        own_ref[block, 1] = unpack(got[2 * packed : 3 * packed])
        for half in range(2):
            patch = unpack(got[half * packed : (half + 1) * packed])

            @pl.when(core == half)
            def _(patch=patch, block=block):
                own_ref[block, 0] = patch

            unit, _ = normalise(patch.astype(F32))
            start = pl.multiple_of((block * 2 + half) * slots, slots)
            first_ref[pl.ds(start, slots), :] = (unit * gain).astype(BF16)


def home_kernel(place_ref, *refs):
    row = place_ref[1]
    got_refs, out_refs = refs[:-2], refs[-2:]
    images, slots, _ = out_refs[0].shape
    half = slots // 2
    for j, got in enumerate(got_refs):
        source = row ^ j
        core, image = source // images, source % images
        place = pl.ds(pl.multiple_of(core * half, half), half)
        for which, out_ref in enumerate(out_refs):
            out_ref[image, place, :] = unpack(got[which])


def scan_kernel(
    starts,
    width,
    core_ref,
    first_ref,
    mask_ref,
    sel_u_ref,
    sel_rc_ref,
    sel_q_ref,
    *refs,
    blocks,
):
    mine_refs, got_refs, refs = refs[:blocks], refs[blocks : 2 * blocks], refs[2 * blocks :]
    scan_body(
        starts,
        width,
        core_ref,
        first_ref,
        mask_ref,
        sel_u_ref,
        sel_rc_ref,
        sel_q_ref,
        mine_refs,
        got_refs,
        *refs,
    )


def scan_body(
    starts,
    width,
    core_ref,
    first_ref,
    mask_ref,
    sel_u_ref,
    sel_rc_ref,
    sel_q_ref,
    mine_refs,
    got_refs,
    q_ref,
    k_ref,
    v_ref,
    scanned_ref,
    mixed_ref,
    table_ref,
    rates_ref,
    wu_ref,
    wqkv_ref,
    late_ref,
    xs,
    xt,
    cols,
    rows,
    scanned_own,
):
    core = core_ref[0]
    blocks = len(mine_refs)
    rows_slots = OWN // blocks

    late = gather_parts(core_ref, mine_refs, got_refs, 0, late_ref)
    wu = dot(late, sel_u_ref[...]).astype(BF16)
    wu_ref[...] = wu
    rates = dot(late, sel_rc_ref[...])
    rates = jnp.concatenate([rates.T, jnp.zeros((LANES, 2 * LANES - D), F32)], axis=1)
    rates_ref[...] = rates
    for third in range(3):
        window = late[:, starts[third] * LANES : (starts[third] + width) * LANES]
        wqkv_ref[third] = dot(window, sel_q_ref[third]).astype(BF16)

    decay, coef = rates[: 4 * STATE], rates[4 * STATE :]

    def lag_row(k):
        powers = jnp.exp(-decay * k) * coef
        return [jnp.sum(powers[d * STATE : (d + 1) * STATE], 0, keepdims=True) for d in range(4)]

    def store_lag(way, lag, row):
        row = row.astype(BF16).astype(F32)
        for lane in range(2):
            table_ref[way, lane, lag + CENTER] = jnp.broadcast_to(
                row[:, lane * LANES : (lane + 1) * LANES], (8, LANES)
            )

    def lag_step(k, _):
        found = lag_row(k.astype(F32))
        for way in range(2):
            store_lag(way, k, found[2 * way])
            store_lag(way, -k, found[2 * way + 1])
        return 0

    lax.fori_loop(1, GRID, lag_step, 0)
    found = lag_row(0.0)
    for way in range(2):
        store_lag(way, 0, found[2 * way] + found[2 * way + 1])

    xs[1, :, D - LANES :] = jnp.zeros((SLOTS, 2 * LANES - D), F32)

    mixed = dot(first_ref[...], wu) * widen(mask_ref[...])
    mixed = mixed.astype(BF16)
    mixed_ref[...] = mixed
    mixed = mixed.astype(F32)
    put_lanes(xs, slice(None), mixed)
    for lane in range(2):
        for j in range(GRID):
            xt[lane, j * GRID : (j + 1) * GRID, :] = xs[lane, pl.ds(j, GRID, stride=GRID), :]

    def scan_step(index, _):
        sublane = pl.multiple_of((index % 4) * 8, 8)
        first = (index // 4) * 8
        for way, src, dst in ((0, xt, rows), (1, xs, cols)):
            for lane in range(2):
                total = block_sum(src, table_ref, way, lane, first, 8, GRID, 0, sublane, 1)
                for t in range(8):
                    place = pl.multiple_of((first + t) * GRID + sublane, 8)
                    dst[lane, pl.ds(place, 8), :] = total[t]
        return 0

    lax.fori_loop(0, 16, scan_step, 0)

    def join_step(i, _):
        place = pl.ds(pl.multiple_of(i * GRID, GRID), GRID)
        mask = mask_ref[place, :]
        both = []
        for lane in range(2):
            down = cols[lane, place, :].astype(BF16).astype(F32)
            both.append((rows[lane, pl.ds(i, GRID, stride=GRID), :] + down) * mask)
        both = jnp.concatenate([both[0], both[1][:, : D - LANES]], axis=1)
        scanned_ref[place, :] = both.astype(BF16)
        return 0

    lax.fori_loop(0, GRID, join_step, 0)

    for block in range(blocks):
        start = pl.multiple_of((block * 2 + core) * rows_slots, rows_slots)
        scanned_own[block * rows_slots : (block + 1) * rows_slots, :] = scanned_ref[
            pl.ds(start, rows_slots), :
        ]

    lane_own = lax.broadcasted_iota(jnp.int32, (OWN, LANES), 1)
    lane_all = lax.broadcasted_iota(jnp.int32, (SLOTS, LANES), 1)
    bias = jnp.where(lane_all == HEAD_DIM, (mask_ref[...] - 1.0) * 1e30, 0.0)
    ones = jnp.where((lane_all == HEAD_DIM) | (lane_all == HEAD_DIM + 1), 1.0, 0.0)
    one_own = jnp.where(lane_own == HEAD_DIM, 1.0, 0.0)
    for h in range(HEADS):
        tile = slice(h * LANES, (h + 1) * LANES)
        q_ref[h] = (
            dot(scanned_own[...], wqkv_ref[0, :, tile]) * HEAD_DIM ** (-0.5) + one_own
        ).astype(BF16)
        k_ref[h] = (dot(scanned_ref[...], wqkv_ref[1, :, tile]) + bias).astype(BF16)
        v_ref[h] = (dot(scanned_ref[...], wqkv_ref[2, :, tile]) + ones).astype(BF16)


def middle_kernel(
    core_ref,
    own_ref,
    mask_ref,
    gains_ref,
    sel_1_ref,
    sel_o_ref,
    sel_2_ref,
    q_ref,
    k_ref,
    v_ref,
    *refs,
):
    blocks = own_ref.shape[0]
    middle_body(
        core_ref,
        own_ref,
        mask_ref,
        gains_ref,
        sel_1_ref,
        sel_o_ref,
        sel_2_ref,
        q_ref,
        k_ref,
        v_ref,
        refs[:blocks],
        refs[blocks : 2 * blocks],
        *refs[2 * blocks :],
    )


def middle_body(
    core_ref,
    own_ref,
    mask_ref,
    gains_ref,
    sel_1_ref,
    sel_o_ref,
    sel_2_ref,
    q_ref,
    k_ref,
    v_ref,
    mine_refs,
    got_refs,
    soft_ref,
    lifted_ref,
    out_ref,
    grad_middle_ref,
    gain_ref,
    keep_ref,
    send_ref,
    early_ref,
    scores,
    wo,
    w1,
    w2,
    att,
    outs,
    sums,
    middle,
    second,
    pre,
    hidden,
    grad_pre,
    wire,
):
    core = core_ref[0]
    blocks, _, rows_slots, _ = own_ref.shape
    parts = early_ref.shape[0]
    per_block = D // blocks
    gain = gains_ref[1:2, :]

    left = gather_parts(core_ref, mine_refs, got_refs, 1, early_ref)
    right = gather_parts(core_ref, mine_refs, got_refs, 2, early_ref)
    span = parts // 2 * LANES
    for half in range(2):
        w1[:, half * FF // 2 : (half + 1) * FF // 2] = dot(
            left[:, half * span : (half + 1) * span], sel_1_ref[...]
        ).astype(BF16)
    out_weight = dot(left, sel_o_ref[...]).astype(BF16)
    for h in range(HEADS):
        wo[h, :HEAD_DIM] = out_weight[h * HEAD_DIM : (h + 1) * HEAD_DIM]
        wo[h, HEAD_DIM:] = jnp.zeros((LANES - HEAD_DIM, D), BF16)
    for g in range(4):
        part = dot(right, sel_2_ref[g])
        for r in range(blocks):
            start = r * 4 * per_block + g * per_block
            w2[start : start + per_block] = part[r * per_block : (r + 1) * per_block].astype(BF16)

    for h in range(HEADS):
        scores[...] = dot_nt(q_ref[h], k_ref[h])

        def soft_step(i, _, h=h):
            place = pl.ds(pl.multiple_of(i * 32, 32), 32)
            values = scores[place, :]
            top = jnp.max(values, -1, keepdims=True)
            soft_ref[h, place, :] = jnp.exp(values - top).astype(BF16)
            return 0

        lax.fori_loop(0, OWN // 32, soft_step, 0)
        raw = dot(soft_ref[h], v_ref[h])
        total = raw[:, HEAD_DIM : HEAD_DIM + 1]
        sums[h] = jnp.broadcast_to(1.0 / total, (OWN, LANES))
        result = raw * sums[h]
        outs[h] = result
        att[h] = result.astype(BF16)

    branch = dot(att[0], wo[0]) + dot(att[1], wo[1]) + dot(att[2], wo[2])
    middle[...] = branch

    def own_mask(block):
        start = pl.multiple_of((block * 2 + core) * rows_slots, rows_slots)
        return widen(mask_ref[pl.ds(start, rows_slots), :])

    def norm_step(block, _):
        place = pl.ds(pl.multiple_of(block * rows_slots, rows_slots), rows_slots)
        mid = own_ref[block, 0].astype(F32) + middle[place, :] * own_mask(block)
        middle[place, :] = mid
        unit, _ = normalise(mid)
        second[place, :] = (unit * gain).astype(BF16)
        return 0

    lax.fori_loop(0, blocks, norm_step, 0)

    pre[...] = dot(second[...], w1[...])
    cot = jnp.concatenate([own_ref[b, 1] for b in range(blocks)], axis=0)
    grad_hidden = scores.at[:, :FF]
    grad_hidden[...] = dot_nt(cot, w2[...])

    def gelu_step(i, _):
        place = pl.ds(pl.multiple_of(i * 16, 16), 16)
        x = pre[place, :]
        phi = 0.5 * (1.0 + lax.erf(x * np.float32(0.5**0.5)))
        hidden[place, :] = (x * phi).astype(BF16)
        slope = phi + x * jnp.exp(x * x * -0.5) * np.float32((2 * np.pi) ** -0.5)
        grad_pre[place, :] = (scores[place, :FF] * slope).astype(BF16)
        return 0

    lax.fori_loop(0, OWN // 16, gelu_step, 0)

    out_ref[...] = (middle[...] + dot(hidden[...], w2[...])).astype(BF16)
    grad_2 = dot_tn(hidden[...], cot).astype(BF16)
    grad_1 = dot_tn(second[...], grad_pre[...]).astype(BF16)
    grad_middle_ref[...] = dot_nt(grad_pre[...], w1[...])

    def back_step(block, total):
        place = pl.ds(pl.multiple_of(block * rows_slots, rows_slots), rows_slots)
        unit, inverse = normalise(middle[place, :])
        grad = grad_middle_ref[place, :]
        total = total + jnp.sum(grad * unit, 0, keepdims=True)
        grad = own_ref[block, 1].astype(F32) + norm_back(grad, gain, unit, inverse)
        grad_middle_ref[place, :] = grad
        second[place, :] = (grad * own_mask(block)).astype(BF16)
        return total

    gain_ref[...] = lax.fori_loop(0, blocks, back_step, jnp.zeros((1, D), F32))

    grad_o = []
    lane_own = lax.broadcasted_iota(jnp.int32, (OWN, LANES), 1)
    for h in range(HEADS):
        grad_o.append(dot_tn(att[h], second[...])[:HEAD_DIM])
        grad_att = dot_nt(second[...], wo[h]).astype(BF16).astype(F32)
        scaled = (grad_att * sums[h]).astype(BF16).astype(F32)
        shift = -jnp.sum(scaled * outs[h], -1, keepdims=True)
        high = shift.astype(BF16).astype(F32)
        lifted = jnp.where(
            lane_own == HEAD_DIM, high, jnp.where(lane_own == HEAD_DIM + 1, shift - high, scaled)
        )
        lifted_ref[h] = lifted.astype(BF16)

    for half in range(2):
        wire[:, half * span : (half + 1) * span] = dot_nt(
            grad_1[:, half * FF // 2 : (half + 1) * FF // 2], sel_1_ref[...]
        )
    grad_o = jnp.concatenate(grad_o, axis=0).astype(BF16)
    wire[...] += dot_nt(grad_o, sel_o_ref[...])

    def deliver(lanes):
        for m in range(parts):
            value = wire[:, m * LANES : (m + 1) * LANES].astype(BF16)

            @pl.when(core == m % 2)
            def _(value=value, m=m):
                put_blocks(keep_ref, m // 2, lanes, value)

            @pl.when(core != m % 2)
            def _(value=value, m=m):
                put_blocks(send_ref, m // 2, lanes, value)

    deliver(slice(0, LANES))
    total = None
    for g in range(4):
        rows = [
            grad_2[r * 4 * per_block + g * per_block : r * 4 * per_block + (g + 1) * per_block]
            for r in range(blocks)
        ]
        part = dot_nt(jnp.concatenate(rows, axis=0), sel_2_ref[g])
        total = part if total is None else total + part
    wire[...] = total
    deliver(slice(LANES, 2 * LANES))


def attention_back_kernel(
    core_ref,
    soft_ref,
    lifted_ref,
    q_ref,
    k_ref,
    v_ref,
    scanned_ref,
    wqkv_ref,
    part_ref,
    grad_w_ref,
    scores,
    grad_scores,
    triple,
    grad_q,
    scanned_own,
    part,
    *,
    blocks,
):
    core = core_ref[0]
    rows_slots = OWN // blocks
    for h in range(HEADS):
        tile = slice(h * LANES, (h + 1) * LANES)
        scores[...] = dot_nt(lifted_ref[h], v_ref[h])

        def back_step(i, _, h=h):
            place = pl.ds(pl.multiple_of(i * 32, 32), 32)
            grad_scores[place, :] = (soft_ref[h, place, :].astype(F32) * scores[place, :]).astype(
                BF16
            )
            return 0

        lax.fori_loop(0, OWN // 32, back_step, 0)
        grad_q[:, tile] = (dot(grad_scores[...], k_ref[h]).astype(BF16) * HEAD_DIM ** (-0.5)).astype(
            BF16
        )
        triple[0, :, tile] = dot_tn(grad_scores[...], q_ref[h]).astype(BF16)
        triple[1, :, tile] = dot_tn(soft_ref[h], lifted_ref[h]).astype(BF16)

    part[...] = dot_nt(triple[0], wqkv_ref[1]) + dot_nt(triple[1], wqkv_ref[2])
    from_q = dot_nt(grad_q[...], wqkv_ref[0])
    for block in range(blocks):
        here = slice(block * rows_slots, (block + 1) * rows_slots)
        place = pl.ds(pl.multiple_of((block * 2 + core) * rows_slots, rows_slots), rows_slots)
        part[place, :] += from_q[here]
        scanned_own[here, :] = scanned_ref[place, :]
    part_ref[...] = part[...].astype(BF16)
    grad_w_ref[0] = dot_tn(scanned_own[...], grad_q[...]).astype(BF16)
    grad_w_ref[1] = dot_tn(scanned_ref[...], triple[0]).astype(BF16)
    grad_w_ref[2] = dot_tn(scanned_ref[...], triple[1]).astype(BF16)


def scan_back_kernel(
    starts,
    width,
    core_ref,
    own_ref,
    mask_ref,
    gains_ref,
    part_ref,
    got_ref,
    mixed_ref,
    first_ref,
    table_ref,
    rates_ref,
    wu_ref,
    grad_middle_ref,
    grad_w_ref,
    gain_two_ref,
    out_own_ref,
    sel_u_ref,
    sel_rc_ref,
    sel_q_ref,
    keep_ref,
    send_ref,
    gains_out_ref,
    *refs,
):
    routed_refs, scratch = refs[:-13], refs[-13:]
    scan_back_body(
        starts,
        width,
        core_ref,
        own_ref,
        mask_ref,
        gains_ref,
        part_ref,
        got_ref,
        mixed_ref,
        first_ref,
        table_ref,
        rates_ref,
        wu_ref,
        grad_middle_ref,
        grad_w_ref,
        gain_two_ref,
        sel_u_ref,
        sel_rc_ref,
        sel_q_ref,
        keep_ref,
        send_ref,
        gains_out_ref,
        *scratch,
    )
    images = len(routed_refs) // 2
    mine = core_ref[0] * images + core_ref[1] % images
    slots = own_ref.shape[2]
    grad = scratch[0]
    for j, routed in enumerate(routed_refs):
        place = pl.ds(pl.multiple_of((mine ^ j) * slots, slots), slots)
        routed[0] = pack(out_own_ref[place, :])
        routed[1] = pack(grad[place, :])


def scan_back_body(
    starts,
    width,
    core_ref,
    own_ref,
    mask_ref,
    gains_ref,
    part_ref,
    got_ref,
    mixed_ref,
    first_ref,
    table_ref,
    rates_ref,
    wu_ref,
    grad_middle_ref,
    grad_w_ref,
    gain_two_ref,
    sel_u_ref,
    sel_rc_ref,
    sel_q_ref,
    keep_ref,
    send_ref,
    gains_out_ref,
    grad_ref,
    gs,
    gt,
    xs,
    xt,
    own,
    rows,
    cols,
    lag_sums,
    lag_rows,
    mixed_back,
    first_own,
    wire,
):
    core = core_ref[0]
    blocks, _, rows_slots, _ = own_ref.shape
    half_rows = rows_slots // GRID
    own_rows = GRID // 2
    parts = sel_rc_ref.shape[0] // LANES
    gain = gains_ref[0:1, :]
    pad = jnp.zeros((SLOTS, 2 * LANES - D), F32)

    xs[1, :, D - LANES :] = pad
    gs[1, :, D - LANES :] = pad
    put_lanes(xs, slice(None), mixed_ref[...].astype(F32))
    grads = (part_ref[...].astype(F32) + got_ref[...].astype(F32)) * widen(mask_ref[...])
    put_lanes(gs, slice(None), grads.astype(BF16).astype(F32))

    def place_of(block):
        return pl.ds(pl.multiple_of((block * 2 + core) * rows_slots, rows_slots), rows_slots)

    for block in range(blocks):
        here = slice(block * rows_slots, (block + 1) * rows_slots)
        first_own[here, :] = first_ref[place_of(block), :]
    for src, dst in ((gs, gt), (xs, xt)):
        for lane in range(2):
            for block in range(blocks):
                here = slice(block * rows_slots, (block + 1) * rows_slots)
                own[lane, here, :] = src[lane, place_of(block), :]
            for j in range(GRID):
                dst[lane, j * own_rows : (j + 1) * own_rows, :] = own[
                    lane, pl.ds(j, own_rows, stride=GRID), :
                ]

    def row_step(index, _):
        sublane = pl.multiple_of((index % 2) * 8, 8)
        first = (index // 2) * 8
        for lane in range(2):
            total = block_sum(gt, table_ref, 0, lane, first, 8, own_rows, 0, sublane, -1)
            for t in range(8):
                rows[lane, pl.ds(pl.multiple_of((first + t) * own_rows + sublane, 8), 8), :] = total[
                    t
                ]
        return 0

    lax.fori_loop(0, 8, row_step, 0)

    def col_step(index, _):
        sublane = pl.multiple_of((index % 4) * 8, 8)
        block = index // 4
        first = (block * 2 + core) * half_rows
        for lane in range(2):
            total = block_sum(gs, table_ref, 1, lane, first, half_rows, GRID, 0, sublane, -1)
            for t in range(half_rows):
                at = pl.multiple_of((block * half_rows + t) * GRID + sublane, 8)
                cols[lane, pl.ds(at, 8), :] = total[t]
        return 0

    lax.fori_loop(0, blocks * 4, col_step, 0)

    lag_sums[...] = jnp.zeros_like(lag_sums)

    def add_lags(way, lane, first, count, base, gref, xref, step, groups):
        total = {}
        for u in range(groups):
            g = [
                gref[lane, pl.ds(pl.multiple_of((first + t) * step + u * 8, 8), 8), :]
                for t in range(count)
            ]
            for s in range(8):
                x = xref[lane, pl.ds(pl.multiple_of((base + s) * step + u * 8, 8), 8), :]
                for t in range(count):
                    term = g[t] * x
                    total[t - s] = term if t - s not in total else total[t - s] + term
        for lag, value in total.items():
            at = first - base + (lag + CENTER)
            lag_sums[way, lane, at] += value

    def lag_row_step(index, _):
        first, base = (index // 4) * 8, (index % 4) * 8
        for lane in range(2):
            add_lags(0, lane, first, 8, base, gt, xt, own_rows, own_rows // 8)
        return 0

    lax.fori_loop(0, 16, lag_row_step, 0)

    def lag_col_step(index, _):
        first, base = ((index // 4) * 2 + core) * half_rows, (index % 4) * 8
        for lane in range(2):
            add_lags(1, lane, first, half_rows, base, gs, xs, GRID, GRID // 8)
        return 0

    lax.fori_loop(0, blocks * 4, lag_col_step, 0)

    for way in range(2):
        for lane in range(2):
            lag_rows[way, :, lane * LANES : (lane + 1) * LANES] = jnp.sum(lag_sums[way, lane], 1)

    decay, coef = rates_ref[: 4 * STATE], rates_ref[4 * STATE :]

    def table_step(k, carry):
        to_rate, to_coef = carry
        lag = k.astype(F32)
        powers = jnp.exp(-decay * lag)
        grads = []
        for way in range(2):
            for at in (CENTER + k, CENTER - k):
                grads.append(
                    jnp.broadcast_to(lag_rows[way, pl.ds(at, 1), :], (STATE, 2 * LANES))
                )
        scaled = jnp.concatenate(grads, axis=0) * powers
        return to_rate - lag * scaled, to_coef + scaled

    zero = jnp.zeros((4 * STATE, 2 * LANES), F32)
    to_rate, to_coef = lax.fori_loop(0, GRID, table_step, (zero, zero))
    grad_rc = jnp.concatenate([to_rate * coef, to_coef], axis=0).T[:D].astype(BF16)

    def join_step(i, _):
        place = pl.ds(pl.multiple_of(i * GRID, GRID), GRID)
        block = i // half_rows
        at = ((block * 2 + core) * half_rows + i % half_rows) * GRID
        mask = mask_ref[pl.ds(pl.multiple_of(at, GRID), GRID), :]
        both = []
        for lane in range(2):
            down = cols[lane, place, :].astype(BF16).astype(F32)
            both.append((rows[lane, pl.ds(i, GRID, stride=own_rows), :] + down) * mask)
        both = jnp.concatenate([both[0], both[1][:, : D - LANES]], axis=1)
        mixed_back[place, :] = both.astype(BF16)
        return 0

    lax.fori_loop(0, own_rows, join_step, 0)
    grad_u = dot_tn(first_own[...], mixed_back[...]).astype(BF16)
    grad_first = dot_nt(mixed_back[...], wu_ref[...])
    gain_one = jnp.zeros((1, D), F32)
    for block in range(blocks):
        here = slice(block * rows_slots, (block + 1) * rows_slots)
        unit, inverse = normalise(own_ref[block, 0].astype(F32))
        grad = grad_first[here]
        gain_one = gain_one + jnp.sum(grad * unit, 0, keepdims=True)
        grad = grad_middle_ref[here, :] + norm_back(grad, gain, unit, inverse)
        grad_ref[here, :] = grad.astype(BF16)

    wire[...] = dot_nt(grad_u, sel_u_ref[...]) + dot_nt(grad_rc, sel_rc_ref[...])
    for third in range(3):
        span = slice(starts[third] * LANES, (starts[third] + width) * LANES)
        wire[:, span] += dot_nt(grad_w_ref[third], sel_q_ref[third])
    for m in range(parts):
        value = wire[:, m * LANES : (m + 1) * LANES].astype(BF16)

        @pl.when(core == m % 2)
        def _(value=value, m=m):
            put_blocks(keep_ref, m // 2, slice(None), value)

        @pl.when(core != m % 2)
        def _(value=value, m=m):
            put_blocks(send_ref, m // 2, slice(None), value)

    lines = []
    for value in (gain_one, gain_two_ref[...]):
        high = value.astype(BF16).astype(F32)
        for piece in (high, value - high):
            lines.append(piece[:, :LANES])
            lines.append(
                jnp.concatenate([piece[:, LANES:], jnp.zeros((1, 2 * LANES - D), F32)], axis=1)
            )
    lines.append(jnp.zeros((8, LANES), F32))
    gains_out_ref[...] = jnp.concatenate(lines, axis=0).astype(BF16)


def split(value):
    high = value.astype(BF16).astype(F32)
    return jnp.concatenate([high, value - high], axis=0)


def early_sum_kernel(place_ref, keep_ref, got_ref, *out_refs):
    for k, out_ref in enumerate(out_refs):
        block = place_ref[1] ^ k
        for z in range(keep_ref.shape[1]):
            total = keep_ref[block, z].astype(F32) + got_ref[block, z].astype(F32)
            out_ref[z] = total.astype(BF16)


def late_sum_kernel(place_ref, keep_ref, got_ref, gains_ref, gains_got_ref, *out_refs):
    depth = keep_ref.shape[1]
    gains = gains_ref[...].astype(F32) + gains_got_ref[...].astype(F32)
    lines = []
    for g in range(2):
        for lane in range(2):
            at = 4 * g + lane
            lines.append(gains[at : at + 1] + gains[at + 2 : at + 3])
    gains = jnp.concatenate([split(jnp.concatenate(lines, axis=0)), jnp.zeros((8, LANES), F32)], axis=0)
    gains = gains.astype(BF16)
    for k, out_ref in enumerate(out_refs):
        block = place_ref[1] ^ k
        rows = keep_ref.shape[2]
        for z in range(depth):
            total = keep_ref[block, z].astype(F32) + got_ref[block, z].astype(F32)
            out_ref[z, :rows] = total.astype(BF16)
            out_ref[z, rows:] = gains


def row_sum_kernel(blocks, place_ref, *refs):
    early_refs, late_refs, out_refs = refs[:blocks], refs[blocks : 2 * blocks], refs[2 * blocks :]
    rows = early_refs[0].shape[1]
    for j, out_ref in enumerate(out_refs):
        z = place_ref[2] ^ j
        early = early_refs[0][z].astype(F32)
        late = late_refs[0][z].astype(F32)
        for k in range(1, blocks):
            early = early + early_refs[k][z].astype(F32)
            late = late + late_refs[k][z].astype(F32)
        out_ref[:rows, LANES:] = early.astype(BF16)
        out_ref[:rows, :LANES] = late[:rows].astype(BF16)
        gains = split(late[rows : rows + 4] + late[rows + 4 : rows + 8])
        gains = jnp.concatenate([gains, jnp.zeros((8, LANES), F32)], axis=0).astype(BF16)
        out_ref[rows:, :LANES] = gains
        out_ref[rows:, LANES:] = jnp.zeros((16, 2 * LANES), BF16)


def final_kernel(parts, *refs):
    final_body(parts, refs[: parts // 2], *refs[parts // 2 :])


def final_body(
    parts,
    got_refs,
    g1_ref,
    g2_ref,
    wu_ref,
    rate_ref,
    coef_ref,
    qkv_ref,
    wo_ref,
    fc1_ref,
    fc2_ref,
):
    a_u, a_r, a_q, (o_u, o_r, o_c, o_q) = late_layout(parts)
    total = got_refs[0][...].astype(F32)
    for ref in got_refs[1:]:
        total = total + ref[...].astype(F32)
    early = total[: fc1_ref.shape[0], LANES:]
    total = total[:, :LANES]
    rows = fc1_ref.shape[0]
    weights, gains = total[:rows], total[rows:]
    turned = weights.T
    wu_ref[...] = turned[o_u : o_u + a_u]
    rate_ref[...] = turned[o_r : o_r + a_r]
    coef_ref[...] = turned[o_c : o_c + a_r]
    qkv_ref[...] = weights[:, o_q : o_q + a_q]
    gains = gains[0:4] + gains[4:8]
    for g, ref in ((0, g1_ref), (1, g2_ref)):
        ref[...] = jnp.concatenate(
            [gains[2 * g : 2 * g + 1], gains[2 * g + 1 : 2 * g + 2, : D - LANES]], axis=1
        )
    a_1, a_o = FF // parts, D // parts
    fc1_ref[...] = early[:, :a_1]
    wo_ref[...] = early[:, :LANES].T[a_1 : a_1 + a_o]
    turned = early[:, LANES:].T
    fc2_ref[...] = jnp.concatenate([turned[g * a_o : (g + 1) * a_o] for g in range(4)], axis=1)


def per_device(
    patches, valid_mask, norm_gains, w_u, decay_rate, out_coef, w_qkv, w_o, w_fc1, w_fc2, cotangent
):
    images, rows_here, _, _ = patches.shape
    depth, blocks = lax.axis_size("z"), lax.axis_size("row")
    parts = 2 * depth
    rows_slots = rows_here // 2 * GRID
    packed_rows = rows_slots * 3 // 2
    core = lax.axis_index("core")
    row = lax.axis_index("row")
    swap = [(0, 1), (1, 0)]
    place = jnp.stack([core, row, lax.axis_index("z")]).astype(jnp.int32)
    shape = jax.ShapeDtypeStruct

    def swapped(value):
        return lax.ppermute(value, "core", swap)

    def exchanged(values, axis):
        size = len(values)
        return [values[0]] + [
            lax.ppermute(values[k], axis, [(i, i ^ k) for i in range(size)]) for k in range(1, size)
        ]

    def to_chips(value, j):
        pairs = []
        for home in range(2):
            for source in range(blocks):
                target, image = divmod(source ^ j, images)
                pairs.append((home * blocks + source, target * blocks + home * images + image))
        return lax.ppermute(value, ("core", "row"), pairs)

    def to_homes(value, j):
        pairs = []
        for source in range(2):
            for chip in range(blocks):
                home, image = divmod(chip, images)
                target = (source * images + image) ^ j
                pairs.append((source * blocks + chip, home * blocks + target))
        return lax.ppermute(value, ("core", "row"), pairs)

    sel_u, sel_rc, sel_q, starts, width = late_selections(parts)
    sel_1, sel_o, sel_2 = early_selections(parts)

    rows_weight = w_u.shape[0]
    payload = shape((3 * packed_rows + GRID, LANES), BF16)
    shard = shape((rows_weight, 3 * LANES), BF16)
    sources = [value.reshape(images, rows_here * GRID, D) for value in (patches, cotangent)]
    if rows_weight % 16 == 0:
        weights, *routed = pl.pallas_call(
            depart_kernel,
            name="depart",
            out_shape=(shard,) + (payload,) * blocks,
            in_specs=[SMEM] + [VMEM] * 10,
            out_specs=[VMEM] * (1 + blocks),
            compiler_params=compiler(LARGE),
        )(
            place,
            w_u.T,
            decay_rate.T,
            out_coef.T,
            w_o.T,
            w_fc2.T,
            w_qkv,
            w_fc1,
            *sources,
            valid_mask,
        )
    else:

        def fill(pieces):
            joined = jnp.concatenate(pieces, axis=1)
            return jnp.pad(joined, ((0, 0), (0, LANES - joined.shape[1])))

        weights = jnp.concatenate(
            [
                fill([w_u, decay_rate, out_coef, w_qkv]),
                fill([w_fc1, w_o]),
                fill([w_fc2[g * rows_weight : (g + 1) * rows_weight] for g in range(4)]),
            ],
            axis=1,
        )
        routed = pl.pallas_call(
            route_kernel,
            name="route",
            out_shape=(payload,) * blocks,
            in_specs=[SMEM] + [VMEM] * 3,
            out_specs=[VMEM] * blocks,
            compiler_params=compiler(LARGE),
        )(place, *sources, valid_mask)

    weights = jnp.concatenate(exchanged([weights] * depth, "z"), axis=0)
    weights = exchanged([weights] * blocks, "row")
    weights = weights + [swapped(value) for value in weights]
    routed = [to_chips(value, j) for j, value in enumerate(routed)]
    own, first, mask = pl.pallas_call(
        norm_kernel,
        name="first_norm",
        out_shape=(
            shape((blocks, 2, rows_slots, D), BF16),
            shape((SLOTS, D), BF16),
            shape((SLOTS, LANES), F32),
        ),
        in_specs=[SMEM] + [VMEM] * (1 + blocks),
        out_specs=[VMEM] * 3,
        compiler_params=compiler(8 << 20),
    )(place, norm_gains, *routed)

    head_own = shape((HEADS, OWN, LANES), BF16)
    head_all = shape((HEADS, SLOTS, LANES), BF16)
    part_scratch = pltpu.VMEM((parts, blocks, rows_weight, LANES), BF16)
    q, k, v, scanned, mixed, table, rates, wu, wqkv = pl.pallas_call(
        lambda *refs: scan_kernel(starts, width, *refs, blocks=blocks),
        name="scan_forward",
        out_shape=(
            head_own,
            head_all,
            head_all,
            shape((SLOTS, D), BF16),
            shape((SLOTS, D), BF16),
            shape((2, 2, LAGS, 8, LANES), F32),
            shape((LANES, 2 * LANES), F32),
            shape((D, D), BF16),
            shape((3, D, TILE), BF16),
        ),
        in_specs=[SMEM] + [VMEM] * (5 + 2 * blocks),
        out_specs=[VMEM] * 9,
        scratch_shapes=[part_scratch]
        + [pltpu.VMEM((2, SLOTS, LANES), F32)] * 4
        + [pltpu.VMEM((OWN, D), BF16)],
        compiler_params=compiler(),
    )(place, first, mask, sel_u, sel_rc, sel_q, *weights)

    wire_early = shape((blocks, depth, rows_weight, 2 * LANES), BF16)
    soft, lifted, out_own, grad_middle, gain_two, early_keep, early_send = pl.pallas_call(
        middle_kernel,
        name="attention_and_feed_forward",
        out_shape=(
            shape((HEADS, OWN, SLOTS), BF16),
            head_own,
            shape((OWN, D), BF16),
            shape((OWN, D), F32),
            shape((1, D), F32),
            wire_early,
            wire_early,
        ),
        in_specs=[SMEM] + [VMEM] * (9 + 2 * blocks),
        out_specs=[VMEM] * 7,
        scratch_shapes=[
            part_scratch,
            pltpu.VMEM((OWN, SLOTS), F32),
            pltpu.VMEM((HEADS, LANES, D), BF16),
            pltpu.VMEM((D, FF), BF16),
            pltpu.VMEM((FF, D), BF16),
            pltpu.VMEM((HEADS, OWN, LANES), BF16),
            pltpu.VMEM((HEADS, OWN, LANES), F32),
            pltpu.VMEM((HEADS, OWN, LANES), F32),
            pltpu.VMEM((OWN, D), F32),
            pltpu.VMEM((OWN, D), BF16),
            pltpu.VMEM((OWN, FF), F32),
            pltpu.VMEM((OWN, FF), BF16),
            pltpu.VMEM((OWN, FF), BF16),
            pltpu.VMEM((D, parts * LANES), F32),
        ],
        compiler_params=compiler(),
    )(place, own, mask, norm_gains, sel_1, sel_o, sel_2, q, k, v, *weights)

    early_recv = swapped(early_send)

    part, grad_w = pl.pallas_call(
        lambda *refs: attention_back_kernel(*refs, blocks=blocks),
        name="attention_backward",
        out_shape=(shape((SLOTS, D), BF16), shape((3, D, TILE), BF16)),
        in_specs=[SMEM] + [VMEM] * 7,
        out_specs=[VMEM] * 2,
        scratch_shapes=[
            pltpu.VMEM((OWN, SLOTS), F32),
            pltpu.VMEM((OWN, SLOTS), BF16),
            pltpu.VMEM((2, SLOTS, TILE), BF16),
            pltpu.VMEM((OWN, TILE), BF16),
            pltpu.VMEM((OWN, D), BF16),
            pltpu.VMEM((SLOTS, D), F32),
        ],
        compiler_params=compiler(),
    )(place, soft, lifted, q, k, v, scanned, wqkv)

    part_got = swapped(part)
    early_keep, early_recv, part = lax.optimization_barrier((early_keep, early_recv, part))
    early = pl.pallas_call(
        early_sum_kernel,
        name="early_sum",
        out_shape=(shape((depth, rows_weight, 2 * LANES), BF16),) * blocks,
        in_specs=[SMEM] + [VMEM] * 2,
        out_specs=[VMEM] * blocks,
        compiler_params=compiler(8 << 20),
    )(place, early_keep, early_recv)
    early, part_got = lax.optimization_barrier((early, part_got))
    early = exchanged(early, "row")
    wire_late = shape((blocks, depth, rows_weight, LANES), BF16)
    payload = shape((2, packed_rows, LANES), BF16)
    late_keep, late_send, gains, *routed = pl.pallas_call(
        lambda *refs: scan_back_kernel(starts, width, *refs),
        name="scan_backward",
        out_shape=(wire_late, wire_late, shape((16, LANES), BF16)) + (payload,) * blocks,
        in_specs=[SMEM] + [VMEM] * 17,
        out_specs=[VMEM] * (3 + blocks),
        scratch_shapes=[
            pltpu.VMEM((OWN, D), BF16),
            pltpu.VMEM((2, SLOTS, LANES), F32),
            pltpu.VMEM((2, OWN, LANES), F32),
            pltpu.VMEM((2, SLOTS, LANES), F32),
            pltpu.VMEM((2, OWN, LANES), F32),
            pltpu.VMEM((2, OWN, LANES), F32),
            pltpu.VMEM((2, OWN, LANES), F32),
            pltpu.VMEM((2, OWN, LANES), F32),
            pltpu.VMEM((2, 2, LAGS, 8, LANES), F32),
            pltpu.VMEM((2, LAGS, 2 * LANES), F32),
            pltpu.VMEM((OWN, D), BF16),
            pltpu.VMEM((OWN, D), BF16),
            pltpu.VMEM((D, parts * LANES), F32),
        ],
        compiler_params=compiler(),
    )(
        place,
        own,
        mask,
        norm_gains,
        part,
        part_got,
        mixed,
        first,
        table,
        rates,
        wu,
        grad_middle,
        grad_w,
        gain_two,
        out_own,
        sel_u,
        sel_rc,
        sel_q,
    )

    late = pl.pallas_call(
        late_sum_kernel,
        name="late_sum",
        out_shape=(shape((depth, rows_weight + 16, LANES), BF16),) * blocks,
        in_specs=[SMEM] + [VMEM] * 4,
        out_specs=[VMEM] * blocks,
        compiler_params=compiler(8 << 20),
    )(place, late_keep, swapped(late_send), gains, swapped(gains))
    late = exchanged(late, "row")
    summed = pl.pallas_call(
        lambda *refs: row_sum_kernel(blocks, *refs),
        name="row_sum",
        out_shape=(shape((rows_weight + 16, 3 * LANES), BF16),) * depth,
        in_specs=[SMEM] + [VMEM] * (2 * blocks),
        out_specs=[VMEM] * depth,
        compiler_params=compiler(8 << 20),
    )(place, *early, *late)
    summed = exchanged(summed, "z")

    routed = [to_homes(value, j) for j, value in enumerate(routed)]
    whole = shape((images, rows_here * GRID, D), BF16)
    block_out, grad_patches = pl.pallas_call(
        home_kernel,
        name="home",
        out_shape=(whole, whole),
        in_specs=[SMEM] + [VMEM] * blocks,
        out_specs=[VMEM] * 2,
        compiler_params=compiler(8 << 20),
    )(place, *routed)

    turned = (4 * STATE // parts, rows_weight)
    g1, g2, f_u, f_rate, f_coef, f_qkv, f_o, f_1, f_2 = pl.pallas_call(
        lambda *refs: final_kernel(parts, *refs),
        name="final_sum",
        out_shape=(
            shape((1, D), F32),
            shape((1, D), F32),
            shape((D // parts, rows_weight), F32),
            shape(turned, F32),
            shape(turned, F32),
            shape((rows_weight, 3 * D // parts), F32),
            shape((D // parts, rows_weight), F32),
            shape((rows_weight, FF // parts), F32),
            shape((D // parts, 4 * rows_weight), F32),
        ),
        in_specs=[VMEM] * depth,
        out_specs=[VMEM] * 9,
        compiler_params=compiler(8 << 20),
    )(*summed)
    return (
        block_out.reshape(patches.shape),
        grad_patches.reshape(patches.shape),
        g1.reshape(D),
        g2.reshape(D),
        f_u.T,
        f_rate.T,
        f_coef.T,
        f_qkv,
        f_o.T,
        f_1,
        f_2.T,
    )


def solution(mesh):
    images, rows = mesh.devices.shape
    fine = Mesh(mesh.devices.reshape(images // 2, 2, rows), ("z", "core", "row"))
    img = ("z", "core")
    grid = P(img, "row", None, None)
    weight = P("row", img)
    in_specs = (grid, P(img, None, None), P()) + (weight,) * 7 + (grid,)
    out_specs = (grid, grid, P(), P()) + (weight,) * 7
    return jax.shard_map(
        per_device, mesh=fine, in_specs=in_specs, out_specs=out_specs, check_vma=False
    )
```

```python
import jax
import jax.numpy as jnp
import numpy as np
from jax import lax
from jax.experimental import pallas as pl
from jax.experimental.pallas import tpu as pltpu
from jax.sharding import Mesh
from jax.sharding import PartitionSpec as P

HEADS = 3
HEAD_DIM = 64
STATE = 16
GRID = 32
SLOTS = GRID * GRID
OWN = SLOTS // 2
D = HEADS * HEAD_DIM
FF = 4 * D
LANES = 128
TILE = HEADS * LANES
LAGS = 2 * GRID
CENTER = GRID - 1
EPS = 1e-05
BF16 = jnp.bfloat16
F32 = jnp.float32


def late_layout(parts):
    a_u, a_r, a_q = D // parts, 4 * STATE // parts, 3 * D // parts
    return a_u, a_r, a_q, (0, a_u, a_u + a_r, a_u + 2 * a_r)


def late_spans(parts):
    a_q = 3 * D // parts
    first = [third * D // a_q for third in range(3)]
    last = [((third + 1) * D - 1) // a_q for third in range(3)]
    width = max(stop - start + 1 for start, stop in zip(first, last))
    return [min(start, parts - width) for start in first], width


def early_selections(parts):
    a_1, a_o = FF // parts, D // parts
    half = parts // 2
    sel_1 = np.zeros((half, LANES, FF // 2), np.float32)
    sel_o = np.zeros((parts, LANES, D), np.float32)
    sel_2 = np.zeros((4, parts, LANES, D), np.float32)
    for m in range(half):
        for col in range(a_1):
            sel_1[m, col, m * a_1 + col] = 1
    for m in range(parts):
        for col in range(a_o):
            sel_o[m, a_1 + col, m * a_o + col] = 1
            for g in range(4):
                sel_2[g, m, g * a_o + col, m * a_o + col] = 1
    return (
        sel_1.reshape(half * LANES, FF // 2).astype(BF16),
        sel_o.reshape(parts * LANES, D).astype(BF16),
        sel_2.reshape(4, parts * LANES, D).astype(BF16),
    )


def lane_and_part(shape):
    place = lax.broadcasted_iota(jnp.int32, shape, 0)
    return place % LANES, place // LANES, lax.broadcasted_iota(jnp.int32, shape, 1)


def put_late_selections(starts, parts, sel_u_ref, sel_rc_ref, sel_q_ref):
    a_u, a_r, a_q, (o_u, o_r, o_c, o_q) = late_layout(parts)

    def put(hit):
        return jnp.where(hit, 1.0, 0.0).astype(BF16)

    lane, part, col = lane_and_part(sel_u_ref.shape)
    sel_u_ref[...] = put((lane < a_u) & (part * a_u + lane == col))
    lane, part, col = lane_and_part(sel_rc_ref.shape)
    rate = (lane >= o_r) & (lane < o_c) & (part * a_r + lane - o_r == col)
    coef = (lane >= o_c) & (lane < o_q) & (part * a_r + lane - o_c + 4 * STATE == col)
    sel_rc_ref[...] = put(rate | coef)
    lane, part, col = lane_and_part(sel_q_ref.shape[1:])
    whole = jnp.where(
        col % LANES < HEAD_DIM, col // LANES * HEAD_DIM + col % LANES, -4 * D
    )
    for third in range(3):
        here = (part + starts[third]) * a_q + lane - o_q - third * D
        sel_q_ref[third] = put((lane >= o_q) & (lane < o_q + a_q) & (here == whole))


def dot(a, b):
    return lax.dot_general(a, b, (((1,), (0,)), ((), ())), preferred_element_type=F32)


def dot_nt(a, b):
    return lax.dot_general(a, b, (((1,), (1,)), ((), ())), preferred_element_type=F32)


def dot_tn(a, b):
    return lax.dot_general(a, b, (((0,), (0,)), ((), ())), preferred_element_type=F32)


def normalise(values):
    center = values - jnp.mean(values, -1, keepdims=True)
    spread = jnp.mean(center * center, -1, keepdims=True)
    inverse = lax.rsqrt(spread + EPS)
    return center * inverse, inverse


def norm_back(grad, gain, unit, inverse):
    scaled = grad * gain
    first = jnp.mean(scaled, -1, keepdims=True)
    second = jnp.mean(scaled * unit, -1, keepdims=True)
    return inverse * (scaled - first - unit * second)


def widen(mask):
    return jnp.concatenate([mask, mask[:, : D - LANES]], axis=1)


def put_blocks(ref, z, lanes, value):
    rows = ref.shape[2]
    for r in range(ref.shape[0]):
        ref[r, z, :, lanes] = value[r * rows : (r + 1) * rows]


def put_late(ref, z, value):
    rows = ref.shape[1]
    depth = ref.shape[0] * rows // D
    for r in range(D // rows):
        ref[r * depth + z] = value[r * rows : (r + 1) * rows]


def put_lanes(ref, rows, values):
    ref[0, rows, :] = values[:, :LANES]
    ref[1, rows, : D - LANES] = values[:, LANES:]


def block_sum(src, table, way, lane, first, count, step, offset, sublane, sign):
    total = [None] * count
    for base in range(0, GRID, 8):
        low, high = -(base + 7), count - 1 - base
        coef = {
            lag: table[way, lane, first * sign + (lag * sign + CENTER)]
            for lag in range(low, high + 1)
        }
        for s in range(base, base + 8):
            x = src[lane, pl.ds(pl.multiple_of(s * step + sublane, 8), 8), :]
            for t in range(count):
                term = coef[t - s] * x
                total[t] = term if total[t] is None else total[t] + term
    return total


def gather_parts(mine_refs, got_refs, block, out_ref):
    core, row, depth = lax.axis_index("core"), lax.axis_index("row"), lax.axis_index("z")
    lanes = slice(block * LANES, (block + 1) * LANES)
    count = out_ref.shape[0] // 2
    rows = out_ref.shape[2]
    for refs, which in ((mine_refs, core), (got_refs, 1 - core)):
        for k, ref in enumerate(refs):
            for j in range(count):
                out_ref[2 * (depth ^ j) + which, row ^ k] = ref[j, :, lanes]
    wide = []
    for m in range(2 * count):
        wide.append(jnp.concatenate([out_ref[m, r] for r in range(out_ref.shape[1])], axis=0))
    return jnp.concatenate(wide, axis=1)


LARGE = 60 << 20


def compiler(limit=24 << 20):
    return pltpu.CompilerParams(vmem_limit_bytes=limit)


VMEM = pl.BlockSpec(memory_space=pltpu.VMEM)


def pack(values):
    half = values.shape[0] // 2
    tail = jnp.concatenate([values[:half, LANES:], values[half:, LANES:]], axis=1)
    return jnp.concatenate([values[:, :LANES], tail], axis=0)


def unpack(packed):
    count = packed.shape[0] * 2 // 3
    tail = packed[count:]
    tail = jnp.concatenate([tail[:, : D - LANES], tail[:, D - LANES :]], axis=0)
    return jnp.concatenate([packed[:count], tail], axis=1)


def pack_weights_kernel(turned_refs, qkv_ref, fc1_ref, out_ref):
    wu, rate, coef, wo, fc2 = [ref[...].astype(F32) for ref in turned_refs]
    rows = qkv_ref.shape[0]
    a_o, a_r = wo.shape[0], rate.shape[0]
    pieces = [wu, rate, coef, wo] + [fc2[:, g * rows : (g + 1) * rows] for g in range(4)]
    joined = jnp.concatenate(pieces, axis=0)
    joined = jnp.concatenate([joined, jnp.zeros((joined.shape[0], LANES - rows), F32)], axis=1)
    joined = joined.T[:rows]
    first, second = a_o + 2 * a_r, 2 * a_o + 2 * a_r

    def fill(parts):
        used = sum(part.shape[1] for part in parts)
        return parts + [jnp.zeros((rows, LANES - used), F32)]

    packed = jnp.concatenate(
        fill([joined[:, :first], qkv_ref[...].astype(F32)])
        + fill([fc1_ref[...].astype(F32), joined[:, first:second]])
        + fill([joined[:, second:]]),
        axis=1,
    ).astype(BF16)
    out_ref[...] = packed


def route_kernel(patch_ref, cot_ref, valid_ref, *out_refs):
    row = lax.axis_index("row")
    images, slots, _ = patch_ref.shape
    half = slots // 2
    packed = half * 3 // 2
    for j, out_ref in enumerate(out_refs):
        target = row ^ j
        core, image = target // images, target % images
        place = pl.ds(pl.multiple_of(core * half, half), half)
        out_ref[:packed] = pack(patch_ref[image, place, :])
        out_ref[packed : 2 * packed] = pack(cot_ref[image, place, :])
        valid = valid_ref[image].astype(F32).astype(BF16)
        out_ref[2 * packed :] = jnp.concatenate(
            [valid, jnp.zeros((GRID, LANES - GRID), BF16)], axis=1
        )


def depart_kernel(*refs):
    turned, (qkv_ref, fc1_ref, patch_ref, cot_ref, valid_ref, out_ref) = refs[:5], refs[5:11]
    pack_weights_kernel(turned, qkv_ref, fc1_ref, out_ref)
    route_kernel(patch_ref, cot_ref, valid_ref, *refs[11:])


def norm_kernel(starts, parts, gains_ref, *refs):
    got_refs, refs = refs[:-6], refs[-6:]
    own_ref, first_ref, mask_ref, *selections = refs
    core, row = lax.axis_index("core"), lax.axis_index("row")
    images = len(got_refs) // 2
    gain = gains_ref[0:1, :]
    slots = own_ref.shape[2]
    packed = slots * 3 // 2
    for j, got in enumerate(got_refs):
        block = (core * images + row % images) ^ j
        patch = unpack(got[:packed])
        own_ref[block, 0] = patch
        own_ref[block, 1] = unpack(got[packed : 2 * packed])
        unit, _ = normalise(patch.astype(F32))
        first_ref[pl.ds(pl.multiple_of(block * slots, slots), slots), :] = (unit * gain).astype(
            BF16
        )
    valid = got_refs[0][2 * packed :].astype(F32).T
    for i in range(GRID):
        mask_ref[i * GRID : (i + 1) * GRID, :] = jnp.broadcast_to(
            valid[:GRID, i : i + 1], (GRID, LANES)
        )
    put_late_selections(starts, parts, *selections)


def home_kernel(*refs):
    row = lax.axis_index("row")
    got_refs, out_refs = refs[:-2], refs[-2:]
    images, slots, _ = out_refs[0].shape
    half = slots // 2
    for j, got in enumerate(got_refs):
        source = row ^ j
        core, image = source // images, source % images
        place = pl.ds(pl.multiple_of(core * half, half), half)
        for which, out_ref in enumerate(out_refs):
            out_ref[image, place, :] = unpack(got[which])


def scan_kernel(
    starts,
    width,
    first_own_ref,
    first_other_ref,
    mask_ref,
    sel_u_ref,
    sel_rc_ref,
    sel_q_ref,
    *refs,
    blocks,
):
    mine_refs, got_refs, refs = refs[:blocks], refs[blocks : 2 * blocks], refs[2 * blocks :]
    scan_body(
        starts,
        width,
        first_own_ref,
        first_other_ref,
        mask_ref,
        sel_u_ref,
        sel_rc_ref,
        sel_q_ref,
        mine_refs,
        got_refs,
        *refs,
    )


def scan_body(
    starts,
    width,
    first_own_ref,
    first_other_ref,
    mask_ref,
    sel_u_ref,
    sel_rc_ref,
    sel_q_ref,
    mine_refs,
    got_refs,
    q_ref,
    k_ref,
    v_ref,
    scanned_ref,
    mixed_ref,
    table_ref,
    rates_ref,
    wu_ref,
    wqkv_ref,
    late_ref,
    xs,
    xt,
    cols,
    rows,
    scanned_own,
    first_ref,
):
    core = lax.axis_index("core")
    blocks = len(mine_refs)
    rows_slots = OWN // blocks

    late = gather_parts(mine_refs, got_refs, 0, late_ref)
    wu = dot(late, sel_u_ref[...]).astype(BF16)
    wu_ref[...] = wu
    rates = dot(late, sel_rc_ref[...])
    rates = jnp.concatenate([rates.T, jnp.zeros((LANES, 2 * LANES - D), F32)], axis=1)
    rates_ref[...] = rates
    for third in range(3):
        window = late[:, starts[third] * LANES : (starts[third] + width) * LANES]
        wqkv_ref[third] = dot(window, sel_q_ref[third]).astype(BF16)

    decay, coef = rates[: 4 * STATE], rates[4 * STATE :]

    def lag_row(k):
        powers = jnp.exp(-decay * k) * coef
        return [jnp.sum(powers[d * STATE : (d + 1) * STATE], 0, keepdims=True) for d in range(4)]

    def store_lag(way, lag, row):
        row = row.astype(BF16).astype(F32)
        for lane in range(2):
            table_ref[way, lane, lag + CENTER] = jnp.broadcast_to(
                row[:, lane * LANES : (lane + 1) * LANES], (8, LANES)
            )

    def lag_step(k, _):
        found = lag_row(k.astype(F32))
        for way in range(2):
            store_lag(way, k, found[2 * way])
            store_lag(way, -k, found[2 * way + 1])
        return 0

    lax.fori_loop(1, GRID, lag_step, 0)
    found = lag_row(0.0)
    for way in range(2):
        store_lag(way, 0, found[2 * way] + found[2 * way + 1])

    xs[1, :, D - LANES :] = jnp.zeros((SLOTS, 2 * LANES - D), F32)

    for block in range(blocks):
        here = slice(block * rows_slots, (block + 1) * rows_slots)
        for ref, which in ((first_own_ref, core), (first_other_ref, 1 - core)):
            start = pl.multiple_of((block * 2 + which) * rows_slots, rows_slots)
            first_ref[pl.ds(start, rows_slots), :] = ref[here, :]
    mixed = dot(first_ref[...], wu) * widen(mask_ref[...])
    mixed = mixed.astype(BF16)
    mixed_ref[...] = mixed
    mixed = mixed.astype(F32)
    put_lanes(xs, slice(None), mixed)
    for lane in range(2):
        for j in range(GRID):
            xt[lane, j * GRID : (j + 1) * GRID, :] = xs[lane, pl.ds(j, GRID, stride=GRID), :]

    def scan_step(index, _):
        sublane = pl.multiple_of((index % 4) * 8, 8)
        first = (index // 4) * 8
        for way, src, dst in ((0, xt, rows), (1, xs, cols)):
            for lane in range(2):
                total = block_sum(src, table_ref, way, lane, first, 8, GRID, 0, sublane, 1)
                for t in range(8):
                    place = pl.multiple_of((first + t) * GRID + sublane, 8)
                    dst[lane, pl.ds(place, 8), :] = total[t]
        return 0

    lax.fori_loop(0, 16, scan_step, 0)

    def join_step(i, _):
        place = pl.ds(pl.multiple_of(i * GRID, GRID), GRID)
        mask = mask_ref[place, :]
        both = []
        for lane in range(2):
            down = cols[lane, place, :].astype(BF16).astype(F32)
            both.append((rows[lane, pl.ds(i, GRID, stride=GRID), :] + down) * mask)
        both = jnp.concatenate([both[0], both[1][:, : D - LANES]], axis=1)
        scanned_ref[place, :] = both.astype(BF16)
        return 0

    lax.fori_loop(0, GRID, join_step, 0)

    for block in range(blocks):
        start = pl.multiple_of((block * 2 + core) * rows_slots, rows_slots)
        scanned_own[block * rows_slots : (block + 1) * rows_slots, :] = scanned_ref[
            pl.ds(start, rows_slots), :
        ]

    lane_own = lax.broadcasted_iota(jnp.int32, (OWN, LANES), 1)
    lane_all = lax.broadcasted_iota(jnp.int32, (SLOTS, LANES), 1)
    bias = jnp.where(lane_all == HEAD_DIM, (mask_ref[...] - 1.0) * 1e30, 0.0)
    ones = jnp.where((lane_all == HEAD_DIM) | (lane_all == HEAD_DIM + 1), 1.0, 0.0)
    one_own = jnp.where(lane_own == HEAD_DIM, 1.0, 0.0)
    for h in range(HEADS):
        tile = slice(h * LANES, (h + 1) * LANES)
        q_ref[h] = (
            dot(scanned_own[...], wqkv_ref[0, :, tile]) * HEAD_DIM ** (-0.5) + one_own
        ).astype(BF16)
        k_ref[h] = (dot(scanned_ref[...], wqkv_ref[1, :, tile]) + bias).astype(BF16)
        v_ref[h] = (dot(scanned_ref[...], wqkv_ref[2, :, tile]) + ones).astype(BF16)


def middle_kernel(
    own_ref,
    mask_ref,
    gains_ref,
    sel_1_ref,
    sel_o_ref,
    sel_2_ref,
    q_ref,
    k_ref,
    v_ref,
    *refs,
):
    blocks = own_ref.shape[0]
    middle_body(
        own_ref,
        mask_ref,
        gains_ref,
        sel_1_ref,
        sel_o_ref,
        sel_2_ref,
        q_ref,
        k_ref,
        v_ref,
        refs[:blocks],
        refs[blocks : 2 * blocks],
        *refs[2 * blocks :],
    )


def middle_body(
    own_ref,
    mask_ref,
    gains_ref,
    sel_1_ref,
    sel_o_ref,
    sel_2_ref,
    q_ref,
    k_ref,
    v_ref,
    mine_refs,
    got_refs,
    soft_ref,
    lifted_ref,
    out_ref,
    grad_middle_ref,
    gain_ref,
    keep_ref,
    send_ref,
    early_ref,
    scores,
    wo,
    w1,
    w2,
    att,
    outs,
    sums,
    middle,
    second,
    pre,
    hidden,
    grad_pre,
    wire,
):
    core = lax.axis_index("core")
    blocks, _, rows_slots, _ = own_ref.shape
    parts = early_ref.shape[0]
    per_block = D // blocks
    gain = gains_ref[1:2, :]

    left = gather_parts(mine_refs, got_refs, 1, early_ref)
    right = gather_parts(mine_refs, got_refs, 2, early_ref)
    span = parts // 2 * LANES
    for half in range(2):
        w1[:, half * FF // 2 : (half + 1) * FF // 2] = dot(
            left[:, half * span : (half + 1) * span], sel_1_ref[...]
        ).astype(BF16)
    out_weight = dot(left, sel_o_ref[...]).astype(BF16)
    for h in range(HEADS):
        wo[h, :HEAD_DIM] = out_weight[h * HEAD_DIM : (h + 1) * HEAD_DIM]
        wo[h, HEAD_DIM:] = jnp.zeros((LANES - HEAD_DIM, D), BF16)
    for g in range(4):
        part = dot(right, sel_2_ref[g])
        for r in range(blocks):
            start = r * 4 * per_block + g * per_block
            w2[start : start + per_block] = part[r * per_block : (r + 1) * per_block].astype(BF16)

    for h in range(HEADS):
        scores[...] = dot_nt(q_ref[h], k_ref[h])

        def soft_step(i, _, h=h):
            place = pl.ds(pl.multiple_of(i * 32, 32), 32)
            values = scores[place, :]
            top = jnp.max(values, -1, keepdims=True)
            soft_ref[h, place, :] = jnp.exp(values - top).astype(BF16)
            return 0

        lax.fori_loop(0, OWN // 32, soft_step, 0)
        raw = dot(soft_ref[h], v_ref[h])
        total = raw[:, HEAD_DIM : HEAD_DIM + 1]
        sums[h] = jnp.broadcast_to(1.0 / total, (OWN, LANES))
        result = raw * sums[h]
        outs[h] = result
        att[h] = result.astype(BF16)

    branch = dot(att[0], wo[0]) + dot(att[1], wo[1]) + dot(att[2], wo[2])
    middle[...] = branch

    def own_mask(block):
        start = pl.multiple_of((block * 2 + core) * rows_slots, rows_slots)
        return widen(mask_ref[pl.ds(start, rows_slots), :])

    def norm_step(block, _):
        place = pl.ds(pl.multiple_of(block * rows_slots, rows_slots), rows_slots)
        mid = own_ref[block, 0].astype(F32) + middle[place, :] * own_mask(block)
        middle[place, :] = mid
        unit, _ = normalise(mid)
        second[place, :] = (unit * gain).astype(BF16)
        return 0

    lax.fori_loop(0, blocks, norm_step, 0)

    pre[...] = dot(second[...], w1[...])
    cot = jnp.concatenate([own_ref[b, 1] for b in range(blocks)], axis=0)
    grad_hidden = scores.at[:, :FF]
    grad_hidden[...] = dot_nt(cot, w2[...])

    def gelu_step(i, _):
        place = pl.ds(pl.multiple_of(i * 16, 16), 16)
        x = pre[place, :]
        phi = 0.5 * (1.0 + lax.erf(x * np.float32(0.5**0.5)))
        hidden[place, :] = (x * phi).astype(BF16)
        slope = phi + x * jnp.exp(x * x * -0.5) * np.float32((2 * np.pi) ** -0.5)
        grad_pre[place, :] = (scores[place, :FF] * slope).astype(BF16)
        return 0

    lax.fori_loop(0, OWN // 16, gelu_step, 0)

    out_ref[...] = (middle[...] + dot(hidden[...], w2[...])).astype(BF16)
    grad_2 = dot_tn(hidden[...], cot).astype(BF16)
    grad_1 = dot_tn(second[...], grad_pre[...]).astype(BF16)
    grad_middle_ref[...] = dot_nt(grad_pre[...], w1[...])

    def back_step(block, total):
        place = pl.ds(pl.multiple_of(block * rows_slots, rows_slots), rows_slots)
        unit, inverse = normalise(middle[place, :])
        grad = grad_middle_ref[place, :]
        total = total + jnp.sum(grad * unit, 0, keepdims=True)
        grad = own_ref[block, 1].astype(F32) + norm_back(grad, gain, unit, inverse)
        grad_middle_ref[place, :] = grad
        second[place, :] = (grad * own_mask(block)).astype(BF16)
        return total

    gain_ref[...] = lax.fori_loop(0, blocks, back_step, jnp.zeros((1, D), F32))

    grad_o = []
    lane_own = lax.broadcasted_iota(jnp.int32, (OWN, LANES), 1)
    for h in range(HEADS):
        grad_o.append(dot_tn(att[h], second[...])[:HEAD_DIM])
        grad_att = dot_nt(second[...], wo[h]).astype(BF16).astype(F32)
        scaled = (grad_att * sums[h]).astype(BF16).astype(F32)
        shift = -jnp.sum(scaled * outs[h], -1, keepdims=True)
        high = shift.astype(BF16).astype(F32)
        lifted = jnp.where(
            lane_own == HEAD_DIM, high, jnp.where(lane_own == HEAD_DIM + 1, shift - high, scaled)
        )
        lifted_ref[h] = lifted.astype(BF16)

    for half in range(2):
        wire[:, half * span : (half + 1) * span] = dot_nt(
            grad_1[:, half * FF // 2 : (half + 1) * FF // 2], sel_1_ref[...]
        )
    grad_o = jnp.concatenate(grad_o, axis=0).astype(BF16)
    wire[...] += dot_nt(grad_o, sel_o_ref[...])

    def deliver(lanes):
        for m in range(parts):
            value = wire[:, m * LANES : (m + 1) * LANES].astype(BF16)

            @pl.when(core == m % 2)
            def _(value=value, m=m):
                put_blocks(keep_ref, m // 2, lanes, value)

            @pl.when(core != m % 2)
            def _(value=value, m=m):
                put_blocks(send_ref, m // 2, lanes, value)

    deliver(slice(0, LANES))
    total = None
    for g in range(4):
        rows = [
            grad_2[r * 4 * per_block + g * per_block : r * 4 * per_block + (g + 1) * per_block]
            for r in range(blocks)
        ]
        part = dot_nt(jnp.concatenate(rows, axis=0), sel_2_ref[g])
        total = part if total is None else total + part
    wire[...] = total
    deliver(slice(LANES, 2 * LANES))


def attention_back_kernel(
    soft_ref,
    lifted_ref,
    q_ref,
    k_ref,
    v_ref,
    scanned_ref,
    wqkv_ref,
    part_ref,
    grad_w_ref,
    scores,
    grad_scores,
    triple,
    grad_q,
    scanned_own,
    part,
    *,
    blocks,
):
    core = lax.axis_index("core")
    rows_slots = OWN // blocks
    for h in range(HEADS):
        tile = slice(h * LANES, (h + 1) * LANES)
        scores[...] = dot_nt(lifted_ref[h], v_ref[h])

        def back_step(i, _, h=h):
            place = pl.ds(pl.multiple_of(i * 32, 32), 32)
            grad_scores[place, :] = (soft_ref[h, place, :].astype(F32) * scores[place, :]).astype(
                BF16
            )
            return 0

        lax.fori_loop(0, OWN // 32, back_step, 0)
        grad_q[:, tile] = (dot(grad_scores[...], k_ref[h]).astype(BF16) * HEAD_DIM ** (-0.5)).astype(
            BF16
        )
        triple[0, :, tile] = dot_tn(grad_scores[...], q_ref[h]).astype(BF16)
        triple[1, :, tile] = dot_tn(soft_ref[h], lifted_ref[h]).astype(BF16)

    part[...] = dot_nt(triple[0], wqkv_ref[1]) + dot_nt(triple[1], wqkv_ref[2])
    from_q = dot_nt(grad_q[...], wqkv_ref[0])
    for block in range(blocks):
        here = slice(block * rows_slots, (block + 1) * rows_slots)
        place = pl.ds(pl.multiple_of((block * 2 + core) * rows_slots, rows_slots), rows_slots)
        part[place, :] += from_q[here]
        scanned_own[here, :] = scanned_ref[place, :]
    part_ref[...] = part[...].astype(BF16)
    grad_w_ref[0] = dot_tn(scanned_own[...], grad_q[...]).astype(BF16)
    grad_w_ref[1] = dot_tn(scanned_ref[...], triple[0]).astype(BF16)
    grad_w_ref[2] = dot_tn(scanned_ref[...], triple[1]).astype(BF16)


def scan_back_kernel(
    starts,
    width,
    own_ref,
    mask_ref,
    part_ref,
    got_ref,
    mixed_ref,
    first_ref,
    table_ref,
    rates_ref,
    wu_ref,
    grad_w_ref,
    gain_two_ref,
    sel_u_ref,
    sel_rc_ref,
    sel_q_ref,
    keep_ref,
    send_ref,
    back_ref,
    gs,
    gt,
    xs,
    xt,
    own,
    rows,
    cols,
    lag_sums,
    lag_rows,
    mixed_back,
    wire,
):
    core = lax.axis_index("core")
    blocks, _, rows_slots, _ = own_ref.shape
    half_rows = rows_slots // GRID
    own_rows = GRID // 2
    parts = sel_rc_ref.shape[0] // LANES
    pad = jnp.zeros((SLOTS, 2 * LANES - D), F32)

    xs[1, :, D - LANES :] = pad
    gs[1, :, D - LANES :] = pad
    put_lanes(xs, slice(None), mixed_ref[...].astype(F32))
    grads = (part_ref[...].astype(F32) + got_ref[...].astype(F32)) * widen(mask_ref[...])
    put_lanes(gs, slice(None), grads.astype(BF16).astype(F32))

    def place_of(block):
        return pl.ds(pl.multiple_of((block * 2 + core) * rows_slots, rows_slots), rows_slots)

    for src, dst in ((gs, gt), (xs, xt)):
        for lane in range(2):
            for block in range(blocks):
                here = slice(block * rows_slots, (block + 1) * rows_slots)
                own[lane, here, :] = src[lane, place_of(block), :]
            for j in range(GRID):
                dst[lane, j * own_rows : (j + 1) * own_rows, :] = own[
                    lane, pl.ds(j, own_rows, stride=GRID), :
                ]

    def row_step(index, _):
        sublane = pl.multiple_of((index % 2) * 8, 8)
        first = (index // 2) * 8
        for lane in range(2):
            total = block_sum(gt, table_ref, 0, lane, first, 8, own_rows, 0, sublane, -1)
            for t in range(8):
                rows[lane, pl.ds(pl.multiple_of((first + t) * own_rows + sublane, 8), 8), :] = total[
                    t
                ]
        return 0

    lax.fori_loop(0, 8, row_step, 0)

    def col_step(index, _):
        sublane = pl.multiple_of((index % 4) * 8, 8)
        block = index // 4
        first = (block * 2 + core) * half_rows
        for lane in range(2):
            total = block_sum(gs, table_ref, 1, lane, first, half_rows, GRID, 0, sublane, -1)
            for t in range(half_rows):
                at = pl.multiple_of((block * half_rows + t) * GRID + sublane, 8)
                cols[lane, pl.ds(at, 8), :] = total[t]
        return 0

    lax.fori_loop(0, blocks * 4, col_step, 0)

    lag_sums[...] = jnp.zeros_like(lag_sums)

    def add_lags(way, lane, first, count, base, gref, xref, step, groups):
        total = {}
        for u in range(groups):
            g = [
                gref[lane, pl.ds(pl.multiple_of((first + t) * step + u * 8, 8), 8), :]
                for t in range(count)
            ]
            for s in range(8):
                x = xref[lane, pl.ds(pl.multiple_of((base + s) * step + u * 8, 8), 8), :]
                for t in range(count):
                    term = g[t] * x
                    total[t - s] = term if t - s not in total else total[t - s] + term
        for lag, value in total.items():
            at = first - base + (lag + CENTER)
            lag_sums[way, lane, at] += value

    def lag_row_step(index, _):
        first, base = (index // 4) * 8, (index % 4) * 8
        for lane in range(2):
            add_lags(0, lane, first, 8, base, gt, xt, own_rows, own_rows // 8)
        return 0

    lax.fori_loop(0, 16, lag_row_step, 0)

    def lag_col_step(index, _):
        first, base = ((index // 4) * 2 + core) * half_rows, (index % 4) * 8
        for lane in range(2):
            add_lags(1, lane, first, half_rows, base, gs, xs, GRID, GRID // 8)
        return 0

    lax.fori_loop(0, blocks * 4, lag_col_step, 0)

    for way in range(2):
        for lane in range(2):
            lag_rows[way, :, lane * LANES : (lane + 1) * LANES] = jnp.sum(lag_sums[way, lane], 1)

    decay, coef = rates_ref[: 4 * STATE], rates_ref[4 * STATE :]

    def table_step(k, carry):
        to_rate, to_coef = carry
        lag = k.astype(F32)
        powers = jnp.exp(-decay * lag)
        grads = []
        for way in range(2):
            for at in (CENTER + k, CENTER - k):
                grads.append(
                    jnp.broadcast_to(lag_rows[way, pl.ds(at, 1), :], (STATE, 2 * LANES))
                )
        scaled = jnp.concatenate(grads, axis=0) * powers
        return to_rate - lag * scaled, to_coef + scaled

    zero = jnp.zeros((4 * STATE, 2 * LANES), F32)
    to_rate, to_coef = lax.fori_loop(0, GRID, table_step, (zero, zero))
    grad_rc = jnp.concatenate([to_rate * coef, to_coef], axis=0).T[:D].astype(BF16)

    def join_step(i, _):
        place = pl.ds(pl.multiple_of(i * GRID, GRID), GRID)
        block = i // half_rows
        at = ((block * 2 + core) * half_rows + i % half_rows) * GRID
        mask = mask_ref[pl.ds(pl.multiple_of(at, GRID), GRID), :]
        both = []
        for lane in range(2):
            down = cols[lane, place, :].astype(BF16).astype(F32)
            both.append((rows[lane, pl.ds(i, GRID, stride=own_rows), :] + down) * mask)
        both = jnp.concatenate([both[0], both[1][:, : D - LANES]], axis=1)
        mixed_back[place, :] = both.astype(BF16)
        return 0

    lax.fori_loop(0, own_rows, join_step, 0)
    grad_u = dot_tn(first_ref[...], mixed_back[...]).astype(BF16)
    grad_first = dot_nt(mixed_back[...], wu_ref[...])
    back_ref[...] = grad_first
    gain_one = jnp.zeros((1, D), F32)
    for block in range(blocks):
        here = slice(block * rows_slots, (block + 1) * rows_slots)
        unit, _ = normalise(own_ref[block, 0].astype(F32))
        gain_one = gain_one + jnp.sum(grad_first[here] * unit, 0, keepdims=True)

    wire[...] = dot_nt(grad_u, sel_u_ref[...]) + dot_nt(grad_rc, sel_rc_ref[...])
    for third in range(3):
        span = slice(starts[third] * LANES, (starts[third] + width) * LANES)
        wire[:, span] += dot_nt(grad_w_ref[third], sel_q_ref[third])
    for m in range(parts):
        value = wire[:, m * LANES : (m + 1) * LANES].astype(BF16)

        @pl.when(core == m % 2)
        def _(value=value, m=m):
            put_late(keep_ref, m // 2, value)

        @pl.when(core != m % 2)
        def _(value=value, m=m):
            put_late(send_ref, m // 2, value)

    lines = []
    for value in (gain_one, gain_two_ref[...]):
        high = value.astype(BF16).astype(F32)
        for piece in (high, value - high):
            lines.append(piece[:, :LANES])
            lines.append(
                jnp.concatenate([piece[:, LANES:], jnp.zeros((1, 2 * LANES - D), F32)], axis=1)
            )
    lines = jnp.concatenate(lines, axis=0).astype(BF16)
    for ref in (keep_ref, send_ref):
        ref[ref.shape[0] - 1, :8] = lines
        ref[ref.shape[0] - 1, 8:] = jnp.zeros((ref.shape[1] - 8, LANES), BF16)


def last_norm_kernel(
    own_ref, gains_ref, back_ref, grad_middle_ref, out_own_ref, *routed_refs
):
    blocks, _, slots, _ = own_ref.shape
    images = blocks // 2
    mine = lax.axis_index("core") * images + lax.axis_index("row") % images
    gain = gains_ref[0:1, :]
    for j, routed in enumerate(routed_refs):
        block = mine ^ j
        place = pl.ds(pl.multiple_of(block * slots, slots), slots)
        unit, inverse = normalise(own_ref[block, 0].astype(F32))
        grad = grad_middle_ref[place, :] + norm_back(back_ref[place, :], gain, unit, inverse)
        routed[0] = pack(out_own_ref[place, :])
        routed[1] = pack(grad.astype(BF16))


def split(value):
    high = value.astype(BF16).astype(F32)
    return jnp.concatenate([high, value - high], axis=0)


def early_sum_kernel(keep_ref, got_ref, *out_refs):
    for k, out_ref in enumerate(out_refs):
        block = lax.axis_index("row") ^ k
        for z in range(keep_ref.shape[1]):
            total = keep_ref[block, z].astype(F32) + got_ref[block, z].astype(F32)
            out_ref[z] = total.astype(BF16)


def late_sum_kernel(keep_ref, got_ref, *out_refs):
    depth, rows, _ = out_refs[0].shape
    rows -= 16
    last = keep_ref.shape[0] - 1
    gains = keep_ref[last, :8].astype(F32) + got_ref[last, :8].astype(F32)
    lines = []
    for g in range(2):
        for lane in range(2):
            at = 4 * g + lane
            lines.append(gains[at : at + 1] + gains[at + 2 : at + 3])
    gains = split(jnp.concatenate(lines, axis=0))
    gains = jnp.concatenate([gains, jnp.zeros((8, LANES), F32)], axis=0).astype(BF16)
    for k, out_ref in enumerate(out_refs):
        block = lax.axis_index("row") ^ k
        for z in range(depth):
            at = block * depth + z
            total = keep_ref[at].astype(F32) + got_ref[at].astype(F32)
            out_ref[z, :rows] = total.astype(BF16)
            out_ref[z, rows:] = gains


def row_sum_kernel(blocks, *refs):
    early_refs, late_refs, out_refs = refs[:blocks], refs[blocks : 2 * blocks], refs[2 * blocks :]
    rows = early_refs[0].shape[1]
    for j, out_ref in enumerate(out_refs):
        z = lax.axis_index("z") ^ j
        early = early_refs[0][z].astype(F32)
        late = late_refs[0][z].astype(F32)
        for k in range(1, blocks):
            early = early + early_refs[k][z].astype(F32)
            late = late + late_refs[k][z].astype(F32)
        out_ref[:rows, LANES:] = early.astype(BF16)
        out_ref[:rows, :LANES] = late[:rows].astype(BF16)
        gains = split(late[rows : rows + 4] + late[rows + 4 : rows + 8])
        gains = jnp.concatenate([gains, jnp.zeros((8, LANES), F32)], axis=0).astype(BF16)
        out_ref[rows:, :LANES] = gains
        out_ref[rows:, LANES:] = jnp.zeros((16, 2 * LANES), BF16)


def final_kernel(parts, *refs):
    final_body(parts, refs[: parts // 2], *refs[parts // 2 :])


def final_body(
    parts,
    got_refs,
    g1_ref,
    g2_ref,
    wu_ref,
    rate_ref,
    coef_ref,
    qkv_ref,
    wo_ref,
    fc1_ref,
    fc2_ref,
):
    a_u, a_r, a_q, (o_u, o_r, o_c, o_q) = late_layout(parts)
    total = got_refs[0][...].astype(F32)
    for ref in got_refs[1:]:
        total = total + ref[...].astype(F32)
    early = total[: fc1_ref.shape[0], LANES:]
    total = total[:, :LANES]
    rows = fc1_ref.shape[0]
    weights, gains = total[:rows], total[rows:]
    turned = weights.T
    wu_ref[...] = turned[o_u : o_u + a_u]
    rate_ref[...] = turned[o_r : o_r + a_r]
    coef_ref[...] = turned[o_c : o_c + a_r]
    qkv_ref[...] = weights[:, o_q : o_q + a_q]
    gains = gains[0:4] + gains[4:8]
    for g, ref in ((0, g1_ref), (1, g2_ref)):
        ref[...] = jnp.concatenate(
            [gains[2 * g : 2 * g + 1], gains[2 * g + 1 : 2 * g + 2, : D - LANES]], axis=1
        )
    a_1, a_o = FF // parts, D // parts
    fc1_ref[...] = early[:, :a_1]
    wo_ref[...] = early[:, :LANES].T[a_1 : a_1 + a_o]
    turned = early[:, LANES:].T
    fc2_ref[...] = jnp.concatenate([turned[g * a_o : (g + 1) * a_o] for g in range(4)], axis=1)


def per_device(
    patches, valid_mask, norm_gains, w_u, decay_rate, out_coef, w_qkv, w_o, w_fc1, w_fc2, cotangent
):
    images, rows_here, _, _ = patches.shape
    depth, blocks = lax.axis_size("z"), lax.axis_size("row")
    parts = 2 * depth
    rows_slots = rows_here // 2 * GRID
    packed_rows = rows_slots * 3 // 2
    swap = [(0, 1), (1, 0)]
    shape = jax.ShapeDtypeStruct

    def swapped(value):
        return lax.ppermute(value, "core", swap)

    def exchanged(values, axis):
        size = len(values)
        return [values[0]] + [
            lax.ppermute(values[k], axis, [(i, i ^ k) for i in range(size)]) for k in range(1, size)
        ]

    def to_chips(value, j):
        pairs = []
        for home in range(2):
            for source in range(blocks):
                target, image = divmod(source ^ j, images)
                pairs.append((home * blocks + source, target * blocks + home * images + image))
        return lax.ppermute(value, ("core", "row"), pairs)

    def to_homes(value, j):
        pairs = []
        for source in range(2):
            for chip in range(blocks):
                home, image = divmod(chip, images)
                target = (source * images + image) ^ j
                pairs.append((source * blocks + chip, home * blocks + target))
        return lax.ppermute(value, ("core", "row"), pairs)

    starts, width = late_spans(parts)
    sel_1, sel_o, sel_2 = early_selections(parts)

    rows_weight = w_u.shape[0]
    payload = shape((2 * packed_rows + GRID, LANES), BF16)
    shard = shape((rows_weight, 3 * LANES), BF16)
    sources = [value.reshape(images, rows_here * GRID, D) for value in (patches, cotangent)]
    if rows_weight % 16 == 0:
        weights, *routed = pl.pallas_call(
            depart_kernel,
            name="depart",
            out_shape=(shard,) + (payload,) * blocks,
            in_specs=[VMEM] * 10,
            out_specs=[VMEM] * (1 + blocks),
            compiler_params=compiler(LARGE),
        )(
                w_u.T,
            decay_rate.T,
            out_coef.T,
            w_o.T,
            w_fc2.T,
            w_qkv,
            w_fc1,
            *sources,
            valid_mask,
        )
    else:

        def fill(pieces):
            joined = jnp.concatenate(pieces, axis=1)
            return jnp.pad(joined, ((0, 0), (0, LANES - joined.shape[1])))

        weights = jnp.concatenate(
            [
                fill([w_u, decay_rate, out_coef, w_qkv]),
                fill([w_fc1, w_o]),
                fill([w_fc2[g * rows_weight : (g + 1) * rows_weight] for g in range(4)]),
            ],
            axis=1,
        )
        routed = pl.pallas_call(
            route_kernel,
            name="route",
            out_shape=(payload,) * blocks,
            in_specs=[VMEM] * 3,
            out_specs=[VMEM] * blocks,
            compiler_params=compiler(LARGE),
        )(*sources, valid_mask)

    weights = jnp.stack(exchanged([weights] * depth, "z"))
    weights = exchanged([weights] * blocks, "row")
    weights = weights + [swapped(value) for value in weights]
    routed = [to_chips(value, j) for j, value in enumerate(routed)]
    own, first_own, mask, sel_u, sel_rc, sel_q = pl.pallas_call(
        lambda *refs: norm_kernel(starts, parts, *refs),
        name="first_norm",
        out_shape=(
            shape((blocks, 2, rows_slots, D), BF16),
            shape((OWN, D), BF16),
            shape((SLOTS, LANES), F32),
            shape((parts * LANES, D), BF16),
            shape((parts * LANES, LANES), BF16),
            shape((3, width * LANES, TILE), BF16),
        ),
        in_specs=[VMEM] * (1 + blocks),
        out_specs=[VMEM] * 6,
        compiler_params=compiler(8 << 20),
    )(norm_gains, *routed)
    first_other = swapped(first_own)

    head_own = shape((HEADS, OWN, LANES), BF16)
    head_all = shape((HEADS, SLOTS, LANES), BF16)
    part_scratch = pltpu.VMEM((parts, blocks, rows_weight, LANES), BF16)
    q, k, v, scanned, mixed, table, rates, wu, wqkv = pl.pallas_call(
        lambda *refs: scan_kernel(starts, width, *refs, blocks=blocks),
        name="scan_forward",
        out_shape=(
            head_own,
            head_all,
            head_all,
            shape((SLOTS, D), BF16),
            shape((SLOTS, D), BF16),
            shape((2, 2, LAGS, 8, LANES), F32),
            shape((LANES, 2 * LANES), F32),
            shape((D, D), BF16),
            shape((3, D, TILE), BF16),
        ),
        in_specs=[VMEM] * (6 + 2 * blocks),
        out_specs=[VMEM] * 9,
        scratch_shapes=[part_scratch]
        + [pltpu.VMEM((2, SLOTS, LANES), F32)] * 4
        + [pltpu.VMEM((OWN, D), BF16), pltpu.VMEM((SLOTS, D), BF16)],
        compiler_params=compiler(),
    )(first_own, first_other, mask, sel_u, sel_rc, sel_q, *weights)

    wire_early = shape((blocks, depth, rows_weight, 2 * LANES), BF16)
    soft, lifted, out_own, grad_middle, gain_two, early_keep, early_send = pl.pallas_call(
        middle_kernel,
        name="attention_and_feed_forward",
        out_shape=(
            shape((HEADS, OWN, SLOTS), BF16),
            head_own,
            shape((OWN, D), BF16),
            shape((OWN, D), F32),
            shape((1, D), F32),
            wire_early,
            wire_early,
        ),
        in_specs=[VMEM] * (9 + 2 * blocks),
        out_specs=[VMEM] * 7,
        scratch_shapes=[
            part_scratch,
            pltpu.VMEM((OWN, SLOTS), F32),
            pltpu.VMEM((HEADS, LANES, D), BF16),
            pltpu.VMEM((D, FF), BF16),
            pltpu.VMEM((FF, D), BF16),
            pltpu.VMEM((HEADS, OWN, LANES), BF16),
            pltpu.VMEM((HEADS, OWN, LANES), F32),
            pltpu.VMEM((HEADS, OWN, LANES), F32),
            pltpu.VMEM((OWN, D), F32),
            pltpu.VMEM((OWN, D), BF16),
            pltpu.VMEM((OWN, FF), F32),
            pltpu.VMEM((OWN, FF), BF16),
            pltpu.VMEM((OWN, FF), BF16),
            pltpu.VMEM((D, parts * LANES), F32),
        ],
        compiler_params=compiler(),
    )(own, mask, norm_gains, sel_1, sel_o, sel_2, q, k, v, *weights)

    early_recv = swapped(early_send)

    part, grad_w = pl.pallas_call(
        lambda *refs: attention_back_kernel(*refs, blocks=blocks),
        name="attention_backward",
        out_shape=(shape((SLOTS, D), BF16), shape((3, D, TILE), BF16)),
        in_specs=[VMEM] * 7,
        out_specs=[VMEM] * 2,
        scratch_shapes=[
            pltpu.VMEM((OWN, SLOTS), F32),
            pltpu.VMEM((OWN, SLOTS), BF16),
            pltpu.VMEM((2, SLOTS, TILE), BF16),
            pltpu.VMEM((OWN, TILE), BF16),
            pltpu.VMEM((OWN, D), BF16),
            pltpu.VMEM((SLOTS, D), F32),
        ],
        compiler_params=compiler(),
    )(soft, lifted, q, k, v, scanned, wqkv)

    part_got = swapped(part)
    early_keep, early_recv, part = lax.optimization_barrier((early_keep, early_recv, part))
    early = pl.pallas_call(
        early_sum_kernel,
        name="early_sum",
        out_shape=(shape((depth, rows_weight, 2 * LANES), BF16),) * blocks,
        in_specs=[VMEM] * 2,
        out_specs=[VMEM] * blocks,
        compiler_params=compiler(8 << 20),
    )(early_keep, early_recv)
    early, part_got = lax.optimization_barrier((early, part_got))
    early = exchanged(early, "row")
    wire_late = shape((blocks * depth + 1, rows_weight, LANES), BF16)
    late_keep, late_send, back = pl.pallas_call(
        lambda *refs: scan_back_kernel(starts, width, *refs),
        name="scan_backward",
        out_shape=(wire_late, wire_late, shape((OWN, D), F32)),
        in_specs=[VMEM] * 14,
        out_specs=[VMEM] * 3,
        scratch_shapes=[
            pltpu.VMEM((2, SLOTS, LANES), F32),
            pltpu.VMEM((2, OWN, LANES), F32),
            pltpu.VMEM((2, SLOTS, LANES), F32),
            pltpu.VMEM((2, OWN, LANES), F32),
            pltpu.VMEM((2, OWN, LANES), F32),
            pltpu.VMEM((2, OWN, LANES), F32),
            pltpu.VMEM((2, OWN, LANES), F32),
            pltpu.VMEM((2, 2, LAGS, 8, LANES), F32),
            pltpu.VMEM((2, LAGS, 2 * LANES), F32),
            pltpu.VMEM((OWN, D), BF16),
            pltpu.VMEM((D, parts * LANES), F32),
        ],
        compiler_params=compiler(),
    )(
        own,
        mask,
        part,
        part_got,
        mixed,
        first_own,
        table,
        rates,
        wu,
        grad_w,
        gain_two,
        sel_u,
        sel_rc,
        sel_q,
    )
    late_keep, late_send, early = lax.optimization_barrier((late_keep, late_send, early))
    late = pl.pallas_call(
        late_sum_kernel,
        name="late_sum",
        out_shape=(shape((depth, rows_weight + 16, LANES), BF16),) * blocks,
        in_specs=[VMEM] * 2,
        out_specs=[VMEM] * blocks,
        compiler_params=compiler(8 << 20),
    )(late_keep, swapped(late_send))
    payload = shape((2, packed_rows, LANES), BF16)
    routed = pl.pallas_call(
        last_norm_kernel,
        name="last_norm",
        out_shape=(payload,) * blocks,
        in_specs=[VMEM] * 5,
        out_specs=[VMEM] * blocks,
        compiler_params=compiler(8 << 20),
    )(own, norm_gains, back, grad_middle, out_own)
    late = exchanged(late, "row")
    summed = pl.pallas_call(
        lambda *refs: row_sum_kernel(blocks, *refs),
        name="row_sum",
        out_shape=(shape((rows_weight + 16, 3 * LANES), BF16),) * depth,
        in_specs=[VMEM] * (2 * blocks),
        out_specs=[VMEM] * depth,
        compiler_params=compiler(8 << 20),
    )(*early, *late)
    summed = exchanged(summed, "z")

    routed = [to_homes(value, j) for j, value in enumerate(routed)]
    whole = shape((images, rows_here * GRID, D), BF16)
    block_out, grad_patches = pl.pallas_call(
        home_kernel,
        name="home",
        out_shape=(whole, whole),
        in_specs=[VMEM] * blocks,
        out_specs=[VMEM] * 2,
        compiler_params=compiler(8 << 20),
    )(*routed)

    turned = (4 * STATE // parts, rows_weight)
    g1, g2, f_u, f_rate, f_coef, f_qkv, f_o, f_1, f_2 = pl.pallas_call(
        lambda *refs: final_kernel(parts, *refs),
        name="final_sum",
        out_shape=(
            shape((1, D), F32),
            shape((1, D), F32),
            shape((D // parts, rows_weight), F32),
            shape(turned, F32),
            shape(turned, F32),
            shape((rows_weight, 3 * D // parts), F32),
            shape((D // parts, rows_weight), F32),
            shape((rows_weight, FF // parts), F32),
            shape((D // parts, 4 * rows_weight), F32),
        ),
        in_specs=[VMEM] * depth,
        out_specs=[VMEM] * 9,
        compiler_params=compiler(8 << 20),
    )(*summed)
    return (
        block_out.reshape(patches.shape),
        grad_patches.reshape(patches.shape),
        g1.reshape(D),
        g2.reshape(D),
        f_u.T,
        f_rate.T,
        f_coef.T,
        f_qkv,
        f_o.T,
        f_1,
        f_2.T,
    )


def solution(mesh):
    images, rows = mesh.devices.shape
    fine = Mesh(mesh.devices.reshape(images // 2, 2, rows), ("z", "core", "row"))
    img = ("z", "core")
    grid = P(img, "row", None, None)
    weight = P("row", img)
    in_specs = (grid, P(img, None, None), P()) + (weight,) * 7 + (grid,)
    out_specs = (grid, grid, P(), P()) + (weight,) * 7
    return jax.shard_map(
        per_device, mesh=fine, in_specs=in_specs, out_specs=out_specs, check_vma=False
    )
```

```python
import jax
import jax.numpy as jnp
import numpy as np
from jax import lax
from jax.experimental import pallas as pl
from jax.experimental.pallas import tpu as pltpu
from jax.sharding import Mesh
from jax.sharding import PartitionSpec as P

HEADS = 3
HEAD_DIM = 64
STATE = 16
GRID = 32
SLOTS = GRID * GRID
OWN = SLOTS // 2
D = HEADS * HEAD_DIM
FF = 4 * D
LANES = 128
TILE = HEADS * LANES
LAGS = 2 * GRID
CENTER = GRID - 1
EPS = 1e-05
BF16 = jnp.bfloat16
F32 = jnp.float32


def late_layout(parts):
    a_u, a_r, a_q = D // parts, 4 * STATE // parts, 3 * D // parts
    return a_u, a_r, a_q, (0, a_u, a_u + a_r, a_u + 2 * a_r)


def late_spans(parts):
    a_q = 3 * D // parts
    first = [third * D // a_q for third in range(3)]
    last = [((third + 1) * D - 1) // a_q for third in range(3)]
    width = max(stop - start + 1 for start, stop in zip(first, last))
    return [min(start, parts - width) for start in first], width


def early_selections(parts):
    a_1, a_o = FF // parts, D // parts
    half = parts // 2
    sel_1 = np.zeros((half, LANES, FF // 2), np.float32)
    sel_o = np.zeros((parts, LANES, D), np.float32)
    sel_2 = np.zeros((4, parts, LANES, D), np.float32)
    for m in range(half):
        for col in range(a_1):
            sel_1[m, col, m * a_1 + col] = 1
    for m in range(parts):
        for col in range(a_o):
            sel_o[m, a_1 + col, m * a_o + col] = 1
            for g in range(4):
                sel_2[g, m, g * a_o + col, m * a_o + col] = 1
    return (
        sel_1.reshape(half * LANES, FF // 2).astype(BF16),
        sel_o.reshape(parts * LANES, D).astype(BF16),
        sel_2.reshape(4, parts * LANES, D).astype(BF16),
    )


def lane_and_part(shape):
    place = lax.broadcasted_iota(jnp.int32, shape, 0)
    return place % LANES, place // LANES, lax.broadcasted_iota(jnp.int32, shape, 1)


def put_late_selections(starts, parts, sel_u_ref, sel_rc_ref, sel_q_ref):
    a_u, a_r, a_q, (o_u, o_r, o_c, o_q) = late_layout(parts)

    def put(hit):
        return jnp.where(hit, 1.0, 0.0).astype(BF16)

    lane, part, col = lane_and_part(sel_u_ref.shape)
    sel_u_ref[...] = put((lane < a_u) & (part * a_u + lane == col))
    lane, part, col = lane_and_part(sel_rc_ref.shape)
    rate = (lane >= o_r) & (lane < o_c) & (part * a_r + lane - o_r == col)
    coef = (lane >= o_c) & (lane < o_q) & (part * a_r + lane - o_c + 4 * STATE == col)
    sel_rc_ref[...] = put(rate | coef)
    lane, part, col = lane_and_part(sel_q_ref.shape[1:])
    whole = jnp.where(
        col % LANES < HEAD_DIM, col // LANES * HEAD_DIM + col % LANES, -4 * D
    )
    for third in range(3):
        here = (part + starts[third]) * a_q + lane - o_q - third * D
        sel_q_ref[third] = put((lane >= o_q) & (lane < o_q + a_q) & (here == whole))


def dot(a, b):
    return lax.dot_general(a, b, (((1,), (0,)), ((), ())), preferred_element_type=F32)


def dot_nt(a, b):
    return lax.dot_general(a, b, (((1,), (1,)), ((), ())), preferred_element_type=F32)


def dot_tn(a, b):
    return lax.dot_general(a, b, (((0,), (0,)), ((), ())), preferred_element_type=F32)


def normalise(values):
    center = values - jnp.mean(values, -1, keepdims=True)
    spread = jnp.mean(center * center, -1, keepdims=True)
    inverse = lax.rsqrt(spread + EPS)
    return center * inverse, inverse


def norm_back(grad, gain, unit, inverse):
    scaled = grad * gain
    first = jnp.mean(scaled, -1, keepdims=True)
    second = jnp.mean(scaled * unit, -1, keepdims=True)
    return inverse * (scaled - first - unit * second)


def widen(mask):
    return jnp.concatenate([mask, mask[:, : D - LANES]], axis=1)


def put_blocks(ref, z, lanes, value):
    rows = ref.shape[2]
    for r in range(ref.shape[0]):
        ref[r, z, :, lanes] = value[r * rows : (r + 1) * rows]


def put_late(ref, z, value):
    rows = ref.shape[1]
    depth = ref.shape[0] * rows // D
    for r in range(D // rows):
        ref[r * depth + z] = value[r * rows : (r + 1) * rows]


def pair_lanes(first, second):
    return jnp.concatenate([first, second], axis=1)


def put_columns(wide, pairs, values):
    wide[...] = values[:, :LANES]
    tail = values[:, LANES:].reshape(values.shape[0] // GRID, 2, GRID // 2, D - LANES)
    tail = pair_lanes(tail[:, 0].reshape(-1, D - LANES), tail[:, 1].reshape(-1, D - LANES))
    pairs[...] = tail


def put_rows(wide, pairs, from_wide, tail, together):
    rows = from_wide.shape[0] // GRID
    together[...] = pair_lanes(tail[: rows // 2 * GRID], tail[rows // 2 * GRID :])
    for j in range(GRID):
        wide[j * rows : (j + 1) * rows, :] = from_wide[pl.ds(j, rows, stride=GRID), :]
        pairs[j * rows // 2 : (j + 1) * rows // 2, :] = together[pl.ds(j, rows // 2, stride=GRID), :]


def units(index):
    return [(0, (index * 2 + u) * 8) for u in range(2)] + [(1, index * 8)]


def block_sum(src, table, way, kind, first, count, sublane, sign):
    total = [None] * count
    step = src[kind].shape[0] // GRID
    for base in range(0, GRID, 8):
        low, high = -(base + 7), count - 1 - base
        coef = {
            lag: table[way, kind, first * sign + (lag * sign + CENTER)]
            for lag in range(low, high + 1)
        }
        for s in range(base, base + 8):
            x = src[kind][pl.ds(pl.multiple_of(s * step + sublane, 8), 8), :]
            for t in range(count):
                term = coef[t - s] * x
                total[t] = term if total[t] is None else total[t] + term
    return total


def join_rows(i, count, rows, cols):
    half = GRID // 2
    narrow = D - LANES
    across = rows[1][pl.ds(i, GRID, stride=count // 2), :]
    found = []
    for which in range(2):
        row = i + which * (count // 2)
        wide = cols[0][pl.ds(pl.multiple_of(row * GRID, GRID), GRID), :].astype(BF16).astype(F32)
        wide = wide + rows[0][pl.ds(i + which * (count // 2), GRID, stride=count), :]
        pairs = cols[1][pl.ds(pl.multiple_of(row * half, half), half), :].astype(BF16).astype(F32)
        tail = jnp.concatenate([pairs[:, :narrow], pairs[:, narrow:]], axis=0)
        tail = tail + across[:, which * narrow : (which + 1) * narrow]
        found.append((row, jnp.concatenate([wide, tail], axis=1)))
    return found


def gather_parts(mine_refs, got_refs, block, out_ref):
    core, row, depth = lax.axis_index("core"), lax.axis_index("row"), lax.axis_index("z")
    lanes = slice(block * LANES, (block + 1) * LANES)
    count = out_ref.shape[0] // 2
    rows = out_ref.shape[2]
    for refs, which in ((mine_refs, core), (got_refs, 1 - core)):
        for k, ref in enumerate(refs):
            for j in range(count):
                out_ref[2 * (depth ^ j) + which, row ^ k] = ref[j, :, lanes]
    wide = []
    for m in range(2 * count):
        wide.append(jnp.concatenate([out_ref[m, r] for r in range(out_ref.shape[1])], axis=0))
    return jnp.concatenate(wide, axis=1)


LARGE = 60 << 20


def compiler(limit=24 << 20):
    return pltpu.CompilerParams(vmem_limit_bytes=limit)


VMEM = pl.BlockSpec(memory_space=pltpu.VMEM)


def pack(values):
    half = values.shape[0] // 2
    tail = jnp.concatenate([values[:half, LANES:], values[half:, LANES:]], axis=1)
    return jnp.concatenate([values[:, :LANES], tail], axis=0)


def unpack(packed):
    count = packed.shape[0] * 2 // 3
    tail = packed[count:]
    tail = jnp.concatenate([tail[:, : D - LANES], tail[:, D - LANES :]], axis=0)
    return jnp.concatenate([packed[:count], tail], axis=1)


def pack_weights_kernel(turned_refs, qkv_ref, fc1_ref, out_ref):
    wu, rate, coef, wo, fc2 = [ref[...].astype(F32) for ref in turned_refs]
    rows = qkv_ref.shape[0]
    a_o, a_r = wo.shape[0], rate.shape[0]
    pieces = [wu, rate, coef, wo] + [fc2[:, g * rows : (g + 1) * rows] for g in range(4)]
    joined = jnp.concatenate(pieces, axis=0)
    joined = jnp.concatenate([joined, jnp.zeros((joined.shape[0], LANES - rows), F32)], axis=1)
    joined = joined.T[:rows]
    first, second = a_o + 2 * a_r, 2 * a_o + 2 * a_r

    def fill(parts):
        used = sum(part.shape[1] for part in parts)
        return parts + [jnp.zeros((rows, LANES - used), F32)]

    packed = jnp.concatenate(
        fill([joined[:, :first], qkv_ref[...].astype(F32)])
        + fill([fc1_ref[...].astype(F32), joined[:, first:second]])
        + fill([joined[:, second:]]),
        axis=1,
    ).astype(BF16)
    out_ref[...] = packed


def route_kernel(patch_ref, cot_ref, valid_ref, *out_refs):
    row = lax.axis_index("row")
    images, slots, _ = patch_ref.shape
    half = slots // 2
    packed = half * 3 // 2
    for j, out_ref in enumerate(out_refs):
        target = row ^ j
        core, image = target // images, target % images
        place = pl.ds(pl.multiple_of(core * half, half), half)
        out_ref[:packed] = pack(patch_ref[image, place, :])
        out_ref[packed : 2 * packed] = pack(cot_ref[image, place, :])
        valid = valid_ref[image].astype(F32).astype(BF16)
        out_ref[2 * packed :] = jnp.concatenate(
            [valid, jnp.zeros((GRID, LANES - GRID), BF16)], axis=1
        )


def depart_kernel(*refs):
    turned, (qkv_ref, fc1_ref, patch_ref, cot_ref, valid_ref, out_ref) = refs[:5], refs[5:11]
    pack_weights_kernel(turned, qkv_ref, fc1_ref, out_ref)
    route_kernel(patch_ref, cot_ref, valid_ref, *refs[11:])


def norm_kernel(starts, parts, gains_ref, *refs):
    got_refs, refs = refs[:-6], refs[-6:]
    own_ref, first_ref, mask_ref, *selections = refs
    core, row = lax.axis_index("core"), lax.axis_index("row")
    images = len(got_refs) // 2
    gain = gains_ref[0:1, :]
    slots = own_ref.shape[2]
    packed = slots * 3 // 2
    for j, got in enumerate(got_refs):
        block = (core * images + row % images) ^ j
        patch = unpack(got[:packed])
        own_ref[block, 0] = patch
        own_ref[block, 1] = unpack(got[packed : 2 * packed])
        unit, _ = normalise(patch.astype(F32))
        first_ref[pl.ds(pl.multiple_of(block * slots, slots), slots), :] = (unit * gain).astype(
            BF16
        )
    valid = got_refs[0][2 * packed :].astype(F32).T
    for i in range(GRID):
        mask_ref[i * GRID : (i + 1) * GRID, :] = jnp.broadcast_to(
            valid[:GRID, i : i + 1], (GRID, LANES)
        )
    put_late_selections(starts, parts, *selections)


def results_of(ref, rows):
    start = ref.shape[0] - 2 * rows
    return ref[start : start + rows], ref[start + rows :]


def choose_kernel(*refs):
    got_refs, out_ref = refs[:-1], refs[-1]
    core, row = lax.axis_index("core"), lax.axis_index("row")
    images, rows = out_ref.shape[0], out_ref.shape[1] // 2
    for k, got in enumerate(got_refs):
        image = row ^ k

        @pl.when(image // images != core)
        def _(got=got, image=image):
            for which, value in enumerate(results_of(got, rows)):
                out_ref[image % images, which * rows : (which + 1) * rows] = value


def home_kernel(swapped_ref, *refs):
    got_refs, out_refs = refs[:-2], refs[-2:]
    core, row = lax.axis_index("core"), lax.axis_index("row")
    images, slots, _ = out_refs[0].shape
    half = slots // 2
    rows = half * 3 // 2
    mine = pl.ds(pl.multiple_of(core * half, half), half)
    theirs = pl.ds(pl.multiple_of((1 - core) * half, half), half)
    for k, got in enumerate(got_refs):
        image = row ^ k

        @pl.when(image // images == core)
        def _(got=got, image=image):
            for out_ref, value in zip(out_refs, results_of(got, rows)):
                out_ref[image % images, mine, :] = unpack(value)

    for image in range(images):
        for which, out_ref in enumerate(out_refs):
            value = swapped_ref[image, which * rows : (which + 1) * rows]
            out_ref[image, theirs, :] = unpack(value)


def scan_kernel(
    starts,
    width,
    first_own_ref,
    first_other_ref,
    mask_ref,
    sel_u_ref,
    sel_rc_ref,
    sel_q_ref,
    *refs,
    blocks,
):
    mine_refs, got_refs, refs = refs[:blocks], refs[blocks : 2 * blocks], refs[2 * blocks :]
    scan_body(
        starts,
        width,
        first_own_ref,
        first_other_ref,
        mask_ref,
        sel_u_ref,
        sel_rc_ref,
        sel_q_ref,
        mine_refs,
        got_refs,
        *refs,
    )


def scan_body(
    starts,
    width,
    first_own_ref,
    first_other_ref,
    mask_ref,
    sel_u_ref,
    sel_rc_ref,
    sel_q_ref,
    mine_refs,
    got_refs,
    q_ref,
    k_ref,
    v_ref,
    scanned_ref,
    mixed_ref,
    table_ref,
    rates_ref,
    wu_ref,
    wqkv_ref,
    late_ref,
    xs_wide,
    xs_pairs,
    xt_wide,
    xt_pairs,
    cols_wide,
    cols_pairs,
    rows_wide,
    rows_pairs,
    scanned_own,
    first_ref,
):
    xs, xt = (xs_wide, xs_pairs), (xt_wide, xt_pairs)
    cols, rows = (cols_wide, cols_pairs), (rows_wide, rows_pairs)
    core = lax.axis_index("core")
    blocks = len(mine_refs)
    rows_slots = OWN // blocks

    late = gather_parts(mine_refs, got_refs, 0, late_ref)
    wu = dot(late, sel_u_ref[...]).astype(BF16)
    wu_ref[...] = wu
    rates = dot(late, sel_rc_ref[...])
    rates = jnp.concatenate([rates.T, jnp.zeros((LANES, 2 * LANES - D), F32)], axis=1)
    rates_ref[...] = rates
    for third in range(3):
        window = late[:, starts[third] * LANES : (starts[third] + width) * LANES]
        wqkv_ref[third] = dot(window, sel_q_ref[third]).astype(BF16)

    decay, coef = rates[: 4 * STATE], rates[4 * STATE :]

    def lag_row(k):
        powers = jnp.exp(-decay * k) * coef
        return [jnp.sum(powers[d * STATE : (d + 1) * STATE], 0, keepdims=True) for d in range(4)]

    def store_lag(way, lag, row):
        row = row.astype(BF16).astype(F32)
        tail = row[:, LANES:D]
        for kind, lanes in enumerate((row[:, :LANES], pair_lanes(tail, tail))):
            table_ref[way, kind, lag + CENTER] = jnp.broadcast_to(lanes, (8, LANES))

    def lag_step(k, _):
        found = lag_row(k.astype(F32))
        for way in range(2):
            store_lag(way, k, found[2 * way])
            store_lag(way, -k, found[2 * way + 1])
        return 0

    lax.fori_loop(0, GRID, lag_step, 0, unroll=4)
    found = lag_row(0.0)
    for way in range(2):
        store_lag(way, 0, found[2 * way] + found[2 * way + 1])


    for block in range(blocks):
        here = slice(block * rows_slots, (block + 1) * rows_slots)
        for ref, which in ((first_own_ref, core), (first_other_ref, 1 - core)):
            start = pl.multiple_of((block * 2 + which) * rows_slots, rows_slots)
            first_ref[pl.ds(start, rows_slots), :] = ref[here, :]
    mixed = dot(first_ref[...], wu) * widen(mask_ref[...])
    mixed = mixed.astype(BF16)
    mixed_ref[...] = mixed
    mixed = mixed.astype(F32)
    put_columns(*xs, mixed)
    put_rows(*xt, xs[0], mixed[:, LANES:], cols[1])

    def scan_step(index, _):
        first = (index // 2) * 8
        for way, src, dst in ((0, xt, rows), (1, xs, cols)):
            for kind, sublane in units(index % 2):
                step = src[kind].shape[0] // GRID
                total = block_sum(src, table_ref, way, kind, first, 8, sublane, 1)
                for t in range(8):
                    place = pl.multiple_of((first + t) * step + sublane, 8)
                    dst[kind][pl.ds(place, 8), :] = total[t]
        return 0

    lax.fori_loop(0, 8, scan_step, 0)

    def join_step(i, _):
        for row, value in join_rows(i, GRID, rows, cols):
            place = pl.ds(pl.multiple_of(row * GRID, GRID), GRID)
            scanned_ref[place, :] = (value * widen(mask_ref[place, :])).astype(BF16)
        return 0

    lax.fori_loop(0, GRID // 2, join_step, 0, unroll=2)

    for block in range(blocks):
        start = pl.multiple_of((block * 2 + core) * rows_slots, rows_slots)
        scanned_own[block * rows_slots : (block + 1) * rows_slots, :] = scanned_ref[
            pl.ds(start, rows_slots), :
        ]

    lane_own = lax.broadcasted_iota(jnp.int32, (OWN, LANES), 1)
    lane_all = lax.broadcasted_iota(jnp.int32, (SLOTS, LANES), 1)
    bias = jnp.where(lane_all == HEAD_DIM, (mask_ref[...] - 1.0) * 1e30, 0.0)
    ones = jnp.where((lane_all == HEAD_DIM) | (lane_all == HEAD_DIM + 1), 1.0, 0.0)
    one_own = jnp.where(lane_own == HEAD_DIM, 1.0, 0.0)
    for h in range(HEADS):
        tile = slice(h * LANES, (h + 1) * LANES)
        q_ref[h] = (
            dot(scanned_own[...], wqkv_ref[0, :, tile]) * HEAD_DIM ** (-0.5) + one_own
        ).astype(BF16)
        k_ref[h] = (dot(scanned_ref[...], wqkv_ref[1, :, tile]) + bias).astype(BF16)
        v_ref[h] = (dot(scanned_ref[...], wqkv_ref[2, :, tile]) + ones).astype(BF16)


def middle_kernel(
    own_ref,
    mask_ref,
    gains_ref,
    sel_1_ref,
    sel_o_ref,
    sel_2_ref,
    q_ref,
    k_ref,
    v_ref,
    *refs,
):
    blocks = own_ref.shape[0]
    middle_body(
        own_ref,
        mask_ref,
        gains_ref,
        sel_1_ref,
        sel_o_ref,
        sel_2_ref,
        q_ref,
        k_ref,
        v_ref,
        refs[:blocks],
        refs[blocks : 2 * blocks],
        *refs[2 * blocks :],
    )


def middle_body(
    own_ref,
    mask_ref,
    gains_ref,
    sel_1_ref,
    sel_o_ref,
    sel_2_ref,
    q_ref,
    k_ref,
    v_ref,
    mine_refs,
    got_refs,
    soft_ref,
    lifted_ref,
    out_ref,
    grad_middle_ref,
    gain_ref,
    keep_ref,
    send_ref,
    early_ref,
    scores,
    wo,
    w1,
    w2,
    att,
    outs,
    sums,
    middle,
    second,
    pre,
    grad_hidden,
    hidden,
    grad_pre,
    wire,
    parted,
):
    core = lax.axis_index("core")
    blocks, _, rows_slots, _ = own_ref.shape
    parts = early_ref.shape[0]
    per_block = D // blocks
    gain = gains_ref[1:2, :]

    left = gather_parts(mine_refs, got_refs, 1, early_ref)
    right = gather_parts(mine_refs, got_refs, 2, early_ref)
    span = parts // 2 * LANES
    for half in range(2):
        w1[:, half * FF // 2 : (half + 1) * FF // 2] = dot(
            left[:, half * span : (half + 1) * span], sel_1_ref[...]
        ).astype(BF16)
    out_weight = dot(left, sel_o_ref[...]).astype(BF16)
    for h in range(HEADS):
        wo[h, :HEAD_DIM] = out_weight[h * HEAD_DIM : (h + 1) * HEAD_DIM]
        wo[h, HEAD_DIM:] = jnp.zeros((LANES - HEAD_DIM, D), BF16)
    for g in range(4):
        part = dot(right, sel_2_ref[g])
        for r in range(blocks):
            start = r * 4 * per_block + g * per_block
            w2[start : start + per_block] = part[r * per_block : (r + 1) * per_block].astype(BF16)

    for h in range(HEADS):
        scores[...] = dot_nt(k_ref[h], q_ref[h])

        def top_step(i, top):
            values = scores[pl.ds(pl.multiple_of(i * 64, 64), 64), :]
            return jnp.maximum(top, jnp.max(values.reshape(8, 8, OWN), 0))

        top = lax.fori_loop(1, SLOTS // 64, top_step, jnp.max(scores[:64].reshape(8, 8, OWN), 0))
        top = jnp.max(top, 0, keepdims=True)

        def soft_step(i, _, h=h, top=top):
            place = pl.ds(pl.multiple_of(i * 128, 128), 128)
            soft_ref[h, place, :] = jnp.exp(scores[place, :] - top).astype(BF16)
            return 0

        lax.fori_loop(0, SLOTS // 128, soft_step, 0)
        raw = dot_tn(soft_ref[h], v_ref[h])
        total = raw[:, HEAD_DIM : HEAD_DIM + 1]
        sums[h] = jnp.broadcast_to(1.0 / total, (OWN, LANES))
        result = raw * sums[h]
        outs[h] = result
        att[h] = result.astype(BF16)

    branch = dot(att[0], wo[0]) + dot(att[1], wo[1]) + dot(att[2], wo[2])
    middle[...] = branch

    def own_mask(block):
        start = pl.multiple_of((block * 2 + core) * rows_slots, rows_slots)
        return widen(mask_ref[pl.ds(start, rows_slots), :])

    def norm_step(block, _):
        place = pl.ds(pl.multiple_of(block * rows_slots, rows_slots), rows_slots)
        mid = own_ref[block, 0].astype(F32) + middle[place, :] * own_mask(block)
        middle[place, :] = mid
        unit, _ = normalise(mid)
        second[place, :] = (unit * gain).astype(BF16)
        return 0

    for block in range(blocks):
        norm_step(block, 0)

    pre[...] = dot(second[...], w1[...])
    cot = jnp.concatenate([own_ref[b, 1] for b in range(blocks)], axis=0)
    grad_hidden[...] = dot_nt(cot, w2[...])

    def gelu_step(i, _):
        place = pl.ds(pl.multiple_of(i * 16, 16), 16)
        x = pre[place, :]
        phi = 0.5 * (1.0 + lax.erf(x * np.float32(0.5**0.5)))
        hidden[place, :] = (x * phi).astype(BF16)
        slope = phi + x * jnp.exp(x * x * -0.5) * np.float32((2 * np.pi) ** -0.5)
        grad_pre[place, :] = (grad_hidden[place, :] * slope).astype(BF16)
        return 0

    lax.fori_loop(0, OWN // 16, gelu_step, 0, unroll=2)

    out_ref[...] = (middle[...] + dot(hidden[...], w2[...])).astype(BF16)
    grad_2 = dot_tn(hidden[...], cot).astype(BF16)
    grad_1 = dot_tn(second[...], grad_pre[...]).astype(BF16)
    grad_middle_ref[...] = dot_nt(grad_pre[...], w1[...])

    def back_step(block, total):
        place = pl.ds(pl.multiple_of(block * rows_slots, rows_slots), rows_slots)
        unit, inverse = normalise(middle[place, :])
        grad = grad_middle_ref[place, :]
        total = total + jnp.sum(grad * unit, 0, keepdims=True)
        grad = own_ref[block, 1].astype(F32) + norm_back(grad, gain, unit, inverse)
        grad_middle_ref[place, :] = grad
        second[place, :] = (grad * own_mask(block)).astype(BF16)
        return total

    gain_two = jnp.zeros((1, D), F32)
    for block in range(blocks):
        gain_two = back_step(block, gain_two)
    gain_ref[...] = gain_two

    grad_o = []
    lane_own = lax.broadcasted_iota(jnp.int32, (OWN, LANES), 1)
    for h in range(HEADS):
        grad_o.append(dot_tn(att[h], second[...])[:HEAD_DIM])
        grad_att = dot_nt(second[...], wo[h]).astype(BF16).astype(F32)
        scaled = (grad_att * sums[h]).astype(BF16).astype(F32)
        shift = -jnp.sum(scaled * outs[h], -1, keepdims=True)
        high = shift.astype(BF16).astype(F32)
        lifted = jnp.where(
            lane_own == HEAD_DIM, high, jnp.where(lane_own == HEAD_DIM + 1, shift - high, scaled)
        )
        lifted_ref[h] = lifted.astype(BF16)

    for half in range(2):
        wire[:, half * span : (half + 1) * span] = dot_nt(
            grad_1[:, half * FF // 2 : (half + 1) * FF // 2], sel_1_ref[...]
        )
    grad_o = jnp.concatenate(grad_o, axis=0).astype(BF16)
    wire[...] += dot_nt(grad_o, sel_o_ref[...])

    def deliver(lanes):
        for m in range(parts):
            parted[m] = wire[:, m * LANES : (m + 1) * LANES].astype(BF16)
        for z in range(parts // 2):
            put_blocks(keep_ref, z, lanes, parted[2 * z + core])
            put_blocks(send_ref, z, lanes, parted[2 * z + 1 - core])

    deliver(slice(0, LANES))
    total = None
    for g in range(4):
        rows = [
            grad_2[r * 4 * per_block + g * per_block : r * 4 * per_block + (g + 1) * per_block]
            for r in range(blocks)
        ]
        part = dot_nt(jnp.concatenate(rows, axis=0), sel_2_ref[g])
        total = part if total is None else total + part
    wire[...] = total
    deliver(slice(LANES, 2 * LANES))


def attention_back_kernel(
    soft_ref,
    lifted_ref,
    q_ref,
    k_ref,
    v_ref,
    scanned_ref,
    wqkv_ref,
    part_ref,
    grad_w_ref,
    scores,
    grad_scores,
    triple,
    grad_q,
    scanned_own,
    part,
    *,
    blocks,
):
    core = lax.axis_index("core")
    rows_slots = OWN // blocks
    for h in range(HEADS):
        tile = slice(h * LANES, (h + 1) * LANES)
        scores[...] = dot_nt(v_ref[h], lifted_ref[h])

        def back_step(i, _, h=h):
            place = pl.ds(pl.multiple_of(i * 64, 64), 64)
            grad_scores[place, :] = (soft_ref[h, place, :].astype(F32) * scores[place, :]).astype(
                BF16
            )
            return 0

        lax.fori_loop(0, SLOTS // 64, back_step, 0)
        grad_q[:, tile] = (dot_tn(grad_scores[...], k_ref[h]).astype(BF16) * HEAD_DIM ** (-0.5)).astype(
            BF16
        )
        triple[0, :, tile] = dot(grad_scores[...], q_ref[h]).astype(BF16)
        triple[1, :, tile] = dot(soft_ref[h], lifted_ref[h]).astype(BF16)

    part[...] = dot_nt(triple[0], wqkv_ref[1]) + dot_nt(triple[1], wqkv_ref[2])
    from_q = dot_nt(grad_q[...], wqkv_ref[0])
    for block in range(blocks):
        here = slice(block * rows_slots, (block + 1) * rows_slots)
        place = pl.ds(pl.multiple_of((block * 2 + core) * rows_slots, rows_slots), rows_slots)
        part[place, :] += from_q[here]
        scanned_own[here, :] = scanned_ref[place, :]
    part_ref[...] = part[...].astype(BF16)
    grad_w_ref[0] = dot_tn(scanned_own[...], grad_q[...]).astype(BF16)
    grad_w_ref[1] = dot_tn(scanned_ref[...], triple[0]).astype(BF16)
    grad_w_ref[2] = dot_tn(scanned_ref[...], triple[1]).astype(BF16)


def scan_back_kernel(
    starts,
    width,
    own_ref,
    mask_ref,
    part_ref,
    got_ref,
    mixed_ref,
    first_ref,
    table_ref,
    rates_ref,
    wu_ref,
    grad_w_ref,
    gain_two_ref,
    sel_u_ref,
    sel_rc_ref,
    sel_q_ref,
    keep_ref,
    send_ref,
    back_ref,
    gs_wide,
    gs_pairs,
    gt_wide,
    gt_pairs,
    xs_wide,
    xs_pairs,
    xt_wide,
    xt_pairs,
    rows_wide,
    rows_pairs,
    cols_wide,
    cols_pairs,
    grads_ref,
    own,
    own_tail,
    together,
    lag_sums,
    lag_rows,
    mixed_back,
    wire,
    parted,
):
    gs, gt = (gs_wide, gs_pairs), (gt_wide, gt_pairs)
    xs, xt = (xs_wide, xs_pairs), (xt_wide, xt_pairs)
    rows, cols = (rows_wide, rows_pairs), (cols_wide, cols_pairs)
    core = lax.axis_index("core")
    blocks, _, rows_slots, _ = own_ref.shape
    half_rows = rows_slots // GRID
    own_rows = GRID // 2
    parts = sel_rc_ref.shape[0] // LANES
    put_columns(*xs, mixed_ref[...].astype(F32))
    grads = (part_ref[...].astype(F32) + got_ref[...].astype(F32)) * widen(mask_ref[...])
    grads = grads.astype(BF16)
    grads_ref[...] = grads
    put_columns(*gs, grads.astype(F32))

    def place_of(block):
        return pl.ds(pl.multiple_of((block * 2 + core) * rows_slots, rows_slots), rows_slots)

    for source, dst in ((grads_ref, gt), (mixed_ref, xt)):
        for block in range(blocks):
            here = slice(block * rows_slots, (block + 1) * rows_slots)
            value = source[place_of(block), :].astype(F32)
            own[here, :] = value[:, :LANES]
            own_tail[here, :] = value[:, LANES:]
        put_rows(*dst, own, own_tail[...], together)

    def row_step(index, _):
        first = index * 8
        for kind, sublane in units(0):
            step = gt[kind].shape[0] // GRID
            total = block_sum(gt, table_ref, 0, kind, first, 8, sublane, -1)
            for t in range(8):
                place = pl.multiple_of((first + t) * step + sublane, 8)
                rows[kind][pl.ds(place, 8), :] = total[t]
        return 0

    lax.fori_loop(0, 4, row_step, 0)

    def col_step(index, _):
        block = index // 2
        first = (block * 2 + core) * half_rows
        for kind, sublane in units(index % 2):
            step = gs[kind].shape[0] // GRID
            total = block_sum(gs, table_ref, 1, kind, first, half_rows, sublane, -1)
            for t in range(half_rows):
                place = pl.multiple_of((block * half_rows + t) * step + sublane, 8)
                cols[kind][pl.ds(place, 8), :] = total[t]
        return 0

    lax.fori_loop(0, blocks * 2, col_step, 0)

    lag_sums[...] = jnp.zeros_like(lag_sums)

    def add_lags(way, kind, first, count, base, gref, xref):
        total = {}
        step = gref[kind].shape[0] // GRID
        for u in range(step // 8):
            g = [
                gref[kind][pl.ds(pl.multiple_of((first + t) * step + u * 8, 8), 8), :]
                for t in range(count)
            ]
            for s in range(8):
                x = xref[kind][pl.ds(pl.multiple_of((base + s) * step + u * 8, 8), 8), :]
                for t in range(count):
                    term = g[t] * x
                    total[t - s] = term if t - s not in total else total[t - s] + term
        for lag, value in total.items():
            at = first - base + (lag + CENTER)
            lag_sums[way, kind, at] += value

    def lag_row_step(index, _):
        for kind in range(2):
            add_lags(0, kind, (index // 4) * 8, 8, (index % 4) * 8, gt, xt)
        return 0

    lax.fori_loop(0, 16, lag_row_step, 0)

    def lag_col_step(index, _):
        first = ((index // 4) * 2 + core) * half_rows
        for kind in range(2):
            add_lags(1, kind, first, half_rows, (index % 4) * 8, gs, xs)
        return 0

    lax.fori_loop(0, blocks * 4, lag_col_step, 0)

    for way in range(2):
        lag_rows[way, :, :LANES] = jnp.sum(lag_sums[way, 0], 1)
        tail = jnp.sum(lag_sums[way, 1], 1)
        tail = tail[:, : D - LANES] + tail[:, D - LANES :]
        lag_rows[way, :, LANES:] = pair_lanes(tail, jnp.zeros_like(tail))

    decay, coef = rates_ref[: 4 * STATE], rates_ref[4 * STATE :]

    def table_step(k, carry):
        to_rate, to_coef = carry
        lag = k.astype(F32)
        powers = jnp.exp(-decay * lag)
        grads = []
        for way in range(2):
            for at in (CENTER + k, CENTER - k):
                grads.append(
                    jnp.broadcast_to(lag_rows[way, pl.ds(at, 1), :], (STATE, 2 * LANES))
                )
        scaled = jnp.concatenate(grads, axis=0) * powers
        return to_rate - lag * scaled, to_coef + scaled

    zero = jnp.zeros((4 * STATE, 2 * LANES), F32)
    to_rate, to_coef = lax.fori_loop(0, GRID, table_step, (zero, zero), unroll=4)
    grad_rc = jnp.concatenate([to_rate * coef, to_coef], axis=0).T[:D].astype(BF16)

    def join_step(i, _):
        for row, value in join_rows(i, own_rows, rows, cols):
            at = ((row // half_rows * 2 + core) * half_rows + row % half_rows) * GRID
            mask = mask_ref[pl.ds(pl.multiple_of(at, GRID), GRID), :]
            place = pl.ds(pl.multiple_of(row * GRID, GRID), GRID)
            mixed_back[place, :] = (value * widen(mask)).astype(BF16)
        return 0

    lax.fori_loop(0, own_rows // 2, join_step, 0, unroll=2)
    grad_u = dot_tn(first_ref[...], mixed_back[...]).astype(BF16)
    grad_first = dot_nt(mixed_back[...], wu_ref[...])
    back_ref[...] = grad_first
    gain_one = jnp.zeros((1, D), F32)
    for block in range(blocks):
        here = slice(block * rows_slots, (block + 1) * rows_slots)
        unit, _ = normalise(own_ref[block, 0].astype(F32))
        gain_one = gain_one + jnp.sum(grad_first[here] * unit, 0, keepdims=True)

    wire[...] = dot_nt(grad_u, sel_u_ref[...]) + dot_nt(grad_rc, sel_rc_ref[...])
    for third in range(3):
        span = slice(starts[third] * LANES, (starts[third] + width) * LANES)
        wire[:, span] += dot_nt(grad_w_ref[third], sel_q_ref[third])
    for m in range(parts):
        parted[m] = wire[:, m * LANES : (m + 1) * LANES].astype(BF16)
    for z in range(parts // 2):
        put_late(keep_ref, z, parted[2 * z + core])
        put_late(send_ref, z, parted[2 * z + 1 - core])

    lines = []
    for value in (gain_one, gain_two_ref[...]):
        high = value.astype(BF16).astype(F32)
        for piece in (high, value - high):
            lines.append(piece[:, :LANES])
            lines.append(
                jnp.concatenate([piece[:, LANES:], jnp.zeros((1, 2 * LANES - D), F32)], axis=1)
            )
    lines = jnp.concatenate(lines, axis=0).astype(BF16)
    for ref in (keep_ref, send_ref):
        ref[ref.shape[0] - 1, :8] = lines
        ref[ref.shape[0] - 1, 8:] = jnp.zeros((ref.shape[1] - 8, LANES), BF16)


def last_norm_kernel(
    own_ref, gains_ref, back_ref, grad_middle_ref, out_own_ref, *routed_refs
):
    _, _, slots, _ = own_ref.shape
    rows = slots * 3 // 2
    gain = gains_ref[0:1, :]
    for k, routed in enumerate(routed_refs):
        block = lax.axis_index("row") ^ k
        place = pl.ds(pl.multiple_of(block * slots, slots), slots)
        unit, inverse = normalise(own_ref[block, 0].astype(F32))
        grad = grad_middle_ref[place, :] + norm_back(back_ref[place, :], gain, unit, inverse)
        routed[:rows] = pack(out_own_ref[place, :])
        routed[rows:] = pack(grad.astype(BF16))


def late_rows(rows):
    return (rows + 31) // 16 * 16


def split(value):
    high = value.astype(BF16).astype(F32)
    return jnp.concatenate([high, value - high], axis=0)


def early_sum_kernel(keep_ref, got_ref, *out_refs):
    for k, out_ref in enumerate(out_refs):
        block = lax.axis_index("row") ^ k
        for z in range(keep_ref.shape[1]):
            total = keep_ref[block, z].astype(F32) + got_ref[block, z].astype(F32)
            out_ref[z] = total.astype(BF16)


def late_sum_kernel(depth, keep_ref, got_ref, *refs):
    count = len(refs) // 2
    routed_refs, out_refs = refs[:count], refs[count:]
    rows = keep_ref.shape[1]
    block_rows = late_rows(rows)
    last = keep_ref.shape[0] - 1
    gains = keep_ref[last, :8].astype(F32) + got_ref[last, :8].astype(F32)
    lines = []
    for g in range(2):
        for lane in range(2):
            at = 4 * g + lane
            lines.append(gains[at : at + 1] + gains[at + 2 : at + 3])
    gains = split(jnp.concatenate(lines, axis=0))
    gains = jnp.concatenate([gains, jnp.zeros((8, LANES), F32)], axis=0)
    fill = jnp.zeros((block_rows - rows - 16, LANES), F32)
    for k, out_ref in enumerate(out_refs):
        block = lax.axis_index("row") ^ k
        for z in range(depth):
            at = block * depth + z
            total = keep_ref[at].astype(F32) + got_ref[at].astype(F32)
            pieces = [gains, total]
            if block_rows > rows + 16:
                pieces.append(fill)
            out_ref[z * block_rows : (z + 1) * block_rows] = jnp.concatenate(pieces, axis=0).astype(
                BF16
            )
        out_ref[depth * block_rows :] = routed_refs[k][...]


def row_sum_kernel(blocks, *refs):
    early_refs, late_refs, out_refs = refs[:blocks], refs[blocks : 2 * blocks], refs[2 * blocks :]
    rows = early_refs[0].shape[1]
    block_rows = late_rows(rows)
    for j, out_ref in enumerate(out_refs):
        z = lax.axis_index("z") ^ j
        place = pl.ds(pl.multiple_of(z * block_rows, 16), block_rows)
        early = early_refs[0][z].astype(F32)
        late = late_refs[0][place, :].astype(F32)
        for k in range(1, blocks):
            early = early + early_refs[k][z].astype(F32)
            late = late + late_refs[k][place, :].astype(F32)
        out_ref[:rows, LANES:] = early.astype(BF16)
        out_ref[:rows, :LANES] = late[16 : 16 + rows].astype(BF16)
        gains = split(late[:4] + late[4:8])
        gains = jnp.concatenate([gains, jnp.zeros((8, LANES), F32)], axis=0).astype(BF16)
        out_ref[rows:, :LANES] = gains
        out_ref[rows:, LANES:] = jnp.zeros((16, 2 * LANES), BF16)


def final_kernel(parts, *refs):
    final_body(parts, refs[: parts // 2], *refs[parts // 2 :])


def final_body(
    parts,
    got_refs,
    g1_ref,
    g2_ref,
    wu_ref,
    rate_ref,
    coef_ref,
    qkv_ref,
    wo_ref,
    fc1_ref,
    fc2_ref,
):
    a_u, a_r, a_q, (o_u, o_r, o_c, o_q) = late_layout(parts)
    total = got_refs[0][...].astype(F32)
    for ref in got_refs[1:]:
        total = total + ref[...].astype(F32)
    early = total[: fc1_ref.shape[0], LANES:]
    total = total[:, :LANES]
    rows = fc1_ref.shape[0]
    weights, gains = total[:rows], total[rows:]
    turned = weights.T
    wu_ref[...] = turned[o_u : o_u + a_u]
    rate_ref[...] = turned[o_r : o_r + a_r]
    coef_ref[...] = turned[o_c : o_c + a_r]
    qkv_ref[...] = weights[:, o_q : o_q + a_q]
    gains = gains[0:4] + gains[4:8]
    for g, ref in ((0, g1_ref), (1, g2_ref)):
        ref[...] = jnp.concatenate(
            [gains[2 * g : 2 * g + 1], gains[2 * g + 1 : 2 * g + 2, : D - LANES]], axis=1
        )
    a_1, a_o = FF // parts, D // parts
    fc1_ref[...] = early[:, :a_1]
    wo_ref[...] = early[:, :LANES].T[a_1 : a_1 + a_o]
    turned = early[:, LANES:].T
    fc2_ref[...] = jnp.concatenate([turned[g * a_o : (g + 1) * a_o] for g in range(4)], axis=1)


def per_device(
    patches, valid_mask, norm_gains, w_u, decay_rate, out_coef, w_qkv, w_o, w_fc1, w_fc2, cotangent
):
    images, rows_here, _, _ = patches.shape
    depth, blocks = lax.axis_size("z"), lax.axis_size("row")
    parts = 2 * depth
    rows_slots = rows_here // 2 * GRID
    packed_rows = rows_slots * 3 // 2
    swap = [(0, 1), (1, 0)]
    shape = jax.ShapeDtypeStruct

    def planes(slots):
        return [pltpu.VMEM((slots, LANES), F32), pltpu.VMEM((slots // 2, LANES), F32)]

    def swapped(value):
        return lax.ppermute(value, "core", swap)

    def exchanged(values, axis):
        size = len(values)
        return [values[0]] + [
            lax.ppermute(values[k], axis, [(i, i ^ k) for i in range(size)]) for k in range(1, size)
        ]

    def to_chips(value, j):
        pairs = []
        for home in range(2):
            for source in range(blocks):
                target, image = divmod(source ^ j, images)
                pairs.append((home * blocks + source, target * blocks + home * images + image))
        return lax.ppermute(value, ("core", "row"), pairs)

    starts, width = late_spans(parts)
    sel_1, sel_o, sel_2 = early_selections(parts)

    rows_weight = w_u.shape[0]
    payload = shape((2 * packed_rows + GRID, LANES), BF16)
    shard = shape((rows_weight, 3 * LANES), BF16)
    sources = [value.reshape(images, rows_here * GRID, D) for value in (patches, cotangent)]
    if rows_weight % 16 == 0:
        weights, *routed = pl.pallas_call(
            depart_kernel,
            name="depart",
            out_shape=(shard,) + (payload,) * blocks,
            in_specs=[VMEM] * 10,
            out_specs=[VMEM] * (1 + blocks),
            compiler_params=compiler(LARGE),
        )(
                w_u.T,
            decay_rate.T,
            out_coef.T,
            w_o.T,
            w_fc2.T,
            w_qkv,
            w_fc1,
            *sources,
            valid_mask,
        )
    else:

        def fill(pieces):
            joined = jnp.concatenate(pieces, axis=1)
            return jnp.pad(joined, ((0, 0), (0, LANES - joined.shape[1])))

        weights = jnp.concatenate(
            [
                fill([w_u, decay_rate, out_coef, w_qkv]),
                fill([w_fc1, w_o]),
                fill([w_fc2[g * rows_weight : (g + 1) * rows_weight] for g in range(4)]),
            ],
            axis=1,
        )
        routed = pl.pallas_call(
            route_kernel,
            name="route",
            out_shape=(payload,) * blocks,
            in_specs=[VMEM] * 3,
            out_specs=[VMEM] * blocks,
            compiler_params=compiler(LARGE),
        )(*sources, valid_mask)

    weights = jnp.stack(exchanged([weights] * depth, "z"))
    weights = exchanged([weights] * blocks, "row")
    weights = weights + [swapped(value) for value in weights]
    routed = [to_chips(value, j) for j, value in enumerate(routed)]
    own, first_own, mask, sel_u, sel_rc, sel_q = pl.pallas_call(
        lambda *refs: norm_kernel(starts, parts, *refs),
        name="first_norm",
        out_shape=(
            shape((blocks, 2, rows_slots, D), BF16),
            shape((OWN, D), BF16),
            shape((SLOTS, LANES), F32),
            shape((parts * LANES, D), BF16),
            shape((parts * LANES, LANES), BF16),
            shape((3, width * LANES, TILE), BF16),
        ),
        in_specs=[VMEM] * (1 + blocks),
        out_specs=[VMEM] * 6,
        compiler_params=compiler(8 << 20),
    )(norm_gains, *routed)
    first_other = swapped(first_own)

    head_own = shape((HEADS, OWN, LANES), BF16)
    head_all = shape((HEADS, SLOTS, LANES), BF16)
    part_scratch = pltpu.VMEM((parts, blocks, rows_weight, LANES), BF16)
    q, k, v, scanned, mixed, table, rates, wu, wqkv = pl.pallas_call(
        lambda *refs: scan_kernel(starts, width, *refs, blocks=blocks),
        name="scan_forward",
        out_shape=(
            head_own,
            head_all,
            head_all,
            shape((SLOTS, D), BF16),
            shape((SLOTS, D), BF16),
            shape((2, 2, LAGS, 8, LANES), F32),
            shape((LANES, 2 * LANES), F32),
            shape((D, D), BF16),
            shape((3, D, TILE), BF16),
        ),
        in_specs=[VMEM] * (6 + 2 * blocks),
        out_specs=[VMEM] * 9,
        scratch_shapes=[part_scratch]
        + planes(SLOTS) * 4
        + [pltpu.VMEM((OWN, D), BF16), pltpu.VMEM((SLOTS, D), BF16)],
        compiler_params=compiler(),
    )(first_own, first_other, mask, sel_u, sel_rc, sel_q, *weights)

    wire_early = shape((blocks, depth, rows_weight, 2 * LANES), BF16)
    soft, lifted, out_own, grad_middle, gain_two, early_keep, early_send = pl.pallas_call(
        middle_kernel,
        name="attention_and_feed_forward",
        out_shape=(
            shape((HEADS, SLOTS, OWN), BF16),
            head_own,
            shape((OWN, D), BF16),
            shape((OWN, D), F32),
            shape((1, D), F32),
            wire_early,
            wire_early,
        ),
        in_specs=[VMEM] * (9 + 2 * blocks),
        out_specs=[VMEM] * 7,
        scratch_shapes=[
            part_scratch,
            pltpu.VMEM((SLOTS, OWN), F32),
            pltpu.VMEM((HEADS, LANES, D), BF16),
            pltpu.VMEM((D, FF), BF16),
            pltpu.VMEM((FF, D), BF16),
            pltpu.VMEM((HEADS, OWN, LANES), BF16),
            pltpu.VMEM((HEADS, OWN, LANES), F32),
            pltpu.VMEM((HEADS, OWN, LANES), F32),
            pltpu.VMEM((OWN, D), F32),
            pltpu.VMEM((OWN, D), BF16),
            pltpu.VMEM((OWN, FF), F32),
            pltpu.VMEM((OWN, FF), F32),
            pltpu.VMEM((OWN, FF), BF16),
            pltpu.VMEM((OWN, FF), BF16),
            pltpu.VMEM((D, parts * LANES), F32),
            pltpu.VMEM((parts, D, LANES), BF16),
        ],
        compiler_params=compiler(),
    )(own, mask, norm_gains, sel_1, sel_o, sel_2, q, k, v, *weights)

    early_recv = swapped(early_send)

    part, grad_w = pl.pallas_call(
        lambda *refs: attention_back_kernel(*refs, blocks=blocks),
        name="attention_backward",
        out_shape=(shape((SLOTS, D), BF16), shape((3, D, TILE), BF16)),
        in_specs=[VMEM] * 7,
        out_specs=[VMEM] * 2,
        scratch_shapes=[
            pltpu.VMEM((SLOTS, OWN), F32),
            pltpu.VMEM((SLOTS, OWN), BF16),
            pltpu.VMEM((2, SLOTS, TILE), BF16),
            pltpu.VMEM((OWN, TILE), BF16),
            pltpu.VMEM((OWN, D), BF16),
            pltpu.VMEM((SLOTS, D), F32),
        ],
        compiler_params=compiler(),
    )(soft, lifted, q, k, v, scanned, wqkv)

    early_keep, early_recv, part = lax.optimization_barrier((early_keep, early_recv, part))
    early = pl.pallas_call(
        early_sum_kernel,
        name="early_sum",
        out_shape=(shape((depth, rows_weight, 2 * LANES), BF16),) * blocks,
        in_specs=[VMEM] * 2,
        out_specs=[VMEM] * blocks,
        compiler_params=compiler(8 << 20),
    )(early_keep, early_recv)
    early, part = lax.optimization_barrier((early, part))
    part_got = swapped(part)
    early = exchanged(early, "row")
    wire_late = shape((blocks * depth + 1, rows_weight, LANES), BF16)
    late_keep, late_send, back = pl.pallas_call(
        lambda *refs: scan_back_kernel(starts, width, *refs),
        name="scan_backward",
        out_shape=(wire_late, wire_late, shape((OWN, D), F32)),
        in_specs=[VMEM] * 14,
        out_specs=[VMEM] * 3,
        scratch_shapes=planes(SLOTS) + planes(OWN) + planes(SLOTS) + planes(OWN) * 3
        + [
            pltpu.VMEM((SLOTS, D), BF16),
            pltpu.VMEM((OWN, LANES), F32),
            pltpu.VMEM((OWN, D - LANES), F32),
            pltpu.VMEM((OWN // 2, LANES), F32),
            pltpu.VMEM((2, 2, LAGS, 8, LANES), F32),
            pltpu.VMEM((2, LAGS, 2 * LANES), F32),
            pltpu.VMEM((OWN, D), BF16),
            pltpu.VMEM((D, parts * LANES), F32),
            pltpu.VMEM((parts, D, LANES), BF16),
        ],
        compiler_params=compiler(),
    )(
        own,
        mask,
        part,
        part_got,
        mixed,
        first_own,
        table,
        rates,
        wu,
        grad_w,
        gain_two,
        sel_u,
        sel_rc,
        sel_q,
    )
    late_keep, late_send, early = lax.optimization_barrier((late_keep, late_send, early))
    payload = shape((2 * packed_rows, LANES), BF16)
    routed = pl.pallas_call(
        last_norm_kernel,
        name="last_norm",
        out_shape=(payload,) * blocks,
        in_specs=[VMEM] * 5,
        out_specs=[VMEM] * blocks,
        compiler_params=compiler(8 << 20),
    )(own, norm_gains, back, grad_middle, out_own)
    payload = shape((depth * late_rows(rows_weight) + 2 * packed_rows, LANES), BF16)
    late = pl.pallas_call(
        lambda *refs: late_sum_kernel(depth, *refs),
        name="late_sum",
        out_shape=(payload,) * blocks,
        in_specs=[VMEM] * (2 + blocks),
        out_specs=[VMEM] * blocks,
        compiler_params=compiler(8 << 20),
    )(late_keep, swapped(late_send), *routed)
    late = exchanged(late, "row")
    summed = pl.pallas_call(
        lambda *refs: row_sum_kernel(blocks, *refs),
        name="row_sum",
        out_shape=(shape((rows_weight + 16, 3 * LANES), BF16),) * depth,
        in_specs=[VMEM] * (2 * blocks),
        out_specs=[VMEM] * depth,
        compiler_params=compiler(8 << 20),
    )(*early, *late)
    summed = exchanged(summed, "z")

    chosen = pl.pallas_call(
        choose_kernel,
        name="choose",
        out_shape=shape((images, 2 * packed_rows, LANES), BF16),
        in_specs=[VMEM] * blocks,
        out_specs=VMEM,
        compiler_params=compiler(8 << 20),
    )(*late)
    whole = shape((images, rows_here * GRID, D), BF16)
    block_out, grad_patches = pl.pallas_call(
        home_kernel,
        name="home",
        out_shape=(whole, whole),
        in_specs=[VMEM] * (1 + blocks),
        out_specs=[VMEM] * 2,
        compiler_params=compiler(8 << 20),
    )(swapped(chosen), *late)

    summed, block_out, grad_patches = lax.optimization_barrier((summed, block_out, grad_patches))
    turned = (4 * STATE // parts, rows_weight)
    g1, g2, f_u, f_rate, f_coef, f_qkv, f_o, f_1, f_2 = pl.pallas_call(
        lambda *refs: final_kernel(parts, *refs),
        name="final_sum",
        out_shape=(
            shape((1, D), F32),
            shape((1, D), F32),
            shape((D // parts, rows_weight), F32),
            shape(turned, F32),
            shape(turned, F32),
            shape((rows_weight, 3 * D // parts), F32),
            shape((D // parts, rows_weight), F32),
            shape((rows_weight, FF // parts), F32),
            shape((D // parts, 4 * rows_weight), F32),
        ),
        in_specs=[VMEM] * depth,
        out_specs=[VMEM] * 9,
        compiler_params=compiler(8 << 20),
    )(*summed)
    return (
        block_out.reshape(patches.shape),
        grad_patches.reshape(patches.shape),
        g1.reshape(D),
        g2.reshape(D),
        f_u.T,
        f_rate.T,
        f_coef.T,
        f_qkv,
        f_o.T,
        f_1,
        f_2.T,
    )


def solution(mesh):
    images, rows = mesh.devices.shape
    fine = Mesh(mesh.devices.reshape(images // 2, 2, rows), ("z", "core", "row"))
    img = ("z", "core")
    grid = P(img, "row", None, None)
    weight = P("row", img)
    in_specs = (grid, P(img, None, None), P()) + (weight,) * 7 + (grid,)
    out_specs = (grid, grid, P(), P()) + (weight,) * 7
    return jax.shard_map(
        per_device, mesh=fine, in_specs=in_specs, out_specs=out_specs, check_vma=False
    )
```

```python
import jax
import jax.numpy as jnp
import numpy as np
from jax import lax
from jax.experimental import pallas as pl
from jax.experimental.pallas import tpu as pltpu
from jax.sharding import Mesh
from jax.sharding import PartitionSpec as P

HEADS = 3
HEAD_DIM = 64
STATE = 16
GRID = 32
SLOTS = GRID * GRID
OWN = SLOTS // 2
D = HEADS * HEAD_DIM
FF = 4 * D
LANES = 128
TILE = HEADS * LANES
LAGS = 2 * GRID
CENTER = GRID - 1
EPS = 1e-05
BF16 = jnp.bfloat16
F32 = jnp.float32


def late_layout(parts):
    a_u, a_r, a_q = D // parts, 4 * STATE // parts, 3 * D // parts
    return a_u, a_r, a_q, (0, a_u, a_u + a_r, a_u + 2 * a_r)


def late_spans(parts):
    a_q = 3 * D // parts
    first = [third * D // a_q for third in range(3)]
    last = [((third + 1) * D - 1) // a_q for third in range(3)]
    width = max(stop - start + 1 for start, stop in zip(first, last))
    return [min(start, parts - width) for start in first], width


def early_selections(parts):
    a_1, a_o = FF // parts, D // parts
    half = parts // 2
    sel_1 = np.zeros((half, LANES, FF // 2), np.float32)
    sel_o = np.zeros((parts, LANES, D), np.float32)
    sel_2 = np.zeros((4, parts, LANES, D), np.float32)
    for m in range(half):
        for col in range(a_1):
            sel_1[m, col, m * a_1 + col] = 1
    for m in range(parts):
        for col in range(a_o):
            sel_o[m, a_1 + col, m * a_o + col] = 1
            for g in range(4):
                sel_2[g, m, g * a_o + col, m * a_o + col] = 1
    return (
        sel_1.reshape(half * LANES, FF // 2).astype(BF16),
        sel_o.reshape(parts * LANES, D).astype(BF16),
        sel_2.reshape(4, parts * LANES, D).astype(BF16),
    )


def lane_and_part(shape):
    place = lax.broadcasted_iota(jnp.int32, shape, 0)
    return place % LANES, place // LANES, lax.broadcasted_iota(jnp.int32, shape, 1)


def put_late_selections(starts, parts, sel_u_ref, sel_rc_ref, sel_q_ref):
    a_u, a_r, a_q, (o_u, o_r, o_c, o_q) = late_layout(parts)

    def put(hit):
        return jnp.where(hit, 1.0, 0.0).astype(BF16)

    lane, part, col = lane_and_part(sel_u_ref.shape)
    sel_u_ref[...] = put((lane < a_u) & (part * a_u + lane == col))
    lane, part, col = lane_and_part(sel_rc_ref.shape)
    rate = (lane >= o_r) & (lane < o_c) & (part * a_r + lane - o_r == col)
    coef = (lane >= o_c) & (lane < o_q) & (part * a_r + lane - o_c + 4 * STATE == col)
    sel_rc_ref[...] = put(rate | coef)
    lane, part, col = lane_and_part(sel_q_ref.shape[1:])
    whole = jnp.where(
        col % LANES < HEAD_DIM, col // LANES * HEAD_DIM + col % LANES, -4 * D
    )
    for third in range(3):
        here = (part + starts[third]) * a_q + lane - o_q - third * D
        sel_q_ref[third] = put((lane >= o_q) & (lane < o_q + a_q) & (here == whole))


def dot(a, b):
    return lax.dot_general(a, b, (((1,), (0,)), ((), ())), preferred_element_type=F32)


def dot_nt(a, b):
    return lax.dot_general(a, b, (((1,), (1,)), ((), ())), preferred_element_type=F32)


def dot_tn(a, b):
    return lax.dot_general(a, b, (((0,), (0,)), ((), ())), preferred_element_type=F32)


def normalise(values):
    center = values - jnp.mean(values, -1, keepdims=True)
    spread = jnp.mean(center * center, -1, keepdims=True)
    inverse = lax.rsqrt(spread + EPS)
    return center * inverse, inverse


def norm_back(grad, gain, unit, inverse):
    scaled = grad * gain
    first = jnp.mean(scaled, -1, keepdims=True)
    second = jnp.mean(scaled * unit, -1, keepdims=True)
    return inverse * (scaled - first - unit * second)


def widen(mask):
    return jnp.concatenate([mask, mask[:, : D - LANES]], axis=1)


def put_blocks(ref, z, lanes, value):
    rows = ref.shape[2]
    for r in range(ref.shape[0]):
        ref[r, z, :, lanes] = value[r * rows : (r + 1) * rows]


def put_late(ref, z, value):
    rows = ref.shape[1]
    depth = ref.shape[0] * rows // D
    for r in range(D // rows):
        ref[r * depth + z] = value[r * rows : (r + 1) * rows]


def pair_lanes(first, second):
    return jnp.concatenate([first, second], axis=1)


def put_columns(wide, pairs, values):
    wide[...] = values[:, :LANES]
    tail = values[:, LANES:].reshape(values.shape[0] // GRID, 2, GRID // 2, D - LANES)
    tail = pair_lanes(tail[:, 0].reshape(-1, D - LANES), tail[:, 1].reshape(-1, D - LANES))
    pairs[...] = tail


def put_rows(wide, pairs, from_wide, tail, together):
    rows = from_wide.shape[0] // GRID
    together[...] = pair_lanes(tail[: rows // 2 * GRID], tail[rows // 2 * GRID :])
    for j in range(GRID):
        wide[j * rows : (j + 1) * rows, :] = from_wide[pl.ds(j, rows, stride=GRID), :]
        pairs[j * rows // 2 : (j + 1) * rows // 2, :] = together[pl.ds(j, rows // 2, stride=GRID), :]


def units(index):
    return [(0, (index * 2 + u) * 8) for u in range(2)] + [(1, index * 8)]


def block_sum(src, table, way, kind, first, count, sublane, sign):
    total = [None] * count
    step = src[kind].shape[0] // GRID
    for base in range(0, GRID, 8):
        low, high = -(base + 7), count - 1 - base
        coef = {
            lag: table[way, kind, first * sign + (lag * sign + CENTER)]
            for lag in range(low, high + 1)
        }
        for s in range(base, base + 8):
            x = src[kind][pl.ds(pl.multiple_of(s * step + sublane, 8), 8), :]
            for t in range(count):
                term = coef[t - s] * x
                total[t] = term if total[t] is None else total[t] + term
    return total


def join_rows(i, count, rows, cols):
    half = GRID // 2
    narrow = D - LANES
    across = rows[1][pl.ds(i, GRID, stride=count // 2), :]
    found = []
    for which in range(2):
        row = i + which * (count // 2)
        wide = cols[0][pl.ds(pl.multiple_of(row * GRID, GRID), GRID), :].astype(BF16).astype(F32)
        wide = wide + rows[0][pl.ds(i + which * (count // 2), GRID, stride=count), :]
        pairs = cols[1][pl.ds(pl.multiple_of(row * half, half), half), :].astype(BF16).astype(F32)
        tail = jnp.concatenate([pairs[:, :narrow], pairs[:, narrow:]], axis=0)
        tail = tail + across[:, which * narrow : (which + 1) * narrow]
        found.append((row, jnp.concatenate([wide, tail], axis=1)))
    return found


def gather_parts(mine_refs, got_refs, block, out_ref):
    core, row, depth = lax.axis_index("core"), lax.axis_index("row"), lax.axis_index("z")
    lanes = slice(block * LANES, (block + 1) * LANES)
    count = out_ref.shape[0] // 2
    rows = out_ref.shape[2]
    for refs, which in ((mine_refs, core), (got_refs, 1 - core)):
        for k, ref in enumerate(refs):
            for j in range(count):
                out_ref[2 * (depth ^ j) + which, row ^ k] = ref[j, :, lanes]
    wide = []
    for m in range(2 * count):
        wide.append(jnp.concatenate([out_ref[m, r] for r in range(out_ref.shape[1])], axis=0))
    return jnp.concatenate(wide, axis=1)


LARGE = 60 << 20


def compiler(limit=24 << 20):
    return pltpu.CompilerParams(vmem_limit_bytes=limit)


VMEM = pl.BlockSpec(memory_space=pltpu.VMEM)


def pack(values):
    half = values.shape[0] // 2
    tail = jnp.concatenate([values[:half, LANES:], values[half:, LANES:]], axis=1)
    return jnp.concatenate([values[:, :LANES], tail], axis=0)


def unpack(packed):
    count = packed.shape[0] * 2 // 3
    tail = packed[count:]
    tail = jnp.concatenate([tail[:, : D - LANES], tail[:, D - LANES :]], axis=0)
    return jnp.concatenate([packed[:count], tail], axis=1)


def pack_weights_kernel(turned_refs, qkv_ref, fc1_ref, out_ref):
    wu, rate, coef, wo, fc2 = [ref[...].astype(F32) for ref in turned_refs]
    rows = qkv_ref.shape[0]
    a_o, a_r = wo.shape[0], rate.shape[0]
    pieces = [wu, rate, coef, wo] + [fc2[:, g * rows : (g + 1) * rows] for g in range(4)]
    joined = jnp.concatenate(pieces, axis=0)
    joined = jnp.concatenate([joined, jnp.zeros((joined.shape[0], LANES - rows), F32)], axis=1)
    joined = joined.T[:rows]
    first, second = a_o + 2 * a_r, 2 * a_o + 2 * a_r

    def fill(parts):
        used = sum(part.shape[1] for part in parts)
        return parts + [jnp.zeros((rows, LANES - used), F32)]

    packed = jnp.concatenate(
        fill([joined[:, :first], qkv_ref[...].astype(F32)])
        + fill([fc1_ref[...].astype(F32), joined[:, first:second]])
        + fill([joined[:, second:]]),
        axis=1,
    ).astype(BF16)
    out_ref[...] = packed


def route_kernel(patch_ref, cot_ref, valid_ref, *out_refs):
    row = lax.axis_index("row")
    images, slots, _ = patch_ref.shape
    half = slots // 2
    packed = half * 3 // 2
    for j, out_ref in enumerate(out_refs):
        target = row ^ j
        core, image = target // images, target % images
        place = pl.ds(pl.multiple_of(core * half, half), half)
        out_ref[:packed] = pack(patch_ref[image, place, :])
        out_ref[packed : 2 * packed] = pack(cot_ref[image, place, :])
        valid = valid_ref[image].astype(F32).astype(BF16)
        out_ref[2 * packed :] = jnp.concatenate(
            [valid, jnp.zeros((GRID, LANES - GRID), BF16)], axis=1
        )


def depart_kernel(*refs):
    turned, (qkv_ref, fc1_ref, patch_ref, cot_ref, valid_ref, out_ref) = refs[:5], refs[5:11]
    pack_weights_kernel(turned, qkv_ref, fc1_ref, out_ref)
    route_kernel(patch_ref, cot_ref, valid_ref, *refs[11:])


def norm_kernel(starts, parts, gains_ref, *refs):
    got_refs, refs = refs[:-6], refs[-6:]
    own_ref, first_ref, mask_ref, *selections = refs
    core, row = lax.axis_index("core"), lax.axis_index("row")
    images = len(got_refs) // 2
    gain = gains_ref[0:1, :]
    slots = own_ref.shape[2]
    packed = slots * 3 // 2
    for j, got in enumerate(got_refs):
        block = (core * images + row % images) ^ j
        patch = unpack(got[:packed])
        own_ref[block, 0] = patch
        own_ref[block, 1] = unpack(got[packed : 2 * packed])
        unit, _ = normalise(patch.astype(F32))
        first_ref[pl.ds(pl.multiple_of(block * slots, slots), slots), :] = (unit * gain).astype(
            BF16
        )
    valid = got_refs[0][2 * packed :].astype(F32).T
    for i in range(GRID):
        mask_ref[i * GRID : (i + 1) * GRID, :] = jnp.broadcast_to(
            valid[:GRID, i : i + 1], (GRID, LANES)
        )
    put_late_selections(starts, parts, *selections)


def fold(packed):
    half = packed.shape[0] // 2
    return jnp.concatenate([packed[:half], packed[half:]], axis=1)


def unfold(folded):
    return jnp.concatenate([folded[:, :LANES], folded[:, LANES:]], axis=0)


def results_of(early_ref, late_ref, rows):
    early_start, late_start = early_ref.shape[0] - rows // 2, late_ref.shape[0] - rows
    return unfold(early_ref[early_start:]), late_ref[late_start:]


def choose_kernel(*refs):
    got_refs, out_ref = refs[:-1], refs[-1]
    blocks = len(got_refs) // 2
    core, row = lax.axis_index("core"), lax.axis_index("row")
    images, rows = out_ref.shape[0], out_ref.shape[1] // 2
    for k, got in enumerate(zip(got_refs[:blocks], got_refs[blocks:])):
        image = row ^ k

        @pl.when(image // images != core)
        def _(got=got, image=image):
            for which, value in enumerate(results_of(*got, rows)):
                out_ref[image % images, which * rows : (which + 1) * rows] = value


def home_kernel(swapped_ref, *refs):
    got_refs, out_refs = refs[:-2], refs[-2:]
    core, row = lax.axis_index("core"), lax.axis_index("row")
    images, slots, _ = out_refs[0].shape
    half = slots // 2
    rows = half * 3 // 2
    blocks = len(got_refs) // 2
    mine = pl.ds(pl.multiple_of(core * half, half), half)
    theirs = pl.ds(pl.multiple_of((1 - core) * half, half), half)
    for k, got in enumerate(zip(got_refs[:blocks], got_refs[blocks:])):
        image = row ^ k

        @pl.when(image // images == core)
        def _(got=got, image=image):
            for out_ref, value in zip(out_refs, results_of(*got, rows)):
                out_ref[image % images, mine, :] = unpack(value)

    for image in range(images):
        for which, out_ref in enumerate(out_refs):
            value = swapped_ref[image, which * rows : (which + 1) * rows]
            out_ref[image, theirs, :] = unpack(value)


def scan_kernel(
    starts,
    width,
    first_own_ref,
    first_other_ref,
    mask_ref,
    sel_u_ref,
    sel_rc_ref,
    sel_q_ref,
    *refs,
    blocks,
):
    mine_refs, got_refs, refs = refs[:blocks], refs[blocks : 2 * blocks], refs[2 * blocks :]
    scan_body(
        starts,
        width,
        first_own_ref,
        first_other_ref,
        mask_ref,
        sel_u_ref,
        sel_rc_ref,
        sel_q_ref,
        mine_refs,
        got_refs,
        *refs,
    )


def scan_body(
    starts,
    width,
    first_own_ref,
    first_other_ref,
    mask_ref,
    sel_u_ref,
    sel_rc_ref,
    sel_q_ref,
    mine_refs,
    got_refs,
    q_ref,
    k_ref,
    v_ref,
    scanned_ref,
    mixed_ref,
    table_ref,
    rates_ref,
    wu_ref,
    wqkv_ref,
    late_ref,
    xs_wide,
    xs_pairs,
    xt_wide,
    xt_pairs,
    cols_wide,
    cols_pairs,
    rows_wide,
    rows_pairs,
    scanned_own,
    first_ref,
):
    xs, xt = (xs_wide, xs_pairs), (xt_wide, xt_pairs)
    cols, rows = (cols_wide, cols_pairs), (rows_wide, rows_pairs)
    core = lax.axis_index("core")
    blocks = len(mine_refs)
    rows_slots = OWN // blocks

    late = gather_parts(mine_refs, got_refs, 0, late_ref)
    wu = dot(late, sel_u_ref[...]).astype(BF16)
    wu_ref[...] = wu
    rates = dot(late, sel_rc_ref[...])
    rates = jnp.concatenate([rates.T, jnp.zeros((LANES, 2 * LANES - D), F32)], axis=1)
    rates_ref[...] = rates
    for third in range(3):
        window = late[:, starts[third] * LANES : (starts[third] + width) * LANES]
        wqkv_ref[third] = dot(window, sel_q_ref[third]).astype(BF16)

    decay, coef = rates[: 4 * STATE], rates[4 * STATE :]

    def lag_row(k):
        powers = jnp.exp(-decay * k) * coef
        return [jnp.sum(powers[d * STATE : (d + 1) * STATE], 0, keepdims=True) for d in range(4)]

    def store_lag(way, lag, row):
        row = row.astype(BF16).astype(F32)
        tail = row[:, LANES:D]
        for kind, lanes in enumerate((row[:, :LANES], pair_lanes(tail, tail))):
            table_ref[way, kind, lag + CENTER] = jnp.broadcast_to(lanes, (8, LANES))

    def lag_step(k, _):
        found = lag_row(k.astype(F32))
        for way in range(2):
            store_lag(way, k, found[2 * way])
            store_lag(way, -k, found[2 * way + 1])
        return 0

    lax.fori_loop(0, GRID, lag_step, 0, unroll=True)
    found = lag_row(0.0)
    for way in range(2):
        store_lag(way, 0, found[2 * way] + found[2 * way + 1])


    for block in range(blocks):
        here = slice(block * rows_slots, (block + 1) * rows_slots)
        for ref, which in ((first_own_ref, core), (first_other_ref, 1 - core)):
            start = pl.multiple_of((block * 2 + which) * rows_slots, rows_slots)
            first_ref[pl.ds(start, rows_slots), :] = ref[here, :]
    mixed = dot(first_ref[...], wu) * widen(mask_ref[...])
    mixed = mixed.astype(BF16)
    mixed_ref[...] = mixed
    mixed = mixed.astype(F32)
    put_columns(*xs, mixed)
    put_rows(*xt, xs[0], mixed[:, LANES:], cols[1])

    def scan_step(index, _):
        first = (index // 2) * 8
        for way, src, dst in ((0, xt, rows), (1, xs, cols)):
            for kind, sublane in units(index % 2):
                step = src[kind].shape[0] // GRID
                total = block_sum(src, table_ref, way, kind, first, 8, sublane, 1)
                for t in range(8):
                    place = pl.multiple_of((first + t) * step + sublane, 8)
                    dst[kind][pl.ds(place, 8), :] = total[t]
        return 0

    lax.fori_loop(0, 8, scan_step, 0, unroll=2)

    def join_step(i, _):
        for row, value in join_rows(i, GRID, rows, cols):
            place = pl.ds(pl.multiple_of(row * GRID, GRID), GRID)
            scanned_ref[place, :] = (value * widen(mask_ref[place, :])).astype(BF16)
        return 0

    lax.fori_loop(0, GRID // 2, join_step, 0, unroll=True)

    for block in range(blocks):
        start = pl.multiple_of((block * 2 + core) * rows_slots, rows_slots)
        scanned_own[block * rows_slots : (block + 1) * rows_slots, :] = scanned_ref[
            pl.ds(start, rows_slots), :
        ]

    lane_own = lax.broadcasted_iota(jnp.int32, (OWN, LANES), 1)
    lane_all = lax.broadcasted_iota(jnp.int32, (SLOTS, LANES), 1)
    bias = jnp.where(lane_all == HEAD_DIM, (mask_ref[...] - 1.0) * 1e30, 0.0)
    ones = jnp.where((lane_all == HEAD_DIM) | (lane_all == HEAD_DIM + 1), 1.0, 0.0)
    one_own = jnp.where(lane_own == HEAD_DIM, 1.0, 0.0)
    for h in range(HEADS):
        tile = slice(h * LANES, (h + 1) * LANES)
        q_ref[h] = (
            dot(scanned_own[...], wqkv_ref[0, :, tile]) * HEAD_DIM ** (-0.5) + one_own
        ).astype(BF16)
        k_ref[h] = (dot(scanned_ref[...], wqkv_ref[1, :, tile]) + bias).astype(BF16)
        v_ref[h] = (dot(scanned_ref[...], wqkv_ref[2, :, tile]) + ones).astype(BF16)


def middle_kernel(
    own_ref,
    mask_ref,
    gains_ref,
    sel_1_ref,
    sel_o_ref,
    sel_2_ref,
    q_ref,
    k_ref,
    v_ref,
    *refs,
):
    blocks = own_ref.shape[0]
    middle_body(
        own_ref,
        mask_ref,
        gains_ref,
        sel_1_ref,
        sel_o_ref,
        sel_2_ref,
        q_ref,
        k_ref,
        v_ref,
        refs[:blocks],
        refs[blocks : 2 * blocks],
        *refs[2 * blocks :],
    )


def middle_body(
    own_ref,
    mask_ref,
    gains_ref,
    sel_1_ref,
    sel_o_ref,
    sel_2_ref,
    q_ref,
    k_ref,
    v_ref,
    mine_refs,
    got_refs,
    soft_ref,
    lifted_ref,
    out_ref,
    grad_middle_ref,
    gain_ref,
    keep_ref,
    send_ref,
    early_ref,
    scores,
    wo,
    w1,
    w2,
    att,
    outs,
    sums,
    middle,
    second,
    pre,
    grad_hidden,
    hidden,
    grad_pre,
    wire,
    parted,
):
    core = lax.axis_index("core")
    blocks, _, rows_slots, _ = own_ref.shape
    parts = early_ref.shape[0]
    per_block = D // blocks
    gain = gains_ref[1:2, :]

    left = gather_parts(mine_refs, got_refs, 1, early_ref)
    right = gather_parts(mine_refs, got_refs, 2, early_ref)
    span = parts // 2 * LANES
    for half in range(2):
        w1[:, half * FF // 2 : (half + 1) * FF // 2] = dot(
            left[:, half * span : (half + 1) * span], sel_1_ref[...]
        ).astype(BF16)
    out_weight = dot(left, sel_o_ref[...]).astype(BF16)
    for h in range(HEADS):
        wo[h, :HEAD_DIM] = out_weight[h * HEAD_DIM : (h + 1) * HEAD_DIM]
        wo[h, HEAD_DIM:] = jnp.zeros((LANES - HEAD_DIM, D), BF16)
    for g in range(4):
        part = dot(right, sel_2_ref[g])
        for r in range(blocks):
            start = r * 4 * per_block + g * per_block
            w2[start : start + per_block] = part[r * per_block : (r + 1) * per_block].astype(BF16)

    for h in range(HEADS):
        scores[...] = dot_nt(k_ref[h], q_ref[h])

        def top_step(i, top):
            values = scores[pl.ds(pl.multiple_of(i * 64, 64), 64), :]
            return jnp.maximum(top, jnp.max(values.reshape(8, 8, OWN), 0))

        top = lax.fori_loop(1, SLOTS // 64, top_step, jnp.max(scores[:64].reshape(8, 8, OWN), 0), unroll=True)
        top = jnp.max(top, 0, keepdims=True)

        def soft_step(i, _, h=h, top=top):
            place = pl.ds(pl.multiple_of(i * 128, 128), 128)
            soft_ref[h, place, :] = jnp.exp(scores[place, :] - top).astype(BF16)
            return 0

        lax.fori_loop(0, SLOTS // 128, soft_step, 0, unroll=True)
        raw = dot_tn(soft_ref[h], v_ref[h])
        total = raw[:, HEAD_DIM : HEAD_DIM + 1]
        sums[h] = jnp.broadcast_to(1.0 / total, (OWN, LANES))
        result = raw * sums[h]
        outs[h] = result
        att[h] = result.astype(BF16)

    branch = dot(att[0], wo[0]) + dot(att[1], wo[1]) + dot(att[2], wo[2])
    middle[...] = branch

    def own_mask(block):
        start = pl.multiple_of((block * 2 + core) * rows_slots, rows_slots)
        return widen(mask_ref[pl.ds(start, rows_slots), :])

    def norm_step(block, _):
        place = pl.ds(pl.multiple_of(block * rows_slots, rows_slots), rows_slots)
        mid = own_ref[block, 0].astype(F32) + middle[place, :] * own_mask(block)
        middle[place, :] = mid
        unit, _ = normalise(mid)
        second[place, :] = (unit * gain).astype(BF16)
        return 0

    for block in range(blocks):
        norm_step(block, 0)

    pre[...] = dot(second[...], w1[...])
    cot = jnp.concatenate([own_ref[b, 1] for b in range(blocks)], axis=0)
    grad_hidden[...] = dot_nt(cot, w2[...])

    def gelu_step(i, _):
        place = pl.ds(pl.multiple_of(i * 16, 16), 16)
        x = pre[place, :]
        phi = 0.5 * (1.0 + lax.erf(x * np.float32(0.5**0.5)))
        hidden[place, :] = (x * phi).astype(BF16)
        slope = phi + x * jnp.exp(x * x * -0.5) * np.float32((2 * np.pi) ** -0.5)
        grad_pre[place, :] = (grad_hidden[place, :] * slope).astype(BF16)
        return 0

    lax.fori_loop(0, OWN // 16, gelu_step, 0, unroll=True)

    out_ref[...] = (middle[...] + dot(hidden[...], w2[...])).astype(BF16)
    grad_2 = dot_tn(hidden[...], cot).astype(BF16)
    grad_1 = dot_tn(second[...], grad_pre[...]).astype(BF16)
    grad_middle_ref[...] = dot_nt(grad_pre[...], w1[...])

    def back_step(block, total):
        place = pl.ds(pl.multiple_of(block * rows_slots, rows_slots), rows_slots)
        unit, inverse = normalise(middle[place, :])
        grad = grad_middle_ref[place, :]
        total = total + jnp.sum(grad * unit, 0, keepdims=True)
        grad = own_ref[block, 1].astype(F32) + norm_back(grad, gain, unit, inverse)
        grad_middle_ref[place, :] = grad
        second[place, :] = (grad * own_mask(block)).astype(BF16)
        return total

    gain_two = jnp.zeros((1, D), F32)
    for block in range(blocks):
        gain_two = back_step(block, gain_two)
    gain_ref[...] = gain_two

    grad_o = []
    lane_own = lax.broadcasted_iota(jnp.int32, (OWN, LANES), 1)
    for h in range(HEADS):
        grad_o.append(dot_tn(att[h], second[...])[:HEAD_DIM])
        grad_att = dot_nt(second[...], wo[h]).astype(BF16).astype(F32)
        scaled = (grad_att * sums[h]).astype(BF16).astype(F32)
        shift = -jnp.sum(scaled * outs[h], -1, keepdims=True)
        high = shift.astype(BF16).astype(F32)
        lifted = jnp.where(
            lane_own == HEAD_DIM, high, jnp.where(lane_own == HEAD_DIM + 1, shift - high, scaled)
        )
        lifted_ref[h] = lifted.astype(BF16)

    for half in range(2):
        wire[:, half * span : (half + 1) * span] = dot_nt(
            grad_1[:, half * FF // 2 : (half + 1) * FF // 2], sel_1_ref[...]
        )
    grad_o = jnp.concatenate(grad_o, axis=0).astype(BF16)
    wire[...] += dot_nt(grad_o, sel_o_ref[...])

    def deliver(lanes):
        for m in range(parts):
            parted[m] = wire[:, m * LANES : (m + 1) * LANES].astype(BF16)
        for z in range(parts // 2):
            put_blocks(keep_ref, z, lanes, parted[2 * z + core])
            put_blocks(send_ref, z, lanes, parted[2 * z + 1 - core])

    deliver(slice(0, LANES))
    total = None
    for g in range(4):
        rows = [
            grad_2[r * 4 * per_block + g * per_block : r * 4 * per_block + (g + 1) * per_block]
            for r in range(blocks)
        ]
        part = dot_nt(jnp.concatenate(rows, axis=0), sel_2_ref[g])
        total = part if total is None else total + part
    wire[...] = total
    deliver(slice(LANES, 2 * LANES))


def attention_back_kernel(
    soft_ref,
    lifted_ref,
    q_ref,
    k_ref,
    v_ref,
    scanned_ref,
    wqkv_ref,
    part_ref,
    grad_w_ref,
    scores,
    grad_scores,
    triple,
    grad_q,
    scanned_own,
    part,
    *,
    blocks,
):
    core = lax.axis_index("core")
    rows_slots = OWN // blocks
    for h in range(HEADS):
        tile = slice(h * LANES, (h + 1) * LANES)
        scores[...] = dot_nt(v_ref[h], lifted_ref[h])

        def back_step(i, _, h=h):
            place = pl.ds(pl.multiple_of(i * 64, 64), 64)
            grad_scores[place, :] = (soft_ref[h, place, :].astype(F32) * scores[place, :]).astype(
                BF16
            )
            return 0

        lax.fori_loop(0, SLOTS // 64, back_step, 0, unroll=True)
        grad_q[:, tile] = (dot_tn(grad_scores[...], k_ref[h]).astype(BF16) * HEAD_DIM ** (-0.5)).astype(
            BF16
        )
        triple[0, :, tile] = dot(grad_scores[...], q_ref[h]).astype(BF16)
        triple[1, :, tile] = dot(soft_ref[h], lifted_ref[h]).astype(BF16)

    part[...] = dot_nt(triple[0], wqkv_ref[1]) + dot_nt(triple[1], wqkv_ref[2])
    from_q = dot_nt(grad_q[...], wqkv_ref[0])
    for block in range(blocks):
        here = slice(block * rows_slots, (block + 1) * rows_slots)
        place = pl.ds(pl.multiple_of((block * 2 + core) * rows_slots, rows_slots), rows_slots)
        part[place, :] += from_q[here]
        scanned_own[here, :] = scanned_ref[place, :]
    part_ref[...] = part[...].astype(BF16)
    grad_w_ref[0] = dot_tn(scanned_own[...], grad_q[...]).astype(BF16)
    grad_w_ref[1] = dot_tn(scanned_ref[...], triple[0]).astype(BF16)
    grad_w_ref[2] = dot_tn(scanned_ref[...], triple[1]).astype(BF16)


def scan_back_kernel(
    starts,
    width,
    own_ref,
    mask_ref,
    part_ref,
    got_ref,
    mixed_ref,
    first_ref,
    table_ref,
    rates_ref,
    wu_ref,
    grad_w_ref,
    gain_two_ref,
    sel_u_ref,
    sel_rc_ref,
    sel_q_ref,
    keep_ref,
    send_ref,
    back_ref,
    gs_wide,
    gs_pairs,
    gt_wide,
    gt_pairs,
    xs_wide,
    xs_pairs,
    xt_wide,
    xt_pairs,
    rows_wide,
    rows_pairs,
    cols_wide,
    cols_pairs,
    grads_ref,
    own,
    own_tail,
    together,
    lag_sums,
    lag_rows,
    mixed_back,
    wire,
    parted,
):
    gs, gt = (gs_wide, gs_pairs), (gt_wide, gt_pairs)
    xs, xt = (xs_wide, xs_pairs), (xt_wide, xt_pairs)
    rows, cols = (rows_wide, rows_pairs), (cols_wide, cols_pairs)
    core = lax.axis_index("core")
    blocks, _, rows_slots, _ = own_ref.shape
    half_rows = rows_slots // GRID
    own_rows = GRID // 2
    parts = sel_rc_ref.shape[0] // LANES
    put_columns(*xs, mixed_ref[...].astype(F32))
    grads = (part_ref[...].astype(F32) + got_ref[...].astype(F32)) * widen(mask_ref[...])
    grads = grads.astype(BF16)
    grads_ref[...] = grads
    put_columns(*gs, grads.astype(F32))

    def place_of(block):
        return pl.ds(pl.multiple_of((block * 2 + core) * rows_slots, rows_slots), rows_slots)

    for source, dst in ((grads_ref, gt), (mixed_ref, xt)):
        for block in range(blocks):
            here = slice(block * rows_slots, (block + 1) * rows_slots)
            value = source[place_of(block), :].astype(F32)
            own[here, :] = value[:, :LANES]
            own_tail[here, :] = value[:, LANES:]
        put_rows(*dst, own, own_tail[...], together)

    def row_step(index, _):
        first = index * 8
        for kind, sublane in units(0):
            step = gt[kind].shape[0] // GRID
            total = block_sum(gt, table_ref, 0, kind, first, 8, sublane, -1)
            for t in range(8):
                place = pl.multiple_of((first + t) * step + sublane, 8)
                rows[kind][pl.ds(place, 8), :] = total[t]
        return 0

    lax.fori_loop(0, 4, row_step, 0, unroll=True)

    def col_step(index, _):
        block = index // 2
        first = (block * 2 + core) * half_rows
        for kind, sublane in units(index % 2):
            step = gs[kind].shape[0] // GRID
            total = block_sum(gs, table_ref, 1, kind, first, half_rows, sublane, -1)
            for t in range(half_rows):
                place = pl.multiple_of((block * half_rows + t) * step + sublane, 8)
                cols[kind][pl.ds(place, 8), :] = total[t]
        return 0

    lax.fori_loop(0, blocks * 2, col_step, 0)

    lag_sums[...] = jnp.zeros_like(lag_sums)

    def add_lags(way, kind, first, count, base, gref, xref):
        total = {}
        step = gref[kind].shape[0] // GRID
        for u in range(step // 8):
            g = [
                gref[kind][pl.ds(pl.multiple_of((first + t) * step + u * 8, 8), 8), :]
                for t in range(count)
            ]
            for s in range(8):
                x = xref[kind][pl.ds(pl.multiple_of((base + s) * step + u * 8, 8), 8), :]
                for t in range(count):
                    term = g[t] * x
                    total[t - s] = term if t - s not in total else total[t - s] + term
        for lag, value in total.items():
            at = first - base + (lag + CENTER)
            lag_sums[way, kind, at] += value

    def lag_row_step(index, _):
        for kind in range(2):
            add_lags(0, kind, (index // 4) * 8, 8, (index % 4) * 8, gt, xt)
        return 0

    lax.fori_loop(0, 16, lag_row_step, 0)

    def lag_col_step(index, _):
        first = ((index // 4) * 2 + core) * half_rows
        for kind in range(2):
            add_lags(1, kind, first, half_rows, (index % 4) * 8, gs, xs)
        return 0

    lax.fori_loop(0, blocks * 4, lag_col_step, 0)

    for way in range(2):
        lag_rows[way, :, :LANES] = jnp.sum(lag_sums[way, 0], 1)
        tail = jnp.sum(lag_sums[way, 1], 1)
        tail = tail[:, : D - LANES] + tail[:, D - LANES :]
        lag_rows[way, :, LANES:] = pair_lanes(tail, jnp.zeros_like(tail))

    decay, coef = rates_ref[: 4 * STATE], rates_ref[4 * STATE :]

    def table_step(k, carry):
        to_rate, to_coef = carry
        lag = k.astype(F32)
        powers = jnp.exp(-decay * lag)
        grads = []
        for way in range(2):
            for at in (CENTER + k, CENTER - k):
                grads.append(
                    jnp.broadcast_to(lag_rows[way, pl.ds(at, 1), :], (STATE, 2 * LANES))
                )
        scaled = jnp.concatenate(grads, axis=0) * powers
        return to_rate - lag * scaled, to_coef + scaled

    zero = jnp.zeros((4 * STATE, 2 * LANES), F32)
    to_rate, to_coef = lax.fori_loop(0, GRID, table_step, (zero, zero), unroll=4)
    grad_rc = jnp.concatenate([to_rate * coef, to_coef], axis=0).T[:D].astype(BF16)

    def join_step(i, _):
        for row, value in join_rows(i, own_rows, rows, cols):
            at = ((row // half_rows * 2 + core) * half_rows + row % half_rows) * GRID
            mask = mask_ref[pl.ds(pl.multiple_of(at, GRID), GRID), :]
            place = pl.ds(pl.multiple_of(row * GRID, GRID), GRID)
            mixed_back[place, :] = (value * widen(mask)).astype(BF16)
        return 0

    lax.fori_loop(0, own_rows // 2, join_step, 0, unroll=True)
    grad_u = dot_tn(first_ref[...], mixed_back[...]).astype(BF16)
    grad_first = dot_nt(mixed_back[...], wu_ref[...])
    back_ref[...] = grad_first
    gain_one = jnp.zeros((1, D), F32)
    for block in range(blocks):
        here = slice(block * rows_slots, (block + 1) * rows_slots)
        unit, _ = normalise(own_ref[block, 0].astype(F32))
        gain_one = gain_one + jnp.sum(grad_first[here] * unit, 0, keepdims=True)

    wire[...] = dot_nt(grad_u, sel_u_ref[...]) + dot_nt(grad_rc, sel_rc_ref[...])
    for third in range(3):
        span = slice(starts[third] * LANES, (starts[third] + width) * LANES)
        wire[:, span] += dot_nt(grad_w_ref[third], sel_q_ref[third])
    for m in range(parts):
        parted[m] = wire[:, m * LANES : (m + 1) * LANES].astype(BF16)
    for z in range(parts // 2):
        put_late(keep_ref, z, parted[2 * z + core])
        put_late(send_ref, z, parted[2 * z + 1 - core])

    lines = []
    for value in (gain_one, gain_two_ref[...]):
        high = value.astype(BF16).astype(F32)
        for piece in (high, value - high):
            lines.append(piece[:, :LANES])
            lines.append(
                jnp.concatenate([piece[:, LANES:], jnp.zeros((1, 2 * LANES - D), F32)], axis=1)
            )
    lines = jnp.concatenate(lines, axis=0).astype(BF16)
    for ref in (keep_ref, send_ref):
        ref[ref.shape[0] - 1, :8] = lines
        ref[ref.shape[0] - 1, 8:] = jnp.zeros((ref.shape[1] - 8, LANES), BF16)


def last_norm_kernel(own_ref, gains_ref, back_ref, grad_middle_ref, *routed_refs):
    _, _, slots, _ = own_ref.shape
    gain = gains_ref[0:1, :]
    for k, routed in enumerate(routed_refs):
        block = lax.axis_index("row") ^ k
        place = pl.ds(pl.multiple_of(block * slots, slots), slots)
        unit, inverse = normalise(own_ref[block, 0].astype(F32))
        grad = grad_middle_ref[place, :] + norm_back(back_ref[place, :], gain, unit, inverse)
        routed[...] = pack(grad.astype(BF16))


def aligned(rows):
    return (rows + 15) // 16 * 16


def spare_lanes(rows, parts):
    return rows >= 32 and 4 * (D // parts) + 32 <= LANES


def split(value):
    high = value.astype(BF16).astype(F32)
    return jnp.concatenate([high, value - high], axis=0)


def early_sum_kernel(out_own_ref, keep_ref, got_ref, *out_refs):
    _, depth, rows, _ = keep_ref.shape
    slots = OWN // len(out_refs)
    block_rows = aligned(rows)
    for k, out_ref in enumerate(out_refs):
        block = lax.axis_index("row") ^ k
        for z in range(depth):
            total = keep_ref[block, z].astype(F32) + got_ref[block, z].astype(F32)
            out_ref[z * block_rows : z * block_rows + rows] = total.astype(BF16)
        place = pl.ds(pl.multiple_of(block * slots, slots), slots)
        out_ref[depth * block_rows :] = fold(pack(out_own_ref[place, :]))


def late_sum_kernel(depth, keep_ref, got_ref, *refs):
    count = len(refs) // 2
    routed_refs, out_refs = refs[:count], refs[count:]
    rows = keep_ref.shape[1]
    block_rows = aligned(rows)
    last = keep_ref.shape[0] - 1
    gains = keep_ref[last, :8].astype(F32) + got_ref[last, :8].astype(F32)
    lines = []
    for g in range(2):
        for lane in range(2):
            at = 4 * g + lane
            lines.append(gains[at : at + 1] + gains[at + 2 : at + 3])
    gains = split(jnp.concatenate(lines, axis=0))
    gains = jnp.concatenate([gains, jnp.zeros((8, LANES), F32)], axis=0).astype(BF16)
    for k, out_ref in enumerate(out_refs):
        block = lax.axis_index("row") ^ k
        for z in range(depth):
            at = block * depth + z
            total = keep_ref[at].astype(F32) + got_ref[at].astype(F32)
            out_ref[z * block_rows : z * block_rows + rows] = total.astype(BF16)
        out_ref[depth * block_rows : depth * block_rows + 16] = gains
        out_ref[depth * block_rows + 16 :] = routed_refs[k][...]


def row_sum_kernel(blocks, depth, rows, *refs):
    early_refs, late_refs, out_refs = refs[:blocks], refs[blocks : 2 * blocks], refs[2 * blocks :]
    block_rows = aligned(rows)
    gains = late_refs[0][depth * block_rows : depth * block_rows + 16].astype(F32)
    for k in range(1, blocks):
        gains = gains + late_refs[k][depth * block_rows : depth * block_rows + 16].astype(F32)
    gains = split(gains[:4] + gains[4:8])
    for j, out_ref in enumerate(out_refs):
        z = lax.axis_index("z") ^ j
        place = pl.ds(pl.multiple_of(z * block_rows, 16), block_rows)
        early = early_refs[0][place, :].astype(F32)
        late = late_refs[0][place, :].astype(F32)
        for k in range(1, blocks):
            early = early + early_refs[k][place, :].astype(F32)
            late = late + late_refs[k][place, :].astype(F32)
        if spare_lanes(rows, 2 * depth):
            chunks = [gains[:, q * 32 : (q + 1) * 32] for q in range(4)]
            chunks.append(jnp.zeros((rows - 32, 32), F32))
            early = jnp.concatenate([early[:, :-32], jnp.concatenate(chunks, axis=0)], axis=1)
        else:
            out_ref[rows:, :LANES] = jnp.concatenate(
                [gains, jnp.zeros((8, LANES), F32)], axis=0
            ).astype(BF16)
            out_ref[rows:, LANES:] = jnp.zeros((16, 2 * LANES), BF16)
        out_ref[:rows, LANES:] = early[:rows].astype(BF16)
        out_ref[:rows, :LANES] = late[:rows].astype(BF16)


def final_kernel(parts, *refs):
    final_body(parts, refs[: parts // 2], *refs[parts // 2 :])


def final_body(
    parts,
    got_refs,
    g1_ref,
    g2_ref,
    wu_ref,
    rate_ref,
    coef_ref,
    qkv_ref,
    wo_ref,
    fc1_ref,
    fc2_ref,
):
    a_u, a_r, a_q, (o_u, o_r, o_c, o_q) = late_layout(parts)
    total = got_refs[0][...].astype(F32)
    for ref in got_refs[1:]:
        total = total + ref[...].astype(F32)
    early = total[: fc1_ref.shape[0], LANES:]
    total = total[:, :LANES]
    rows = fc1_ref.shape[0]
    weights = total[:rows]
    if spare_lanes(rows, parts):
        gains = jnp.concatenate(
            [early[q * 8 : (q + 1) * 8, 2 * LANES - 32 :] for q in range(4)], axis=1
        )
    else:
        gains = total[rows:]
    turned = weights.T
    wu_ref[...] = turned[o_u : o_u + a_u]
    rate_ref[...] = turned[o_r : o_r + a_r]
    coef_ref[...] = turned[o_c : o_c + a_r]
    qkv_ref[...] = weights[:, o_q : o_q + a_q]
    gains = gains[0:4] + gains[4:8]
    for g, ref in ((0, g1_ref), (1, g2_ref)):
        ref[...] = jnp.concatenate(
            [gains[2 * g : 2 * g + 1], gains[2 * g + 1 : 2 * g + 2, : D - LANES]], axis=1
        )
    a_1, a_o = FF // parts, D // parts
    fc1_ref[...] = early[:, :a_1]
    wo_ref[...] = early[:, :LANES].T[a_1 : a_1 + a_o]
    turned = early[:, LANES:].T
    fc2_ref[...] = jnp.concatenate([turned[g * a_o : (g + 1) * a_o] for g in range(4)], axis=1)


def per_device(
    patches, valid_mask, norm_gains, w_u, decay_rate, out_coef, w_qkv, w_o, w_fc1, w_fc2, cotangent
):
    images, rows_here, _, _ = patches.shape
    depth, blocks = lax.axis_size("z"), lax.axis_size("row")
    parts = 2 * depth
    rows_slots = rows_here // 2 * GRID
    packed_rows = rows_slots * 3 // 2
    swap = [(0, 1), (1, 0)]
    shape = jax.ShapeDtypeStruct

    def planes(slots):
        return [pltpu.VMEM((slots, LANES), F32), pltpu.VMEM((slots // 2, LANES), F32)]

    def swapped(value):
        return lax.ppermute(value, "core", swap)

    def exchanged(values, axis):
        size = len(values)
        return [values[0]] + [
            lax.ppermute(values[k], axis, [(i, i ^ k) for i in range(size)]) for k in range(1, size)
        ]

    def to_chips(value, j):
        pairs = []
        for home in range(2):
            for source in range(blocks):
                target, image = divmod(source ^ j, images)
                pairs.append((home * blocks + source, target * blocks + home * images + image))
        return lax.ppermute(value, ("core", "row"), pairs)

    starts, width = late_spans(parts)
    sel_1, sel_o, sel_2 = early_selections(parts)

    rows_weight = w_u.shape[0]
    payload = shape((2 * packed_rows + GRID, LANES), BF16)
    shard = shape((rows_weight, 3 * LANES), BF16)
    sources = [value.reshape(images, rows_here * GRID, D) for value in (patches, cotangent)]
    if rows_weight % 16 == 0:
        weights, *routed = pl.pallas_call(
            depart_kernel,
            name="depart",
            out_shape=(shard,) + (payload,) * blocks,
            in_specs=[VMEM] * 10,
            out_specs=[VMEM] * (1 + blocks),
            compiler_params=compiler(LARGE),
        )(
                w_u.T,
            decay_rate.T,
            out_coef.T,
            w_o.T,
            w_fc2.T,
            w_qkv,
            w_fc1,
            *sources,
            valid_mask,
        )
    else:

        def fill(pieces):
            joined = jnp.concatenate(pieces, axis=1)
            return jnp.pad(joined, ((0, 0), (0, LANES - joined.shape[1])))

        weights = jnp.concatenate(
            [
                fill([w_u, decay_rate, out_coef, w_qkv]),
                fill([w_fc1, w_o]),
                fill([w_fc2[g * rows_weight : (g + 1) * rows_weight] for g in range(4)]),
            ],
            axis=1,
        )
        routed = pl.pallas_call(
            route_kernel,
            name="route",
            out_shape=(payload,) * blocks,
            in_specs=[VMEM] * 3,
            out_specs=[VMEM] * blocks,
            compiler_params=compiler(LARGE),
        )(*sources, valid_mask)

    weights = jnp.stack(exchanged([weights] * depth, "z"))
    weights = exchanged([weights] * blocks, "row")
    weights = weights + [swapped(value) for value in weights]
    routed = [to_chips(value, j) for j, value in enumerate(routed)]
    own, first_own, mask, sel_u, sel_rc, sel_q = pl.pallas_call(
        lambda *refs: norm_kernel(starts, parts, *refs),
        name="first_norm",
        out_shape=(
            shape((blocks, 2, rows_slots, D), BF16),
            shape((OWN, D), BF16),
            shape((SLOTS, LANES), F32),
            shape((parts * LANES, D), BF16),
            shape((parts * LANES, LANES), BF16),
            shape((3, width * LANES, TILE), BF16),
        ),
        in_specs=[VMEM] * (1 + blocks),
        out_specs=[VMEM] * 6,
        compiler_params=compiler(8 << 20),
    )(norm_gains, *routed)
    first_other = swapped(first_own)

    head_own = shape((HEADS, OWN, LANES), BF16)
    head_all = shape((HEADS, SLOTS, LANES), BF16)
    part_scratch = pltpu.VMEM((parts, blocks, rows_weight, LANES), BF16)
    q, k, v, scanned, mixed, table, rates, wu, wqkv = pl.pallas_call(
        lambda *refs: scan_kernel(starts, width, *refs, blocks=blocks),
        name="scan_forward",
        out_shape=(
            head_own,
            head_all,
            head_all,
            shape((SLOTS, D), BF16),
            shape((SLOTS, D), BF16),
            shape((2, 2, LAGS, 8, LANES), F32),
            shape((LANES, 2 * LANES), F32),
            shape((D, D), BF16),
            shape((3, D, TILE), BF16),
        ),
        in_specs=[VMEM] * (6 + 2 * blocks),
        out_specs=[VMEM] * 9,
        scratch_shapes=[part_scratch]
        + planes(SLOTS) * 4
        + [pltpu.VMEM((OWN, D), BF16), pltpu.VMEM((SLOTS, D), BF16)],
        compiler_params=compiler(),
    )(first_own, first_other, mask, sel_u, sel_rc, sel_q, *weights)

    wire_early = shape((blocks, depth, rows_weight, 2 * LANES), BF16)
    soft, lifted, out_own, grad_middle, gain_two, early_keep, early_send = pl.pallas_call(
        middle_kernel,
        name="attention_and_feed_forward",
        out_shape=(
            shape((HEADS, SLOTS, OWN), BF16),
            head_own,
            shape((OWN, D), BF16),
            shape((OWN, D), F32),
            shape((1, D), F32),
            wire_early,
            wire_early,
        ),
        in_specs=[VMEM] * (9 + 2 * blocks),
        out_specs=[VMEM] * 7,
        scratch_shapes=[
            part_scratch,
            pltpu.VMEM((SLOTS, OWN), F32),
            pltpu.VMEM((HEADS, LANES, D), BF16),
            pltpu.VMEM((D, FF), BF16),
            pltpu.VMEM((FF, D), BF16),
            pltpu.VMEM((HEADS, OWN, LANES), BF16),
            pltpu.VMEM((HEADS, OWN, LANES), F32),
            pltpu.VMEM((HEADS, OWN, LANES), F32),
            pltpu.VMEM((OWN, D), F32),
            pltpu.VMEM((OWN, D), BF16),
            pltpu.VMEM((OWN, FF), F32),
            pltpu.VMEM((OWN, FF), F32),
            pltpu.VMEM((OWN, FF), BF16),
            pltpu.VMEM((OWN, FF), BF16),
            pltpu.VMEM((D, parts * LANES), F32),
            pltpu.VMEM((parts, D, LANES), BF16),
        ],
        compiler_params=compiler(),
    )(own, mask, norm_gains, sel_1, sel_o, sel_2, q, k, v, *weights)

    early_recv = swapped(early_send)

    part, grad_w = pl.pallas_call(
        lambda *refs: attention_back_kernel(*refs, blocks=blocks),
        name="attention_backward",
        out_shape=(shape((SLOTS, D), BF16), shape((3, D, TILE), BF16)),
        in_specs=[VMEM] * 7,
        out_specs=[VMEM] * 2,
        scratch_shapes=[
            pltpu.VMEM((SLOTS, OWN), F32),
            pltpu.VMEM((SLOTS, OWN), BF16),
            pltpu.VMEM((2, SLOTS, TILE), BF16),
            pltpu.VMEM((OWN, TILE), BF16),
            pltpu.VMEM((OWN, D), BF16),
            pltpu.VMEM((SLOTS, D), F32),
        ],
        compiler_params=compiler(),
    )(soft, lifted, q, k, v, scanned, wqkv)

    early_keep, early_recv, part = lax.optimization_barrier((early_keep, early_recv, part))
    payload = shape((depth * aligned(rows_weight) + packed_rows // 2, 2 * LANES), BF16)
    early = pl.pallas_call(
        early_sum_kernel,
        name="early_sum",
        out_shape=(payload,) * blocks,
        in_specs=[VMEM] * 3,
        out_specs=[VMEM] * blocks,
        compiler_params=compiler(8 << 20),
    )(out_own, early_keep, early_recv)
    early, part = lax.optimization_barrier((early, part))
    part_got = swapped(part)
    early = exchanged(early, "row")
    wire_late = shape((blocks * depth + 1, rows_weight, LANES), BF16)
    late_keep, late_send, back = pl.pallas_call(
        lambda *refs: scan_back_kernel(starts, width, *refs),
        name="scan_backward",
        out_shape=(wire_late, wire_late, shape((OWN, D), F32)),
        in_specs=[VMEM] * 14,
        out_specs=[VMEM] * 3,
        scratch_shapes=planes(SLOTS) + planes(OWN) + planes(SLOTS) + planes(OWN) * 3
        + [
            pltpu.VMEM((SLOTS, D), BF16),
            pltpu.VMEM((OWN, LANES), F32),
            pltpu.VMEM((OWN, D - LANES), F32),
            pltpu.VMEM((OWN // 2, LANES), F32),
            pltpu.VMEM((2, 2, LAGS, 8, LANES), F32),
            pltpu.VMEM((2, LAGS, 2 * LANES), F32),
            pltpu.VMEM((OWN, D), BF16),
            pltpu.VMEM((D, parts * LANES), F32),
            pltpu.VMEM((parts, D, LANES), BF16),
        ],
        compiler_params=compiler(),
    )(
        own,
        mask,
        part,
        part_got,
        mixed,
        first_own,
        table,
        rates,
        wu,
        grad_w,
        gain_two,
        sel_u,
        sel_rc,
        sel_q,
    )
    late_keep, late_send, early = lax.optimization_barrier((late_keep, late_send, early))
    payload = shape((packed_rows, LANES), BF16)
    routed = pl.pallas_call(
        last_norm_kernel,
        name="last_norm",
        out_shape=(payload,) * blocks,
        in_specs=[VMEM] * 4,
        out_specs=[VMEM] * blocks,
        compiler_params=compiler(8 << 20),
    )(own, norm_gains, back, grad_middle)
    payload = shape((depth * aligned(rows_weight) + 16 + packed_rows, LANES), BF16)
    late = pl.pallas_call(
        lambda *refs: late_sum_kernel(depth, *refs),
        name="late_sum",
        out_shape=(payload,) * blocks,
        in_specs=[VMEM] * (2 + blocks),
        out_specs=[VMEM] * blocks,
        compiler_params=compiler(8 << 20),
    )(late_keep, swapped(late_send), *routed)
    late = exchanged(late, "row")
    final_rows = rows_weight if spare_lanes(rows_weight, parts) else rows_weight + 16
    summed = pl.pallas_call(
        lambda *refs: row_sum_kernel(blocks, depth, rows_weight, *refs),
        name="row_sum",
        out_shape=(shape((final_rows, 3 * LANES), BF16),) * depth,
        in_specs=[VMEM] * (2 * blocks),
        out_specs=[VMEM] * depth,
        compiler_params=compiler(8 << 20),
    )(*early, *late)
    summed = exchanged(summed, "z")

    chosen = pl.pallas_call(
        choose_kernel,
        name="choose",
        out_shape=shape((images, 2 * packed_rows, LANES), BF16),
        in_specs=[VMEM] * (2 * blocks),
        out_specs=VMEM,
        compiler_params=compiler(8 << 20),
    )(*early, *late)
    whole = shape((images, rows_here * GRID, D), BF16)
    block_out, grad_patches = pl.pallas_call(
        home_kernel,
        name="home",
        out_shape=(whole, whole),
        in_specs=[VMEM] * (1 + 2 * blocks),
        out_specs=[VMEM] * 2,
        compiler_params=compiler(8 << 20),
    )(swapped(chosen), *early, *late)

    summed, block_out, grad_patches = lax.optimization_barrier((summed, block_out, grad_patches))
    turned = (4 * STATE // parts, rows_weight)
    g1, g2, f_u, f_rate, f_coef, f_qkv, f_o, f_1, f_2 = pl.pallas_call(
        lambda *refs: final_kernel(parts, *refs),
        name="final_sum",
        out_shape=(
            shape((1, D), F32),
            shape((1, D), F32),
            shape((D // parts, rows_weight), F32),
            shape(turned, F32),
            shape(turned, F32),
            shape((rows_weight, 3 * D // parts), F32),
            shape((D // parts, rows_weight), F32),
            shape((rows_weight, FF // parts), F32),
            shape((D // parts, 4 * rows_weight), F32),
        ),
        in_specs=[VMEM] * depth,
        out_specs=[VMEM] * 9,
        compiler_params=compiler(8 << 20),
    )(*summed)
    return (
        block_out.reshape(patches.shape),
        grad_patches.reshape(patches.shape),
        g1.reshape(D),
        g2.reshape(D),
        f_u.T,
        f_rate.T,
        f_coef.T,
        f_qkv,
        f_o.T,
        f_1,
        f_2.T,
    )


def solution(mesh):
    images, rows = mesh.devices.shape
    fine = Mesh(mesh.devices.reshape(images // 2, 2, rows), ("z", "core", "row"))
    img = ("z", "core")
    grid = P(img, "row", None, None)
    weight = P("row", img)
    in_specs = (grid, P(img, None, None), P()) + (weight,) * 7 + (grid,)
    out_specs = (grid, grid, P(), P()) + (weight,) * 7
    return jax.shard_map(
        per_device, mesh=fine, in_specs=in_specs, out_specs=out_specs, check_vma=False
    )
```

```python
import jax
import jax.numpy as jnp
import numpy as np
from jax import lax
from jax.experimental import pallas as pl
from jax.experimental.pallas import tpu as pltpu
from jax.sharding import Mesh
from jax.sharding import PartitionSpec as P

HEADS = 3
HEAD_DIM = 64
STATE = 16
GRID = 32
SLOTS = GRID * GRID
OWN = SLOTS // 2
D = HEADS * HEAD_DIM
FF = 4 * D
LANES = 128
TILE = HEADS * LANES
LAGS = 2 * GRID
CENTER = GRID - 1
EPS = 1e-05
BF16 = jnp.bfloat16
F32 = jnp.float32


def late_layout(parts):
    a_u, a_r, a_q = D // parts, 4 * STATE // parts, 3 * D // parts
    return a_u, a_r, a_q, (0, a_u, a_u + a_r, a_u + 2 * a_r)


def late_spans(parts):
    a_q = 3 * D // parts
    first = [third * D // a_q for third in range(3)]
    last = [((third + 1) * D - 1) // a_q for third in range(3)]
    width = max(stop - start + 1 for start, stop in zip(first, last))
    return [min(start, parts - width) for start in first], width


def early_selections(parts):
    a_1, a_o = FF // parts, D // parts
    half = parts // 2
    sel_1 = np.zeros((half, LANES, FF // 2), np.float32)
    sel_o = np.zeros((parts, LANES, D), np.float32)
    sel_2 = np.zeros((4, parts, LANES, D), np.float32)
    for m in range(half):
        for col in range(a_1):
            sel_1[m, col, m * a_1 + col] = 1
    for m in range(parts):
        for col in range(a_o):
            sel_o[m, a_1 + col, m * a_o + col] = 1
            for g in range(4):
                sel_2[g, m, g * a_o + col, m * a_o + col] = 1
    return (
        sel_1.reshape(half * LANES, FF // 2).astype(BF16),
        sel_o.reshape(parts * LANES, D).astype(BF16),
        sel_2.reshape(4, parts * LANES, D).astype(BF16),
    )


def lane_and_part(shape):
    place = lax.broadcasted_iota(jnp.int32, shape, 0)
    return place % LANES, place // LANES, lax.broadcasted_iota(jnp.int32, shape, 1)


def put_late_selections(starts, parts, sel_u_ref, sel_rc_ref, sel_q_ref):
    a_u, a_r, a_q, (o_u, o_r, o_c, o_q) = late_layout(parts)

    def put(hit):
        return jnp.where(hit, 1.0, 0.0).astype(BF16)

    lane, part, col = lane_and_part(sel_u_ref.shape)
    sel_u_ref[...] = put((lane < a_u) & (part * a_u + lane == col))
    lane, part, col = lane_and_part(sel_rc_ref.shape)
    rate = (lane >= o_r) & (lane < o_c) & (part * a_r + lane - o_r == col)
    coef = (lane >= o_c) & (lane < o_q) & (part * a_r + lane - o_c + 4 * STATE == col)
    sel_rc_ref[...] = put(rate | coef)
    lane, part, col = lane_and_part(sel_q_ref.shape[1:])
    whole = jnp.where(
        col % LANES < HEAD_DIM, col // LANES * HEAD_DIM + col % LANES, -4 * D
    )
    for third in range(3):
        here = (part + starts[third]) * a_q + lane - o_q - third * D
        sel_q_ref[third] = put((lane >= o_q) & (lane < o_q + a_q) & (here == whole))


def dot(a, b):
    return lax.dot_general(a, b, (((1,), (0,)), ((), ())), preferred_element_type=F32)


def dot_nt(a, b):
    return lax.dot_general(a, b, (((1,), (1,)), ((), ())), preferred_element_type=F32)


def dot_tn(a, b):
    return lax.dot_general(a, b, (((0,), (0,)), ((), ())), preferred_element_type=F32)


def normalise(values):
    center = values - jnp.mean(values, -1, keepdims=True)
    spread = jnp.mean(center * center, -1, keepdims=True)
    inverse = lax.rsqrt(spread + EPS)
    return center * inverse, inverse


def norm_back(grad, gain, unit, inverse):
    scaled = grad * gain
    first = jnp.mean(scaled, -1, keepdims=True)
    second = jnp.mean(scaled * unit, -1, keepdims=True)
    return inverse * (scaled - first - unit * second)


def widen(mask):
    return jnp.concatenate([mask, mask[:, : D - LANES]], axis=1)


def put_blocks(ref, z, lanes, value):
    rows = ref.shape[2]
    for r in range(ref.shape[0]):
        ref[r, z, :, lanes] = value[r * rows : (r + 1) * rows]


def put_late(ref, z, value):
    rows = ref.shape[1]
    depth = ref.shape[0] * rows // D
    for r in range(D // rows):
        ref[r * depth + z] = value[r * rows : (r + 1) * rows]


def pair_lanes(first, second):
    return jnp.concatenate([first, second], axis=1)


def put_columns(wide, pairs, values):
    wide[...] = values[:, :LANES]
    tail = values[:, LANES:].reshape(values.shape[0] // GRID, 2, GRID // 2, D - LANES)
    tail = pair_lanes(tail[:, 0].reshape(-1, D - LANES), tail[:, 1].reshape(-1, D - LANES))
    pairs[...] = tail


def put_rows(wide, pairs, from_wide, tail, together):
    rows = from_wide.shape[0] // GRID
    together[...] = pair_lanes(tail[: rows // 2 * GRID], tail[rows // 2 * GRID :])
    for j in range(GRID):
        wide[j * rows : (j + 1) * rows, :] = from_wide[pl.ds(j, rows, stride=GRID), :]
        pairs[j * rows // 2 : (j + 1) * rows // 2, :] = together[pl.ds(j, rows // 2, stride=GRID), :]


def units(index):
    return [(0, (index * 2 + u) * 8) for u in range(2)] + [(1, index * 8)]


def lag_tables(lags):
    lines = []
    near = lags[16:47]
    for table in (near, lags[0:31] - near, lags[32:63] - near):
        center = table[8:23]
        for part in (center, table[0:15] - center, table[16:31] - center):
            lines += [part, jnp.zeros((1, LANES), F32)]
    return jnp.concatenate(lines, axis=0)


def plus(left, right):
    return [a + b for a, b in zip(left, right)]


def own_places(own_rows):
    if own_rows is None:
        return list(range(8)), 0
    places = [i // own_rows * 2 * own_rows + i % own_rows for i in range(4)]
    return places, lax.axis_index("core") * own_rows


def three(left, right, work):
    a, b = len(left) // 2, len(right) // 2
    work(0, plus(left[:a], left[a:]), plus(right[:b], right[b:]))
    work(1, left[:a], right[b:])
    work(2, left[a:], right[:b])


def add_lags(sums, way, kind, sublane, grads, values, own_rows=None):
    step = values[kind].shape[0] // GRID
    places, shift = own_places(own_rows)

    def line(ref, at):
        return ref[kind][pl.ds(pl.multiple_of(at * step + sublane, 8), 8), :]

    g = [line(grads, base + place + shift) for base in range(0, GRID, 8) for place in places]
    x = [line(values, s) for s in range(GRID)]

    def leaf(first, second, g, x):
        total = {}
        for i, t in enumerate(places):
            for s in range(8):
                term = g[i] * x[s]
                total[t - s] = term if t - s not in total else total[t - s] + term
        start = (first * 3 + second) * 16 + 7
        for lag, value in total.items():
            sums[way, kind, start + lag + shift] += value

    three(g, x, lambda p, g, x: three(g, x, lambda q, g, x: leaf(p, q, g, x)))


def gather_lags(sums, way, kind):
    def join(parts, reach):
        found = [None] * (2 * (2 * reach + 1) + 1)
        width = 2 * reach - 1
        middle = [a - b - c for a, b, c in zip(*parts)]
        for start, part in ((reach, middle), (0, parts[1]), (2 * reach, parts[2])):
            for i in range(width):
                at = start + i
                found[at] = part[i] if found[at] is None else found[at] + part[i]
        return found[: 4 * reach - 1]

    thirds = []
    for first in range(3):
        tables = [
            [sums[way, kind, (first * 3 + second) * 16 + i] for i in range(15)]
            for second in range(3)
        ]
        thirds.append(join(tables, 8))
    return join(thirds, 16)


def toeplitz(src, table, way, kind, sublane, sign, own_rows=None):
    step = src[kind].shape[0] // GRID
    places, shift = own_places(own_rows)
    shift = shift * sign

    def leaf(x, first, second):
        if sign < 0:
            first, second = (0, 2, 1)[first], (0, 2, 1)[second]
        start = (first * 3 + second) * 16 + 7
        coef = {}
        total = [None] * len(places)
        for s in range(8):
            for i, t in enumerate(places):
                lag = t - s
                if lag not in coef:
                    line = table[way, kind, pl.ds(start + lag * sign + shift, 1), :]
                    coef[lag] = jnp.broadcast_to(line, (8, LANES))
                term = coef[lag] * x[s]
                total[i] = term if total[i] is None else total[i] + term
        return total

    def quarter(x, first):
        middle = leaf(plus(x[:8], x[8:]), first, 0)
        return plus(middle, leaf(x[8:], first, 1)) + plus(middle, leaf(x[:8], first, 2))

    x = [src[kind][pl.ds(pl.multiple_of(s * step + sublane, 8), 8), :] for s in range(GRID)]
    middle = quarter(plus(x[:16], x[16:]), 0)
    return plus(middle, quarter(x[16:], 1)) + plus(middle, quarter(x[:16], 2))


def join_rows(i, count, rows, cols):
    half = GRID // 2
    narrow = D - LANES
    across = rows[1][pl.ds(i, GRID, stride=count // 2), :]
    found = []
    for which in range(2):
        row = i + which * (count // 2)
        wide = cols[0][pl.ds(pl.multiple_of(row * GRID, GRID), GRID), :].astype(BF16).astype(F32)
        wide = wide + rows[0][pl.ds(i + which * (count // 2), GRID, stride=count), :]
        pairs = cols[1][pl.ds(pl.multiple_of(row * half, half), half), :].astype(BF16).astype(F32)
        tail = jnp.concatenate([pairs[:, :narrow], pairs[:, narrow:]], axis=0)
        tail = tail + across[:, which * narrow : (which + 1) * narrow]
        found.append((row, jnp.concatenate([wide, tail], axis=1)))
    return found


def gather_parts(mine_refs, got_refs, block, out_ref):
    core, row, depth = lax.axis_index("core"), lax.axis_index("row"), lax.axis_index("z")
    lanes = slice(block * LANES, (block + 1) * LANES)
    count = out_ref.shape[0] // 2
    rows = out_ref.shape[2]
    for refs, which in ((mine_refs, core), (got_refs, 1 - core)):
        for k, ref in enumerate(refs):
            for j in range(count):
                out_ref[2 * (depth ^ j) + which, row ^ k] = ref[j, :, lanes]
    wide = []
    for m in range(2 * count):
        wide.append(jnp.concatenate([out_ref[m, r] for r in range(out_ref.shape[1])], axis=0))
    return jnp.concatenate(wide, axis=1)


LARGE = 60 << 20


def compiler(limit=24 << 20):
    return pltpu.CompilerParams(vmem_limit_bytes=limit)


VMEM = pl.BlockSpec(memory_space=pltpu.VMEM)


def pack(values):
    half = values.shape[0] // 2
    tail = jnp.concatenate([values[:half, LANES:], values[half:, LANES:]], axis=1)
    return jnp.concatenate([values[:, :LANES], tail], axis=0)


def unpack(packed):
    count = packed.shape[0] * 2 // 3
    tail = packed[count:]
    tail = jnp.concatenate([tail[:, : D - LANES], tail[:, D - LANES :]], axis=0)
    return jnp.concatenate([packed[:count], tail], axis=1)


def pack_weights_kernel(turned_refs, qkv_ref, fc1_ref, out_ref):
    wu, rate, coef, wo, fc2 = [ref[...].astype(F32) for ref in turned_refs]
    rows = qkv_ref.shape[0]
    a_o, a_r = wo.shape[0], rate.shape[0]
    pieces = [wu, rate, coef, wo] + [fc2[:, g * rows : (g + 1) * rows] for g in range(4)]
    joined = jnp.concatenate(pieces, axis=0)
    joined = jnp.concatenate([joined, jnp.zeros((joined.shape[0], LANES - rows), F32)], axis=1)
    joined = joined.T[:rows]
    first, second = a_o + 2 * a_r, 2 * a_o + 2 * a_r

    def fill(parts):
        used = sum(part.shape[1] for part in parts)
        return parts + [jnp.zeros((rows, LANES - used), F32)]

    packed = jnp.concatenate(
        fill([joined[:, :first], qkv_ref[...].astype(F32)])
        + fill([fc1_ref[...].astype(F32), joined[:, first:second]])
        + fill([joined[:, second:]]),
        axis=1,
    ).astype(BF16)
    out_ref[...] = packed


def route_kernel(patch_ref, cot_ref, valid_ref, *out_refs):
    row = lax.axis_index("row")
    images, slots, _ = patch_ref.shape
    half = slots // 2
    packed = half * 3 // 2
    for j, out_ref in enumerate(out_refs):
        target = row ^ j
        core, image = target // images, target % images
        place = pl.ds(pl.multiple_of(core * half, half), half)
        out_ref[:packed] = pack(patch_ref[image, place, :])
        out_ref[packed : 2 * packed] = pack(cot_ref[image, place, :])
        valid = valid_ref[image].astype(F32).astype(BF16)
        out_ref[2 * packed :] = jnp.concatenate(
            [valid, jnp.zeros((GRID, LANES - GRID), BF16)], axis=1
        )


def depart_kernel(*refs):
    turned, (qkv_ref, fc1_ref, patch_ref, cot_ref, valid_ref, out_ref) = refs[:5], refs[5:11]
    pack_weights_kernel(turned, qkv_ref, fc1_ref, out_ref)
    route_kernel(patch_ref, cot_ref, valid_ref, *refs[11:])


def norm_kernel(starts, parts, gains_ref, *refs):
    got_refs, refs = refs[:-6], refs[-6:]
    own_ref, first_ref, mask_ref, *selections = refs
    core, row = lax.axis_index("core"), lax.axis_index("row")
    images = len(got_refs) // 2
    gain = gains_ref[0:1, :]
    slots = own_ref.shape[2]
    packed = slots * 3 // 2
    for j, got in enumerate(got_refs):
        block = (core * images + row % images) ^ j
        patch = unpack(got[:packed])
        own_ref[block, 0] = patch
        own_ref[block, 1] = unpack(got[packed : 2 * packed])
        unit, _ = normalise(patch.astype(F32))
        first_ref[pl.ds(pl.multiple_of(block * slots, slots), slots), :] = (unit * gain).astype(
            BF16
        )
    valid = got_refs[0][2 * packed :].astype(F32).T
    for i in range(GRID):
        mask_ref[i * GRID : (i + 1) * GRID, :] = jnp.broadcast_to(
            valid[:GRID, i : i + 1], (GRID, LANES)
        )
    put_late_selections(starts, parts, *selections)


def fold(packed):
    half = packed.shape[0] // 2
    return jnp.concatenate([packed[:half], packed[half:]], axis=1)


def unfold(folded):
    return jnp.concatenate([folded[:, :LANES], folded[:, LANES:]], axis=0)


def results_of(early_ref, late_ref, rows):
    early_start, late_start = early_ref.shape[0] - rows // 2, late_ref.shape[0] - rows
    return unfold(early_ref[early_start:]), late_ref[late_start:]


def choose_kernel(*refs):
    got_refs, out_ref = refs[:-1], refs[-1]
    blocks = len(got_refs) // 2
    core, row = lax.axis_index("core"), lax.axis_index("row")
    images, rows = out_ref.shape[0], out_ref.shape[1] // 2
    for k, got in enumerate(zip(got_refs[:blocks], got_refs[blocks:])):
        image = row ^ k

        @pl.when(image // images != core)
        def _(got=got, image=image):
            for which, value in enumerate(results_of(*got, rows)):
                out_ref[image % images, which * rows : (which + 1) * rows] = value


def home_kernel(swapped_ref, *refs):
    got_refs, out_refs = refs[:-2], refs[-2:]
    core, row = lax.axis_index("core"), lax.axis_index("row")
    images, slots, _ = out_refs[0].shape
    half = slots // 2
    rows = half * 3 // 2
    blocks = len(got_refs) // 2
    mine = pl.ds(pl.multiple_of(core * half, half), half)
    theirs = pl.ds(pl.multiple_of((1 - core) * half, half), half)
    for k, got in enumerate(zip(got_refs[:blocks], got_refs[blocks:])):
        image = row ^ k

        @pl.when(image // images == core)
        def _(got=got, image=image):
            for out_ref, value in zip(out_refs, results_of(*got, rows)):
                out_ref[image % images, mine, :] = unpack(value)

    for image in range(images):
        for which, out_ref in enumerate(out_refs):
            value = swapped_ref[image, which * rows : (which + 1) * rows]
            out_ref[image, theirs, :] = unpack(value)


def scan_kernel(
    starts,
    width,
    first_own_ref,
    first_other_ref,
    mask_ref,
    sel_u_ref,
    sel_rc_ref,
    sel_q_ref,
    *refs,
    blocks,
):
    mine_refs, got_refs, refs = refs[:blocks], refs[blocks : 2 * blocks], refs[2 * blocks :]
    scan_body(
        starts,
        width,
        first_own_ref,
        first_other_ref,
        mask_ref,
        sel_u_ref,
        sel_rc_ref,
        sel_q_ref,
        mine_refs,
        got_refs,
        *refs,
    )


def scan_body(
    starts,
    width,
    first_own_ref,
    first_other_ref,
    mask_ref,
    sel_u_ref,
    sel_rc_ref,
    sel_q_ref,
    mine_refs,
    got_refs,
    q_ref,
    k_ref,
    v_ref,
    scanned_ref,
    mixed_ref,
    table_ref,
    rates_ref,
    wu_ref,
    wqkv_ref,
    late_ref,
    xs_wide,
    xs_pairs,
    xt_wide,
    xt_pairs,
    cols_wide,
    cols_pairs,
    rows_wide,
    rows_pairs,
    scanned_own,
    first_ref,
    lags,
):
    xs, xt = (xs_wide, xs_pairs), (xt_wide, xt_pairs)
    cols, rows = (cols_wide, cols_pairs), (rows_wide, rows_pairs)
    core = lax.axis_index("core")
    blocks = len(mine_refs)
    rows_slots = OWN // blocks

    late = gather_parts(mine_refs, got_refs, 0, late_ref)
    wu = dot(late, sel_u_ref[...]).astype(BF16)
    wu_ref[...] = wu
    rates = dot(late, sel_rc_ref[...])
    rates = jnp.concatenate([rates.T, jnp.zeros((LANES, 2 * LANES - D), F32)], axis=1)
    rates_ref[...] = rates
    for third in range(3):
        window = late[:, starts[third] * LANES : (starts[third] + width) * LANES]
        wqkv_ref[third] = dot(window, sel_q_ref[third]).astype(BF16)

    decay, coef = rates[: 4 * STATE], rates[4 * STATE :]

    def lag_row(k):
        powers = jnp.exp(-decay * k) * coef
        return [jnp.sum(powers[d * STATE : (d + 1) * STATE], 0, keepdims=True) for d in range(4)]

    def store_lag(way, lag, row):
        row = row.astype(BF16).astype(F32)
        tail = row[:, LANES:D]
        for kind, lanes in enumerate((row[:, :LANES], pair_lanes(tail, tail))):
            lags[way, kind, pl.ds(lag + CENTER, 1), :] = lanes

    def lag_step(k, _):
        found = lag_row(k.astype(F32))
        for way in range(2):
            store_lag(way, k, found[2 * way])
            store_lag(way, -k, found[2 * way + 1])
        return 0

    lax.fori_loop(0, GRID, lag_step, 0, unroll=True)
    found = lag_row(0.0)
    for way in range(2):
        store_lag(way, 0, found[2 * way] + found[2 * way + 1])
        for kind in range(2):
            table_ref[way, kind] = lag_tables(lags[way, kind])


    for block in range(blocks):
        here = slice(block * rows_slots, (block + 1) * rows_slots)
        for ref, which in ((first_own_ref, core), (first_other_ref, 1 - core)):
            start = pl.multiple_of((block * 2 + which) * rows_slots, rows_slots)
            first_ref[pl.ds(start, rows_slots), :] = ref[here, :]
    mixed = dot(first_ref[...], wu) * widen(mask_ref[...])
    mixed = mixed.astype(BF16)
    mixed_ref[...] = mixed
    mixed = mixed.astype(F32)
    put_columns(*xs, mixed)
    put_rows(*xt, xs[0], mixed[:, LANES:], cols[1])

    def scan_step(index, _):
        for way, src, dst in ((0, xt, rows), (1, xs, cols)):
            for kind, sublane in units(index):
                step = src[kind].shape[0] // GRID
                for t, value in enumerate(toeplitz(src, table_ref, way, kind, sublane, 1)):
                    dst[kind][pl.ds(pl.multiple_of(t * step + sublane, 8), 8), :] = value
        return 0

    lax.fori_loop(0, 2, scan_step, 0, unroll=True)

    def join_step(i, _):
        for row, value in join_rows(i, GRID, rows, cols):
            place = pl.ds(pl.multiple_of(row * GRID, GRID), GRID)
            scanned_ref[place, :] = (value * widen(mask_ref[place, :])).astype(BF16)
        return 0

    lax.fori_loop(0, GRID // 2, join_step, 0, unroll=True)

    for block in range(blocks):
        start = pl.multiple_of((block * 2 + core) * rows_slots, rows_slots)
        scanned_own[block * rows_slots : (block + 1) * rows_slots, :] = scanned_ref[
            pl.ds(start, rows_slots), :
        ]

    lane_own = lax.broadcasted_iota(jnp.int32, (OWN, LANES), 1)
    lane_all = lax.broadcasted_iota(jnp.int32, (SLOTS, LANES), 1)
    bias = jnp.where(lane_all == HEAD_DIM, (mask_ref[...] - 1.0) * 1e30, 0.0)
    ones = jnp.where((lane_all == HEAD_DIM) | (lane_all == HEAD_DIM + 1), 1.0, 0.0)
    one_own = jnp.where(lane_own == HEAD_DIM, 1.0, 0.0)
    for h in range(HEADS):
        tile = slice(h * LANES, (h + 1) * LANES)
        q_ref[h] = (
            dot(scanned_own[...], wqkv_ref[0, :, tile]) * HEAD_DIM ** (-0.5) + one_own
        ).astype(BF16)
        k_ref[h] = (dot(scanned_ref[...], wqkv_ref[1, :, tile]) + bias).astype(BF16)
        v_ref[h] = (dot(scanned_ref[...], wqkv_ref[2, :, tile]) + ones).astype(BF16)


def middle_kernel(
    own_ref,
    mask_ref,
    gains_ref,
    sel_1_ref,
    sel_o_ref,
    sel_2_ref,
    q_ref,
    k_ref,
    v_ref,
    *refs,
):
    blocks = own_ref.shape[0]
    middle_body(
        own_ref,
        mask_ref,
        gains_ref,
        sel_1_ref,
        sel_o_ref,
        sel_2_ref,
        q_ref,
        k_ref,
        v_ref,
        refs[:blocks],
        refs[blocks : 2 * blocks],
        *refs[2 * blocks :],
    )


def middle_body(
    own_ref,
    mask_ref,
    gains_ref,
    sel_1_ref,
    sel_o_ref,
    sel_2_ref,
    q_ref,
    k_ref,
    v_ref,
    mine_refs,
    got_refs,
    soft_ref,
    lifted_ref,
    out_ref,
    grad_middle_ref,
    gain_ref,
    keep_ref,
    send_ref,
    early_ref,
    scores,
    wo,
    w1,
    w2,
    att,
    outs,
    sums,
    middle,
    second,
    pre,
    grad_hidden,
    hidden,
    grad_pre,
    wire,
    parted,
):
    core = lax.axis_index("core")
    blocks, _, rows_slots, _ = own_ref.shape
    parts = early_ref.shape[0]
    per_block = D // blocks
    gain = gains_ref[1:2, :]

    left = gather_parts(mine_refs, got_refs, 1, early_ref)
    right = gather_parts(mine_refs, got_refs, 2, early_ref)
    span = parts // 2 * LANES
    for half in range(2):
        w1[:, half * FF // 2 : (half + 1) * FF // 2] = dot(
            left[:, half * span : (half + 1) * span], sel_1_ref[...]
        ).astype(BF16)
    out_weight = dot(left, sel_o_ref[...]).astype(BF16)
    for h in range(HEADS):
        wo[h, :HEAD_DIM] = out_weight[h * HEAD_DIM : (h + 1) * HEAD_DIM]
        wo[h, HEAD_DIM:] = jnp.zeros((LANES - HEAD_DIM, D), BF16)
    for g in range(4):
        part = dot(right, sel_2_ref[g])
        for r in range(blocks):
            start = r * 4 * per_block + g * per_block
            w2[start : start + per_block] = part[r * per_block : (r + 1) * per_block].astype(BF16)

    for h in range(HEADS):
        scores[...] = dot_nt(k_ref[h], q_ref[h])

        def top_step(i, top):
            values = scores[pl.ds(pl.multiple_of(i * 64, 64), 64), :]
            return jnp.maximum(top, jnp.max(values.reshape(8, 8, OWN), 0))

        top = lax.fori_loop(1, SLOTS // 64, top_step, jnp.max(scores[:64].reshape(8, 8, OWN), 0), unroll=True)
        top = jnp.max(top, 0, keepdims=True)

        def soft_step(i, _, h=h, top=top):
            place = pl.ds(pl.multiple_of(i * 128, 128), 128)
            soft_ref[h, place, :] = jnp.exp(scores[place, :] - top).astype(BF16)
            return 0

        lax.fori_loop(0, SLOTS // 128, soft_step, 0, unroll=True)
        raw = dot_tn(soft_ref[h], v_ref[h])
        total = raw[:, HEAD_DIM : HEAD_DIM + 1]
        sums[h] = jnp.broadcast_to(1.0 / total, (OWN, LANES))
        result = raw * sums[h]
        outs[h] = result
        att[h] = result.astype(BF16)

    branch = dot(att[0], wo[0]) + dot(att[1], wo[1]) + dot(att[2], wo[2])
    middle[...] = branch

    def own_mask(block):
        start = pl.multiple_of((block * 2 + core) * rows_slots, rows_slots)
        return widen(mask_ref[pl.ds(start, rows_slots), :])

    def norm_step(block, _):
        place = pl.ds(pl.multiple_of(block * rows_slots, rows_slots), rows_slots)
        mid = own_ref[block, 0].astype(F32) + middle[place, :] * own_mask(block)
        middle[place, :] = mid
        unit, _ = normalise(mid)
        second[place, :] = (unit * gain).astype(BF16)
        return 0

    for block in range(blocks):
        norm_step(block, 0)

    pre[...] = dot(second[...], w1[...])
    cot = jnp.concatenate([own_ref[b, 1] for b in range(blocks)], axis=0)
    grad_hidden[...] = dot_nt(cot, w2[...])

    def gelu_step(i, _):
        place = pl.ds(pl.multiple_of(i * 16, 16), 16)
        x = pre[place, :]
        phi = 0.5 * (1.0 + lax.erf(x * np.float32(0.5**0.5)))
        hidden[place, :] = (x * phi).astype(BF16)
        slope = phi + x * jnp.exp(x * x * -0.5) * np.float32((2 * np.pi) ** -0.5)
        grad_pre[place, :] = (grad_hidden[place, :] * slope).astype(BF16)
        return 0

    lax.fori_loop(0, OWN // 16, gelu_step, 0, unroll=True)

    out_ref[...] = (middle[...] + dot(hidden[...], w2[...])).astype(BF16)
    grad_2 = dot_tn(hidden[...], cot).astype(BF16)
    grad_1 = dot_tn(second[...], grad_pre[...]).astype(BF16)
    grad_middle_ref[...] = dot_nt(grad_pre[...], w1[...])

    def back_step(block, total):
        place = pl.ds(pl.multiple_of(block * rows_slots, rows_slots), rows_slots)
        unit, inverse = normalise(middle[place, :])
        grad = grad_middle_ref[place, :]
        total = total + jnp.sum(grad * unit, 0, keepdims=True)
        grad = own_ref[block, 1].astype(F32) + norm_back(grad, gain, unit, inverse)
        grad_middle_ref[place, :] = grad
        second[place, :] = (grad * own_mask(block)).astype(BF16)
        return total

    gain_two = jnp.zeros((1, D), F32)
    for block in range(blocks):
        gain_two = back_step(block, gain_two)
    gain_ref[...] = gain_two

    grad_o = []
    lane_own = lax.broadcasted_iota(jnp.int32, (OWN, LANES), 1)
    for h in range(HEADS):
        grad_o.append(dot_tn(att[h], second[...])[:HEAD_DIM])
        grad_att = dot_nt(second[...], wo[h]).astype(BF16).astype(F32)
        scaled = (grad_att * sums[h]).astype(BF16).astype(F32)
        shift = -jnp.sum(scaled * outs[h], -1, keepdims=True)
        high = shift.astype(BF16).astype(F32)
        lifted = jnp.where(
            lane_own == HEAD_DIM, high, jnp.where(lane_own == HEAD_DIM + 1, shift - high, scaled)
        )
        lifted_ref[h] = lifted.astype(BF16)

    for half in range(2):
        wire[:, half * span : (half + 1) * span] = dot_nt(
            grad_1[:, half * FF // 2 : (half + 1) * FF // 2], sel_1_ref[...]
        )
    grad_o = jnp.concatenate(grad_o, axis=0).astype(BF16)
    wire[...] += dot_nt(grad_o, sel_o_ref[...])

    def deliver(lanes):
        for m in range(parts):
            parted[m] = wire[:, m * LANES : (m + 1) * LANES].astype(BF16)
        for z in range(parts // 2):
            put_blocks(keep_ref, z, lanes, parted[2 * z + core])
            put_blocks(send_ref, z, lanes, parted[2 * z + 1 - core])

    deliver(slice(0, LANES))
    total = None
    for g in range(4):
        rows = [
            grad_2[r * 4 * per_block + g * per_block : r * 4 * per_block + (g + 1) * per_block]
            for r in range(blocks)
        ]
        part = dot_nt(jnp.concatenate(rows, axis=0), sel_2_ref[g])
        total = part if total is None else total + part
    wire[...] = total
    deliver(slice(LANES, 2 * LANES))


def attention_back_kernel(
    soft_ref,
    lifted_ref,
    q_ref,
    k_ref,
    v_ref,
    scanned_ref,
    wqkv_ref,
    part_ref,
    grad_w_ref,
    scores,
    grad_scores,
    triple,
    grad_q,
    scanned_own,
    part,
    *,
    blocks,
):
    core = lax.axis_index("core")
    rows_slots = OWN // blocks
    for h in range(HEADS):
        tile = slice(h * LANES, (h + 1) * LANES)
        scores[...] = dot_nt(v_ref[h], lifted_ref[h])

        def back_step(i, _, h=h):
            place = pl.ds(pl.multiple_of(i * 64, 64), 64)
            grad_scores[place, :] = (soft_ref[h, place, :].astype(F32) * scores[place, :]).astype(
                BF16
            )
            return 0

        lax.fori_loop(0, SLOTS // 64, back_step, 0, unroll=True)
        grad_q[:, tile] = (dot_tn(grad_scores[...], k_ref[h]).astype(BF16) * HEAD_DIM ** (-0.5)).astype(
            BF16
        )
        triple[0, :, tile] = dot(grad_scores[...], q_ref[h]).astype(BF16)
        triple[1, :, tile] = dot(soft_ref[h], lifted_ref[h]).astype(BF16)

    part[...] = dot_nt(triple[0], wqkv_ref[1]) + dot_nt(triple[1], wqkv_ref[2])
    from_q = dot_nt(grad_q[...], wqkv_ref[0])
    for block in range(blocks):
        here = slice(block * rows_slots, (block + 1) * rows_slots)
        place = pl.ds(pl.multiple_of((block * 2 + core) * rows_slots, rows_slots), rows_slots)
        part[place, :] += from_q[here]
        scanned_own[here, :] = scanned_ref[place, :]
    part_ref[...] = part[...].astype(BF16)
    grad_w_ref[0] = dot_tn(scanned_own[...], grad_q[...]).astype(BF16)
    grad_w_ref[1] = dot_tn(scanned_ref[...], triple[0]).astype(BF16)
    grad_w_ref[2] = dot_tn(scanned_ref[...], triple[1]).astype(BF16)


def scan_back_kernel(
    starts,
    width,
    own_ref,
    mask_ref,
    part_ref,
    got_ref,
    mixed_ref,
    first_ref,
    table_ref,
    rates_ref,
    wu_ref,
    grad_w_ref,
    gain_two_ref,
    sel_u_ref,
    sel_rc_ref,
    sel_q_ref,
    keep_ref,
    send_ref,
    back_ref,
    gs_wide,
    gs_pairs,
    gt_wide,
    gt_pairs,
    xs_wide,
    xs_pairs,
    xt_wide,
    xt_pairs,
    rows_wide,
    rows_pairs,
    cols_wide,
    cols_pairs,
    grads_ref,
    own,
    own_tail,
    together,
    lag_sums,
    lag_lines,
    lag_rows,
    mixed_back,
    wire,
    parted,
):
    gs, gt = (gs_wide, gs_pairs), (gt_wide, gt_pairs)
    xs, xt = (xs_wide, xs_pairs), (xt_wide, xt_pairs)
    rows, cols = (rows_wide, rows_pairs), (cols_wide, cols_pairs)
    core = lax.axis_index("core")
    blocks, _, rows_slots, _ = own_ref.shape
    half_rows = rows_slots // GRID
    own_rows = GRID // 2
    parts = sel_rc_ref.shape[0] // LANES
    put_columns(*xs, mixed_ref[...].astype(F32))
    grads = (part_ref[...].astype(F32) + got_ref[...].astype(F32)) * widen(mask_ref[...])
    grads = grads.astype(BF16)
    grads_ref[...] = grads
    put_columns(*gs, grads.astype(F32))

    def place_of(block):
        return pl.ds(pl.multiple_of((block * 2 + core) * rows_slots, rows_slots), rows_slots)

    for source, dst in ((grads_ref, gt), (mixed_ref, xt)):
        for block in range(blocks):
            here = slice(block * rows_slots, (block + 1) * rows_slots)
            value = source[place_of(block), :].astype(F32)
            own[here, :] = value[:, :LANES]
            own_tail[here, :] = value[:, LANES:]
        put_rows(*dst, own, own_tail[...], together)

    for kind, sublane in units(0):
        step = gt[kind].shape[0] // GRID
        for t, value in enumerate(toeplitz(gt, table_ref, 0, kind, sublane, -1)):
            rows[kind][t * step + sublane : t * step + sublane + 8, :] = value

    def col_step(index, _):
        for kind, sublane in units(index):
            step = gs[kind].shape[0] // GRID
            found = toeplitz(gs, table_ref, 1, kind, sublane, -1, half_rows)
            for t, value in enumerate(found):
                cols[kind][pl.ds(pl.multiple_of(t * step + sublane, 8), 8), :] = value
        return 0

    lax.fori_loop(0, 2, col_step, 0)

    lag_sums[...] = jnp.zeros_like(lag_sums)

    for kind, sublane in units(0):
        add_lags(lag_sums, 0, kind, sublane, gt, xt)

    def lag_step(index, _):
        for kind, sublane in units(index):
            add_lags(lag_sums, 1, kind, sublane, gs, xs, half_rows)
        return 0

    lax.fori_loop(0, 2, lag_step, 0)
    for way in range(2):
        for kind in range(2):
            for lag, value in enumerate(gather_lags(lag_sums, way, kind)):
                lag_lines[way, kind, lag] = value
            lag_lines[way, kind, LAGS - 1] = jnp.zeros((8, LANES), F32)

    for way in range(2):
        lag_rows[way, :, :LANES] = jnp.sum(lag_lines[way, 0], 1)
        tail = jnp.sum(lag_lines[way, 1], 1)
        tail = tail[:, : D - LANES] + tail[:, D - LANES :]
        lag_rows[way, :, LANES:] = pair_lanes(tail, jnp.zeros_like(tail))

    decay, coef = rates_ref[: 4 * STATE], rates_ref[4 * STATE :]

    def table_step(k, carry):
        to_rate, to_coef = carry
        lag = k.astype(F32)
        powers = jnp.exp(-decay * lag)
        grads = []
        for way in range(2):
            for at in (CENTER + k, CENTER - k):
                grads.append(
                    jnp.broadcast_to(lag_rows[way, pl.ds(at, 1), :], (STATE, 2 * LANES))
                )
        scaled = jnp.concatenate(grads, axis=0) * powers
        return to_rate - lag * scaled, to_coef + scaled

    zero = jnp.zeros((4 * STATE, 2 * LANES), F32)
    to_rate, to_coef = lax.fori_loop(0, GRID, table_step, (zero, zero), unroll=4)
    grad_rc = jnp.concatenate([to_rate * coef, to_coef], axis=0).T[:D].astype(BF16)

    def join_step(i, _):
        for row, value in join_rows(i, own_rows, rows, cols):
            at = ((row // half_rows * 2 + core) * half_rows + row % half_rows) * GRID
            mask = mask_ref[pl.ds(pl.multiple_of(at, GRID), GRID), :]
            place = pl.ds(pl.multiple_of(row * GRID, GRID), GRID)
            mixed_back[place, :] = (value * widen(mask)).astype(BF16)
        return 0

    lax.fori_loop(0, own_rows // 2, join_step, 0, unroll=True)
    grad_u = dot_tn(first_ref[...], mixed_back[...]).astype(BF16)
    grad_first = dot_nt(mixed_back[...], wu_ref[...])
    back_ref[...] = grad_first
    gain_one = jnp.zeros((1, D), F32)
    for block in range(blocks):
        here = slice(block * rows_slots, (block + 1) * rows_slots)
        unit, _ = normalise(own_ref[block, 0].astype(F32))
        gain_one = gain_one + jnp.sum(grad_first[here] * unit, 0, keepdims=True)

    wire[...] = dot_nt(grad_u, sel_u_ref[...]) + dot_nt(grad_rc, sel_rc_ref[...])
    for third in range(3):
        span = slice(starts[third] * LANES, (starts[third] + width) * LANES)
        wire[:, span] += dot_nt(grad_w_ref[third], sel_q_ref[third])
    for m in range(parts):
        parted[m] = wire[:, m * LANES : (m + 1) * LANES].astype(BF16)
    for z in range(parts // 2):
        put_late(keep_ref, z, parted[2 * z + core])
        put_late(send_ref, z, parted[2 * z + 1 - core])

    lines = []
    for value in (gain_one, gain_two_ref[...]):
        high = value.astype(BF16).astype(F32)
        for piece in (high, value - high):
            lines.append(piece[:, :LANES])
            lines.append(
                jnp.concatenate([piece[:, LANES:], jnp.zeros((1, 2 * LANES - D), F32)], axis=1)
            )
    lines = jnp.concatenate(lines, axis=0).astype(BF16)
    for ref in (keep_ref, send_ref):
        ref[ref.shape[0] - 1, :8] = lines
        ref[ref.shape[0] - 1, 8:] = jnp.zeros((ref.shape[1] - 8, LANES), BF16)


def last_norm_kernel(own_ref, gains_ref, back_ref, grad_middle_ref, *routed_refs):
    _, _, slots, _ = own_ref.shape
    gain = gains_ref[0:1, :]
    for k, routed in enumerate(routed_refs):
        block = lax.axis_index("row") ^ k
        place = pl.ds(pl.multiple_of(block * slots, slots), slots)
        unit, inverse = normalise(own_ref[block, 0].astype(F32))
        grad = grad_middle_ref[place, :] + norm_back(back_ref[place, :], gain, unit, inverse)
        routed[...] = pack(grad.astype(BF16))


def aligned(rows):
    return (rows + 15) // 16 * 16


def spare_lanes(rows, parts):
    return rows >= 32 and 4 * (D // parts) + 32 <= LANES


def split(value):
    high = value.astype(BF16).astype(F32)
    return jnp.concatenate([high, value - high], axis=0)


def early_sum_kernel(out_own_ref, keep_ref, got_ref, *out_refs):
    _, depth, rows, _ = keep_ref.shape
    slots = OWN // len(out_refs)
    block_rows = aligned(rows)
    for k, out_ref in enumerate(out_refs):
        block = lax.axis_index("row") ^ k
        for z in range(depth):
            total = keep_ref[block, z].astype(F32) + got_ref[block, z].astype(F32)
            out_ref[z * block_rows : z * block_rows + rows] = total.astype(BF16)
        place = pl.ds(pl.multiple_of(block * slots, slots), slots)
        out_ref[depth * block_rows :] = fold(pack(out_own_ref[place, :]))


def late_sum_kernel(depth, keep_ref, got_ref, *refs):
    count = len(refs) // 2
    routed_refs, out_refs = refs[:count], refs[count:]
    rows = keep_ref.shape[1]
    block_rows = aligned(rows)
    last = keep_ref.shape[0] - 1
    gains = keep_ref[last, :8].astype(F32) + got_ref[last, :8].astype(F32)
    lines = []
    for g in range(2):
        for lane in range(2):
            at = 4 * g + lane
            lines.append(gains[at : at + 1] + gains[at + 2 : at + 3])
    gains = split(jnp.concatenate(lines, axis=0))
    gains = jnp.concatenate([gains, jnp.zeros((8, LANES), F32)], axis=0).astype(BF16)
    for k, out_ref in enumerate(out_refs):
        block = lax.axis_index("row") ^ k
        for z in range(depth):
            at = block * depth + z
            total = keep_ref[at].astype(F32) + got_ref[at].astype(F32)
            out_ref[z * block_rows : z * block_rows + rows] = total.astype(BF16)
        out_ref[depth * block_rows : depth * block_rows + 16] = gains
        out_ref[depth * block_rows + 16 :] = routed_refs[k][...]


def row_sum_kernel(blocks, depth, rows, *refs):
    early_refs, late_refs, out_refs = refs[:blocks], refs[blocks : 2 * blocks], refs[2 * blocks :]
    block_rows = aligned(rows)
    gains = late_refs[0][depth * block_rows : depth * block_rows + 16].astype(F32)
    for k in range(1, blocks):
        gains = gains + late_refs[k][depth * block_rows : depth * block_rows + 16].astype(F32)
    gains = split(gains[:4] + gains[4:8])
    for j, out_ref in enumerate(out_refs):
        z = lax.axis_index("z") ^ j
        place = pl.ds(pl.multiple_of(z * block_rows, 16), block_rows)
        early = early_refs[0][place, :].astype(F32)
        late = late_refs[0][place, :].astype(F32)
        for k in range(1, blocks):
            early = early + early_refs[k][place, :].astype(F32)
            late = late + late_refs[k][place, :].astype(F32)
        if spare_lanes(rows, 2 * depth):
            chunks = [gains[:, q * 32 : (q + 1) * 32] for q in range(4)]
            chunks.append(jnp.zeros((rows - 32, 32), F32))
            early = jnp.concatenate([early[:, :-32], jnp.concatenate(chunks, axis=0)], axis=1)
        else:
            out_ref[rows:, :LANES] = jnp.concatenate(
                [gains, jnp.zeros((8, LANES), F32)], axis=0
            ).astype(BF16)
            out_ref[rows:, LANES:] = jnp.zeros((16, 2 * LANES), BF16)
        out_ref[:rows, LANES:] = early[:rows].astype(BF16)
        out_ref[:rows, :LANES] = late[:rows].astype(BF16)


def final_kernel(parts, *refs):
    final_body(parts, refs[: parts // 2], *refs[parts // 2 :])


def final_body(
    parts,
    got_refs,
    g1_ref,
    g2_ref,
    wu_ref,
    rate_ref,
    coef_ref,
    qkv_ref,
    wo_ref,
    fc1_ref,
    fc2_ref,
):
    a_u, a_r, a_q, (o_u, o_r, o_c, o_q) = late_layout(parts)
    total = got_refs[0][...].astype(F32)
    for ref in got_refs[1:]:
        total = total + ref[...].astype(F32)
    early = total[: fc1_ref.shape[0], LANES:]
    total = total[:, :LANES]
    rows = fc1_ref.shape[0]
    weights = total[:rows]
    if spare_lanes(rows, parts):
        gains = jnp.concatenate(
            [early[q * 8 : (q + 1) * 8, 2 * LANES - 32 :] for q in range(4)], axis=1
        )
    else:
        gains = total[rows:]
    turned = weights.T
    wu_ref[...] = turned[o_u : o_u + a_u]
    rate_ref[...] = turned[o_r : o_r + a_r]
    coef_ref[...] = turned[o_c : o_c + a_r]
    qkv_ref[...] = weights[:, o_q : o_q + a_q]
    gains = gains[0:4] + gains[4:8]
    for g, ref in ((0, g1_ref), (1, g2_ref)):
        ref[...] = jnp.concatenate(
            [gains[2 * g : 2 * g + 1], gains[2 * g + 1 : 2 * g + 2, : D - LANES]], axis=1
        )
    a_1, a_o = FF // parts, D // parts
    fc1_ref[...] = early[:, :a_1]
    wo_ref[...] = early[:, :LANES].T[a_1 : a_1 + a_o]
    turned = early[:, LANES:].T
    fc2_ref[...] = jnp.concatenate([turned[g * a_o : (g + 1) * a_o] for g in range(4)], axis=1)


def per_device(
    patches, valid_mask, norm_gains, w_u, decay_rate, out_coef, w_qkv, w_o, w_fc1, w_fc2, cotangent
):
    images, rows_here, _, _ = patches.shape
    depth, blocks = lax.axis_size("z"), lax.axis_size("row")
    parts = 2 * depth
    rows_slots = rows_here // 2 * GRID
    packed_rows = rows_slots * 3 // 2
    swap = [(0, 1), (1, 0)]
    shape = jax.ShapeDtypeStruct

    def planes(slots):
        return [pltpu.VMEM((slots, LANES), F32), pltpu.VMEM((slots // 2, LANES), F32)]

    def swapped(value):
        return lax.ppermute(value, "core", swap)

    def exchanged(values, axis):
        size = len(values)
        return [values[0]] + [
            lax.ppermute(values[k], axis, [(i, i ^ k) for i in range(size)]) for k in range(1, size)
        ]

    def to_chips(value, j):
        pairs = []
        for home in range(2):
            for source in range(blocks):
                target, image = divmod(source ^ j, images)
                pairs.append((home * blocks + source, target * blocks + home * images + image))
        return lax.ppermute(value, ("core", "row"), pairs)

    starts, width = late_spans(parts)
    sel_1, sel_o, sel_2 = early_selections(parts)

    rows_weight = w_u.shape[0]
    payload = shape((2 * packed_rows + GRID, LANES), BF16)
    shard = shape((rows_weight, 3 * LANES), BF16)
    sources = [value.reshape(images, rows_here * GRID, D) for value in (patches, cotangent)]
    if rows_weight % 16 == 0:
        weights, *routed = pl.pallas_call(
            depart_kernel,
            name="depart",
            out_shape=(shard,) + (payload,) * blocks,
            in_specs=[VMEM] * 10,
            out_specs=[VMEM] * (1 + blocks),
            compiler_params=compiler(LARGE),
        )(
                w_u.T,
            decay_rate.T,
            out_coef.T,
            w_o.T,
            w_fc2.T,
            w_qkv,
            w_fc1,
            *sources,
            valid_mask,
        )
    else:

        def fill(pieces):
            joined = jnp.concatenate(pieces, axis=1)
            return jnp.pad(joined, ((0, 0), (0, LANES - joined.shape[1])))

        weights = jnp.concatenate(
            [
                fill([w_u, decay_rate, out_coef, w_qkv]),
                fill([w_fc1, w_o]),
                fill([w_fc2[g * rows_weight : (g + 1) * rows_weight] for g in range(4)]),
            ],
            axis=1,
        )
        routed = pl.pallas_call(
            route_kernel,
            name="route",
            out_shape=(payload,) * blocks,
            in_specs=[VMEM] * 3,
            out_specs=[VMEM] * blocks,
            compiler_params=compiler(LARGE),
        )(*sources, valid_mask)

    weights = jnp.stack(exchanged([weights] * depth, "z"))
    weights = exchanged([weights] * blocks, "row")
    weights = weights + [swapped(value) for value in weights]
    routed = [to_chips(value, j) for j, value in enumerate(routed)]
    own, first_own, mask, sel_u, sel_rc, sel_q = pl.pallas_call(
        lambda *refs: norm_kernel(starts, parts, *refs),
        name="first_norm",
        out_shape=(
            shape((blocks, 2, rows_slots, D), BF16),
            shape((OWN, D), BF16),
            shape((SLOTS, LANES), F32),
            shape((parts * LANES, D), BF16),
            shape((parts * LANES, LANES), BF16),
            shape((3, width * LANES, TILE), BF16),
        ),
        in_specs=[VMEM] * (1 + blocks),
        out_specs=[VMEM] * 6,
        compiler_params=compiler(8 << 20),
    )(norm_gains, *routed)
    first_other = swapped(first_own)

    head_own = shape((HEADS, OWN, LANES), BF16)
    head_all = shape((HEADS, SLOTS, LANES), BF16)
    part_scratch = pltpu.VMEM((parts, blocks, rows_weight, LANES), BF16)
    q, k, v, scanned, mixed, table, rates, wu, wqkv = pl.pallas_call(
        lambda *refs: scan_kernel(starts, width, *refs, blocks=blocks),
        name="scan_forward",
        out_shape=(
            head_own,
            head_all,
            head_all,
            shape((SLOTS, D), BF16),
            shape((SLOTS, D), BF16),
            shape((2, 2, 9 * 16, LANES), F32),
            shape((LANES, 2 * LANES), F32),
            shape((D, D), BF16),
            shape((3, D, TILE), BF16),
        ),
        in_specs=[VMEM] * (6 + 2 * blocks),
        out_specs=[VMEM] * 9,
        scratch_shapes=[part_scratch]
        + planes(SLOTS) * 4
        + [pltpu.VMEM((OWN, D), BF16), pltpu.VMEM((SLOTS, D), BF16)]
        + [pltpu.VMEM((2, 2, LAGS, LANES), F32)],
        compiler_params=compiler(),
    )(first_own, first_other, mask, sel_u, sel_rc, sel_q, *weights)

    wire_early = shape((blocks, depth, rows_weight, 2 * LANES), BF16)
    soft, lifted, out_own, grad_middle, gain_two, early_keep, early_send = pl.pallas_call(
        middle_kernel,
        name="attention_and_feed_forward",
        out_shape=(
            shape((HEADS, SLOTS, OWN), BF16),
            head_own,
            shape((OWN, D), BF16),
            shape((OWN, D), F32),
            shape((1, D), F32),
            wire_early,
            wire_early,
        ),
        in_specs=[VMEM] * (9 + 2 * blocks),
        out_specs=[VMEM] * 7,
        scratch_shapes=[
            part_scratch,
            pltpu.VMEM((SLOTS, OWN), F32),
            pltpu.VMEM((HEADS, LANES, D), BF16),
            pltpu.VMEM((D, FF), BF16),
            pltpu.VMEM((FF, D), BF16),
            pltpu.VMEM((HEADS, OWN, LANES), BF16),
            pltpu.VMEM((HEADS, OWN, LANES), F32),
            pltpu.VMEM((HEADS, OWN, LANES), F32),
            pltpu.VMEM((OWN, D), F32),
            pltpu.VMEM((OWN, D), BF16),
            pltpu.VMEM((OWN, FF), F32),
            pltpu.VMEM((OWN, FF), F32),
            pltpu.VMEM((OWN, FF), BF16),
            pltpu.VMEM((OWN, FF), BF16),
            pltpu.VMEM((D, parts * LANES), F32),
            pltpu.VMEM((parts, D, LANES), BF16),
        ],
        compiler_params=compiler(),
    )(own, mask, norm_gains, sel_1, sel_o, sel_2, q, k, v, *weights)

    early_recv = swapped(early_send)

    part, grad_w = pl.pallas_call(
        lambda *refs: attention_back_kernel(*refs, blocks=blocks),
        name="attention_backward",
        out_shape=(shape((SLOTS, D), BF16), shape((3, D, TILE), BF16)),
        in_specs=[VMEM] * 7,
        out_specs=[VMEM] * 2,
        scratch_shapes=[
            pltpu.VMEM((SLOTS, OWN), F32),
            pltpu.VMEM((SLOTS, OWN), BF16),
            pltpu.VMEM((2, SLOTS, TILE), BF16),
            pltpu.VMEM((OWN, TILE), BF16),
            pltpu.VMEM((OWN, D), BF16),
            pltpu.VMEM((SLOTS, D), F32),
        ],
        compiler_params=compiler(),
    )(soft, lifted, q, k, v, scanned, wqkv)

    early_keep, early_recv, part = lax.optimization_barrier((early_keep, early_recv, part))
    payload = shape((depth * aligned(rows_weight) + packed_rows // 2, 2 * LANES), BF16)
    early = pl.pallas_call(
        early_sum_kernel,
        name="early_sum",
        out_shape=(payload,) * blocks,
        in_specs=[VMEM] * 3,
        out_specs=[VMEM] * blocks,
        compiler_params=compiler(8 << 20),
    )(out_own, early_keep, early_recv)
    early, part = lax.optimization_barrier((early, part))
    part_got = swapped(part)
    early = exchanged(early, "row")
    wire_late = shape((blocks * depth + 1, rows_weight, LANES), BF16)
    late_keep, late_send, back = pl.pallas_call(
        lambda *refs: scan_back_kernel(starts, width, *refs),
        name="scan_backward",
        out_shape=(wire_late, wire_late, shape((OWN, D), F32)),
        in_specs=[VMEM] * 14,
        out_specs=[VMEM] * 3,
        scratch_shapes=planes(SLOTS) + planes(OWN) + planes(SLOTS) + planes(OWN) * 3
        + [
            pltpu.VMEM((SLOTS, D), BF16),
            pltpu.VMEM((OWN, LANES), F32),
            pltpu.VMEM((OWN, D - LANES), F32),
            pltpu.VMEM((OWN // 2, LANES), F32),
            pltpu.VMEM((2, 2, 9 * 16, 8, LANES), F32),
            pltpu.VMEM((2, 2, LAGS, 8, LANES), F32),
            pltpu.VMEM((2, LAGS, 2 * LANES), F32),
            pltpu.VMEM((OWN, D), BF16),
            pltpu.VMEM((D, parts * LANES), F32),
            pltpu.VMEM((parts, D, LANES), BF16),
        ],
        compiler_params=compiler(),
    )(
        own,
        mask,
        part,
        part_got,
        mixed,
        first_own,
        table,
        rates,
        wu,
        grad_w,
        gain_two,
        sel_u,
        sel_rc,
        sel_q,
    )
    late_keep, late_send, early = lax.optimization_barrier((late_keep, late_send, early))
    payload = shape((packed_rows, LANES), BF16)
    routed = pl.pallas_call(
        last_norm_kernel,
        name="last_norm",
        out_shape=(payload,) * blocks,
        in_specs=[VMEM] * 4,
        out_specs=[VMEM] * blocks,
        compiler_params=compiler(8 << 20),
    )(own, norm_gains, back, grad_middle)
    payload = shape((depth * aligned(rows_weight) + 16 + packed_rows, LANES), BF16)
    late = pl.pallas_call(
        lambda *refs: late_sum_kernel(depth, *refs),
        name="late_sum",
        out_shape=(payload,) * blocks,
        in_specs=[VMEM] * (2 + blocks),
        out_specs=[VMEM] * blocks,
        compiler_params=compiler(8 << 20),
    )(late_keep, swapped(late_send), *routed)
    late = exchanged(late, "row")
    final_rows = rows_weight if spare_lanes(rows_weight, parts) else rows_weight + 16
    summed = pl.pallas_call(
        lambda *refs: row_sum_kernel(blocks, depth, rows_weight, *refs),
        name="row_sum",
        out_shape=(shape((final_rows, 3 * LANES), BF16),) * depth,
        in_specs=[VMEM] * (2 * blocks),
        out_specs=[VMEM] * depth,
        compiler_params=compiler(8 << 20),
    )(*early, *late)
    summed = exchanged(summed, "z")

    chosen = pl.pallas_call(
        choose_kernel,
        name="choose",
        out_shape=shape((images, 2 * packed_rows, LANES), BF16),
        in_specs=[VMEM] * (2 * blocks),
        out_specs=VMEM,
        compiler_params=compiler(8 << 20),
    )(*early, *late)
    whole = shape((images, rows_here * GRID, D), BF16)
    block_out, grad_patches = pl.pallas_call(
        home_kernel,
        name="home",
        out_shape=(whole, whole),
        in_specs=[VMEM] * (1 + 2 * blocks),
        out_specs=[VMEM] * 2,
        compiler_params=compiler(8 << 20),
    )(swapped(chosen), *early, *late)

    summed, block_out, grad_patches = lax.optimization_barrier((summed, block_out, grad_patches))
    turned = (4 * STATE // parts, rows_weight)
    g1, g2, f_u, f_rate, f_coef, f_qkv, f_o, f_1, f_2 = pl.pallas_call(
        lambda *refs: final_kernel(parts, *refs),
        name="final_sum",
        out_shape=(
            shape((1, D), F32),
            shape((1, D), F32),
            shape((D // parts, rows_weight), F32),
            shape(turned, F32),
            shape(turned, F32),
            shape((rows_weight, 3 * D // parts), F32),
            shape((D // parts, rows_weight), F32),
            shape((rows_weight, FF // parts), F32),
            shape((D // parts, 4 * rows_weight), F32),
        ),
        in_specs=[VMEM] * depth,
        out_specs=[VMEM] * 9,
        compiler_params=compiler(8 << 20),
    )(*summed)
    return (
        block_out.reshape(patches.shape),
        grad_patches.reshape(patches.shape),
        g1.reshape(D),
        g2.reshape(D),
        f_u.T,
        f_rate.T,
        f_coef.T,
        f_qkv,
        f_o.T,
        f_1,
        f_2.T,
    )


def solution(mesh):
    images, rows = mesh.devices.shape
    fine = Mesh(mesh.devices.reshape(images // 2, 2, rows), ("z", "core", "row"))
    img = ("z", "core")
    grid = P(img, "row", None, None)
    weight = P("row", img)
    in_specs = (grid, P(img, None, None), P()) + (weight,) * 7 + (grid,)
    out_specs = (grid, grid, P(), P()) + (weight,) * 7
    return jax.shard_map(
        per_device, mesh=fine, in_specs=in_specs, out_specs=out_specs, check_vma=False
    )
```

```python
import jax
import jax.numpy as jnp
import numpy as np
from jax import lax
from jax.experimental import pallas as pl
from jax.experimental.pallas import tpu as pltpu
from jax.sharding import Mesh
from jax.sharding import PartitionSpec as P

HEADS = 3
HEAD_DIM = 64
STATE = 16
GRID = 32
SLOTS = GRID * GRID
OWN = SLOTS // 2
D = HEADS * HEAD_DIM
FF = 4 * D
LANES = 128
TILE = HEADS * LANES
LAGS = 2 * GRID
CENTER = GRID - 1
EPS = 1e-05
BF16 = jnp.bfloat16
F32 = jnp.float32


def late_layout(parts):
    a_u, a_r, a_q = D // parts, 4 * STATE // parts, 3 * D // parts
    return a_u, a_r, a_q, (0, a_u, a_u + a_r, a_u + 2 * a_r)


def late_spans(parts):
    a_q = 3 * D // parts
    first = [third * D // a_q for third in range(3)]
    last = [((third + 1) * D - 1) // a_q for third in range(3)]
    width = max(stop - start + 1 for start, stop in zip(first, last))
    return [min(start, parts - width) for start in first], width


def early_selections(parts):
    a_1, a_o = FF // parts, D // parts
    half = parts // 2
    sel_1 = np.zeros((half, LANES, FF // 2), np.float32)
    sel_o = np.zeros((parts, LANES, D), np.float32)
    sel_2 = np.zeros((4, parts, LANES, D), np.float32)
    for m in range(half):
        for col in range(a_1):
            sel_1[m, col, m * a_1 + col] = 1
    for m in range(parts):
        for col in range(a_o):
            sel_o[m, a_1 + col, m * a_o + col] = 1
            for g in range(4):
                sel_2[g, m, g * a_o + col, m * a_o + col] = 1
    return (
        sel_1.reshape(half * LANES, FF // 2).astype(BF16),
        sel_o.reshape(parts * LANES, D).astype(BF16),
        sel_2.reshape(4, parts * LANES, D).astype(BF16),
    )


def lane_and_part(shape):
    place = lax.broadcasted_iota(jnp.int32, shape, 0)
    return place % LANES, place // LANES, lax.broadcasted_iota(jnp.int32, shape, 1)


def put_late_selections(starts, parts, sel_u_ref, sel_rc_ref, sel_q_ref):
    a_u, a_r, a_q, (o_u, o_r, o_c, o_q) = late_layout(parts)

    def put(hit):
        return jnp.where(hit, 1.0, 0.0).astype(BF16)

    lane, part, col = lane_and_part(sel_u_ref.shape)
    sel_u_ref[...] = put((lane < a_u) & (part * a_u + lane == col))
    lane, part, col = lane_and_part(sel_rc_ref.shape)
    rate = (lane >= o_r) & (lane < o_c) & (part * a_r + lane - o_r == col)
    coef = (lane >= o_c) & (lane < o_q) & (part * a_r + lane - o_c + 4 * STATE == col)
    sel_rc_ref[...] = put(rate | coef)
    lane, part, col = lane_and_part(sel_q_ref.shape[1:])
    whole = jnp.where(
        col % LANES < HEAD_DIM, col // LANES * HEAD_DIM + col % LANES, -4 * D
    )
    for third in range(3):
        here = (part + starts[third]) * a_q + lane - o_q - third * D
        sel_q_ref[third] = put((lane >= o_q) & (lane < o_q + a_q) & (here == whole))


def dot(a, b):
    return lax.dot_general(a, b, (((1,), (0,)), ((), ())), preferred_element_type=F32)


def dot_nt(a, b):
    return lax.dot_general(a, b, (((1,), (1,)), ((), ())), preferred_element_type=F32)


def dot_tn(a, b):
    return lax.dot_general(a, b, (((0,), (0,)), ((), ())), preferred_element_type=F32)


def normalise(values):
    center = values - jnp.mean(values, -1, keepdims=True)
    spread = jnp.mean(center * center, -1, keepdims=True)
    inverse = lax.rsqrt(spread + EPS)
    return center * inverse, inverse


def norm_back(grad, gain, unit, inverse):
    scaled = grad * gain
    first = jnp.mean(scaled, -1, keepdims=True)
    second = jnp.mean(scaled * unit, -1, keepdims=True)
    return inverse * (scaled - first - unit * second)


def widen(mask):
    return jnp.concatenate([mask, mask[:, : D - LANES]], axis=1)


def put_blocks(ref, z, lanes, value):
    rows = ref.shape[2]
    for r in range(ref.shape[0]):
        ref[r, z, :, lanes] = value[r * rows : (r + 1) * rows]


def put_late(ref, z, value):
    rows = ref.shape[1]
    depth = ref.shape[0] * rows // D
    for r in range(D // rows):
        ref[r * depth + z] = value[r * rows : (r + 1) * rows]


def pair_lanes(first, second):
    return jnp.concatenate([first, second], axis=1)


def put_columns(wide, pairs, values):
    wide[...] = values[:, :LANES]
    tail = values[:, LANES:].reshape(values.shape[0] // GRID, 2, GRID // 2, D - LANES)
    tail = pair_lanes(tail[:, 0].reshape(-1, D - LANES), tail[:, 1].reshape(-1, D - LANES))
    pairs[...] = tail


def put_rows(wide, pairs, from_wide, tail, together):
    rows = from_wide.shape[0] // GRID
    together[...] = pair_lanes(tail[: rows // 2 * GRID], tail[rows // 2 * GRID :])
    for j in range(GRID):
        wide[j * rows : (j + 1) * rows, :] = from_wide[pl.ds(j, rows, stride=GRID), :]
        pairs[j * rows // 2 : (j + 1) * rows // 2, :] = together[pl.ds(j, rows // 2, stride=GRID), :]


def units(index):
    return [(0, (index * 2 + u) * 8) for u in range(2)] + [(1, index * 8)]


def lag_tables(lags):
    lines = []
    near = lags[16:47]
    for table in (near, lags[0:31] - near, lags[32:63] - near):
        center = table[8:23]
        for part in (center, table[0:15] - center, table[16:31] - center):
            lines += [part, jnp.zeros((1, LANES), F32)]
    return jnp.concatenate(lines, axis=0)


def plus(left, right):
    return [a + b for a, b in zip(left, right)]


def own_places(own_rows):
    if own_rows is None:
        return list(range(8)), 0
    places = [i // own_rows * 2 * own_rows + i % own_rows for i in range(4)]
    return places, lax.axis_index("core") * own_rows


def three(left, right, work):
    a, b = len(left) // 2, len(right) // 2
    work(0, plus(left[:a], left[a:]), plus(right[:b], right[b:]))
    work(1, left[:a], right[b:])
    work(2, left[a:], right[:b])


def add_lags(sums, way, kind, sublane, grads, values, own_rows=None):
    step = values[kind].shape[0] // GRID
    places, shift = own_places(own_rows)

    def line(ref, at):
        return ref[kind][pl.ds(pl.multiple_of(at * step + sublane, 8), 8), :]

    g = [line(grads, base + place + shift) for base in range(0, GRID, 8) for place in places]
    x = [line(values, s) for s in range(GRID)]

    def leaf(first, second, g, x):
        total = {}
        for i, t in enumerate(places):
            for s in range(8):
                term = g[i] * x[s]
                total[t - s] = term if t - s not in total else total[t - s] + term
        start = (first * 3 + second) * 16 + 7
        for lag, value in total.items():
            sums[way, kind, start + lag + shift] += value

    three(g, x, lambda p, g, x: three(g, x, lambda q, g, x: leaf(p, q, g, x)))


def gather_lags(sums, way, kind):
    def join(parts, reach):
        found = [None] * (2 * (2 * reach + 1) + 1)
        width = 2 * reach - 1
        middle = [a - b - c for a, b, c in zip(*parts)]
        for start, part in ((reach, middle), (0, parts[1]), (2 * reach, parts[2])):
            for i in range(width):
                at = start + i
                found[at] = part[i] if found[at] is None else found[at] + part[i]
        return found[: 4 * reach - 1]

    thirds = []
    for first in range(3):
        tables = [
            [sums[way, kind, (first * 3 + second) * 16 + i] for i in range(15)]
            for second in range(3)
        ]
        thirds.append(join(tables, 8))
    return join(thirds, 16)


def toeplitz(src, table, way, kind, sublane, sign, own_rows=None):
    step = src[kind].shape[0] // GRID
    places, shift = own_places(own_rows)
    shift = shift * sign

    def leaf(x, first, second):
        if sign < 0:
            first, second = (0, 2, 1)[first], (0, 2, 1)[second]
        start = (first * 3 + second) * 16 + 7
        coef = {}
        total = [None] * len(places)
        for s in range(8):
            for i, t in enumerate(places):
                lag = t - s
                if lag not in coef:
                    line = table[way, kind, pl.ds(start + lag * sign + shift, 1), :]
                    coef[lag] = jnp.broadcast_to(line, (8, LANES))
                term = coef[lag] * x[s]
                total[i] = term if total[i] is None else total[i] + term
        return total

    def quarter(x, first):
        middle = leaf(plus(x[:8], x[8:]), first, 0)
        return plus(middle, leaf(x[8:], first, 1)) + plus(middle, leaf(x[:8], first, 2))

    x = [src[kind][pl.ds(pl.multiple_of(s * step + sublane, 8), 8), :] for s in range(GRID)]
    middle = quarter(plus(x[:16], x[16:]), 0)
    return plus(middle, quarter(x[16:], 1)) + plus(middle, quarter(x[:16], 2))


def join_rows(i, count, rows, cols):
    half = GRID // 2
    narrow = D - LANES
    across = rows[1][pl.ds(i, GRID, stride=count // 2), :]
    found = []
    for which in range(2):
        row = i + which * (count // 2)
        wide = cols[0][pl.ds(pl.multiple_of(row * GRID, GRID), GRID), :].astype(BF16).astype(F32)
        wide = wide + rows[0][pl.ds(i + which * (count // 2), GRID, stride=count), :]
        pairs = cols[1][pl.ds(pl.multiple_of(row * half, half), half), :].astype(BF16).astype(F32)
        tail = jnp.concatenate([pairs[:, :narrow], pairs[:, narrow:]], axis=0)
        tail = tail + across[:, which * narrow : (which + 1) * narrow]
        found.append((row, jnp.concatenate([wide, tail], axis=1)))
    return found


def gather_parts(mine_refs, got_refs, block, out_ref):
    core, row, depth = lax.axis_index("core"), lax.axis_index("row"), lax.axis_index("z")
    lanes = slice(block * LANES, (block + 1) * LANES)
    count = out_ref.shape[0] // 2
    rows = out_ref.shape[2]
    for refs, which in ((mine_refs, core), (got_refs, 1 - core)):
        for k, ref in enumerate(refs):
            for j in range(count):
                out_ref[2 * (depth ^ j) + which, row ^ k] = ref[j, :, lanes]
    wide = []
    for m in range(2 * count):
        wide.append(jnp.concatenate([out_ref[m, r] for r in range(out_ref.shape[1])], axis=0))
    return jnp.concatenate(wide, axis=1)


LARGE = 60 << 20


def compiler(limit=24 << 20):
    return pltpu.CompilerParams(vmem_limit_bytes=limit)


VMEM = pl.BlockSpec(memory_space=pltpu.VMEM)


def pack(values):
    half = values.shape[0] // 2
    tail = jnp.concatenate([values[:half, LANES:], values[half:, LANES:]], axis=1)
    return jnp.concatenate([values[:, :LANES], tail], axis=0)


def unpack(packed):
    count = packed.shape[0] * 2 // 3
    tail = packed[count:]
    tail = jnp.concatenate([tail[:, : D - LANES], tail[:, D - LANES :]], axis=0)
    return jnp.concatenate([packed[:count], tail], axis=1)


def pack_weights_kernel(turned_refs, qkv_ref, fc1_ref, out_ref):
    wu, rate, coef, wo, fc2 = [ref[...].astype(F32) for ref in turned_refs]
    rows = qkv_ref.shape[0]
    a_o, a_r = wo.shape[0], rate.shape[0]
    pieces = [wu, rate, coef, wo] + [fc2[:, g * rows : (g + 1) * rows] for g in range(4)]
    joined = jnp.concatenate(pieces, axis=0)
    joined = jnp.concatenate([joined, jnp.zeros((joined.shape[0], LANES - rows), F32)], axis=1)
    joined = joined.T[:rows]
    first, second = a_o + 2 * a_r, 2 * a_o + 2 * a_r

    def fill(parts):
        used = sum(part.shape[1] for part in parts)
        return parts + [jnp.zeros((rows, LANES - used), F32)]

    packed = jnp.concatenate(
        fill([joined[:, :first], qkv_ref[...].astype(F32)])
        + fill([fc1_ref[...].astype(F32), joined[:, first:second]])
        + fill([joined[:, second:]]),
        axis=1,
    ).astype(BF16)
    out_ref[...] = packed


def route_kernel(patch_ref, cot_ref, valid_ref, *out_refs):
    row = lax.axis_index("row")
    images, slots, _ = patch_ref.shape
    half = slots // 2
    packed = half * 3 // 2
    for j, out_ref in enumerate(out_refs):
        target = row ^ j
        core, image = target // images, target % images
        place = pl.ds(pl.multiple_of(core * half, half), half)
        out_ref[:packed] = pack(patch_ref[image, place, :])
        out_ref[packed : 2 * packed] = pack(cot_ref[image, place, :])
        valid = valid_ref[image].astype(F32).astype(BF16)
        out_ref[2 * packed :] = jnp.concatenate(
            [valid, jnp.zeros((GRID, LANES - GRID), BF16)], axis=1
        )


def depart_kernel(*refs):
    turned, (qkv_ref, fc1_ref, patch_ref, cot_ref, valid_ref, out_ref) = refs[:5], refs[5:11]
    pack_weights_kernel(turned, qkv_ref, fc1_ref, out_ref)
    route_kernel(patch_ref, cot_ref, valid_ref, *refs[11:])


def norm_kernel(starts, parts, gains_ref, *refs):
    got_refs, refs = refs[:-6], refs[-6:]
    own_ref, first_ref, mask_ref, *selections = refs
    core, row = lax.axis_index("core"), lax.axis_index("row")
    images = len(got_refs) // 2
    gain = gains_ref[0:1, :]
    slots = own_ref.shape[2]
    packed = slots * 3 // 2
    for j, got in enumerate(got_refs):
        block = (core * images + row % images) ^ j
        patch = unpack(got[:packed])
        own_ref[block, 0] = patch
        own_ref[block, 1] = unpack(got[packed : 2 * packed])
        unit, _ = normalise(patch.astype(F32))
        first_ref[pl.ds(pl.multiple_of(block * slots, slots), slots), :] = (unit * gain).astype(
            BF16
        )
    valid = got_refs[0][2 * packed :].astype(F32).T
    for i in range(GRID):
        mask_ref[i * GRID : (i + 1) * GRID, :] = jnp.broadcast_to(
            valid[:GRID, i : i + 1], (GRID, LANES)
        )
    put_late_selections(starts, parts, *selections)


def fold(packed):
    half = packed.shape[0] // 2
    return jnp.concatenate([packed[:half], packed[half:]], axis=1)


def unfold(folded):
    return jnp.concatenate([folded[:, :LANES], folded[:, LANES:]], axis=0)


def results_of(early_ref, late_ref, rows):
    early_start, late_start = early_ref.shape[0] - rows // 2, late_ref.shape[0] - rows
    return unfold(early_ref[early_start:]), late_ref[late_start:]


def choose_kernel(*refs):
    got_refs, out_ref = refs[:-1], refs[-1]
    blocks = len(got_refs) // 2
    core, row = lax.axis_index("core"), lax.axis_index("row")
    images, rows = out_ref.shape[0], out_ref.shape[1] // 2
    for k, got in enumerate(zip(got_refs[:blocks], got_refs[blocks:])):
        image = row ^ k

        @pl.when(image // images != core)
        def _(got=got, image=image):
            for which, value in enumerate(results_of(*got, rows)):
                out_ref[image % images, which * rows : (which + 1) * rows] = value


def home_kernel(swapped_ref, *refs):
    got_refs, out_refs = refs[:-2], refs[-2:]
    core, row = lax.axis_index("core"), lax.axis_index("row")
    images, slots, _ = out_refs[0].shape
    half = slots // 2
    rows = half * 3 // 2
    blocks = len(got_refs) // 2
    mine = pl.ds(pl.multiple_of(core * half, half), half)
    theirs = pl.ds(pl.multiple_of((1 - core) * half, half), half)
    for k, got in enumerate(zip(got_refs[:blocks], got_refs[blocks:])):
        image = row ^ k

        @pl.when(image // images == core)
        def _(got=got, image=image):
            for out_ref, value in zip(out_refs, results_of(*got, rows)):
                out_ref[image % images, mine, :] = unpack(value)

    for image in range(images):
        for which, out_ref in enumerate(out_refs):
            value = swapped_ref[image, which * rows : (which + 1) * rows]
            out_ref[image, theirs, :] = unpack(value)


def scan_kernel(
    starts,
    width,
    first_own_ref,
    first_other_ref,
    mask_ref,
    sel_u_ref,
    sel_rc_ref,
    sel_q_ref,
    *refs,
    blocks,
):
    mine_refs, got_refs, refs = refs[:blocks], refs[blocks : 2 * blocks], refs[2 * blocks :]
    scan_body(
        starts,
        width,
        first_own_ref,
        first_other_ref,
        mask_ref,
        sel_u_ref,
        sel_rc_ref,
        sel_q_ref,
        mine_refs,
        got_refs,
        *refs,
    )


def scan_body(
    starts,
    width,
    first_own_ref,
    first_other_ref,
    mask_ref,
    sel_u_ref,
    sel_rc_ref,
    sel_q_ref,
    mine_refs,
    got_refs,
    q_ref,
    k_ref,
    v_ref,
    scanned_ref,
    mixed_ref,
    table_ref,
    rates_ref,
    wu_ref,
    wqkv_ref,
    late_ref,
    xs_wide,
    xs_pairs,
    xt_wide,
    xt_pairs,
    cols_wide,
    cols_pairs,
    rows_wide,
    rows_pairs,
    scanned_own,
    first_ref,
    lags,
):
    xs, xt = (xs_wide, xs_pairs), (xt_wide, xt_pairs)
    cols, rows = (cols_wide, cols_pairs), (rows_wide, rows_pairs)
    core = lax.axis_index("core")
    blocks = len(mine_refs)
    rows_slots = OWN // blocks

    late = gather_parts(mine_refs, got_refs, 0, late_ref)
    wu = dot(late, sel_u_ref[...]).astype(BF16)
    wu_ref[...] = wu
    rates = dot(late, sel_rc_ref[...])
    rates = jnp.concatenate([rates.T, jnp.zeros((LANES, 2 * LANES - D), F32)], axis=1)
    rates_ref[...] = rates
    for third in range(3):
        window = late[:, starts[third] * LANES : (starts[third] + width) * LANES]
        wqkv_ref[third] = dot(window, sel_q_ref[third]).astype(BF16)

    decay, coef = rates[: 4 * STATE], rates[4 * STATE :]

    def lag_row(k):
        powers = jnp.exp(-decay * k) * coef
        return [jnp.sum(powers[d * STATE : (d + 1) * STATE], 0, keepdims=True) for d in range(4)]

    def store_lag(way, lag, row):
        row = row.astype(BF16).astype(F32)
        tail = row[:, LANES:D]
        for kind, lanes in enumerate((row[:, :LANES], pair_lanes(tail, tail))):
            lags[way, kind, pl.ds(lag + CENTER, 1), :] = lanes

    def lag_step(k, _):
        found = lag_row(k.astype(F32))
        for way in range(2):
            store_lag(way, k, found[2 * way])
            store_lag(way, -k, found[2 * way + 1])
        return 0

    lax.fori_loop(0, GRID, lag_step, 0, unroll=True)
    found = lag_row(0.0)
    for way in range(2):
        store_lag(way, 0, found[2 * way] + found[2 * way + 1])
        for kind in range(2):
            table_ref[way, kind] = lag_tables(lags[way, kind])


    for block in range(blocks):
        here = slice(block * rows_slots, (block + 1) * rows_slots)
        for ref, which in ((first_own_ref, core), (first_other_ref, 1 - core)):
            start = pl.multiple_of((block * 2 + which) * rows_slots, rows_slots)
            first_ref[pl.ds(start, rows_slots), :] = ref[here, :]
    mixed = dot(first_ref[...], wu) * widen(mask_ref[...])
    mixed = mixed.astype(BF16)
    mixed_ref[...] = mixed
    mixed = mixed.astype(F32)
    put_columns(*xs, mixed)
    put_rows(*xt, xs[0], mixed[:, LANES:], cols[1])

    def scan_step(index, _):
        for way, src, dst in ((0, xt, rows), (1, xs, cols)):
            for kind, sublane in units(index):
                step = src[kind].shape[0] // GRID
                for t, value in enumerate(toeplitz(src, table_ref, way, kind, sublane, 1)):
                    dst[kind][pl.ds(pl.multiple_of(t * step + sublane, 8), 8), :] = value
        return 0

    lax.fori_loop(0, 2, scan_step, 0, unroll=True)

    def join_step(i, _):
        for row, value in join_rows(i, GRID, rows, cols):
            place = pl.ds(pl.multiple_of(row * GRID, GRID), GRID)
            scanned_ref[place, :] = (value * widen(mask_ref[place, :])).astype(BF16)
        return 0

    lax.fori_loop(0, GRID // 2, join_step, 0, unroll=True)

    for block in range(blocks):
        start = pl.multiple_of((block * 2 + core) * rows_slots, rows_slots)
        scanned_own[block * rows_slots : (block + 1) * rows_slots, :] = scanned_ref[
            pl.ds(start, rows_slots), :
        ]

    lane_own = lax.broadcasted_iota(jnp.int32, (OWN, LANES), 1)
    lane_all = lax.broadcasted_iota(jnp.int32, (SLOTS, LANES), 1)
    bias = jnp.where(lane_all == HEAD_DIM, (mask_ref[...] - 1.0) * 1e30, 0.0)
    ones = jnp.where((lane_all == HEAD_DIM) | (lane_all == HEAD_DIM + 1), 1.0, 0.0)
    one_own = jnp.where(lane_own == HEAD_DIM, 1.0, 0.0)
    found = dot(scanned_own[...], wqkv_ref[0]) * HEAD_DIM ** (-0.5)
    for h in range(HEADS):
        q_ref[h] = (found[:, h * LANES : (h + 1) * LANES] + one_own).astype(BF16)
    targets = [(k_ref, h, 1, bias) for h in range(HEADS)] + [(v_ref, h, 2, ones) for h in range(HEADS)]
    for pair in range(HEADS):
        two = targets[2 * pair : 2 * pair + 2]
        weight = [wqkv_ref[third, :, h * LANES : (h + 1) * LANES] for _, h, third, _ in two]
        found = dot(scanned_ref[...], jnp.concatenate(weight, axis=1))
        for i, (ref, h, _, extra) in enumerate(two):
            ref[h] = (found[:, i * LANES : (i + 1) * LANES] + extra).astype(BF16)


def middle_kernel(
    own_ref,
    mask_ref,
    gains_ref,
    sel_1_ref,
    sel_o_ref,
    sel_2_ref,
    q_ref,
    k_ref,
    v_ref,
    *refs,
):
    blocks = own_ref.shape[0]
    middle_body(
        own_ref,
        mask_ref,
        gains_ref,
        sel_1_ref,
        sel_o_ref,
        sel_2_ref,
        q_ref,
        k_ref,
        v_ref,
        refs[:blocks],
        refs[blocks : 2 * blocks],
        *refs[2 * blocks :],
    )


def middle_body(
    own_ref,
    mask_ref,
    gains_ref,
    sel_1_ref,
    sel_o_ref,
    sel_2_ref,
    q_ref,
    k_ref,
    v_ref,
    mine_refs,
    got_refs,
    soft_ref,
    lifted_ref,
    out_ref,
    grad_middle_ref,
    gain_ref,
    keep_ref,
    send_ref,
    early_ref,
    scores,
    wo,
    w1,
    w2,
    att,
    outs,
    sums,
    middle,
    second,
    pre,
    grad_hidden,
    hidden,
    grad_pre,
    wire,
    parted,
):
    core = lax.axis_index("core")
    blocks, _, rows_slots, _ = own_ref.shape
    parts = early_ref.shape[0]
    per_block = D // blocks
    gain = gains_ref[1:2, :]

    left = gather_parts(mine_refs, got_refs, 1, early_ref)
    right = gather_parts(mine_refs, got_refs, 2, early_ref)
    span = parts // 2 * LANES
    for half in range(2):
        w1[:, half * FF // 2 : (half + 1) * FF // 2] = dot(
            left[:, half * span : (half + 1) * span], sel_1_ref[...]
        ).astype(BF16)
    out_weight = dot(left, sel_o_ref[...]).astype(BF16)
    for h in range(HEADS):
        wo[h, :HEAD_DIM] = out_weight[h * HEAD_DIM : (h + 1) * HEAD_DIM]
        wo[h, HEAD_DIM:] = jnp.zeros((LANES - HEAD_DIM, D), BF16)
    for g in range(4):
        part = dot(right, sel_2_ref[g])
        for r in range(blocks):
            start = r * 4 * per_block + g * per_block
            w2[start : start + per_block] = part[r * per_block : (r + 1) * per_block].astype(BF16)

    for h in range(HEADS):
        scores[...] = dot_nt(k_ref[h], q_ref[h])

        def top_step(i, top):
            values = scores[pl.ds(pl.multiple_of(i * 64, 64), 64), :]
            return jnp.maximum(top, jnp.max(values.reshape(8, 8, OWN), 0))

        top = lax.fori_loop(1, SLOTS // 64, top_step, jnp.max(scores[:64].reshape(8, 8, OWN), 0), unroll=True)
        top = jnp.max(top, 0, keepdims=True)

        def soft_step(i, _, h=h, top=top):
            place = pl.ds(pl.multiple_of(i * 128, 128), 128)
            soft_ref[h, place, :] = jnp.exp(scores[place, :] - top).astype(BF16)
            return 0

        lax.fori_loop(0, SLOTS // 128, soft_step, 0, unroll=True)
        raw = dot_tn(v_ref[h], soft_ref[h]).T
        total = raw[:, HEAD_DIM : HEAD_DIM + 1]
        sums[h] = jnp.broadcast_to(1.0 / total, (OWN, LANES))
        result = raw * sums[h]
        outs[h] = result
        att[h] = result.astype(BF16)

    branch = dot(att[0], wo[0]) + dot(att[1], wo[1]) + dot(att[2], wo[2])
    middle[...] = branch

    def own_mask(block):
        start = pl.multiple_of((block * 2 + core) * rows_slots, rows_slots)
        return widen(mask_ref[pl.ds(start, rows_slots), :])

    def norm_step(block, _):
        place = pl.ds(pl.multiple_of(block * rows_slots, rows_slots), rows_slots)
        mid = own_ref[block, 0].astype(F32) + middle[place, :] * own_mask(block)
        middle[place, :] = mid
        unit, _ = normalise(mid)
        second[place, :] = (unit * gain).astype(BF16)
        return 0

    for block in range(blocks):
        norm_step(block, 0)

    pre[...] = dot(second[...], w1[...])
    cot = jnp.concatenate([own_ref[b, 1] for b in range(blocks)], axis=0)
    grad_hidden[...] = dot_nt(cot, w2[...])

    def gelu_step(i, _):
        place = pl.ds(pl.multiple_of(i * 16, 16), 16)
        x = pre[place, :]
        phi = 0.5 * (1.0 + lax.erf(x * np.float32(0.5**0.5)))
        hidden[place, :] = (x * phi).astype(BF16)
        slope = phi + x * jnp.exp(x * x * -0.5) * np.float32((2 * np.pi) ** -0.5)
        grad_pre[place, :] = (grad_hidden[place, :] * slope).astype(BF16)
        return 0

    lax.fori_loop(0, OWN // 16, gelu_step, 0, unroll=True)

    out_ref[...] = (middle[...] + dot(hidden[...], w2[...])).astype(BF16)
    grad_2 = dot_tn(hidden[...], cot).astype(BF16)
    grad_1 = dot_tn(second[...], grad_pre[...]).astype(BF16)
    grad_middle_ref[...] = dot_nt(grad_pre[...], w1[...])

    def back_step(block, total):
        place = pl.ds(pl.multiple_of(block * rows_slots, rows_slots), rows_slots)
        unit, inverse = normalise(middle[place, :])
        grad = grad_middle_ref[place, :]
        total = total + jnp.sum(grad * unit, 0, keepdims=True)
        grad = own_ref[block, 1].astype(F32) + norm_back(grad, gain, unit, inverse)
        grad_middle_ref[place, :] = grad
        second[place, :] = (grad * own_mask(block)).astype(BF16)
        return total

    gain_two = jnp.zeros((1, D), F32)
    for block in range(blocks):
        gain_two = back_step(block, gain_two)
    gain_ref[...] = gain_two

    grad_o = []
    lane_own = lax.broadcasted_iota(jnp.int32, (OWN, LANES), 1)
    for h in range(HEADS):
        grad_o.append(dot_tn(att[h], second[...])[:HEAD_DIM])
        grad_att = dot_nt(second[...], wo[h]).astype(BF16).astype(F32)
        scaled = (grad_att * sums[h]).astype(BF16).astype(F32)
        shift = -jnp.sum(scaled * outs[h], -1, keepdims=True)
        high = shift.astype(BF16).astype(F32)
        lifted = jnp.where(
            lane_own == HEAD_DIM, high, jnp.where(lane_own == HEAD_DIM + 1, shift - high, scaled)
        )
        lifted_ref[h] = lifted.astype(BF16)

    for half in range(2):
        wire[:, half * span : (half + 1) * span] = dot_nt(
            grad_1[:, half * FF // 2 : (half + 1) * FF // 2], sel_1_ref[...]
        )
    grad_o = jnp.concatenate(grad_o, axis=0).astype(BF16)
    wire[...] += dot_nt(grad_o, sel_o_ref[...])

    def deliver(lanes):
        for m in range(parts):
            parted[m] = wire[:, m * LANES : (m + 1) * LANES].astype(BF16)
        for z in range(parts // 2):
            put_blocks(keep_ref, z, lanes, parted[2 * z + core])
            put_blocks(send_ref, z, lanes, parted[2 * z + 1 - core])

    deliver(slice(0, LANES))
    total = None
    for g in range(4):
        rows = [
            grad_2[r * 4 * per_block + g * per_block : r * 4 * per_block + (g + 1) * per_block]
            for r in range(blocks)
        ]
        part = dot_nt(jnp.concatenate(rows, axis=0), sel_2_ref[g])
        total = part if total is None else total + part
    wire[...] = total
    deliver(slice(LANES, 2 * LANES))


def attention_back_kernel(
    soft_ref,
    lifted_ref,
    q_ref,
    k_ref,
    v_ref,
    scanned_ref,
    wqkv_ref,
    part_ref,
    grad_w_ref,
    scores,
    grad_scores,
    triple,
    grad_q,
    scanned_own,
    part,
    *,
    blocks,
):
    core = lax.axis_index("core")
    rows_slots = OWN // blocks
    for h in range(HEADS):
        tile = slice(h * LANES, (h + 1) * LANES)
        scores[...] = dot_nt(v_ref[h], lifted_ref[h])

        def back_step(i, _, h=h):
            place = pl.ds(pl.multiple_of(i * 64, 64), 64)
            grad_scores[place, :] = (soft_ref[h, place, :].astype(F32) * scores[place, :]).astype(
                BF16
            )
            return 0

        lax.fori_loop(0, SLOTS // 64, back_step, 0, unroll=True)
        grad_q[:, tile] = (dot_tn(k_ref[h], grad_scores[...]).T.astype(BF16) * HEAD_DIM ** (-0.5)).astype(
            BF16
        )
        triple[0, :, tile] = dot(grad_scores[...], q_ref[h]).astype(BF16)
        triple[1, :, tile] = dot(soft_ref[h], lifted_ref[h]).astype(BF16)

    part[...] = dot_nt(triple[0], wqkv_ref[1]) + dot_nt(triple[1], wqkv_ref[2])
    from_q = dot_nt(grad_q[...], wqkv_ref[0])
    for block in range(blocks):
        here = slice(block * rows_slots, (block + 1) * rows_slots)
        place = pl.ds(pl.multiple_of((block * 2 + core) * rows_slots, rows_slots), rows_slots)
        part[place, :] += from_q[here]
        scanned_own[here, :] = scanned_ref[place, :]
    part_ref[...] = part[...].astype(BF16)
    grad_w_ref[0] = dot_tn(scanned_own[...], grad_q[...]).astype(BF16)
    grad_w_ref[1] = dot_tn(scanned_ref[...], triple[0]).astype(BF16)
    grad_w_ref[2] = dot_tn(scanned_ref[...], triple[1]).astype(BF16)


def scan_back_kernel(
    starts,
    width,
    own_ref,
    mask_ref,
    part_ref,
    got_ref,
    mixed_ref,
    first_ref,
    table_ref,
    rates_ref,
    wu_ref,
    grad_w_ref,
    gain_two_ref,
    sel_u_ref,
    sel_rc_ref,
    sel_q_ref,
    keep_ref,
    send_ref,
    back_ref,
    gs_wide,
    gs_pairs,
    gt_wide,
    gt_pairs,
    xs_wide,
    xs_pairs,
    xt_wide,
    xt_pairs,
    rows_wide,
    rows_pairs,
    cols_wide,
    cols_pairs,
    grads_ref,
    own,
    own_tail,
    together,
    lag_sums,
    lag_lines,
    lag_rows,
    mixed_back,
    wire,
    parted,
):
    gs, gt = (gs_wide, gs_pairs), (gt_wide, gt_pairs)
    xs, xt = (xs_wide, xs_pairs), (xt_wide, xt_pairs)
    rows, cols = (rows_wide, rows_pairs), (cols_wide, cols_pairs)
    core = lax.axis_index("core")
    blocks, _, rows_slots, _ = own_ref.shape
    half_rows = rows_slots // GRID
    own_rows = GRID // 2
    parts = sel_rc_ref.shape[0] // LANES
    put_columns(*xs, mixed_ref[...].astype(F32))
    grads = (part_ref[...].astype(F32) + got_ref[...].astype(F32)) * widen(mask_ref[...])
    grads = grads.astype(BF16)
    grads_ref[...] = grads
    put_columns(*gs, grads.astype(F32))

    def place_of(block):
        return pl.ds(pl.multiple_of((block * 2 + core) * rows_slots, rows_slots), rows_slots)

    for source, dst in ((grads_ref, gt), (mixed_ref, xt)):
        for block in range(blocks):
            here = slice(block * rows_slots, (block + 1) * rows_slots)
            value = source[place_of(block), :].astype(F32)
            own[here, :] = value[:, :LANES]
            own_tail[here, :] = value[:, LANES:]
        put_rows(*dst, own, own_tail[...], together)

    for kind, sublane in units(0):
        step = gt[kind].shape[0] // GRID
        for t, value in enumerate(toeplitz(gt, table_ref, 0, kind, sublane, -1)):
            rows[kind][t * step + sublane : t * step + sublane + 8, :] = value

    def col_step(index, _):
        for kind, sublane in units(index):
            step = gs[kind].shape[0] // GRID
            found = toeplitz(gs, table_ref, 1, kind, sublane, -1, half_rows)
            for t, value in enumerate(found):
                cols[kind][pl.ds(pl.multiple_of(t * step + sublane, 8), 8), :] = value
        return 0

    lax.fori_loop(0, 2, col_step, 0)

    lag_sums[...] = jnp.zeros_like(lag_sums)

    for kind, sublane in units(0):
        add_lags(lag_sums, 0, kind, sublane, gt, xt)

    def lag_step(index, _):
        for kind, sublane in units(index):
            add_lags(lag_sums, 1, kind, sublane, gs, xs, half_rows)
        return 0

    lax.fori_loop(0, 2, lag_step, 0)
    for way in range(2):
        for kind in range(2):
            for lag, value in enumerate(gather_lags(lag_sums, way, kind)):
                lag_lines[way, kind, lag] = value
            lag_lines[way, kind, LAGS - 1] = jnp.zeros((8, LANES), F32)

    for way in range(2):
        lag_rows[way, :, :LANES] = jnp.sum(lag_lines[way, 0], 1)
        tail = jnp.sum(lag_lines[way, 1], 1)
        tail = tail[:, : D - LANES] + tail[:, D - LANES :]
        lag_rows[way, :, LANES:] = pair_lanes(tail, jnp.zeros_like(tail))

    decay, coef = rates_ref[: 4 * STATE], rates_ref[4 * STATE :]

    to_rate, to_coef = [], []
    for d in range(4):
        way, side = divmod(d, 2)
        rate = decay[d * STATE : (d + 1) * STATE]
        rate_sum = jnp.zeros((STATE, 2 * LANES), F32)
        coef_sum = jnp.broadcast_to(lag_rows[way, CENTER : CENTER + 1, :], (STATE, 2 * LANES))
        for k in range(1, GRID):
            at = CENTER - k if side else CENTER + k
            line = jnp.broadcast_to(lag_rows[way, at : at + 1, :], (STATE, 2 * LANES))
            scaled = line * jnp.exp(rate * float(-k))
            coef_sum = coef_sum + scaled
            rate_sum = rate_sum - scaled * float(k)
        to_rate.append(rate_sum)
        to_coef.append(coef_sum)
    to_rate, to_coef = jnp.concatenate(to_rate, axis=0), jnp.concatenate(to_coef, axis=0)
    grad_rc = jnp.concatenate([to_rate * coef, to_coef], axis=0).T[:D].astype(BF16)

    def join_step(i, _):
        for row, value in join_rows(i, own_rows, rows, cols):
            at = ((row // half_rows * 2 + core) * half_rows + row % half_rows) * GRID
            mask = mask_ref[pl.ds(pl.multiple_of(at, GRID), GRID), :]
            place = pl.ds(pl.multiple_of(row * GRID, GRID), GRID)
            mixed_back[place, :] = (value * widen(mask)).astype(BF16)
        return 0

    lax.fori_loop(0, own_rows // 2, join_step, 0, unroll=True)
    grad_u = dot_tn(first_ref[...], mixed_back[...]).astype(BF16)
    grad_first = dot_nt(mixed_back[...], wu_ref[...])
    back_ref[...] = grad_first
    gain_one = jnp.zeros((1, D), F32)
    for block in range(blocks):
        here = slice(block * rows_slots, (block + 1) * rows_slots)
        unit, _ = normalise(own_ref[block, 0].astype(F32))
        gain_one = gain_one + jnp.sum(grad_first[here] * unit, 0, keepdims=True)

    wire[...] = dot_nt(grad_u, sel_u_ref[...]) + dot_nt(grad_rc, sel_rc_ref[...])
    for third in range(3):
        span = slice(starts[third] * LANES, (starts[third] + width) * LANES)
        wire[:, span] += dot_nt(grad_w_ref[third], sel_q_ref[third])
    for m in range(parts):
        parted[m] = wire[:, m * LANES : (m + 1) * LANES].astype(BF16)
    for z in range(parts // 2):
        put_late(keep_ref, z, parted[2 * z + core])
        put_late(send_ref, z, parted[2 * z + 1 - core])

    lines = []
    for value in (gain_one, gain_two_ref[...]):
        high = value.astype(BF16).astype(F32)
        for piece in (high, value - high):
            lines.append(piece[:, :LANES])
            lines.append(
                jnp.concatenate([piece[:, LANES:], jnp.zeros((1, 2 * LANES - D), F32)], axis=1)
            )
    lines = jnp.concatenate(lines, axis=0).astype(BF16)
    for ref in (keep_ref, send_ref):
        ref[ref.shape[0] - 1, :8] = lines
        ref[ref.shape[0] - 1, 8:] = jnp.zeros((ref.shape[1] - 8, LANES), BF16)


def last_norm_kernel(own_ref, gains_ref, back_ref, grad_middle_ref, *routed_refs):
    _, _, slots, _ = own_ref.shape
    gain = gains_ref[0:1, :]
    for k, routed in enumerate(routed_refs):
        block = lax.axis_index("row") ^ k
        place = pl.ds(pl.multiple_of(block * slots, slots), slots)
        unit, inverse = normalise(own_ref[block, 0].astype(F32))
        grad = grad_middle_ref[place, :] + norm_back(back_ref[place, :], gain, unit, inverse)
        routed[...] = pack(grad.astype(BF16))


def aligned(rows):
    return (rows + 15) // 16 * 16


def spare_lanes(rows, parts):
    return rows >= 32 and 4 * (D // parts) + 32 <= LANES


def split(value):
    high = value.astype(BF16).astype(F32)
    return jnp.concatenate([high, value - high], axis=0)


def early_sum_kernel(out_own_ref, keep_ref, got_ref, *out_refs):
    _, depth, rows, _ = keep_ref.shape
    slots = OWN // len(out_refs)
    block_rows = aligned(rows)
    for k, out_ref in enumerate(out_refs):
        block = lax.axis_index("row") ^ k
        for z in range(depth):
            total = keep_ref[block, z].astype(F32) + got_ref[block, z].astype(F32)
            out_ref[z * block_rows : z * block_rows + rows] = total.astype(BF16)
        place = pl.ds(pl.multiple_of(block * slots, slots), slots)
        out_ref[depth * block_rows :] = fold(pack(out_own_ref[place, :]))


def late_sum_kernel(depth, keep_ref, got_ref, *refs):
    count = len(refs) // 2
    routed_refs, out_refs = refs[:count], refs[count:]
    rows = keep_ref.shape[1]
    block_rows = aligned(rows)
    last = keep_ref.shape[0] - 1
    gains = keep_ref[last, :8].astype(F32) + got_ref[last, :8].astype(F32)
    lines = []
    for g in range(2):
        for lane in range(2):
            at = 4 * g + lane
            lines.append(gains[at : at + 1] + gains[at + 2 : at + 3])
    gains = split(jnp.concatenate(lines, axis=0))
    gains = jnp.concatenate([gains, jnp.zeros((8, LANES), F32)], axis=0).astype(BF16)
    for k, out_ref in enumerate(out_refs):
        block = lax.axis_index("row") ^ k
        for z in range(depth):
            at = block * depth + z
            total = keep_ref[at].astype(F32) + got_ref[at].astype(F32)
            out_ref[z * block_rows : z * block_rows + rows] = total.astype(BF16)
        out_ref[depth * block_rows : depth * block_rows + 16] = gains
        out_ref[depth * block_rows + 16 :] = routed_refs[k][...]


def row_sum_kernel(blocks, depth, rows, *refs):
    early_refs, late_refs, out_refs = refs[:blocks], refs[blocks : 2 * blocks], refs[2 * blocks :]
    block_rows = aligned(rows)
    gains = late_refs[0][depth * block_rows : depth * block_rows + 16].astype(F32)
    for k in range(1, blocks):
        gains = gains + late_refs[k][depth * block_rows : depth * block_rows + 16].astype(F32)
    gains = split(gains[:4] + gains[4:8])
    for j, out_ref in enumerate(out_refs):
        z = lax.axis_index("z") ^ j
        place = pl.ds(pl.multiple_of(z * block_rows, 16), block_rows)
        early = early_refs[0][place, :].astype(F32)
        late = late_refs[0][place, :].astype(F32)
        for k in range(1, blocks):
            early = early + early_refs[k][place, :].astype(F32)
            late = late + late_refs[k][place, :].astype(F32)
        if spare_lanes(rows, 2 * depth):
            chunks = [gains[:, q * 32 : (q + 1) * 32] for q in range(4)]
            chunks.append(jnp.zeros((rows - 32, 32), F32))
            early = jnp.concatenate([early[:, :-32], jnp.concatenate(chunks, axis=0)], axis=1)
        else:
            out_ref[rows:, :LANES] = jnp.concatenate(
                [gains, jnp.zeros((8, LANES), F32)], axis=0
            ).astype(BF16)
            out_ref[rows:, LANES:] = jnp.zeros((16, 2 * LANES), BF16)
        out_ref[:rows, LANES:] = early[:rows].astype(BF16)
        out_ref[:rows, :LANES] = late[:rows].astype(BF16)


def final_kernel(parts, *refs):
    final_body(parts, refs[: parts // 2], *refs[parts // 2 :])


def final_body(
    parts,
    got_refs,
    g1_ref,
    g2_ref,
    wu_ref,
    rate_ref,
    coef_ref,
    qkv_ref,
    wo_ref,
    fc1_ref,
    fc2_ref,
):
    a_u, a_r, a_q, (o_u, o_r, o_c, o_q) = late_layout(parts)
    total = got_refs[0][...].astype(F32)
    for ref in got_refs[1:]:
        total = total + ref[...].astype(F32)
    early = total[: fc1_ref.shape[0], LANES:]
    total = total[:, :LANES]
    rows = fc1_ref.shape[0]
    weights = total[:rows]
    if spare_lanes(rows, parts):
        gains = jnp.concatenate(
            [early[q * 8 : (q + 1) * 8, 2 * LANES - 32 :] for q in range(4)], axis=1
        )
    else:
        gains = total[rows:]
    turned = weights.T
    wu_ref[...] = turned[o_u : o_u + a_u]
    rate_ref[...] = turned[o_r : o_r + a_r]
    coef_ref[...] = turned[o_c : o_c + a_r]
    qkv_ref[...] = weights[:, o_q : o_q + a_q]
    gains = gains[0:4] + gains[4:8]
    for g, ref in ((0, g1_ref), (1, g2_ref)):
        ref[...] = jnp.concatenate(
            [gains[2 * g : 2 * g + 1], gains[2 * g + 1 : 2 * g + 2, : D - LANES]], axis=1
        )
    a_1, a_o = FF // parts, D // parts
    fc1_ref[...] = early[:, :a_1]
    wo_ref[...] = early[:, :LANES].T[a_1 : a_1 + a_o]
    turned = early[:, LANES:].T
    fc2_ref[...] = jnp.concatenate([turned[g * a_o : (g + 1) * a_o] for g in range(4)], axis=1)


def per_device(
    patches, valid_mask, norm_gains, w_u, decay_rate, out_coef, w_qkv, w_o, w_fc1, w_fc2, cotangent
):
    images, rows_here, _, _ = patches.shape
    depth, blocks = lax.axis_size("z"), lax.axis_size("row")
    parts = 2 * depth
    rows_slots = rows_here // 2 * GRID
    packed_rows = rows_slots * 3 // 2
    swap = [(0, 1), (1, 0)]
    shape = jax.ShapeDtypeStruct

    def planes(slots):
        return [pltpu.VMEM((slots, LANES), F32), pltpu.VMEM((slots // 2, LANES), F32)]

    def swapped(value):
        return lax.ppermute(value, "core", swap)

    def exchanged(values, axis):
        size = len(values)
        return [values[0]] + [
            lax.ppermute(values[k], axis, [(i, i ^ k) for i in range(size)]) for k in range(1, size)
        ]

    def to_chips(value, j):
        pairs = []
        for home in range(2):
            for source in range(blocks):
                target, image = divmod(source ^ j, images)
                pairs.append((home * blocks + source, target * blocks + home * images + image))
        return lax.ppermute(value, ("core", "row"), pairs)

    starts, width = late_spans(parts)
    sel_1, sel_o, sel_2 = early_selections(parts)

    rows_weight = w_u.shape[0]
    payload = shape((2 * packed_rows + GRID, LANES), BF16)
    shard = shape((rows_weight, 3 * LANES), BF16)
    sources = [value.reshape(images, rows_here * GRID, D) for value in (patches, cotangent)]
    if rows_weight % 16 == 0:
        weights, *routed = pl.pallas_call(
            depart_kernel,
            name="depart",
            out_shape=(shard,) + (payload,) * blocks,
            in_specs=[VMEM] * 10,
            out_specs=[VMEM] * (1 + blocks),
            compiler_params=compiler(LARGE),
        )(
                w_u.T,
            decay_rate.T,
            out_coef.T,
            w_o.T,
            w_fc2.T,
            w_qkv,
            w_fc1,
            *sources,
            valid_mask,
        )
    else:

        def fill(pieces):
            joined = jnp.concatenate(pieces, axis=1)
            return jnp.pad(joined, ((0, 0), (0, LANES - joined.shape[1])))

        weights = jnp.concatenate(
            [
                fill([w_u, decay_rate, out_coef, w_qkv]),
                fill([w_fc1, w_o]),
                fill([w_fc2[g * rows_weight : (g + 1) * rows_weight] for g in range(4)]),
            ],
            axis=1,
        )
        routed = pl.pallas_call(
            route_kernel,
            name="route",
            out_shape=(payload,) * blocks,
            in_specs=[VMEM] * 3,
            out_specs=[VMEM] * blocks,
            compiler_params=compiler(LARGE),
        )(*sources, valid_mask)

    weights = jnp.stack(exchanged([weights] * depth, "z"))
    weights = exchanged([weights] * blocks, "row")
    weights = weights + [swapped(value) for value in weights]
    routed = [to_chips(value, j) for j, value in enumerate(routed)]
    own, first_own, mask, sel_u, sel_rc, sel_q = pl.pallas_call(
        lambda *refs: norm_kernel(starts, parts, *refs),
        name="first_norm",
        out_shape=(
            shape((blocks, 2, rows_slots, D), BF16),
            shape((OWN, D), BF16),
            shape((SLOTS, LANES), F32),
            shape((parts * LANES, D), BF16),
            shape((parts * LANES, LANES), BF16),
            shape((3, width * LANES, TILE), BF16),
        ),
        in_specs=[VMEM] * (1 + blocks),
        out_specs=[VMEM] * 6,
        compiler_params=compiler(8 << 20),
    )(norm_gains, *routed)
    first_other = swapped(first_own)

    head_own = shape((HEADS, OWN, LANES), BF16)
    head_all = shape((HEADS, SLOTS, LANES), BF16)
    part_scratch = pltpu.VMEM((parts, blocks, rows_weight, LANES), BF16)
    q, k, v, scanned, mixed, table, rates, wu, wqkv = pl.pallas_call(
        lambda *refs: scan_kernel(starts, width, *refs, blocks=blocks),
        name="scan_forward",
        out_shape=(
            head_own,
            head_all,
            head_all,
            shape((SLOTS, D), BF16),
            shape((SLOTS, D), BF16),
            shape((2, 2, 9 * 16, LANES), F32),
            shape((LANES, 2 * LANES), F32),
            shape((D, D), BF16),
            shape((3, D, TILE), BF16),
        ),
        in_specs=[VMEM] * (6 + 2 * blocks),
        out_specs=[VMEM] * 9,
        scratch_shapes=[part_scratch]
        + planes(SLOTS) * 4
        + [pltpu.VMEM((OWN, D), BF16), pltpu.VMEM((SLOTS, D), BF16)]
        + [pltpu.VMEM((2, 2, LAGS, LANES), F32)],
        compiler_params=compiler(),
    )(first_own, first_other, mask, sel_u, sel_rc, sel_q, *weights)

    wire_early = shape((blocks, depth, rows_weight, 2 * LANES), BF16)
    soft, lifted, out_own, grad_middle, gain_two, early_keep, early_send = pl.pallas_call(
        middle_kernel,
        name="attention_and_feed_forward",
        out_shape=(
            shape((HEADS, SLOTS, OWN), BF16),
            head_own,
            shape((OWN, D), BF16),
            shape((OWN, D), F32),
            shape((1, D), F32),
            wire_early,
            wire_early,
        ),
        in_specs=[VMEM] * (9 + 2 * blocks),
        out_specs=[VMEM] * 7,
        scratch_shapes=[
            part_scratch,
            pltpu.VMEM((SLOTS, OWN), F32),
            pltpu.VMEM((HEADS, LANES, D), BF16),
            pltpu.VMEM((D, FF), BF16),
            pltpu.VMEM((FF, D), BF16),
            pltpu.VMEM((HEADS, OWN, LANES), BF16),
            pltpu.VMEM((HEADS, OWN, LANES), F32),
            pltpu.VMEM((HEADS, OWN, LANES), F32),
            pltpu.VMEM((OWN, D), F32),
            pltpu.VMEM((OWN, D), BF16),
            pltpu.VMEM((OWN, FF), F32),
            pltpu.VMEM((OWN, FF), F32),
            pltpu.VMEM((OWN, FF), BF16),
            pltpu.VMEM((OWN, FF), BF16),
            pltpu.VMEM((D, parts * LANES), F32),
            pltpu.VMEM((parts, D, LANES), BF16),
        ],
        compiler_params=compiler(),
    )(own, mask, norm_gains, sel_1, sel_o, sel_2, q, k, v, *weights)

    early_recv = swapped(early_send)

    part, grad_w = pl.pallas_call(
        lambda *refs: attention_back_kernel(*refs, blocks=blocks),
        name="attention_backward",
        out_shape=(shape((SLOTS, D), BF16), shape((3, D, TILE), BF16)),
        in_specs=[VMEM] * 7,
        out_specs=[VMEM] * 2,
        scratch_shapes=[
            pltpu.VMEM((SLOTS, OWN), F32),
            pltpu.VMEM((SLOTS, OWN), BF16),
            pltpu.VMEM((2, SLOTS, TILE), BF16),
            pltpu.VMEM((OWN, TILE), BF16),
            pltpu.VMEM((OWN, D), BF16),
            pltpu.VMEM((SLOTS, D), F32),
        ],
        compiler_params=compiler(),
    )(soft, lifted, q, k, v, scanned, wqkv)

    early_keep, early_recv, part = lax.optimization_barrier((early_keep, early_recv, part))
    payload = shape((depth * aligned(rows_weight) + packed_rows // 2, 2 * LANES), BF16)
    early = pl.pallas_call(
        early_sum_kernel,
        name="early_sum",
        out_shape=(payload,) * blocks,
        in_specs=[VMEM] * 3,
        out_specs=[VMEM] * blocks,
        compiler_params=compiler(8 << 20),
    )(out_own, early_keep, early_recv)
    early, part = lax.optimization_barrier((early, part))
    part_got = swapped(part)
    early = exchanged(early, "row")
    wire_late = shape((blocks * depth + 1, rows_weight, LANES), BF16)
    late_keep, late_send, back = pl.pallas_call(
        lambda *refs: scan_back_kernel(starts, width, *refs),
        name="scan_backward",
        out_shape=(wire_late, wire_late, shape((OWN, D), F32)),
        in_specs=[VMEM] * 14,
        out_specs=[VMEM] * 3,
        scratch_shapes=planes(SLOTS) + planes(OWN) + planes(SLOTS) + planes(OWN) * 3
        + [
            pltpu.VMEM((SLOTS, D), BF16),
            pltpu.VMEM((OWN, LANES), F32),
            pltpu.VMEM((OWN, D - LANES), F32),
            pltpu.VMEM((OWN // 2, LANES), F32),
            pltpu.VMEM((2, 2, 9 * 16, 8, LANES), F32),
            pltpu.VMEM((2, 2, LAGS, 8, LANES), F32),
            pltpu.VMEM((2, LAGS, 2 * LANES), F32),
            pltpu.VMEM((OWN, D), BF16),
            pltpu.VMEM((D, parts * LANES), F32),
            pltpu.VMEM((parts, D, LANES), BF16),
        ],
        compiler_params=compiler(),
    )(
        own,
        mask,
        part,
        part_got,
        mixed,
        first_own,
        table,
        rates,
        wu,
        grad_w,
        gain_two,
        sel_u,
        sel_rc,
        sel_q,
    )
    late_keep, late_send, early = lax.optimization_barrier((late_keep, late_send, early))
    payload = shape((packed_rows, LANES), BF16)
    routed = pl.pallas_call(
        last_norm_kernel,
        name="last_norm",
        out_shape=(payload,) * blocks,
        in_specs=[VMEM] * 4,
        out_specs=[VMEM] * blocks,
        compiler_params=compiler(8 << 20),
    )(own, norm_gains, back, grad_middle)
    payload = shape((depth * aligned(rows_weight) + 16 + packed_rows, LANES), BF16)
    late = pl.pallas_call(
        lambda *refs: late_sum_kernel(depth, *refs),
        name="late_sum",
        out_shape=(payload,) * blocks,
        in_specs=[VMEM] * (2 + blocks),
        out_specs=[VMEM] * blocks,
        compiler_params=compiler(8 << 20),
    )(late_keep, swapped(late_send), *routed)
    late = exchanged(late, "row")
    final_rows = rows_weight if spare_lanes(rows_weight, parts) else rows_weight + 16
    summed = pl.pallas_call(
        lambda *refs: row_sum_kernel(blocks, depth, rows_weight, *refs),
        name="row_sum",
        out_shape=(shape((final_rows, 3 * LANES), BF16),) * depth,
        in_specs=[VMEM] * (2 * blocks),
        out_specs=[VMEM] * depth,
        compiler_params=compiler(8 << 20),
    )(*early, *late)
    summed = exchanged(summed, "z")

    chosen = pl.pallas_call(
        choose_kernel,
        name="choose",
        out_shape=shape((images, 2 * packed_rows, LANES), BF16),
        in_specs=[VMEM] * (2 * blocks),
        out_specs=VMEM,
        compiler_params=compiler(8 << 20),
    )(*early, *late)
    whole = shape((images, rows_here * GRID, D), BF16)
    block_out, grad_patches = pl.pallas_call(
        home_kernel,
        name="home",
        out_shape=(whole, whole),
        in_specs=[VMEM] * (1 + 2 * blocks),
        out_specs=[VMEM] * 2,
        compiler_params=compiler(8 << 20),
    )(swapped(chosen), *early, *late)

    summed, block_out, grad_patches = lax.optimization_barrier((summed, block_out, grad_patches))
    turned = (4 * STATE // parts, rows_weight)
    g1, g2, f_u, f_rate, f_coef, f_qkv, f_o, f_1, f_2 = pl.pallas_call(
        lambda *refs: final_kernel(parts, *refs),
        name="final_sum",
        out_shape=(
            shape((1, D), F32),
            shape((1, D), F32),
            shape((D // parts, rows_weight), F32),
            shape(turned, F32),
            shape(turned, F32),
            shape((rows_weight, 3 * D // parts), F32),
            shape((D // parts, rows_weight), F32),
            shape((rows_weight, FF // parts), F32),
            shape((D // parts, 4 * rows_weight), F32),
        ),
        in_specs=[VMEM] * depth,
        out_specs=[VMEM] * 9,
        compiler_params=compiler(8 << 20),
    )(*summed)
    return (
        block_out.reshape(patches.shape),
        grad_patches.reshape(patches.shape),
        g1.reshape(D),
        g2.reshape(D),
        f_u.T,
        f_rate.T,
        f_coef.T,
        f_qkv,
        f_o.T,
        f_1,
        f_2.T,
    )


def solution(mesh):
    images, rows = mesh.devices.shape
    fine = Mesh(mesh.devices.reshape(images // 2, 2, rows), ("z", "core", "row"))
    img = ("z", "core")
    grid = P(img, "row", None, None)
    weight = P("row", img)
    in_specs = (grid, P(img, None, None), P()) + (weight,) * 7 + (grid,)
    out_specs = (grid, grid, P(), P()) + (weight,) * 7
    return jax.shard_map(
        per_device, mesh=fine, in_specs=in_specs, out_specs=out_specs, check_vma=False
    )
```

```python
import jax
import jax.numpy as jnp
import numpy as np
from jax import lax
from jax.experimental import pallas as pl
from jax.experimental.pallas import tpu as pltpu
from jax.sharding import Mesh
from jax.sharding import PartitionSpec as P

HEADS = 3
HEAD_DIM = 64
STATE = 16
GRID = 32
SLOTS = GRID * GRID
OWN = SLOTS // 2
D = HEADS * HEAD_DIM
FF = 4 * D
LANES = 128
TILE = HEADS * LANES
LAGS = 2 * GRID
CENTER = GRID - 1
EPS = 1e-05
BF16 = jnp.bfloat16
F32 = jnp.float32


def late_layout(parts):
    a_u, a_r, a_q = D // parts, 4 * STATE // parts, 3 * D // parts
    return a_u, a_r, a_q, (0, a_u, a_u + a_r, a_u + 2 * a_r)


def late_spans(parts):
    a_q = 3 * D // parts
    first = [third * D // a_q for third in range(3)]
    last = [((third + 1) * D - 1) // a_q for third in range(3)]
    width = max(stop - start + 1 for start, stop in zip(first, last))
    return [min(start, parts - width) for start in first], width


def early_selections(parts):
    a_1, a_o = FF // parts, D // parts
    half = parts // 2
    sel_1 = np.zeros((half, LANES, FF // 2), np.float32)
    sel_o = np.zeros((parts, LANES, D), np.float32)
    sel_2 = np.zeros((4, parts, LANES, D), np.float32)
    for m in range(half):
        for col in range(a_1):
            sel_1[m, col, m * a_1 + col] = 1
    for m in range(parts):
        for col in range(a_o):
            sel_o[m, a_1 + col, m * a_o + col] = 1
            for g in range(4):
                sel_2[g, m, g * a_o + col, m * a_o + col] = 1
    return (
        sel_1.reshape(half * LANES, FF // 2).astype(BF16),
        sel_o.reshape(parts * LANES, D).astype(BF16),
        sel_2.reshape(4, parts * LANES, D).astype(BF16),
    )


def lane_and_part(shape):
    place = lax.broadcasted_iota(jnp.int32, shape, 0)
    return place % LANES, place // LANES, lax.broadcasted_iota(jnp.int32, shape, 1)


def put_late_selections(starts, parts, sel_u_ref, sel_rc_ref, sel_q_ref):
    a_u, a_r, a_q, (o_u, o_r, o_c, o_q) = late_layout(parts)

    def put(hit):
        return jnp.where(hit, 1.0, 0.0).astype(BF16)

    lane, part, col = lane_and_part(sel_u_ref.shape)
    sel_u_ref[...] = put((lane < a_u) & (part * a_u + lane == col))
    lane, part, col = lane_and_part(sel_rc_ref.shape)
    rate = (lane >= o_r) & (lane < o_c) & (part * a_r + lane - o_r == col)
    coef = (lane >= o_c) & (lane < o_q) & (part * a_r + lane - o_c + 4 * STATE == col)
    sel_rc_ref[...] = put(rate | coef)
    lane, part, col = lane_and_part(sel_q_ref.shape[1:])
    whole = jnp.where(
        col % LANES < HEAD_DIM, col // LANES * HEAD_DIM + col % LANES, -4 * D
    )
    for third in range(3):
        here = (part + starts[third]) * a_q + lane - o_q - third * D
        sel_q_ref[third] = put((lane >= o_q) & (lane < o_q + a_q) & (here == whole))


def dot(a, b):
    return lax.dot_general(a, b, (((1,), (0,)), ((), ())), preferred_element_type=F32)


def dot_nt(a, b):
    return lax.dot_general(a, b, (((1,), (1,)), ((), ())), preferred_element_type=F32)


def dot_tn(a, b):
    return lax.dot_general(a, b, (((0,), (0,)), ((), ())), preferred_element_type=F32)


def normalise(values):
    center = values - jnp.mean(values, -1, keepdims=True)
    spread = jnp.mean(center * center, -1, keepdims=True)
    inverse = lax.rsqrt(spread + EPS)
    return center * inverse, inverse


def norm_back(grad, gain, unit, inverse):
    scaled = grad * gain
    first = jnp.mean(scaled, -1, keepdims=True)
    second = jnp.mean(scaled * unit, -1, keepdims=True)
    return inverse * (scaled - first - unit * second)


def widen(mask):
    return jnp.concatenate([mask, mask[:, : D - LANES]], axis=1)


def put_blocks(ref, z, lanes, value):
    rows = ref.shape[2]
    for r in range(ref.shape[0]):
        ref[r, z, :, lanes] = value[r * rows : (r + 1) * rows]


def put_late(ref, z, value):
    rows = ref.shape[1]
    depth = ref.shape[0] * rows // D
    for r in range(D // rows):
        ref[r * depth + z] = value[r * rows : (r + 1) * rows]


def pair_lanes(first, second):
    return jnp.concatenate([first, second], axis=1)


def put_columns(wide, pairs, values):
    wide[...] = values[:, :LANES]
    tail = values[:, LANES:].reshape(values.shape[0] // GRID, 2, GRID // 2, D - LANES)
    tail = pair_lanes(tail[:, 0].reshape(-1, D - LANES), tail[:, 1].reshape(-1, D - LANES))
    pairs[...] = tail


def put_rows(wide, pairs, from_wide, tail, together):
    rows = from_wide.shape[0] // GRID
    together[...] = pair_lanes(tail[: rows // 2 * GRID], tail[rows // 2 * GRID :])
    for j in range(GRID):
        wide[j * rows : (j + 1) * rows, :] = from_wide[pl.ds(j, rows, stride=GRID), :]
        pairs[j * rows // 2 : (j + 1) * rows // 2, :] = together[pl.ds(j, rows // 2, stride=GRID), :]


def units(index):
    return [(0, (index * 2 + u) * 8) for u in range(2)] + [(1, index * 8)]


def lag_tables(lags):
    lines = []
    near = lags[16:47]
    for table in (near, lags[0:31] - near, lags[32:63] - near):
        center = table[8:23]
        for part in (center, table[0:15] - center, table[16:31] - center):
            lines += [part, jnp.zeros((1, LANES), F32)]
    return jnp.concatenate(lines, axis=0)


def plus(left, right):
    return [a + b for a, b in zip(left, right)]


def own_places(own_rows):
    if own_rows is None:
        return list(range(8)), 0
    places = [i // own_rows * 2 * own_rows + i % own_rows for i in range(4)]
    return places, lax.axis_index("core") * own_rows


def three(left, right, work):
    a, b = len(left) // 2, len(right) // 2
    work(0, plus(left[:a], left[a:]), plus(right[:b], right[b:]))
    work(1, left[:a], right[b:])
    work(2, left[a:], right[:b])


def add_lags(sums, way, kind, sublane, grads, values, own_rows=None):
    step = values[kind].shape[0] // GRID
    places, shift = own_places(own_rows)

    def line(ref, at):
        return ref[kind][pl.ds(pl.multiple_of(at * step + sublane, 8), 8), :]

    g = [line(grads, base + place + shift) for base in range(0, GRID, 8) for place in places]
    x = [line(values, s) for s in range(GRID)]

    def leaf(first, second, g, x):
        total = {}
        for i, t in enumerate(places):
            for s in range(8):
                term = g[i] * x[s]
                total[t - s] = term if t - s not in total else total[t - s] + term
        start = (first * 3 + second) * 16 + 7
        for lag, value in total.items():
            sums[way, kind, start + lag + shift] += value

    three(g, x, lambda p, g, x: three(g, x, lambda q, g, x: leaf(p, q, g, x)))


def gather_lags(sums, way, kind):
    def join(parts, reach):
        found = [None] * (2 * (2 * reach + 1) + 1)
        width = 2 * reach - 1
        middle = [a - b - c for a, b, c in zip(*parts)]
        for start, part in ((reach, middle), (0, parts[1]), (2 * reach, parts[2])):
            for i in range(width):
                at = start + i
                found[at] = part[i] if found[at] is None else found[at] + part[i]
        return found[: 4 * reach - 1]

    thirds = []
    for first in range(3):
        tables = [
            [sums[way, kind, (first * 3 + second) * 16 + i] for i in range(15)]
            for second in range(3)
        ]
        thirds.append(join(tables, 8))
    return join(thirds, 16)


def toeplitz(src, table, way, kind, sublane, sign, own_rows=None):
    step = src[kind].shape[0] // GRID
    places, shift = own_places(own_rows)
    shift = shift * sign

    def leaf(x, first, second):
        if sign < 0:
            first, second = (0, 2, 1)[first], (0, 2, 1)[second]
        start = (first * 3 + second) * 16 + 7
        coef = {}
        total = [None] * len(places)
        for s in range(8):
            for i, t in enumerate(places):
                lag = t - s
                if lag not in coef:
                    line = table[way, kind, pl.ds(start + lag * sign + shift, 1), :]
                    coef[lag] = jnp.broadcast_to(line, (8, LANES))
                term = coef[lag] * x[s]
                total[i] = term if total[i] is None else total[i] + term
        return total

    def quarter(x, first):
        middle = leaf(plus(x[:8], x[8:]), first, 0)
        return plus(middle, leaf(x[8:], first, 1)) + plus(middle, leaf(x[:8], first, 2))

    x = [src[kind][pl.ds(pl.multiple_of(s * step + sublane, 8), 8), :] for s in range(GRID)]
    middle = quarter(plus(x[:16], x[16:]), 0)
    return plus(middle, quarter(x[16:], 1)) + plus(middle, quarter(x[:16], 2))


def join_rows(i, count, rows, cols):
    half = GRID // 2
    narrow = D - LANES
    across = rows[1][pl.ds(i, GRID, stride=count // 2), :]
    found = []
    for which in range(2):
        row = i + which * (count // 2)
        wide = cols[0][pl.ds(pl.multiple_of(row * GRID, GRID), GRID), :].astype(BF16).astype(F32)
        wide = wide + rows[0][pl.ds(i + which * (count // 2), GRID, stride=count), :]
        pairs = cols[1][pl.ds(pl.multiple_of(row * half, half), half), :].astype(BF16).astype(F32)
        tail = jnp.concatenate([pairs[:, :narrow], pairs[:, narrow:]], axis=0)
        tail = tail + across[:, which * narrow : (which + 1) * narrow]
        found.append((row, jnp.concatenate([wide, tail], axis=1)))
    return found


def gather_parts(mine_refs, got_refs, block, out_ref):
    core, row, depth = lax.axis_index("core"), lax.axis_index("row"), lax.axis_index("z")
    lanes = slice(block * LANES, (block + 1) * LANES)
    count = out_ref.shape[0] // 2
    rows = out_ref.shape[2]
    for refs, which in ((mine_refs, core), (got_refs, 1 - core)):
        for k, ref in enumerate(refs):
            for j in range(count):
                out_ref[2 * (depth ^ j) + which, row ^ k] = ref[j, :, lanes]
    wide = []
    for m in range(2 * count):
        wide.append(jnp.concatenate([out_ref[m, r] for r in range(out_ref.shape[1])], axis=0))
    return jnp.concatenate(wide, axis=1)


LARGE = 60 << 20


def compiler(limit=24 << 20):
    return pltpu.CompilerParams(vmem_limit_bytes=limit)


VMEM = pl.BlockSpec(memory_space=pltpu.VMEM)


def pack(values):
    half = values.shape[0] // 2
    tail = jnp.concatenate([values[:half, LANES:], values[half:, LANES:]], axis=1)
    return jnp.concatenate([values[:, :LANES], tail], axis=0)


def unpack(packed):
    count = packed.shape[0] * 2 // 3
    tail = packed[count:]
    tail = jnp.concatenate([tail[:, : D - LANES], tail[:, D - LANES :]], axis=0)
    return jnp.concatenate([packed[:count], tail], axis=1)


def pack_weights_kernel(turned_refs, qkv_ref, fc1_ref, out_ref):
    wu, rate, coef, wo, fc2 = [ref[...].astype(F32) for ref in turned_refs]
    rows = qkv_ref.shape[0]
    a_o, a_r = wo.shape[0], rate.shape[0]
    pieces = [wu, rate, coef, wo] + [fc2[:, g * rows : (g + 1) * rows] for g in range(4)]
    joined = jnp.concatenate(pieces, axis=0)
    joined = jnp.concatenate([joined, jnp.zeros((joined.shape[0], LANES - rows), F32)], axis=1)
    joined = joined.T[:rows]
    first, second = a_o + 2 * a_r, 2 * a_o + 2 * a_r

    def fill(parts):
        used = sum(part.shape[1] for part in parts)
        return parts + [jnp.zeros((rows, LANES - used), F32)]

    packed = jnp.concatenate(
        fill([joined[:, :first], qkv_ref[...].astype(F32)])
        + fill([fc1_ref[...].astype(F32), joined[:, first:second]])
        + fill([joined[:, second:]]),
        axis=1,
    ).astype(BF16)
    out_ref[...] = packed


def route_kernel(patch_ref, cot_ref, valid_ref, *out_refs):
    row = lax.axis_index("row")
    images, slots, _ = patch_ref.shape
    half = slots // 2
    packed = half * 3 // 2
    for j, out_ref in enumerate(out_refs):
        target = row ^ j
        core, image = target // images, target % images
        place = pl.ds(pl.multiple_of(core * half, half), half)
        out_ref[:packed] = pack(patch_ref[image, place, :])
        out_ref[packed : 2 * packed] = pack(cot_ref[image, place, :])
        valid = valid_ref[image].astype(F32).astype(BF16)
        out_ref[2 * packed :] = jnp.concatenate(
            [valid, jnp.zeros((GRID, LANES - GRID), BF16)], axis=1
        )


def depart_kernel(*refs):
    turned, (qkv_ref, fc1_ref, patch_ref, cot_ref, valid_ref, out_ref) = refs[:5], refs[5:11]
    pack_weights_kernel(turned, qkv_ref, fc1_ref, out_ref)
    route_kernel(patch_ref, cot_ref, valid_ref, *refs[11:])


def norm_kernel(starts, parts, gains_ref, *refs):
    got_refs, refs = refs[:-6], refs[-6:]
    own_ref, first_ref, mask_ref, *selections = refs
    core, row = lax.axis_index("core"), lax.axis_index("row")
    images = len(got_refs) // 2
    gain = gains_ref[0:1, :]
    slots = own_ref.shape[2]
    packed = slots * 3 // 2
    for j, got in enumerate(got_refs):
        block = (core * images + row % images) ^ j
        patch = unpack(got[:packed])
        own_ref[block, 0] = patch
        own_ref[block, 1] = unpack(got[packed : 2 * packed])
        unit, _ = normalise(patch.astype(F32))
        first_ref[pl.ds(pl.multiple_of(block * slots, slots), slots), :] = (unit * gain).astype(
            BF16
        )
    valid = got_refs[0][2 * packed :].astype(F32).T
    for i in range(GRID):
        mask_ref[i * GRID : (i + 1) * GRID, :] = jnp.broadcast_to(
            valid[:GRID, i : i + 1], (GRID, LANES)
        )
    put_late_selections(starts, parts, *selections)


def fold(packed):
    half = packed.shape[0] // 2
    return jnp.concatenate([packed[:half], packed[half:]], axis=1)


def unfold(folded):
    return jnp.concatenate([folded[:, :LANES], folded[:, LANES:]], axis=0)


def results_of(early_ref, late_ref, rows):
    early_start, late_start = early_ref.shape[0] - rows // 2, late_ref.shape[0] - rows
    return unfold(early_ref[early_start:]), late_ref[late_start:]


def choose_kernel(*refs):
    got_refs, out_ref = refs[:-1], refs[-1]
    blocks = len(got_refs) // 2
    core, row = lax.axis_index("core"), lax.axis_index("row")
    images, rows = out_ref.shape[0], out_ref.shape[1] // 2
    for k, got in enumerate(zip(got_refs[:blocks], got_refs[blocks:])):
        image = row ^ k

        @pl.when(image // images != core)
        def _(got=got, image=image):
            for which, value in enumerate(results_of(*got, rows)):
                out_ref[image % images, which * rows : (which + 1) * rows] = value


def home_kernel(swapped_ref, *refs):
    got_refs, out_refs = refs[:-2], refs[-2:]
    core, row = lax.axis_index("core"), lax.axis_index("row")
    images, slots, _ = out_refs[0].shape
    half = slots // 2
    rows = half * 3 // 2
    blocks = len(got_refs) // 2
    mine = pl.ds(pl.multiple_of(core * half, half), half)
    theirs = pl.ds(pl.multiple_of((1 - core) * half, half), half)
    for k, got in enumerate(zip(got_refs[:blocks], got_refs[blocks:])):
        image = row ^ k

        @pl.when(image // images == core)
        def _(got=got, image=image):
            for out_ref, value in zip(out_refs, results_of(*got, rows)):
                out_ref[image % images, mine, :] = unpack(value)

    for image in range(images):
        for which, out_ref in enumerate(out_refs):
            value = swapped_ref[image, which * rows : (which + 1) * rows]
            out_ref[image, theirs, :] = unpack(value)


def scan_kernel(
    starts,
    width,
    first_own_ref,
    first_other_ref,
    mask_ref,
    sel_u_ref,
    sel_rc_ref,
    sel_q_ref,
    *refs,
    blocks,
):
    mine_refs, got_refs, refs = refs[:blocks], refs[blocks : 2 * blocks], refs[2 * blocks :]
    scan_body(
        starts,
        width,
        first_own_ref,
        first_other_ref,
        mask_ref,
        sel_u_ref,
        sel_rc_ref,
        sel_q_ref,
        mine_refs,
        got_refs,
        *refs,
    )


def scan_body(
    starts,
    width,
    first_own_ref,
    first_other_ref,
    mask_ref,
    sel_u_ref,
    sel_rc_ref,
    sel_q_ref,
    mine_refs,
    got_refs,
    q_ref,
    k_ref,
    v_ref,
    scanned_ref,
    mixed_ref,
    table_ref,
    rates_ref,
    wu_ref,
    wqkv_ref,
    late_ref,
    xs_wide,
    xs_pairs,
    xt_wide,
    xt_pairs,
    cols_wide,
    cols_pairs,
    rows_wide,
    rows_pairs,
    scanned_own,
    first_ref,
    lags,
):
    xs, xt = (xs_wide, xs_pairs), (xt_wide, xt_pairs)
    cols, rows = (cols_wide, cols_pairs), (rows_wide, rows_pairs)
    core = lax.axis_index("core")
    blocks = len(mine_refs)
    rows_slots = OWN // blocks

    late = gather_parts(mine_refs, got_refs, 0, late_ref)
    wu = dot(late, sel_u_ref[...]).astype(BF16)
    wu_ref[...] = wu
    rates = dot(late, sel_rc_ref[...])
    rates = jnp.concatenate([rates.T, jnp.zeros((LANES, 2 * LANES - D), F32)], axis=1)
    rates_ref[...] = rates
    for third in range(3):
        window = late[:, starts[third] * LANES : (starts[third] + width) * LANES]
        wqkv_ref[third] = dot(window, sel_q_ref[third]).astype(BF16)

    decay, coef = rates[: 4 * STATE], rates[4 * STATE :]

    def lag_row(k):
        powers = jnp.exp(-decay * k) * coef
        return [jnp.sum(powers[d * STATE : (d + 1) * STATE], 0, keepdims=True) for d in range(4)]

    def store_lag(way, lag, row):
        row = row.astype(BF16).astype(F32)
        tail = row[:, LANES:D]
        for kind, lanes in enumerate((row[:, :LANES], pair_lanes(tail, tail))):
            lags[way, kind, pl.ds(lag + CENTER, 1), :] = lanes

    def lag_step(k, _):
        found = lag_row(k.astype(F32))
        for way in range(2):
            store_lag(way, k, found[2 * way])
            store_lag(way, -k, found[2 * way + 1])
        return 0

    lax.fori_loop(0, GRID, lag_step, 0, unroll=True)
    found = lag_row(0.0)
    for way in range(2):
        store_lag(way, 0, found[2 * way] + found[2 * way + 1])
        for kind in range(2):
            table_ref[way, kind] = lag_tables(lags[way, kind])


    for block in range(blocks):
        here = slice(block * rows_slots, (block + 1) * rows_slots)
        for ref, which in ((first_own_ref, core), (first_other_ref, 1 - core)):
            start = pl.multiple_of((block * 2 + which) * rows_slots, rows_slots)
            first_ref[pl.ds(start, rows_slots), :] = ref[here, :]
    mixed = dot(first_ref[...], wu) * widen(mask_ref[...])
    mixed = mixed.astype(BF16)
    mixed_ref[...] = mixed
    mixed = mixed.astype(F32)
    put_columns(*xs, mixed)
    put_rows(*xt, xs[0], mixed[:, LANES:], cols[1])

    def scan_step(index, _):
        for way, src, dst in ((0, xt, rows), (1, xs, cols)):
            for kind, sublane in units(index):
                step = src[kind].shape[0] // GRID
                for t, value in enumerate(toeplitz(src, table_ref, way, kind, sublane, 1)):
                    dst[kind][pl.ds(pl.multiple_of(t * step + sublane, 8), 8), :] = value
        return 0

    lax.fori_loop(0, 2, scan_step, 0, unroll=True)

    def join_step(i, _):
        for row, value in join_rows(i, GRID, rows, cols):
            place = pl.ds(pl.multiple_of(row * GRID, GRID), GRID)
            scanned_ref[place, :] = (value * widen(mask_ref[place, :])).astype(BF16)
        return 0

    lax.fori_loop(0, GRID // 2, join_step, 0, unroll=True)

    for block in range(blocks):
        start = pl.multiple_of((block * 2 + core) * rows_slots, rows_slots)
        scanned_own[block * rows_slots : (block + 1) * rows_slots, :] = scanned_ref[
            pl.ds(start, rows_slots), :
        ]

    lane_own = lax.broadcasted_iota(jnp.int32, (OWN, LANES), 1)
    lane_all = lax.broadcasted_iota(jnp.int32, (SLOTS, LANES), 1)
    bias = jnp.where(lane_all == HEAD_DIM, (mask_ref[...] - 1.0) * 1e30, 0.0)
    ones = jnp.where((lane_all == HEAD_DIM) | (lane_all == HEAD_DIM + 1), 1.0, 0.0)
    one_own = jnp.where(lane_own == HEAD_DIM, 1.0, 0.0)
    found = dot(scanned_own[...], wqkv_ref[0]) * HEAD_DIM ** (-0.5)
    for h in range(HEADS):
        q_ref[h] = (found[:, h * LANES : (h + 1) * LANES] + one_own).astype(BF16)
    targets = [(k_ref, h, 1, bias) for h in range(HEADS)] + [(v_ref, h, 2, ones) for h in range(HEADS)]
    for pair in range(HEADS):
        two = targets[2 * pair : 2 * pair + 2]
        weight = [wqkv_ref[third, :, h * LANES : (h + 1) * LANES] for _, h, third, _ in two]
        found = dot(scanned_ref[...], jnp.concatenate(weight, axis=1))
        for i, (ref, h, _, extra) in enumerate(two):
            ref[h] = (found[:, i * LANES : (i + 1) * LANES] + extra).astype(BF16)


def middle_kernel(
    own_ref,
    mask_ref,
    gains_ref,
    sel_1_ref,
    sel_o_ref,
    sel_2_ref,
    q_ref,
    k_ref,
    v_ref,
    *refs,
):
    blocks = own_ref.shape[0]
    middle_body(
        own_ref,
        mask_ref,
        gains_ref,
        sel_1_ref,
        sel_o_ref,
        sel_2_ref,
        q_ref,
        k_ref,
        v_ref,
        refs[:blocks],
        refs[blocks : 2 * blocks],
        *refs[2 * blocks :],
    )


def middle_body(
    own_ref,
    mask_ref,
    gains_ref,
    sel_1_ref,
    sel_o_ref,
    sel_2_ref,
    q_ref,
    k_ref,
    v_ref,
    mine_refs,
    got_refs,
    soft_ref,
    lifted_ref,
    out_ref,
    grad_middle_ref,
    gain_ref,
    keep_ref,
    send_ref,
    early_ref,
    scores,
    wo,
    w1,
    w2,
    att,
    outs,
    sums,
    middle,
    second,
    pre,
    grad_hidden,
    hidden,
    grad_pre,
    wire,
    parted,
):
    core = lax.axis_index("core")
    blocks, _, rows_slots, _ = own_ref.shape
    parts = early_ref.shape[0]
    per_block = D // blocks
    gain = gains_ref[1:2, :]

    left = gather_parts(mine_refs, got_refs, 1, early_ref)
    right = gather_parts(mine_refs, got_refs, 2, early_ref)
    span = parts // 2 * LANES
    for half in range(2):
        w1[:, half * FF // 2 : (half + 1) * FF // 2] = dot(
            left[:, half * span : (half + 1) * span], sel_1_ref[...]
        ).astype(BF16)
    out_weight = dot(left, sel_o_ref[...]).astype(BF16)
    for h in range(HEADS):
        wo[h, :HEAD_DIM] = out_weight[h * HEAD_DIM : (h + 1) * HEAD_DIM]
        wo[h, HEAD_DIM:] = jnp.zeros((LANES - HEAD_DIM, D), BF16)
    for g in range(4):
        part = dot(right, sel_2_ref[g])
        for r in range(blocks):
            start = r * 4 * per_block + g * per_block
            w2[start : start + per_block] = part[r * per_block : (r + 1) * per_block].astype(BF16)

    for h in range(HEADS):
        scores[...] = dot_nt(k_ref[h], q_ref[h])

        def top_step(i, top):
            values = scores[pl.ds(pl.multiple_of(i * 64, 64), 64), :]
            return jnp.maximum(top, jnp.max(values.reshape(8, 8, OWN), 0))

        top = lax.fori_loop(1, SLOTS // 64, top_step, jnp.max(scores[:64].reshape(8, 8, OWN), 0), unroll=True)
        top = jnp.max(top, 0, keepdims=True)

        def soft_step(i, _, h=h, top=top):
            place = pl.ds(pl.multiple_of(i * 128, 128), 128)
            soft_ref[h, place, :] = jnp.exp(scores[place, :] - top).astype(BF16)
            return 0

        lax.fori_loop(0, SLOTS // 128, soft_step, 0, unroll=True)
        raw = dot_tn(v_ref[h], soft_ref[h]).T
        total = raw[:, HEAD_DIM : HEAD_DIM + 1]
        sums[h] = jnp.broadcast_to(1.0 / total, (OWN, LANES))
        result = raw * sums[h]
        outs[h] = result
        att[h] = result.astype(BF16)

    branch = dot(att[0], wo[0]) + dot(att[1], wo[1]) + dot(att[2], wo[2])
    middle[...] = branch

    def own_mask(block):
        start = pl.multiple_of((block * 2 + core) * rows_slots, rows_slots)
        return widen(mask_ref[pl.ds(start, rows_slots), :])

    def norm_step(block, _):
        place = pl.ds(pl.multiple_of(block * rows_slots, rows_slots), rows_slots)
        mid = own_ref[block, 0].astype(F32) + middle[place, :] * own_mask(block)
        middle[place, :] = mid
        unit, _ = normalise(mid)
        second[place, :] = (unit * gain).astype(BF16)
        return 0

    for block in range(blocks):
        norm_step(block, 0)

    pre[...] = dot(second[...], w1[...])
    cot = jnp.concatenate([own_ref[b, 1] for b in range(blocks)], axis=0)
    grad_hidden[...] = dot_nt(cot, w2[...])

    def gelu_step(i, _):
        place = pl.ds(pl.multiple_of(i * 16, 16), 16)
        x = pre[place, :]
        phi = 0.5 * (1.0 + lax.erf(x * np.float32(0.5**0.5)))
        hidden[place, :] = (x * phi).astype(BF16)
        slope = phi + x * jnp.exp(x * x * -0.5) * np.float32((2 * np.pi) ** -0.5)
        grad_pre[place, :] = (grad_hidden[place, :] * slope).astype(BF16)
        return 0

    lax.fori_loop(0, OWN // 16, gelu_step, 0, unroll=True)

    out_ref[...] = (middle[...] + dot(hidden[...], w2[...])).astype(BF16)
    grad_2 = dot_tn(hidden[...], cot).astype(BF16)
    grad_1 = dot_tn(second[...], grad_pre[...]).astype(BF16)
    grad_middle_ref[...] = dot_nt(grad_pre[...], w1[...])

    def back_step(block, total):
        place = pl.ds(pl.multiple_of(block * rows_slots, rows_slots), rows_slots)
        unit, inverse = normalise(middle[place, :])
        grad = grad_middle_ref[place, :]
        total = total + jnp.sum(grad * unit, 0, keepdims=True)
        grad = own_ref[block, 1].astype(F32) + norm_back(grad, gain, unit, inverse)
        grad_middle_ref[place, :] = grad
        second[place, :] = (grad * own_mask(block)).astype(BF16)
        return total

    gain_two = jnp.zeros((1, D), F32)
    for block in range(blocks):
        gain_two = back_step(block, gain_two)
    gain_ref[...] = gain_two

    grad_o = []
    lane_own = lax.broadcasted_iota(jnp.int32, (OWN, LANES), 1)
    for h in range(HEADS):
        grad_o.append(dot_tn(att[h], second[...])[:HEAD_DIM])
        grad_att = dot_nt(second[...], wo[h]).astype(BF16).astype(F32)
        scaled = (grad_att * sums[h]).astype(BF16).astype(F32)
        shift = -jnp.sum(scaled * outs[h], -1, keepdims=True)
        high = shift.astype(BF16).astype(F32)
        lifted = jnp.where(
            lane_own == HEAD_DIM, high, jnp.where(lane_own == HEAD_DIM + 1, shift - high, scaled)
        )
        lifted_ref[h] = lifted.astype(BF16)

    for half in range(2):
        wire[:, half * span : (half + 1) * span] = dot_nt(
            grad_1[:, half * FF // 2 : (half + 1) * FF // 2], sel_1_ref[...]
        )
    grad_o = jnp.concatenate(grad_o, axis=0).astype(BF16)
    wire[...] += dot_nt(grad_o, sel_o_ref[...])

    def deliver(lanes):
        for m in range(parts):
            parted[m] = wire[:, m * LANES : (m + 1) * LANES].astype(BF16)
        for z in range(parts // 2):
            put_blocks(keep_ref, z, lanes, parted[2 * z + core])
            put_blocks(send_ref, z, lanes, parted[2 * z + 1 - core])

    deliver(slice(0, LANES))
    total = None
    for g in range(4):
        rows = [
            grad_2[r * 4 * per_block + g * per_block : r * 4 * per_block + (g + 1) * per_block]
            for r in range(blocks)
        ]
        part = dot_nt(jnp.concatenate(rows, axis=0), sel_2_ref[g])
        total = part if total is None else total + part
    wire[...] = total
    deliver(slice(LANES, 2 * LANES))


def attention_back_kernel(
    soft_ref,
    lifted_ref,
    q_ref,
    k_ref,
    v_ref,
    wqkv_ref,
    part_ref,
    triple,
    grad_q,
    scores,
    grad_scores,
    part,
    *,
    blocks,
):
    core = lax.axis_index("core")
    rows_slots = OWN // blocks
    for h in range(HEADS):
        tile = slice(h * LANES, (h + 1) * LANES)
        scores[...] = dot_nt(v_ref[h], lifted_ref[h])

        def back_step(i, _, h=h):
            place = pl.ds(pl.multiple_of(i * 64, 64), 64)
            grad_scores[place, :] = (soft_ref[h, place, :].astype(F32) * scores[place, :]).astype(
                BF16
            )
            return 0

        lax.fori_loop(0, SLOTS // 64, back_step, 0, unroll=True)
        grad_q[:, tile] = (dot_tn(k_ref[h], grad_scores[...]).T.astype(BF16) * HEAD_DIM ** (-0.5)).astype(
            BF16
        )
        triple[0, :, tile] = dot(grad_scores[...], q_ref[h]).astype(BF16)
        triple[1, :, tile] = dot(soft_ref[h], lifted_ref[h]).astype(BF16)

    part[...] = dot_nt(triple[0], wqkv_ref[1]) + dot_nt(triple[1], wqkv_ref[2])
    from_q = dot_nt(grad_q[...], wqkv_ref[0])
    for block in range(blocks):
        here = slice(block * rows_slots, (block + 1) * rows_slots)
        place = pl.ds(pl.multiple_of((block * 2 + core) * rows_slots, rows_slots), rows_slots)
        part[place, :] += from_q[here]
    part_ref[...] = part[...].astype(BF16)


def scan_back_kernel(
    starts,
    width,
    own_ref,
    mask_ref,
    part_ref,
    got_ref,
    mixed_ref,
    first_ref,
    table_ref,
    rates_ref,
    wu_ref,
    triple_ref,
    grad_q_ref,
    scanned_ref,
    gain_two_ref,
    sel_u_ref,
    sel_rc_ref,
    sel_q_ref,
    keep_ref,
    send_ref,
    back_ref,
    gs_wide,
    gs_pairs,
    gt_wide,
    gt_pairs,
    xs_wide,
    xs_pairs,
    xt_wide,
    xt_pairs,
    rows_wide,
    rows_pairs,
    cols_wide,
    cols_pairs,
    grads_ref,
    own,
    own_tail,
    together,
    lag_sums,
    lag_lines,
    lag_rows,
    mixed_back,
    wire,
    parted,
    grad_w_ref,
):
    gs, gt = (gs_wide, gs_pairs), (gt_wide, gt_pairs)
    xs, xt = (xs_wide, xs_pairs), (xt_wide, xt_pairs)
    rows, cols = (rows_wide, rows_pairs), (cols_wide, cols_pairs)
    core = lax.axis_index("core")
    blocks, _, rows_slots, _ = own_ref.shape
    half_rows = rows_slots // GRID
    own_rows = GRID // 2
    parts = sel_rc_ref.shape[0] // LANES
    put_columns(*xs, mixed_ref[...].astype(F32))
    grads = (part_ref[...].astype(F32) + got_ref[...].astype(F32)) * widen(mask_ref[...])
    grads = grads.astype(BF16)
    grads_ref[...] = grads
    put_columns(*gs, grads.astype(F32))

    def place_of(block):
        return pl.ds(pl.multiple_of((block * 2 + core) * rows_slots, rows_slots), rows_slots)

    for source, dst in ((grads_ref, gt), (mixed_ref, xt)):
        for block in range(blocks):
            here = slice(block * rows_slots, (block + 1) * rows_slots)
            value = source[place_of(block), :].astype(F32)
            own[here, :] = value[:, :LANES]
            own_tail[here, :] = value[:, LANES:]
        put_rows(*dst, own, own_tail[...], together)

    grad_w = [None, dot_tn(scanned_ref[...], triple_ref[0]), dot_tn(scanned_ref[...], triple_ref[1])]
    for block in range(blocks):
        here = slice(block * rows_slots, (block + 1) * rows_slots)
        term = dot_tn(scanned_ref[place_of(block), :], grad_q_ref[here, :])
        grad_w[0] = term if block == 0 else grad_w[0] + term
    for third in range(3):
        grad_w_ref[third] = grad_w[third].astype(BF16)

    for kind, sublane in units(0):
        step = gt[kind].shape[0] // GRID
        for t, value in enumerate(toeplitz(gt, table_ref, 0, kind, sublane, -1)):
            rows[kind][t * step + sublane : t * step + sublane + 8, :] = value

    def col_step(index, _):
        for kind, sublane in units(index):
            step = gs[kind].shape[0] // GRID
            found = toeplitz(gs, table_ref, 1, kind, sublane, -1, half_rows)
            for t, value in enumerate(found):
                cols[kind][pl.ds(pl.multiple_of(t * step + sublane, 8), 8), :] = value
        return 0

    lax.fori_loop(0, 2, col_step, 0)

    lag_sums[...] = jnp.zeros_like(lag_sums)

    for kind, sublane in units(0):
        add_lags(lag_sums, 0, kind, sublane, gt, xt)

    def lag_step(index, _):
        for kind, sublane in units(index):
            add_lags(lag_sums, 1, kind, sublane, gs, xs, half_rows)
        return 0

    lax.fori_loop(0, 2, lag_step, 0)
    for way in range(2):
        for kind in range(2):
            for lag, value in enumerate(gather_lags(lag_sums, way, kind)):
                lag_lines[way, kind, lag] = value
            lag_lines[way, kind, LAGS - 1] = jnp.zeros((8, LANES), F32)

    for way in range(2):
        lag_rows[way, :, :LANES] = jnp.sum(lag_lines[way, 0], 1)
        tail = jnp.sum(lag_lines[way, 1], 1)
        tail = tail[:, : D - LANES] + tail[:, D - LANES :]
        lag_rows[way, :, LANES:] = pair_lanes(tail, jnp.zeros_like(tail))

    decay, coef = rates_ref[: 4 * STATE], rates_ref[4 * STATE :]

    to_rate, to_coef = [], []
    for d in range(4):
        way, side = divmod(d, 2)
        rate = decay[d * STATE : (d + 1) * STATE]
        rate_sum = jnp.zeros((STATE, 2 * LANES), F32)
        coef_sum = jnp.broadcast_to(lag_rows[way, CENTER : CENTER + 1, :], (STATE, 2 * LANES))
        for k in range(1, GRID):
            at = CENTER - k if side else CENTER + k
            line = jnp.broadcast_to(lag_rows[way, at : at + 1, :], (STATE, 2 * LANES))
            scaled = line * jnp.exp(rate * float(-k))
            coef_sum = coef_sum + scaled
            rate_sum = rate_sum - scaled * float(k)
        to_rate.append(rate_sum)
        to_coef.append(coef_sum)
    to_rate, to_coef = jnp.concatenate(to_rate, axis=0), jnp.concatenate(to_coef, axis=0)
    grad_rc = jnp.concatenate([to_rate * coef, to_coef], axis=0).T[:D].astype(BF16)

    def join_step(i, _):
        for row, value in join_rows(i, own_rows, rows, cols):
            at = ((row // half_rows * 2 + core) * half_rows + row % half_rows) * GRID
            mask = mask_ref[pl.ds(pl.multiple_of(at, GRID), GRID), :]
            place = pl.ds(pl.multiple_of(row * GRID, GRID), GRID)
            mixed_back[place, :] = (value * widen(mask)).astype(BF16)
        return 0

    lax.fori_loop(0, own_rows // 2, join_step, 0, unroll=True)
    grad_u = dot_tn(first_ref[...], mixed_back[...]).astype(BF16)
    grad_first = dot_nt(mixed_back[...], wu_ref[...])
    back_ref[...] = grad_first
    gain_one = jnp.zeros((1, D), F32)
    for block in range(blocks):
        here = slice(block * rows_slots, (block + 1) * rows_slots)
        unit, _ = normalise(own_ref[block, 0].astype(F32))
        gain_one = gain_one + jnp.sum(grad_first[here] * unit, 0, keepdims=True)

    wire[...] = dot_nt(grad_u, sel_u_ref[...]) + dot_nt(grad_rc, sel_rc_ref[...])
    for third in range(3):
        span = slice(starts[third] * LANES, (starts[third] + width) * LANES)
        wire[:, span] += dot_nt(grad_w_ref[third], sel_q_ref[third])
    for m in range(parts):
        parted[m] = wire[:, m * LANES : (m + 1) * LANES].astype(BF16)
    for z in range(parts // 2):
        put_late(keep_ref, z, parted[2 * z + core])
        put_late(send_ref, z, parted[2 * z + 1 - core])

    lines = []
    for value in (gain_one, gain_two_ref[...]):
        high = value.astype(BF16).astype(F32)
        for piece in (high, value - high):
            lines.append(piece[:, :LANES])
            lines.append(
                jnp.concatenate([piece[:, LANES:], jnp.zeros((1, 2 * LANES - D), F32)], axis=1)
            )
    lines = jnp.concatenate(lines, axis=0).astype(BF16)
    for ref in (keep_ref, send_ref):
        ref[ref.shape[0] - 1, :8] = lines
        ref[ref.shape[0] - 1, 8:] = jnp.zeros((ref.shape[1] - 8, LANES), BF16)


def last_norm_kernel(own_ref, gains_ref, back_ref, grad_middle_ref, *routed_refs):
    _, _, slots, _ = own_ref.shape
    gain = gains_ref[0:1, :]
    for k, routed in enumerate(routed_refs):
        block = lax.axis_index("row") ^ k
        place = pl.ds(pl.multiple_of(block * slots, slots), slots)
        unit, inverse = normalise(own_ref[block, 0].astype(F32))
        grad = grad_middle_ref[place, :] + norm_back(back_ref[place, :], gain, unit, inverse)
        routed[...] = pack(grad.astype(BF16))


def aligned(rows):
    return (rows + 15) // 16 * 16


def spare_lanes(rows, parts):
    return rows >= 32 and 4 * (D // parts) + 32 <= LANES


def split(value):
    high = value.astype(BF16).astype(F32)
    return jnp.concatenate([high, value - high], axis=0)


def early_sum_kernel(out_own_ref, keep_ref, got_ref, *out_refs):
    _, depth, rows, _ = keep_ref.shape
    slots = OWN // len(out_refs)
    block_rows = aligned(rows)
    for k, out_ref in enumerate(out_refs):
        block = lax.axis_index("row") ^ k
        for z in range(depth):
            total = keep_ref[block, z].astype(F32) + got_ref[block, z].astype(F32)
            out_ref[z * block_rows : z * block_rows + rows] = total.astype(BF16)
        place = pl.ds(pl.multiple_of(block * slots, slots), slots)
        out_ref[depth * block_rows :] = fold(pack(out_own_ref[place, :]))


def late_sum_kernel(depth, keep_ref, got_ref, *refs):
    count = len(refs) // 2
    routed_refs, out_refs = refs[:count], refs[count:]
    rows = keep_ref.shape[1]
    block_rows = aligned(rows)
    last = keep_ref.shape[0] - 1
    gains = keep_ref[last, :8].astype(F32) + got_ref[last, :8].astype(F32)
    lines = []
    for g in range(2):
        for lane in range(2):
            at = 4 * g + lane
            lines.append(gains[at : at + 1] + gains[at + 2 : at + 3])
    gains = split(jnp.concatenate(lines, axis=0))
    gains = jnp.concatenate([gains, jnp.zeros((8, LANES), F32)], axis=0).astype(BF16)
    for k, out_ref in enumerate(out_refs):
        block = lax.axis_index("row") ^ k
        for z in range(depth):
            at = block * depth + z
            total = keep_ref[at].astype(F32) + got_ref[at].astype(F32)
            out_ref[z * block_rows : z * block_rows + rows] = total.astype(BF16)
        out_ref[depth * block_rows : depth * block_rows + 16] = gains
        out_ref[depth * block_rows + 16 :] = routed_refs[k][...]


def row_sum_kernel(blocks, depth, rows, *refs):
    early_refs, late_refs, out_refs = refs[:blocks], refs[blocks : 2 * blocks], refs[2 * blocks :]
    block_rows = aligned(rows)
    gains = late_refs[0][depth * block_rows : depth * block_rows + 16].astype(F32)
    for k in range(1, blocks):
        gains = gains + late_refs[k][depth * block_rows : depth * block_rows + 16].astype(F32)
    gains = split(gains[:4] + gains[4:8])
    for j, out_ref in enumerate(out_refs):
        z = lax.axis_index("z") ^ j
        place = pl.ds(pl.multiple_of(z * block_rows, 16), block_rows)
        early = early_refs[0][place, :].astype(F32)
        late = late_refs[0][place, :].astype(F32)
        for k in range(1, blocks):
            early = early + early_refs[k][place, :].astype(F32)
            late = late + late_refs[k][place, :].astype(F32)
        if spare_lanes(rows, 2 * depth):
            chunks = [gains[:, q * 32 : (q + 1) * 32] for q in range(4)]
            chunks.append(jnp.zeros((rows - 32, 32), F32))
            early = jnp.concatenate([early[:, :-32], jnp.concatenate(chunks, axis=0)], axis=1)
        else:
            out_ref[rows:, :LANES] = jnp.concatenate(
                [gains, jnp.zeros((8, LANES), F32)], axis=0
            ).astype(BF16)
            out_ref[rows:, LANES:] = jnp.zeros((16, 2 * LANES), BF16)
        out_ref[:rows, LANES:] = early[:rows].astype(BF16)
        out_ref[:rows, :LANES] = late[:rows].astype(BF16)


def final_kernel(parts, *refs):
    final_body(parts, refs[: parts // 2], *refs[parts // 2 :])


def final_body(
    parts,
    got_refs,
    g1_ref,
    g2_ref,
    wu_ref,
    rate_ref,
    coef_ref,
    qkv_ref,
    wo_ref,
    fc1_ref,
    fc2_ref,
):
    a_u, a_r, a_q, (o_u, o_r, o_c, o_q) = late_layout(parts)
    total = got_refs[0][...].astype(F32)
    for ref in got_refs[1:]:
        total = total + ref[...].astype(F32)
    early = total[: fc1_ref.shape[0], LANES:]
    total = total[:, :LANES]
    rows = fc1_ref.shape[0]
    weights = total[:rows]
    if spare_lanes(rows, parts):
        gains = jnp.concatenate(
            [early[q * 8 : (q + 1) * 8, 2 * LANES - 32 :] for q in range(4)], axis=1
        )
    else:
        gains = total[rows:]
    turned = weights.T
    wu_ref[...] = turned[o_u : o_u + a_u]
    rate_ref[...] = turned[o_r : o_r + a_r]
    coef_ref[...] = turned[o_c : o_c + a_r]
    qkv_ref[...] = weights[:, o_q : o_q + a_q]
    gains = gains[0:4] + gains[4:8]
    for g, ref in ((0, g1_ref), (1, g2_ref)):
        ref[...] = jnp.concatenate(
            [gains[2 * g : 2 * g + 1], gains[2 * g + 1 : 2 * g + 2, : D - LANES]], axis=1
        )
    a_1, a_o = FF // parts, D // parts
    fc1_ref[...] = early[:, :a_1]
    wo_ref[...] = early[:, :LANES].T[a_1 : a_1 + a_o]
    turned = early[:, LANES:].T
    fc2_ref[...] = jnp.concatenate([turned[g * a_o : (g + 1) * a_o] for g in range(4)], axis=1)


def per_device(
    patches, valid_mask, norm_gains, w_u, decay_rate, out_coef, w_qkv, w_o, w_fc1, w_fc2, cotangent
):
    images, rows_here, _, _ = patches.shape
    depth, blocks = lax.axis_size("z"), lax.axis_size("row")
    parts = 2 * depth
    rows_slots = rows_here // 2 * GRID
    packed_rows = rows_slots * 3 // 2
    swap = [(0, 1), (1, 0)]
    shape = jax.ShapeDtypeStruct

    def planes(slots):
        return [pltpu.VMEM((slots, LANES), F32), pltpu.VMEM((slots // 2, LANES), F32)]

    def swapped(value):
        return lax.ppermute(value, "core", swap)

    def exchanged(values, axis):
        size = len(values)
        return [values[0]] + [
            lax.ppermute(values[k], axis, [(i, i ^ k) for i in range(size)]) for k in range(1, size)
        ]

    def to_chips(value, j):
        pairs = []
        for home in range(2):
            for source in range(blocks):
                target, image = divmod(source ^ j, images)
                pairs.append((home * blocks + source, target * blocks + home * images + image))
        return lax.ppermute(value, ("core", "row"), pairs)

    starts, width = late_spans(parts)
    sel_1, sel_o, sel_2 = early_selections(parts)

    rows_weight = w_u.shape[0]
    payload = shape((2 * packed_rows + GRID, LANES), BF16)
    shard = shape((rows_weight, 3 * LANES), BF16)
    sources = [value.reshape(images, rows_here * GRID, D) for value in (patches, cotangent)]
    if rows_weight % 16 == 0:
        weights, *routed = pl.pallas_call(
            depart_kernel,
            name="depart",
            out_shape=(shard,) + (payload,) * blocks,
            in_specs=[VMEM] * 10,
            out_specs=[VMEM] * (1 + blocks),
            compiler_params=compiler(LARGE),
        )(
                w_u.T,
            decay_rate.T,
            out_coef.T,
            w_o.T,
            w_fc2.T,
            w_qkv,
            w_fc1,
            *sources,
            valid_mask,
        )
    else:

        def fill(pieces):
            joined = jnp.concatenate(pieces, axis=1)
            return jnp.pad(joined, ((0, 0), (0, LANES - joined.shape[1])))

        weights = jnp.concatenate(
            [
                fill([w_u, decay_rate, out_coef, w_qkv]),
                fill([w_fc1, w_o]),
                fill([w_fc2[g * rows_weight : (g + 1) * rows_weight] for g in range(4)]),
            ],
            axis=1,
        )
        routed = pl.pallas_call(
            route_kernel,
            name="route",
            out_shape=(payload,) * blocks,
            in_specs=[VMEM] * 3,
            out_specs=[VMEM] * blocks,
            compiler_params=compiler(LARGE),
        )(*sources, valid_mask)

    weights = jnp.stack(exchanged([weights] * depth, "z"))
    weights = exchanged([weights] * blocks, "row")
    weights = weights + [swapped(value) for value in weights]
    routed = [to_chips(value, j) for j, value in enumerate(routed)]
    own, first_own, mask, sel_u, sel_rc, sel_q = pl.pallas_call(
        lambda *refs: norm_kernel(starts, parts, *refs),
        name="first_norm",
        out_shape=(
            shape((blocks, 2, rows_slots, D), BF16),
            shape((OWN, D), BF16),
            shape((SLOTS, LANES), F32),
            shape((parts * LANES, D), BF16),
            shape((parts * LANES, LANES), BF16),
            shape((3, width * LANES, TILE), BF16),
        ),
        in_specs=[VMEM] * (1 + blocks),
        out_specs=[VMEM] * 6,
        compiler_params=compiler(8 << 20),
    )(norm_gains, *routed)
    first_other = swapped(first_own)

    head_own = shape((HEADS, OWN, LANES), BF16)
    head_all = shape((HEADS, SLOTS, LANES), BF16)
    part_scratch = pltpu.VMEM((parts, blocks, rows_weight, LANES), BF16)
    q, k, v, scanned, mixed, table, rates, wu, wqkv = pl.pallas_call(
        lambda *refs: scan_kernel(starts, width, *refs, blocks=blocks),
        name="scan_forward",
        out_shape=(
            head_own,
            head_all,
            head_all,
            shape((SLOTS, D), BF16),
            shape((SLOTS, D), BF16),
            shape((2, 2, 9 * 16, LANES), F32),
            shape((LANES, 2 * LANES), F32),
            shape((D, D), BF16),
            shape((3, D, TILE), BF16),
        ),
        in_specs=[VMEM] * (6 + 2 * blocks),
        out_specs=[VMEM] * 9,
        scratch_shapes=[part_scratch]
        + planes(SLOTS) * 4
        + [pltpu.VMEM((OWN, D), BF16), pltpu.VMEM((SLOTS, D), BF16)]
        + [pltpu.VMEM((2, 2, LAGS, LANES), F32)],
        compiler_params=compiler(),
    )(first_own, first_other, mask, sel_u, sel_rc, sel_q, *weights)

    wire_early = shape((blocks, depth, rows_weight, 2 * LANES), BF16)
    soft, lifted, out_own, grad_middle, gain_two, early_keep, early_send = pl.pallas_call(
        middle_kernel,
        name="attention_and_feed_forward",
        out_shape=(
            shape((HEADS, SLOTS, OWN), BF16),
            head_own,
            shape((OWN, D), BF16),
            shape((OWN, D), F32),
            shape((1, D), F32),
            wire_early,
            wire_early,
        ),
        in_specs=[VMEM] * (9 + 2 * blocks),
        out_specs=[VMEM] * 7,
        scratch_shapes=[
            part_scratch,
            pltpu.VMEM((SLOTS, OWN), F32),
            pltpu.VMEM((HEADS, LANES, D), BF16),
            pltpu.VMEM((D, FF), BF16),
            pltpu.VMEM((FF, D), BF16),
            pltpu.VMEM((HEADS, OWN, LANES), BF16),
            pltpu.VMEM((HEADS, OWN, LANES), F32),
            pltpu.VMEM((HEADS, OWN, LANES), F32),
            pltpu.VMEM((OWN, D), F32),
            pltpu.VMEM((OWN, D), BF16),
            pltpu.VMEM((OWN, FF), F32),
            pltpu.VMEM((OWN, FF), F32),
            pltpu.VMEM((OWN, FF), BF16),
            pltpu.VMEM((OWN, FF), BF16),
            pltpu.VMEM((D, parts * LANES), F32),
            pltpu.VMEM((parts, D, LANES), BF16),
        ],
        compiler_params=compiler(),
    )(own, mask, norm_gains, sel_1, sel_o, sel_2, q, k, v, *weights)

    early_recv = swapped(early_send)

    part, triple, grad_q = pl.pallas_call(
        lambda *refs: attention_back_kernel(*refs, blocks=blocks),
        name="attention_backward",
        out_shape=(
            shape((SLOTS, D), BF16),
            shape((2, SLOTS, TILE), BF16),
            shape((OWN, TILE), BF16),
        ),
        in_specs=[VMEM] * 6,
        out_specs=[VMEM] * 3,
        scratch_shapes=[
            pltpu.VMEM((SLOTS, OWN), F32),
            pltpu.VMEM((SLOTS, OWN), BF16),
            pltpu.VMEM((SLOTS, D), F32),
        ],
        compiler_params=compiler(),
    )(soft, lifted, q, k, v, wqkv)

    early_keep, early_recv, part = lax.optimization_barrier((early_keep, early_recv, part))
    payload = shape((depth * aligned(rows_weight) + packed_rows // 2, 2 * LANES), BF16)
    early = pl.pallas_call(
        early_sum_kernel,
        name="early_sum",
        out_shape=(payload,) * blocks,
        in_specs=[VMEM] * 3,
        out_specs=[VMEM] * blocks,
        compiler_params=compiler(8 << 20),
    )(out_own, early_keep, early_recv)
    early, part = lax.optimization_barrier((early, part))
    part_got = swapped(part)
    early = exchanged(early, "row")
    wire_late = shape((blocks * depth + 1, rows_weight, LANES), BF16)
    late_keep, late_send, back = pl.pallas_call(
        lambda *refs: scan_back_kernel(starts, width, *refs),
        name="scan_backward",
        out_shape=(wire_late, wire_late, shape((OWN, D), F32)),
        in_specs=[VMEM] * 16,
        out_specs=[VMEM] * 3,
        scratch_shapes=planes(SLOTS) + planes(OWN) + planes(SLOTS) + planes(OWN) * 3
        + [
            pltpu.VMEM((SLOTS, D), BF16),
            pltpu.VMEM((OWN, LANES), F32),
            pltpu.VMEM((OWN, D - LANES), F32),
            pltpu.VMEM((OWN // 2, LANES), F32),
            pltpu.VMEM((2, 2, 9 * 16, 8, LANES), F32),
            pltpu.VMEM((2, 2, LAGS, 8, LANES), F32),
            pltpu.VMEM((2, LAGS, 2 * LANES), F32),
            pltpu.VMEM((OWN, D), BF16),
            pltpu.VMEM((D, parts * LANES), F32),
            pltpu.VMEM((parts, D, LANES), BF16),
            pltpu.VMEM((3, D, TILE), BF16),
        ],
        compiler_params=compiler(),
    )(
        own,
        mask,
        part,
        part_got,
        mixed,
        first_own,
        table,
        rates,
        wu,
        triple,
        grad_q,
        scanned,
        gain_two,
        sel_u,
        sel_rc,
        sel_q,
    )
    late_keep, late_send, early = lax.optimization_barrier((late_keep, late_send, early))
    payload = shape((packed_rows, LANES), BF16)
    routed = pl.pallas_call(
        last_norm_kernel,
        name="last_norm",
        out_shape=(payload,) * blocks,
        in_specs=[VMEM] * 4,
        out_specs=[VMEM] * blocks,
        compiler_params=compiler(8 << 20),
    )(own, norm_gains, back, grad_middle)
    payload = shape((depth * aligned(rows_weight) + 16 + packed_rows, LANES), BF16)
    late = pl.pallas_call(
        lambda *refs: late_sum_kernel(depth, *refs),
        name="late_sum",
        out_shape=(payload,) * blocks,
        in_specs=[VMEM] * (2 + blocks),
        out_specs=[VMEM] * blocks,
        compiler_params=compiler(8 << 20),
    )(late_keep, swapped(late_send), *routed)
    late = exchanged(late, "row")
    final_rows = rows_weight if spare_lanes(rows_weight, parts) else rows_weight + 16
    summed = pl.pallas_call(
        lambda *refs: row_sum_kernel(blocks, depth, rows_weight, *refs),
        name="row_sum",
        out_shape=(shape((final_rows, 3 * LANES), BF16),) * depth,
        in_specs=[VMEM] * (2 * blocks),
        out_specs=[VMEM] * depth,
        compiler_params=compiler(8 << 20),
    )(*early, *late)
    summed = exchanged(summed, "z")

    chosen = pl.pallas_call(
        choose_kernel,
        name="choose",
        out_shape=shape((images, 2 * packed_rows, LANES), BF16),
        in_specs=[VMEM] * (2 * blocks),
        out_specs=VMEM,
        compiler_params=compiler(8 << 20),
    )(*early, *late)
    whole = shape((images, rows_here * GRID, D), BF16)
    block_out, grad_patches = pl.pallas_call(
        home_kernel,
        name="home",
        out_shape=(whole, whole),
        in_specs=[VMEM] * (1 + 2 * blocks),
        out_specs=[VMEM] * 2,
        compiler_params=compiler(8 << 20),
    )(swapped(chosen), *early, *late)

    summed, block_out, grad_patches = lax.optimization_barrier((summed, block_out, grad_patches))
    turned = (4 * STATE // parts, rows_weight)
    g1, g2, f_u, f_rate, f_coef, f_qkv, f_o, f_1, f_2 = pl.pallas_call(
        lambda *refs: final_kernel(parts, *refs),
        name="final_sum",
        out_shape=(
            shape((1, D), F32),
            shape((1, D), F32),
            shape((D // parts, rows_weight), F32),
            shape(turned, F32),
            shape(turned, F32),
            shape((rows_weight, 3 * D // parts), F32),
            shape((D // parts, rows_weight), F32),
            shape((rows_weight, FF // parts), F32),
            shape((D // parts, 4 * rows_weight), F32),
        ),
        in_specs=[VMEM] * depth,
        out_specs=[VMEM] * 9,
        compiler_params=compiler(8 << 20),
    )(*summed)
    return (
        block_out.reshape(patches.shape),
        grad_patches.reshape(patches.shape),
        g1.reshape(D),
        g2.reshape(D),
        f_u.T,
        f_rate.T,
        f_coef.T,
        f_qkv,
        f_o.T,
        f_1,
        f_2.T,
    )


def solution(mesh):
    images, rows = mesh.devices.shape
    fine = Mesh(mesh.devices.reshape(images // 2, 2, rows), ("z", "core", "row"))
    img = ("z", "core")
    grid = P(img, "row", None, None)
    weight = P("row", img)
    in_specs = (grid, P(img, None, None), P()) + (weight,) * 7 + (grid,)
    out_specs = (grid, grid, P(), P()) + (weight,) * 7
    return jax.shard_map(
        per_device, mesh=fine, in_specs=in_specs, out_specs=out_specs, check_vma=False
    )
```

```python
import jax
import jax.numpy as jnp
import numpy as np
from jax import lax
from jax.experimental import pallas as pl
from jax.experimental.pallas import tpu as pltpu
from jax.sharding import Mesh
from jax.sharding import PartitionSpec as P

HEADS = 3
HEAD_DIM = 64
STATE = 16
GRID = 32
SLOTS = GRID * GRID
OWN = SLOTS // 2
D = HEADS * HEAD_DIM
FF = 4 * D
LANES = 128
TILE = HEADS * LANES
LAGS = 2 * GRID
CENTER = GRID - 1
EPS = 1e-05
BF16 = jnp.bfloat16
F32 = jnp.float32


def late_layout(parts):
    a_u, a_r, a_q = D // parts, 4 * STATE // parts, 3 * D // parts
    return a_u, a_r, a_q, (0, a_u, a_u + a_r, a_u + 2 * a_r)


def late_spans(parts):
    a_q = 3 * D // parts
    first = [third * D // a_q for third in range(3)]
    last = [((third + 1) * D - 1) // a_q for third in range(3)]
    width = max(stop - start + 1 for start, stop in zip(first, last))
    return [min(start, parts - width) for start in first], width


def early_selections(parts):
    a_1, a_o = FF // parts, D // parts
    half = parts // 2
    sel_1 = np.zeros((half, LANES, FF // 2), np.float32)
    sel_o = np.zeros((parts, LANES, D), np.float32)
    sel_2 = np.zeros((4, parts, LANES, D), np.float32)
    for m in range(half):
        for col in range(a_1):
            sel_1[m, col, m * a_1 + col] = 1
    for m in range(parts):
        for col in range(a_o):
            sel_o[m, a_1 + col, m * a_o + col] = 1
            for g in range(4):
                sel_2[g, m, g * a_o + col, m * a_o + col] = 1
    return (
        sel_1.reshape(half * LANES, FF // 2).astype(BF16),
        sel_o.reshape(parts * LANES, D).astype(BF16),
        sel_2.reshape(4, parts * LANES, D).astype(BF16),
    )


def lane_and_part(shape):
    place = lax.broadcasted_iota(jnp.int32, shape, 0)
    return place % LANES, place // LANES, lax.broadcasted_iota(jnp.int32, shape, 1)


def put_late_selections(starts, parts, sel_u_ref, sel_rc_ref, sel_q_ref):
    a_u, a_r, a_q, (o_u, o_r, o_c, o_q) = late_layout(parts)

    def put(hit):
        return jnp.where(hit, 1.0, 0.0).astype(BF16)

    lane, part, col = lane_and_part(sel_u_ref.shape)
    sel_u_ref[...] = put((lane < a_u) & (part * a_u + lane == col))
    lane, part, col = lane_and_part(sel_rc_ref.shape)
    rate = (lane >= o_r) & (lane < o_c) & (part * a_r + lane - o_r == col)
    coef = (lane >= o_c) & (lane < o_q) & (part * a_r + lane - o_c + 4 * STATE == col)
    sel_rc_ref[...] = put(rate | coef)
    lane, part, col = lane_and_part(sel_q_ref.shape[1:])
    whole = jnp.where(
        col % LANES < HEAD_DIM, col // LANES * HEAD_DIM + col % LANES, -4 * D
    )
    for third in range(3):
        here = (part + starts[third]) * a_q + lane - o_q - third * D
        sel_q_ref[third] = put((lane >= o_q) & (lane < o_q + a_q) & (here == whole))


def dot(a, b):
    return lax.dot_general(a, b, (((1,), (0,)), ((), ())), preferred_element_type=F32)


def dot_nt(a, b):
    return lax.dot_general(a, b, (((1,), (1,)), ((), ())), preferred_element_type=F32)


def dot_tn(a, b):
    return lax.dot_general(a, b, (((0,), (0,)), ((), ())), preferred_element_type=F32)


def normalise(values):
    center = values - jnp.mean(values, -1, keepdims=True)
    spread = jnp.mean(center * center, -1, keepdims=True)
    inverse = lax.rsqrt(spread + EPS)
    return center * inverse, inverse


def norm_back(grad, gain, unit, inverse):
    scaled = grad * gain
    first = jnp.mean(scaled, -1, keepdims=True)
    second = jnp.mean(scaled * unit, -1, keepdims=True)
    return inverse * (scaled - first - unit * second)


def widen(mask):
    return jnp.concatenate([mask, mask[:, : D - LANES]], axis=1)


def put_blocks(ref, z, lanes, value):
    rows = ref.shape[2]
    for r in range(ref.shape[0]):
        ref[r, z, :, lanes] = value[r * rows : (r + 1) * rows]


def put_late(ref, z, value):
    rows = ref.shape[1]
    depth = ref.shape[0] * rows // D
    for r in range(D // rows):
        ref[r * depth + z] = value[r * rows : (r + 1) * rows]


def pair_lanes(first, second):
    return jnp.concatenate([first, second], axis=1)


def put_columns(wide, pairs, values):
    wide[...] = values[:, :LANES]
    tail = values[:, LANES:].reshape(values.shape[0] // GRID, 2, GRID // 2, D - LANES)
    tail = pair_lanes(tail[:, 0].reshape(-1, D - LANES), tail[:, 1].reshape(-1, D - LANES))
    pairs[...] = tail


def put_rows(wide, pairs, from_wide, tail, together):
    rows = from_wide.shape[0] // GRID
    together[...] = pair_lanes(tail[: rows // 2 * GRID], tail[rows // 2 * GRID :])
    for j in range(GRID):
        wide[j * rows : (j + 1) * rows, :] = from_wide[pl.ds(j, rows, stride=GRID), :]
        pairs[j * rows // 2 : (j + 1) * rows // 2, :] = together[pl.ds(j, rows // 2, stride=GRID), :]


def units(index):
    return [(0, (index * 2 + u) * 8) for u in range(2)] + [(1, index * 8)]


def lag_tables(lags):
    lines = []
    near = lags[16:47]
    for table in (near, lags[0:31] - near, lags[32:63] - near):
        center = table[8:23]
        for part in (center, table[0:15] - center, table[16:31] - center):
            lines += [part, jnp.zeros((1, LANES), F32)]
    return jnp.concatenate(lines, axis=0)


def plus(left, right):
    return [a + b for a, b in zip(left, right)]


def own_places(own_rows):
    if own_rows is None:
        return list(range(8)), 0
    places = [i // own_rows * 2 * own_rows + i % own_rows for i in range(4)]
    return places, lax.axis_index("core") * own_rows


def three(left, right, work):
    a, b = len(left) // 2, len(right) // 2
    work(0, plus(left[:a], left[a:]), plus(right[:b], right[b:]))
    work(1, left[:a], right[b:])
    work(2, left[a:], right[:b])


def add_lags(sums, way, kind, sublane, grads, values, own_rows=None):
    step = values[kind].shape[0] // GRID
    places, shift = own_places(own_rows)

    def line(ref, at):
        return ref[kind][pl.ds(pl.multiple_of(at * step + sublane, 8), 8), :]

    g = [line(grads, base + place + shift) for base in range(0, GRID, 8) for place in places]
    x = [line(values, s) for s in range(GRID)]

    def leaf(first, second, g, x):
        total = {}
        for i, t in enumerate(places):
            for s in range(8):
                term = g[i] * x[s]
                total[t - s] = term if t - s not in total else total[t - s] + term
        start = (first * 3 + second) * 16 + 7
        for lag, value in total.items():
            sums[way, kind, start + lag + shift] += value

    three(g, x, lambda p, g, x: three(g, x, lambda q, g, x: leaf(p, q, g, x)))


def gather_lags(sums, way, kind):
    def join(parts, reach):
        found = [None] * (2 * (2 * reach + 1) + 1)
        width = 2 * reach - 1
        middle = [a - b - c for a, b, c in zip(*parts)]
        for start, part in ((reach, middle), (0, parts[1]), (2 * reach, parts[2])):
            for i in range(width):
                at = start + i
                found[at] = part[i] if found[at] is None else found[at] + part[i]
        return found[: 4 * reach - 1]

    thirds = []
    for first in range(3):
        tables = [
            [sums[way, kind, (first * 3 + second) * 16 + i] for i in range(15)]
            for second in range(3)
        ]
        thirds.append(join(tables, 8))
    return join(thirds, 16)


def toeplitz(src, table, way, kind, sublane, sign, own_rows=None):
    step = src[kind].shape[0] // GRID
    places, shift = own_places(own_rows)
    shift = shift * sign

    def leaf(x, first, second):
        if sign < 0:
            first, second = (0, 2, 1)[first], (0, 2, 1)[second]
        start = (first * 3 + second) * 16 + 7
        coef = {}
        total = [None] * len(places)
        for s in range(8):
            for i, t in enumerate(places):
                lag = t - s
                if lag not in coef:
                    line = table[way, kind, pl.ds(start + lag * sign + shift, 1), :]
                    coef[lag] = jnp.broadcast_to(line, (8, LANES))
                term = coef[lag] * x[s]
                total[i] = term if total[i] is None else total[i] + term
        return total

    def quarter(x, first):
        middle = leaf(plus(x[:8], x[8:]), first, 0)
        return plus(middle, leaf(x[8:], first, 1)) + plus(middle, leaf(x[:8], first, 2))

    x = [src[kind][pl.ds(pl.multiple_of(s * step + sublane, 8), 8), :] for s in range(GRID)]
    middle = quarter(plus(x[:16], x[16:]), 0)
    return plus(middle, quarter(x[16:], 1)) + plus(middle, quarter(x[:16], 2))


def join_rows(i, count, rows, cols):
    half = GRID // 2
    narrow = D - LANES
    across = rows[1][pl.ds(i, GRID, stride=count // 2), :]
    found = []
    for which in range(2):
        row = i + which * (count // 2)
        wide = cols[0][pl.ds(pl.multiple_of(row * GRID, GRID), GRID), :].astype(BF16).astype(F32)
        wide = wide + rows[0][pl.ds(i + which * (count // 2), GRID, stride=count), :]
        pairs = cols[1][pl.ds(pl.multiple_of(row * half, half), half), :].astype(BF16).astype(F32)
        tail = jnp.concatenate([pairs[:, :narrow], pairs[:, narrow:]], axis=0)
        tail = tail + across[:, which * narrow : (which + 1) * narrow]
        found.append((row, jnp.concatenate([wide, tail], axis=1)))
    return found


def gather_parts(mine_refs, got_refs, block, out_ref):
    core, row, depth = lax.axis_index("core"), lax.axis_index("row"), lax.axis_index("z")
    lanes = slice(block * LANES, (block + 1) * LANES)
    count = out_ref.shape[0] // 2
    rows = out_ref.shape[2]
    for refs, which in ((mine_refs, core), (got_refs, 1 - core)):
        for k, ref in enumerate(refs):
            for j in range(count):
                out_ref[2 * (depth ^ j) + which, row ^ k] = ref[j, :, lanes]
    wide = []
    for m in range(2 * count):
        wide.append(jnp.concatenate([out_ref[m, r] for r in range(out_ref.shape[1])], axis=0))
    return jnp.concatenate(wide, axis=1)


LARGE = 60 << 20


def compiler(limit=24 << 20):
    return pltpu.CompilerParams(vmem_limit_bytes=limit)


VMEM = pl.BlockSpec(memory_space=pltpu.VMEM)


def pack(values):
    half = values.shape[0] // 2
    tail = jnp.concatenate([values[:half, LANES:], values[half:, LANES:]], axis=1)
    return jnp.concatenate([values[:, :LANES], tail], axis=0)


def unpack(packed):
    count = packed.shape[0] * 2 // 3
    tail = packed[count:]
    tail = jnp.concatenate([tail[:, : D - LANES], tail[:, D - LANES :]], axis=0)
    return jnp.concatenate([packed[:count], tail], axis=1)


def pack_weights_kernel(turned_refs, qkv_ref, fc1_ref, out_ref):
    wu, rate, coef, wo, fc2 = [ref[...].astype(F32) for ref in turned_refs]
    rows = qkv_ref.shape[0]
    a_o, a_r = wo.shape[0], rate.shape[0]
    pieces = [wu, rate, coef, wo] + [fc2[:, g * rows : (g + 1) * rows] for g in range(4)]
    joined = jnp.concatenate(pieces, axis=0)
    joined = jnp.concatenate([joined, jnp.zeros((joined.shape[0], LANES - rows), F32)], axis=1)
    joined = joined.T[:rows]
    first, second = a_o + 2 * a_r, 2 * a_o + 2 * a_r

    def fill(parts):
        used = sum(part.shape[1] for part in parts)
        return parts + [jnp.zeros((rows, LANES - used), F32)]

    packed = jnp.concatenate(
        fill([joined[:, :first], qkv_ref[...].astype(F32)])
        + fill([fc1_ref[...].astype(F32), joined[:, first:second]])
        + fill([joined[:, second:]]),
        axis=1,
    ).astype(BF16)
    out_ref[...] = packed


def route_kernel(patch_ref, cot_ref, valid_ref, *out_refs):
    row = lax.axis_index("row")
    images, slots, _ = patch_ref.shape
    half = slots // 2
    packed = half * 3 // 2
    for j, out_ref in enumerate(out_refs):
        target = row ^ j
        core, image = target // images, target % images
        place = pl.ds(pl.multiple_of(core * half, half), half)
        out_ref[:packed] = pack(patch_ref[image, place, :])
        out_ref[packed : 2 * packed] = pack(cot_ref[image, place, :])
        valid = valid_ref[image].astype(F32)
        valid = jnp.concatenate([valid[8 * q : 8 * q + 8] for q in range(4)], axis=1)
        out_ref[2 * packed :] = jnp.concatenate([valid, jnp.zeros((8, LANES), F32)], axis=0).astype(
            BF16
        )


def depart_kernel(*refs):
    turned, (qkv_ref, fc1_ref, patch_ref, cot_ref, valid_ref, out_ref) = refs[:5], refs[5:11]
    pack_weights_kernel(turned, qkv_ref, fc1_ref, out_ref)
    route_kernel(patch_ref, cot_ref, valid_ref, *refs[11:])


def norm_kernel(starts, parts, gains_ref, *refs):
    got_refs, refs = refs[:-6], refs[-6:]
    own_ref, first_ref, mask_ref, *selections = refs
    core, row = lax.axis_index("core"), lax.axis_index("row")
    images = len(got_refs) // 2
    gain = gains_ref[0:1, :]
    slots = own_ref.shape[2]
    packed = slots * 3 // 2
    for j, got in enumerate(got_refs):
        block = (core * images + row % images) ^ j
        patch = unpack(got[:packed])
        own_ref[block, 0] = patch
        own_ref[block, 1] = unpack(got[packed : 2 * packed])
        unit, _ = normalise(patch.astype(F32))
        first_ref[pl.ds(pl.multiple_of(block * slots, slots), slots), :] = (unit * gain).astype(
            BF16
        )
    valid = got_refs[0][2 * packed :].astype(F32)
    valid = jnp.concatenate([valid[:8, q * GRID : (q + 1) * GRID] for q in range(4)], axis=0)
    valid = jnp.concatenate([valid, jnp.zeros((GRID, LANES - GRID), F32)], axis=1).T
    for i in range(GRID):
        mask_ref[i * GRID : (i + 1) * GRID, :] = jnp.broadcast_to(
            valid[:GRID, i : i + 1], (GRID, LANES)
        )
    put_late_selections(starts, parts, *selections)


def fold(packed):
    half = packed.shape[0] // 2
    return jnp.concatenate([packed[:half], packed[half:]], axis=1)


def unfold(folded):
    return jnp.concatenate([folded[:, :LANES], folded[:, LANES:]], axis=0)


def results_of(early_ref, late_ref, rows):
    early_start, late_start = early_ref.shape[0] - rows // 2, late_ref.shape[0] - rows
    return unfold(early_ref[early_start:]), late_ref[late_start:]


def choose_kernel(*refs):
    got_refs, out_ref = refs[:-1], refs[-1]
    blocks = len(got_refs) // 2
    core, row = lax.axis_index("core"), lax.axis_index("row")
    images, rows = out_ref.shape[0], out_ref.shape[1] // 2
    for k, got in enumerate(zip(got_refs[:blocks], got_refs[blocks:])):
        image = row ^ k

        @pl.when(image // images != core)
        def _(got=got, image=image):
            for which, value in enumerate(results_of(*got, rows)):
                out_ref[image % images, which * rows : (which + 1) * rows] = value


def home_kernel(swapped_ref, *refs):
    got_refs, out_refs = refs[:-2], refs[-2:]
    core, row = lax.axis_index("core"), lax.axis_index("row")
    images, slots, _ = out_refs[0].shape
    half = slots // 2
    rows = half * 3 // 2
    blocks = len(got_refs) // 2
    mine = pl.ds(pl.multiple_of(core * half, half), half)
    theirs = pl.ds(pl.multiple_of((1 - core) * half, half), half)
    for k, got in enumerate(zip(got_refs[:blocks], got_refs[blocks:])):
        image = row ^ k

        @pl.when(image // images == core)
        def _(got=got, image=image):
            for out_ref, value in zip(out_refs, results_of(*got, rows)):
                out_ref[image % images, mine, :] = unpack(value)

    for image in range(images):
        for which, out_ref in enumerate(out_refs):
            value = swapped_ref[image, which * rows : (which + 1) * rows]
            out_ref[image, theirs, :] = unpack(value)


def scan_kernel(
    starts,
    width,
    first_own_ref,
    first_other_ref,
    mask_ref,
    sel_u_ref,
    sel_rc_ref,
    sel_q_ref,
    *refs,
    blocks,
):
    mine_refs, got_refs, refs = refs[:blocks], refs[blocks : 2 * blocks], refs[2 * blocks :]
    scan_body(
        starts,
        width,
        first_own_ref,
        first_other_ref,
        mask_ref,
        sel_u_ref,
        sel_rc_ref,
        sel_q_ref,
        mine_refs,
        got_refs,
        *refs,
    )


def scan_body(
    starts,
    width,
    first_own_ref,
    first_other_ref,
    mask_ref,
    sel_u_ref,
    sel_rc_ref,
    sel_q_ref,
    mine_refs,
    got_refs,
    q_ref,
    k_ref,
    v_ref,
    scanned_ref,
    mixed_ref,
    table_ref,
    rates_ref,
    wu_ref,
    wqkv_ref,
    late_ref,
    xs_wide,
    xs_pairs,
    xt_wide,
    xt_pairs,
    cols_wide,
    cols_pairs,
    rows_wide,
    rows_pairs,
    scanned_own,
    first_ref,
    lags,
):
    xs, xt = (xs_wide, xs_pairs), (xt_wide, xt_pairs)
    cols, rows = (cols_wide, cols_pairs), (rows_wide, rows_pairs)
    core = lax.axis_index("core")
    blocks = len(mine_refs)
    rows_slots = OWN // blocks

    late = gather_parts(mine_refs, got_refs, 0, late_ref)
    wu = dot(late, sel_u_ref[...]).astype(BF16)
    wu_ref[...] = wu
    rates = dot(late, sel_rc_ref[...])
    rates = jnp.concatenate([rates.T, jnp.zeros((LANES, 2 * LANES - D), F32)], axis=1)
    rates_ref[...] = rates
    for third in range(3):
        window = late[:, starts[third] * LANES : (starts[third] + width) * LANES]
        wqkv_ref[third] = dot(window, sel_q_ref[third]).astype(BF16)

    decay, coef = rates[: 4 * STATE], rates[4 * STATE :]

    def lag_row(k):
        powers = jnp.exp(-decay * k) * coef
        return [jnp.sum(powers[d * STATE : (d + 1) * STATE], 0, keepdims=True) for d in range(4)]

    def store_lag(way, lag, row):
        row = row.astype(BF16).astype(F32)
        tail = row[:, LANES:D]
        for kind, lanes in enumerate((row[:, :LANES], pair_lanes(tail, tail))):
            lags[way, kind, pl.ds(lag + CENTER, 1), :] = lanes

    def lag_step(k, _):
        found = lag_row(k.astype(F32))
        for way in range(2):
            store_lag(way, k, found[2 * way])
            store_lag(way, -k, found[2 * way + 1])
        return 0

    lax.fori_loop(0, GRID, lag_step, 0, unroll=True)
    found = lag_row(0.0)
    for way in range(2):
        store_lag(way, 0, found[2 * way] + found[2 * way + 1])
        for kind in range(2):
            table_ref[way, kind] = lag_tables(lags[way, kind])


    for block in range(blocks):
        here = slice(block * rows_slots, (block + 1) * rows_slots)
        for ref, which in ((first_own_ref, core), (first_other_ref, 1 - core)):
            start = pl.multiple_of((block * 2 + which) * rows_slots, rows_slots)
            first_ref[pl.ds(start, rows_slots), :] = ref[here, :]
    mixed = dot(first_ref[...], wu) * widen(mask_ref[...])
    mixed = mixed.astype(BF16)
    mixed_ref[...] = mixed
    mixed = mixed.astype(F32)
    put_columns(*xs, mixed)
    put_rows(*xt, xs[0], mixed[:, LANES:], cols[1])

    def scan_step(index, _):
        for way, src, dst in ((0, xt, rows), (1, xs, cols)):
            for kind, sublane in units(index):
                step = src[kind].shape[0] // GRID
                for t, value in enumerate(toeplitz(src, table_ref, way, kind, sublane, 1)):
                    dst[kind][pl.ds(pl.multiple_of(t * step + sublane, 8), 8), :] = value
        return 0

    lax.fori_loop(0, 2, scan_step, 0, unroll=True)

    def join_step(i, _):
        for row, value in join_rows(i, GRID, rows, cols):
            place = pl.ds(pl.multiple_of(row * GRID, GRID), GRID)
            scanned_ref[place, :] = (value * widen(mask_ref[place, :])).astype(BF16)
        return 0

    lax.fori_loop(0, GRID // 2, join_step, 0, unroll=True)

    for block in range(blocks):
        start = pl.multiple_of((block * 2 + core) * rows_slots, rows_slots)
        scanned_own[block * rows_slots : (block + 1) * rows_slots, :] = scanned_ref[
            pl.ds(start, rows_slots), :
        ]

    lane_own = lax.broadcasted_iota(jnp.int32, (OWN, LANES), 1)
    lane_all = lax.broadcasted_iota(jnp.int32, (SLOTS, LANES), 1)
    bias = jnp.where(lane_all == HEAD_DIM, (mask_ref[...] - 1.0) * 1e30, 0.0)
    ones = jnp.where((lane_all == HEAD_DIM) | (lane_all == HEAD_DIM + 1), 1.0, 0.0)
    one_own = jnp.where(lane_own == HEAD_DIM, 1.0, 0.0)
    found = dot(scanned_own[...], wqkv_ref[0]) * HEAD_DIM ** (-0.5)
    for h in range(HEADS):
        q_ref[h] = (found[:, h * LANES : (h + 1) * LANES] + one_own).astype(BF16)
    targets = [(k_ref, h, 1, bias) for h in range(HEADS)] + [(v_ref, h, 2, ones) for h in range(HEADS)]
    for pair in range(HEADS):
        two = targets[2 * pair : 2 * pair + 2]
        weight = [wqkv_ref[third, :, h * LANES : (h + 1) * LANES] for _, h, third, _ in two]
        found = dot(scanned_ref[...], jnp.concatenate(weight, axis=1))
        for i, (ref, h, _, extra) in enumerate(two):
            ref[h] = (found[:, i * LANES : (i + 1) * LANES] + extra).astype(BF16)


def middle_kernel(
    own_ref,
    mask_ref,
    gains_ref,
    sel_1_ref,
    sel_o_ref,
    sel_2_ref,
    q_ref,
    k_ref,
    v_ref,
    *refs,
):
    blocks = own_ref.shape[0]
    middle_body(
        own_ref,
        mask_ref,
        gains_ref,
        sel_1_ref,
        sel_o_ref,
        sel_2_ref,
        q_ref,
        k_ref,
        v_ref,
        refs[:blocks],
        refs[blocks : 2 * blocks],
        *refs[2 * blocks :],
    )


def middle_body(
    own_ref,
    mask_ref,
    gains_ref,
    sel_1_ref,
    sel_o_ref,
    sel_2_ref,
    q_ref,
    k_ref,
    v_ref,
    mine_refs,
    got_refs,
    soft_ref,
    lifted_ref,
    out_ref,
    grad_middle_ref,
    gain_ref,
    keep_ref,
    send_ref,
    early_ref,
    scores,
    wo,
    w1,
    w2,
    att,
    outs,
    sums,
    middle,
    second,
    pre,
    grad_hidden,
    hidden,
    grad_pre,
    wire,
    parted,
):
    core = lax.axis_index("core")
    blocks, _, rows_slots, _ = own_ref.shape
    parts = early_ref.shape[0]
    per_block = D // blocks
    gain = gains_ref[1:2, :]

    left = gather_parts(mine_refs, got_refs, 1, early_ref)
    right = gather_parts(mine_refs, got_refs, 2, early_ref)
    span = parts // 2 * LANES
    for half in range(2):
        w1[:, half * FF // 2 : (half + 1) * FF // 2] = dot(
            left[:, half * span : (half + 1) * span], sel_1_ref[...]
        ).astype(BF16)
    out_weight = dot(left, sel_o_ref[...]).astype(BF16)
    for h in range(HEADS):
        wo[h, :HEAD_DIM] = out_weight[h * HEAD_DIM : (h + 1) * HEAD_DIM]
        wo[h, HEAD_DIM:] = jnp.zeros((LANES - HEAD_DIM, D), BF16)
    for g in range(4):
        part = dot(right, sel_2_ref[g])
        for r in range(blocks):
            start = r * 4 * per_block + g * per_block
            w2[start : start + per_block] = part[r * per_block : (r + 1) * per_block].astype(BF16)

    for h in range(HEADS):
        scores[...] = dot_nt(k_ref[h], q_ref[h])

        def top_step(i, top):
            values = scores[pl.ds(pl.multiple_of(i * 64, 64), 64), :]
            return jnp.maximum(top, jnp.max(values.reshape(8, 8, OWN), 0))

        top = lax.fori_loop(1, SLOTS // 64, top_step, jnp.max(scores[:64].reshape(8, 8, OWN), 0), unroll=True)
        top = jnp.max(top, 0, keepdims=True)

        def soft_step(i, _, h=h, top=top):
            place = pl.ds(pl.multiple_of(i * 128, 128), 128)
            soft_ref[h, place, :] = jnp.exp(scores[place, :] - top).astype(BF16)
            return 0

        lax.fori_loop(0, SLOTS // 128, soft_step, 0, unroll=True)
        raw = dot_tn(v_ref[h], soft_ref[h]).T
        total = raw[:, HEAD_DIM : HEAD_DIM + 1]
        sums[h] = jnp.broadcast_to(1.0 / total, (OWN, LANES))
        result = raw * sums[h]
        outs[h] = result
        att[h] = result.astype(BF16)

    branch = dot(att[0], wo[0]) + dot(att[1], wo[1]) + dot(att[2], wo[2])
    middle[...] = branch

    def own_mask(block):
        start = pl.multiple_of((block * 2 + core) * rows_slots, rows_slots)
        return widen(mask_ref[pl.ds(start, rows_slots), :])

    def norm_step(block, _):
        place = pl.ds(pl.multiple_of(block * rows_slots, rows_slots), rows_slots)
        mid = own_ref[block, 0].astype(F32) + middle[place, :] * own_mask(block)
        middle[place, :] = mid
        unit, _ = normalise(mid)
        second[place, :] = (unit * gain).astype(BF16)
        return 0

    for block in range(blocks):
        norm_step(block, 0)

    pre[...] = dot(second[...], w1[...])
    cot = jnp.concatenate([own_ref[b, 1] for b in range(blocks)], axis=0)
    grad_hidden[...] = dot_nt(cot, w2[...])

    def gelu_step(i, _):
        place = pl.ds(pl.multiple_of(i * 16, 16), 16)
        x = pre[place, :]
        phi = 0.5 * (1.0 + lax.erf(x * np.float32(0.5**0.5)))
        hidden[place, :] = (x * phi).astype(BF16)
        slope = phi + x * jnp.exp(x * x * -0.5) * np.float32((2 * np.pi) ** -0.5)
        grad_pre[place, :] = (grad_hidden[place, :] * slope).astype(BF16)
        return 0

    lax.fori_loop(0, OWN // 16, gelu_step, 0, unroll=True)

    out_ref[...] = (middle[...] + dot(hidden[...], w2[...])).astype(BF16)
    grad_2 = dot_tn(hidden[...], cot).astype(BF16)
    grad_1 = dot_tn(second[...], grad_pre[...]).astype(BF16)
    grad_middle_ref[...] = dot_nt(grad_pre[...], w1[...])

    def back_step(block, total):
        place = pl.ds(pl.multiple_of(block * rows_slots, rows_slots), rows_slots)
        unit, inverse = normalise(middle[place, :])
        grad = grad_middle_ref[place, :]
        total = total + jnp.sum(grad * unit, 0, keepdims=True)
        grad = own_ref[block, 1].astype(F32) + norm_back(grad, gain, unit, inverse)
        grad_middle_ref[place, :] = grad
        second[place, :] = (grad * own_mask(block)).astype(BF16)
        return total

    gain_two = jnp.zeros((1, D), F32)
    for block in range(blocks):
        gain_two = back_step(block, gain_two)
    gain_ref[...] = gain_two

    grad_o = []
    lane_own = lax.broadcasted_iota(jnp.int32, (OWN, LANES), 1)
    for h in range(HEADS):
        grad_o.append(dot_tn(att[h], second[...])[:HEAD_DIM])
        grad_att = dot_nt(second[...], wo[h]).astype(BF16).astype(F32)
        scaled = (grad_att * sums[h]).astype(BF16).astype(F32)
        shift = -jnp.sum(scaled * outs[h], -1, keepdims=True)
        high = shift.astype(BF16).astype(F32)
        lifted = jnp.where(
            lane_own == HEAD_DIM, high, jnp.where(lane_own == HEAD_DIM + 1, shift - high, scaled)
        )
        lifted_ref[h] = lifted.astype(BF16)

    for half in range(2):
        wire[:, half * span : (half + 1) * span] = dot_nt(
            grad_1[:, half * FF // 2 : (half + 1) * FF // 2], sel_1_ref[...]
        )
    grad_o = jnp.concatenate(grad_o, axis=0).astype(BF16)
    wire[...] += dot_nt(grad_o, sel_o_ref[...])

    def deliver(lanes):
        for m in range(parts):
            parted[m] = wire[:, m * LANES : (m + 1) * LANES].astype(BF16)
        for z in range(parts // 2):
            put_blocks(keep_ref, z, lanes, parted[2 * z + core])
            put_blocks(send_ref, z, lanes, parted[2 * z + 1 - core])

    deliver(slice(0, LANES))
    total = None
    for g in range(4):
        rows = [
            grad_2[r * 4 * per_block + g * per_block : r * 4 * per_block + (g + 1) * per_block]
            for r in range(blocks)
        ]
        part = dot_nt(jnp.concatenate(rows, axis=0), sel_2_ref[g])
        total = part if total is None else total + part
    wire[...] = total
    deliver(slice(LANES, 2 * LANES))


def attention_back_kernel(
    soft_ref,
    lifted_ref,
    q_ref,
    k_ref,
    v_ref,
    wqkv_ref,
    part_ref,
    triple,
    grad_q,
    scores,
    grad_scores,
    part,
    *,
    blocks,
):
    core = lax.axis_index("core")
    rows_slots = OWN // blocks
    for h in range(HEADS):
        tile = slice(h * LANES, (h + 1) * LANES)
        scores[...] = dot_nt(v_ref[h], lifted_ref[h])

        def back_step(i, _, h=h):
            place = pl.ds(pl.multiple_of(i * 64, 64), 64)
            grad_scores[place, :] = (soft_ref[h, place, :].astype(F32) * scores[place, :]).astype(
                BF16
            )
            return 0

        lax.fori_loop(0, SLOTS // 64, back_step, 0, unroll=True)
        grad_q[:, tile] = (dot_tn(k_ref[h], grad_scores[...]).T.astype(BF16) * HEAD_DIM ** (-0.5)).astype(
            BF16
        )
        triple[0, :, tile] = dot(grad_scores[...], q_ref[h]).astype(BF16)
        triple[1, :, tile] = dot(soft_ref[h], lifted_ref[h]).astype(BF16)

    part[...] = dot_nt(triple[0], wqkv_ref[1]) + dot_nt(triple[1], wqkv_ref[2])
    from_q = dot_nt(grad_q[...], wqkv_ref[0])
    for block in range(blocks):
        here = slice(block * rows_slots, (block + 1) * rows_slots)
        place = pl.ds(pl.multiple_of((block * 2 + core) * rows_slots, rows_slots), rows_slots)
        part[place, :] += from_q[here]
    part_ref[...] = part[...].astype(BF16)


def scan_back_kernel(
    starts,
    width,
    own_ref,
    mask_ref,
    part_ref,
    got_ref,
    mixed_ref,
    first_ref,
    table_ref,
    rates_ref,
    wu_ref,
    triple_ref,
    grad_q_ref,
    scanned_ref,
    gain_two_ref,
    sel_u_ref,
    sel_rc_ref,
    sel_q_ref,
    keep_ref,
    send_ref,
    back_ref,
    gs_wide,
    gs_pairs,
    gt_wide,
    gt_pairs,
    xs_wide,
    xs_pairs,
    xt_wide,
    xt_pairs,
    rows_wide,
    rows_pairs,
    cols_wide,
    cols_pairs,
    grads_ref,
    own,
    own_tail,
    together,
    lag_sums,
    lag_lines,
    lag_rows,
    mixed_back,
    wire,
    parted,
    grad_w_ref,
):
    gs, gt = (gs_wide, gs_pairs), (gt_wide, gt_pairs)
    xs, xt = (xs_wide, xs_pairs), (xt_wide, xt_pairs)
    rows, cols = (rows_wide, rows_pairs), (cols_wide, cols_pairs)
    core = lax.axis_index("core")
    blocks, _, rows_slots, _ = own_ref.shape
    half_rows = rows_slots // GRID
    own_rows = GRID // 2
    parts = sel_rc_ref.shape[0] // LANES
    put_columns(*xs, mixed_ref[...].astype(F32))
    grads = (part_ref[...].astype(F32) + got_ref[...].astype(F32)) * widen(mask_ref[...])
    grads = grads.astype(BF16)
    grads_ref[...] = grads
    put_columns(*gs, grads.astype(F32))

    def place_of(block):
        return pl.ds(pl.multiple_of((block * 2 + core) * rows_slots, rows_slots), rows_slots)

    for source, dst in ((grads_ref, gt), (mixed_ref, xt)):
        for block in range(blocks):
            here = slice(block * rows_slots, (block + 1) * rows_slots)
            value = source[place_of(block), :].astype(F32)
            own[here, :] = value[:, :LANES]
            own_tail[here, :] = value[:, LANES:]
        put_rows(*dst, own, own_tail[...], together)

    grad_w = [None, dot_tn(scanned_ref[...], triple_ref[0]), dot_tn(scanned_ref[...], triple_ref[1])]
    for block in range(blocks):
        here = slice(block * rows_slots, (block + 1) * rows_slots)
        term = dot_tn(scanned_ref[place_of(block), :], grad_q_ref[here, :])
        grad_w[0] = term if block == 0 else grad_w[0] + term
    for third in range(3):
        grad_w_ref[third] = grad_w[third].astype(BF16)

    for kind, sublane in units(0):
        step = gt[kind].shape[0] // GRID
        for t, value in enumerate(toeplitz(gt, table_ref, 0, kind, sublane, -1)):
            rows[kind][t * step + sublane : t * step + sublane + 8, :] = value

    def col_step(index, _):
        for kind, sublane in units(index):
            step = gs[kind].shape[0] // GRID
            found = toeplitz(gs, table_ref, 1, kind, sublane, -1, half_rows)
            for t, value in enumerate(found):
                cols[kind][pl.ds(pl.multiple_of(t * step + sublane, 8), 8), :] = value
        return 0

    lax.fori_loop(0, 2, col_step, 0)

    lag_sums[...] = jnp.zeros_like(lag_sums)

    for kind, sublane in units(0):
        add_lags(lag_sums, 0, kind, sublane, gt, xt)

    def lag_step(index, _):
        for kind, sublane in units(index):
            add_lags(lag_sums, 1, kind, sublane, gs, xs, half_rows)
        return 0

    lax.fori_loop(0, 2, lag_step, 0)
    for way in range(2):
        for kind in range(2):
            for lag, value in enumerate(gather_lags(lag_sums, way, kind)):
                lag_lines[way, kind, lag] = value
            lag_lines[way, kind, LAGS - 1] = jnp.zeros((8, LANES), F32)

    for way in range(2):
        lag_rows[way, :, :LANES] = jnp.sum(lag_lines[way, 0], 1)
        tail = jnp.sum(lag_lines[way, 1], 1)
        tail = tail[:, : D - LANES] + tail[:, D - LANES :]
        lag_rows[way, :, LANES:] = pair_lanes(tail, jnp.zeros_like(tail))

    decay, coef = rates_ref[: 4 * STATE], rates_ref[4 * STATE :]

    to_rate, to_coef = [], []
    for d in range(4):
        way, side = divmod(d, 2)
        rate = decay[d * STATE : (d + 1) * STATE]
        rate_sum = jnp.zeros((STATE, 2 * LANES), F32)
        coef_sum = jnp.broadcast_to(lag_rows[way, CENTER : CENTER + 1, :], (STATE, 2 * LANES))
        for k in range(1, GRID):
            at = CENTER - k if side else CENTER + k
            line = jnp.broadcast_to(lag_rows[way, at : at + 1, :], (STATE, 2 * LANES))
            scaled = line * jnp.exp(rate * float(-k))
            coef_sum = coef_sum + scaled
            rate_sum = rate_sum - scaled * float(k)
        to_rate.append(rate_sum)
        to_coef.append(coef_sum)
    to_rate, to_coef = jnp.concatenate(to_rate, axis=0), jnp.concatenate(to_coef, axis=0)
    grad_rc = jnp.concatenate([to_rate * coef, to_coef], axis=0).T[:D].astype(BF16)

    def join_step(i, _):
        for row, value in join_rows(i, own_rows, rows, cols):
            at = ((row // half_rows * 2 + core) * half_rows + row % half_rows) * GRID
            mask = mask_ref[pl.ds(pl.multiple_of(at, GRID), GRID), :]
            place = pl.ds(pl.multiple_of(row * GRID, GRID), GRID)
            mixed_back[place, :] = (value * widen(mask)).astype(BF16)
        return 0

    lax.fori_loop(0, own_rows // 2, join_step, 0, unroll=True)
    grad_u = dot_tn(first_ref[...], mixed_back[...]).astype(BF16)
    grad_first = dot_nt(mixed_back[...], wu_ref[...])
    back_ref[...] = grad_first
    gain_one = jnp.zeros((1, D), F32)
    for block in range(blocks):
        here = slice(block * rows_slots, (block + 1) * rows_slots)
        unit, _ = normalise(own_ref[block, 0].astype(F32))
        gain_one = gain_one + jnp.sum(grad_first[here] * unit, 0, keepdims=True)

    wire[...] = dot_nt(grad_u, sel_u_ref[...]) + dot_nt(grad_rc, sel_rc_ref[...])
    for third in range(3):
        span = slice(starts[third] * LANES, (starts[third] + width) * LANES)
        wire[:, span] += dot_nt(grad_w_ref[third], sel_q_ref[third])
    for m in range(parts):
        parted[m] = wire[:, m * LANES : (m + 1) * LANES].astype(BF16)
    for z in range(parts // 2):
        put_late(keep_ref, z, parted[2 * z + core])
        put_late(send_ref, z, parted[2 * z + 1 - core])

    lines = []
    for value in (gain_one, gain_two_ref[...]):
        high = value.astype(BF16).astype(F32)
        for piece in (high, value - high):
            lines.append(piece[:, :LANES])
            lines.append(
                jnp.concatenate([piece[:, LANES:], jnp.zeros((1, 2 * LANES - D), F32)], axis=1)
            )
    lines = jnp.concatenate(lines, axis=0).astype(BF16)
    for ref in (keep_ref, send_ref):
        ref[ref.shape[0] - 1, :8] = lines
        ref[ref.shape[0] - 1, 8:] = jnp.zeros((ref.shape[1] - 8, LANES), BF16)


def last_norm_kernel(own_ref, gains_ref, back_ref, grad_middle_ref, *routed_refs):
    _, _, slots, _ = own_ref.shape
    gain = gains_ref[0:1, :]
    for k, routed in enumerate(routed_refs):
        block = lax.axis_index("row") ^ k
        place = pl.ds(pl.multiple_of(block * slots, slots), slots)
        unit, inverse = normalise(own_ref[block, 0].astype(F32))
        grad = grad_middle_ref[place, :] + norm_back(back_ref[place, :], gain, unit, inverse)
        routed[...] = pack(grad.astype(BF16))


def aligned(rows):
    return (rows + 15) // 16 * 16


def spare_lanes(rows, parts):
    return rows >= 32 and 4 * (D // parts) + 32 <= LANES


def split(value):
    high = value.astype(BF16).astype(F32)
    return jnp.concatenate([high, value - high], axis=0)


def early_sum_kernel(out_own_ref, keep_ref, got_ref, *out_refs):
    _, depth, rows, _ = keep_ref.shape
    slots = OWN // len(out_refs)
    block_rows = aligned(rows)
    for k, out_ref in enumerate(out_refs):
        block = lax.axis_index("row") ^ k
        for z in range(depth):
            total = keep_ref[block, z].astype(F32) + got_ref[block, z].astype(F32)
            out_ref[z * block_rows : z * block_rows + rows] = total.astype(BF16)
        place = pl.ds(pl.multiple_of(block * slots, slots), slots)
        out_ref[depth * block_rows :] = fold(pack(out_own_ref[place, :]))


def late_sum_kernel(depth, keep_ref, got_ref, *refs):
    count = len(refs) // 2
    routed_refs, out_refs = refs[:count], refs[count:]
    rows = keep_ref.shape[1]
    block_rows = aligned(rows)
    last = keep_ref.shape[0] - 1
    gains = keep_ref[last, :8].astype(F32) + got_ref[last, :8].astype(F32)
    lines = []
    for g in range(2):
        for lane in range(2):
            at = 4 * g + lane
            lines.append(gains[at : at + 1] + gains[at + 2 : at + 3])
    gains = split(jnp.concatenate(lines, axis=0))
    gains = jnp.concatenate([gains, jnp.zeros((8, LANES), F32)], axis=0).astype(BF16)
    for k, out_ref in enumerate(out_refs):
        block = lax.axis_index("row") ^ k
        for z in range(depth):
            at = block * depth + z
            total = keep_ref[at].astype(F32) + got_ref[at].astype(F32)
            out_ref[z * block_rows : z * block_rows + rows] = total.astype(BF16)
        out_ref[depth * block_rows : depth * block_rows + 16] = gains
        out_ref[depth * block_rows + 16 :] = routed_refs[k][...]


def row_sum_kernel(blocks, depth, rows, *refs):
    early_refs, late_refs, out_refs = refs[:blocks], refs[blocks : 2 * blocks], refs[2 * blocks :]
    block_rows = aligned(rows)
    gains = late_refs[0][depth * block_rows : depth * block_rows + 16].astype(F32)
    for k in range(1, blocks):
        gains = gains + late_refs[k][depth * block_rows : depth * block_rows + 16].astype(F32)
    gains = split(gains[:4] + gains[4:8])
    for j, out_ref in enumerate(out_refs):
        z = lax.axis_index("z") ^ j
        place = pl.ds(pl.multiple_of(z * block_rows, 16), block_rows)
        early = early_refs[0][place, :].astype(F32)
        late = late_refs[0][place, :].astype(F32)
        for k in range(1, blocks):
            early = early + early_refs[k][place, :].astype(F32)
            late = late + late_refs[k][place, :].astype(F32)
        if spare_lanes(rows, 2 * depth):
            chunks = [gains[:, q * 32 : (q + 1) * 32] for q in range(4)]
            chunks.append(jnp.zeros((rows - 32, 32), F32))
            early = jnp.concatenate([early[:, :-32], jnp.concatenate(chunks, axis=0)], axis=1)
        else:
            out_ref[rows:, :LANES] = jnp.concatenate(
                [gains, jnp.zeros((8, LANES), F32)], axis=0
            ).astype(BF16)
            out_ref[rows:, LANES:] = jnp.zeros((16, 2 * LANES), BF16)
        out_ref[:rows, LANES:] = early[:rows].astype(BF16)
        out_ref[:rows, :LANES] = late[:rows].astype(BF16)


def final_kernel(parts, *refs):
    final_body(parts, refs[: parts // 2], *refs[parts // 2 :])


def final_body(
    parts,
    got_refs,
    g1_ref,
    g2_ref,
    wu_ref,
    rate_ref,
    coef_ref,
    qkv_ref,
    wo_ref,
    fc1_ref,
    fc2_ref,
):
    a_u, a_r, a_q, (o_u, o_r, o_c, o_q) = late_layout(parts)
    total = got_refs[0][...].astype(F32)
    for ref in got_refs[1:]:
        total = total + ref[...].astype(F32)
    early = total[: fc1_ref.shape[0], LANES:]
    total = total[:, :LANES]
    rows = fc1_ref.shape[0]
    weights = total[:rows]
    if spare_lanes(rows, parts):
        gains = jnp.concatenate(
            [early[q * 8 : (q + 1) * 8, 2 * LANES - 32 :] for q in range(4)], axis=1
        )
    else:
        gains = total[rows:]
    turned = weights.T
    wu_ref[...] = turned[o_u : o_u + a_u]
    rate_ref[...] = turned[o_r : o_r + a_r]
    coef_ref[...] = turned[o_c : o_c + a_r]
    qkv_ref[...] = weights[:, o_q : o_q + a_q]
    gains = gains[0:4] + gains[4:8]
    for g, ref in ((0, g1_ref), (1, g2_ref)):
        ref[...] = jnp.concatenate(
            [gains[2 * g : 2 * g + 1], gains[2 * g + 1 : 2 * g + 2, : D - LANES]], axis=1
        )
    a_1, a_o = FF // parts, D // parts
    fc1_ref[...] = early[:, :a_1]
    wo_ref[...] = early[:, :LANES].T[a_1 : a_1 + a_o]
    turned = early[:, LANES:].T
    fc2_ref[...] = jnp.concatenate([turned[g * a_o : (g + 1) * a_o] for g in range(4)], axis=1)


def per_device(
    patches, valid_mask, norm_gains, w_u, decay_rate, out_coef, w_qkv, w_o, w_fc1, w_fc2, cotangent
):
    images, rows_here, _, _ = patches.shape
    depth, blocks = lax.axis_size("z"), lax.axis_size("row")
    parts = 2 * depth
    rows_slots = rows_here // 2 * GRID
    packed_rows = rows_slots * 3 // 2
    swap = [(0, 1), (1, 0)]
    shape = jax.ShapeDtypeStruct

    def planes(slots):
        return [pltpu.VMEM((slots, LANES), F32), pltpu.VMEM((slots // 2, LANES), F32)]

    def swapped(value):
        return lax.ppermute(value, "core", swap)

    def exchanged(values, axis):
        size = len(values)
        return [values[0]] + [
            lax.ppermute(values[k], axis, [(i, i ^ k) for i in range(size)]) for k in range(1, size)
        ]

    def to_chips(value, j):
        pairs = []
        for home in range(2):
            for source in range(blocks):
                target, image = divmod(source ^ j, images)
                pairs.append((home * blocks + source, target * blocks + home * images + image))
        return lax.ppermute(value, ("core", "row"), pairs)

    starts, width = late_spans(parts)
    sel_1, sel_o, sel_2 = early_selections(parts)

    rows_weight = w_u.shape[0]
    payload = shape((2 * packed_rows + 16, LANES), BF16)
    shard = shape((rows_weight, 3 * LANES), BF16)
    sources = [value.reshape(images, rows_here * GRID, D) for value in (patches, cotangent)]
    if rows_weight % 16 == 0:
        weights, *routed = pl.pallas_call(
            depart_kernel,
            name="depart",
            out_shape=(shard,) + (payload,) * blocks,
            in_specs=[VMEM] * 10,
            out_specs=[VMEM] * (1 + blocks),
            compiler_params=compiler(LARGE),
        )(
                w_u.T,
            decay_rate.T,
            out_coef.T,
            w_o.T,
            w_fc2.T,
            w_qkv,
            w_fc1,
            *sources,
            valid_mask,
        )
    else:

        def fill(pieces):
            joined = jnp.concatenate(pieces, axis=1)
            return jnp.pad(joined, ((0, 0), (0, LANES - joined.shape[1])))

        weights = jnp.concatenate(
            [
                fill([w_u, decay_rate, out_coef, w_qkv]),
                fill([w_fc1, w_o]),
                fill([w_fc2[g * rows_weight : (g + 1) * rows_weight] for g in range(4)]),
            ],
            axis=1,
        )
        routed = pl.pallas_call(
            route_kernel,
            name="route",
            out_shape=(payload,) * blocks,
            in_specs=[VMEM] * 3,
            out_specs=[VMEM] * blocks,
            compiler_params=compiler(LARGE),
        )(*sources, valid_mask)

    weights = jnp.stack(exchanged([weights] * depth, "z"))
    weights = exchanged([weights] * blocks, "row")
    weights = weights + [swapped(value) for value in weights]
    routed = [to_chips(value, j) for j, value in enumerate(routed)]
    own, first_own, mask, sel_u, sel_rc, sel_q = pl.pallas_call(
        lambda *refs: norm_kernel(starts, parts, *refs),
        name="first_norm",
        out_shape=(
            shape((blocks, 2, rows_slots, D), BF16),
            shape((OWN, D), BF16),
            shape((SLOTS, LANES), F32),
            shape((parts * LANES, D), BF16),
            shape((parts * LANES, LANES), BF16),
            shape((3, width * LANES, TILE), BF16),
        ),
        in_specs=[VMEM] * (1 + blocks),
        out_specs=[VMEM] * 6,
        compiler_params=compiler(8 << 20),
    )(norm_gains, *routed)
    first_other = swapped(first_own)

    head_own = shape((HEADS, OWN, LANES), BF16)
    head_all = shape((HEADS, SLOTS, LANES), BF16)
    part_scratch = pltpu.VMEM((parts, blocks, rows_weight, LANES), BF16)
    q, k, v, scanned, mixed, table, rates, wu, wqkv = pl.pallas_call(
        lambda *refs: scan_kernel(starts, width, *refs, blocks=blocks),
        name="scan_forward",
        out_shape=(
            head_own,
            head_all,
            head_all,
            shape((SLOTS, D), BF16),
            shape((SLOTS, D), BF16),
            shape((2, 2, 9 * 16, LANES), F32),
            shape((LANES, 2 * LANES), F32),
            shape((D, D), BF16),
            shape((3, D, TILE), BF16),
        ),
        in_specs=[VMEM] * (6 + 2 * blocks),
        out_specs=[VMEM] * 9,
        scratch_shapes=[part_scratch]
        + planes(SLOTS) * 4
        + [pltpu.VMEM((OWN, D), BF16), pltpu.VMEM((SLOTS, D), BF16)]
        + [pltpu.VMEM((2, 2, LAGS, LANES), F32)],
        compiler_params=compiler(),
    )(first_own, first_other, mask, sel_u, sel_rc, sel_q, *weights)

    wire_early = shape((blocks, depth, rows_weight, 2 * LANES), BF16)
    soft, lifted, out_own, grad_middle, gain_two, early_keep, early_send = pl.pallas_call(
        middle_kernel,
        name="attention_and_feed_forward",
        out_shape=(
            shape((HEADS, SLOTS, OWN), BF16),
            head_own,
            shape((OWN, D), BF16),
            shape((OWN, D), F32),
            shape((1, D), F32),
            wire_early,
            wire_early,
        ),
        in_specs=[VMEM] * (9 + 2 * blocks),
        out_specs=[VMEM] * 7,
        scratch_shapes=[
            part_scratch,
            pltpu.VMEM((SLOTS, OWN), F32),
            pltpu.VMEM((HEADS, LANES, D), BF16),
            pltpu.VMEM((D, FF), BF16),
            pltpu.VMEM((FF, D), BF16),
            pltpu.VMEM((HEADS, OWN, LANES), BF16),
            pltpu.VMEM((HEADS, OWN, LANES), F32),
            pltpu.VMEM((HEADS, OWN, LANES), F32),
            pltpu.VMEM((OWN, D), F32),
            pltpu.VMEM((OWN, D), BF16),
            pltpu.VMEM((OWN, FF), F32),
            pltpu.VMEM((OWN, FF), F32),
            pltpu.VMEM((OWN, FF), BF16),
            pltpu.VMEM((OWN, FF), BF16),
            pltpu.VMEM((D, parts * LANES), F32),
            pltpu.VMEM((parts, D, LANES), BF16),
        ],
        compiler_params=compiler(),
    )(own, mask, norm_gains, sel_1, sel_o, sel_2, q, k, v, *weights)

    early_recv = swapped(early_send)

    part, triple, grad_q = pl.pallas_call(
        lambda *refs: attention_back_kernel(*refs, blocks=blocks),
        name="attention_backward",
        out_shape=(
            shape((SLOTS, D), BF16),
            shape((2, SLOTS, TILE), BF16),
            shape((OWN, TILE), BF16),
        ),
        in_specs=[VMEM] * 6,
        out_specs=[VMEM] * 3,
        scratch_shapes=[
            pltpu.VMEM((SLOTS, OWN), F32),
            pltpu.VMEM((SLOTS, OWN), BF16),
            pltpu.VMEM((SLOTS, D), F32),
        ],
        compiler_params=compiler(),
    )(soft, lifted, q, k, v, wqkv)

    early_keep, early_recv, part = lax.optimization_barrier((early_keep, early_recv, part))
    payload = shape((depth * aligned(rows_weight) + packed_rows // 2, 2 * LANES), BF16)
    early = pl.pallas_call(
        early_sum_kernel,
        name="early_sum",
        out_shape=(payload,) * blocks,
        in_specs=[VMEM] * 3,
        out_specs=[VMEM] * blocks,
        compiler_params=compiler(8 << 20),
    )(out_own, early_keep, early_recv)
    early, part = lax.optimization_barrier((early, part))
    part_got = swapped(part)
    early = exchanged(early, "row")
    wire_late = shape((blocks * depth + 1, rows_weight, LANES), BF16)
    late_keep, late_send, back = pl.pallas_call(
        lambda *refs: scan_back_kernel(starts, width, *refs),
        name="scan_backward",
        out_shape=(wire_late, wire_late, shape((OWN, D), F32)),
        in_specs=[VMEM] * 16,
        out_specs=[VMEM] * 3,
        scratch_shapes=planes(SLOTS) + planes(OWN) + planes(SLOTS) + planes(OWN) * 3
        + [
            pltpu.VMEM((SLOTS, D), BF16),
            pltpu.VMEM((OWN, LANES), F32),
            pltpu.VMEM((OWN, D - LANES), F32),
            pltpu.VMEM((OWN // 2, LANES), F32),
            pltpu.VMEM((2, 2, 9 * 16, 8, LANES), F32),
            pltpu.VMEM((2, 2, LAGS, 8, LANES), F32),
            pltpu.VMEM((2, LAGS, 2 * LANES), F32),
            pltpu.VMEM((OWN, D), BF16),
            pltpu.VMEM((D, parts * LANES), F32),
            pltpu.VMEM((parts, D, LANES), BF16),
            pltpu.VMEM((3, D, TILE), BF16),
        ],
        compiler_params=compiler(),
    )(
        own,
        mask,
        part,
        part_got,
        mixed,
        first_own,
        table,
        rates,
        wu,
        triple,
        grad_q,
        scanned,
        gain_two,
        sel_u,
        sel_rc,
        sel_q,
    )
    late_keep, late_send, early = lax.optimization_barrier((late_keep, late_send, early))
    payload = shape((packed_rows, LANES), BF16)
    routed = pl.pallas_call(
        last_norm_kernel,
        name="last_norm",
        out_shape=(payload,) * blocks,
        in_specs=[VMEM] * 4,
        out_specs=[VMEM] * blocks,
        compiler_params=compiler(8 << 20),
    )(own, norm_gains, back, grad_middle)
    payload = shape((depth * aligned(rows_weight) + 16 + packed_rows, LANES), BF16)
    late = pl.pallas_call(
        lambda *refs: late_sum_kernel(depth, *refs),
        name="late_sum",
        out_shape=(payload,) * blocks,
        in_specs=[VMEM] * (2 + blocks),
        out_specs=[VMEM] * blocks,
        compiler_params=compiler(8 << 20),
    )(late_keep, swapped(late_send), *routed)
    late = exchanged(late, "row")
    final_rows = rows_weight if spare_lanes(rows_weight, parts) else rows_weight + 16
    summed = pl.pallas_call(
        lambda *refs: row_sum_kernel(blocks, depth, rows_weight, *refs),
        name="row_sum",
        out_shape=(shape((final_rows, 3 * LANES), BF16),) * depth,
        in_specs=[VMEM] * (2 * blocks),
        out_specs=[VMEM] * depth,
        compiler_params=compiler(8 << 20),
    )(*early, *late)
    summed = exchanged(summed, "z")

    chosen = pl.pallas_call(
        choose_kernel,
        name="choose",
        out_shape=shape((images, 2 * packed_rows, LANES), BF16),
        in_specs=[VMEM] * (2 * blocks),
        out_specs=VMEM,
        compiler_params=compiler(8 << 20),
    )(*early, *late)
    whole = shape((images, rows_here * GRID, D), BF16)
    block_out, grad_patches = pl.pallas_call(
        home_kernel,
        name="home",
        out_shape=(whole, whole),
        in_specs=[VMEM] * (1 + 2 * blocks),
        out_specs=[VMEM] * 2,
        compiler_params=compiler(8 << 20),
    )(swapped(chosen), *early, *late)

    summed, block_out, grad_patches = lax.optimization_barrier((summed, block_out, grad_patches))
    turned = (4 * STATE // parts, rows_weight)
    g1, g2, f_u, f_rate, f_coef, f_qkv, f_o, f_1, f_2 = pl.pallas_call(
        lambda *refs: final_kernel(parts, *refs),
        name="final_sum",
        out_shape=(
            shape((1, D), F32),
            shape((1, D), F32),
            shape((D // parts, rows_weight), F32),
            shape(turned, F32),
            shape(turned, F32),
            shape((rows_weight, 3 * D // parts), F32),
            shape((D // parts, rows_weight), F32),
            shape((rows_weight, FF // parts), F32),
            shape((D // parts, 4 * rows_weight), F32),
        ),
        in_specs=[VMEM] * depth,
        out_specs=[VMEM] * 9,
        compiler_params=compiler(8 << 20),
    )(*summed)
    return (
        block_out.reshape(patches.shape),
        grad_patches.reshape(patches.shape),
        g1.reshape(D),
        g2.reshape(D),
        f_u.T,
        f_rate.T,
        f_coef.T,
        f_qkv,
        f_o.T,
        f_1,
        f_2.T,
    )


def solution(mesh):
    images, rows = mesh.devices.shape
    fine = Mesh(mesh.devices.reshape(images // 2, 2, rows), ("z", "core", "row"))
    img = ("z", "core")
    grid = P(img, "row", None, None)
    weight = P("row", img)
    in_specs = (grid, P(img, None, None), P()) + (weight,) * 7 + (grid,)
    out_specs = (grid, grid, P(), P()) + (weight,) * 7
    return jax.shard_map(
        per_device, mesh=fine, in_specs=in_specs, out_specs=out_specs, check_vma=False
    )
```
